128 devices in a mesh: ctx: 16 (over z, x), exp: 8 (over y, core).
Axes of the slice: x: 4, y: 4, z: 4, core: 2. Of those that a mesh axis runs over, the one named last changes fastest.
Arguments:
- tokens: bfloat16 [8, 2048, 768], P('exp', 'ctx'), may hold values from -6 to 6
- gain_attn: bfloat16 [768], P(('ctx', 'exp')), may hold values from 0.5 to 1.5
- w_qkv: bfloat16 [768, 2304], P(('ctx', 'exp')), may hold values from -0.21875 to 0.21875
- w_attn_out: bfloat16 [768, 768], P(('ctx', 'exp')), may hold values from -1.75 to 1.75
- rel_table: bfloat16 [32, 12], replicated, may hold values from -4 to 4
- gain_moe: bfloat16 [768], P(('ctx', 'exp')), may hold values from 0.5 to 1.5
- w_in: bfloat16 [128, 768, 1536], P(('ctx', 'exp')), may hold values from -0.21875 to 0.21875
- w_out: bfloat16 [128, 1536, 768], P(('ctx', 'exp')), may hold values from -0.109375 to 0.109375
- expert_ids: int32 [8, 2048, 2], P('exp', 'ctx'), may hold values from 0 to 63, all different within a row; in each aligned block of 128 rows (0 to 127, 128 to 255, ..., all dimensions but the last counted through in order) at most 8 rows name the same one
- gate_values: float32 [8, 2048, 2], P('exp', 'ctx'), may hold values from 0.25 to 1
- doc_ids: int32 [8, 2048], P('exp', 'ctx'), may hold values from 0 to 3, never falling along the last dimension, each value on 1 to 1984 neighbouring positions
- cotangent: bfloat16 [8, 2048, 768], P('exp', 'ctx'), may hold values from -6 to 6
Outputs:
- block_out: bfloat16 [8, 2048, 768], P('exp', 'ctx')
- input_grad: bfloat16 [8, 2048, 768], P('exp', 'ctx')
- gate_grad: float32 [8, 2048, 2], P('exp', 'ctx')
- gain_attn_grad: float32 [768], P(('ctx', 'exp'))
- qkv_grad: float32 [768, 2304], P(('ctx', 'exp'))
- attn_out_grad: float32 [768, 768], P(('ctx', 'exp'))
- table_grad: float32 [32, 12], replicated
- gain_moe_grad: float32 [768], P(('ctx', 'exp'))
- expert_in_grad: float32 [128, 768, 1536], P(('ctx', 'exp'))
- expert_out_grad: float32 [128, 1536, 768], P(('ctx', 'exp'))
The draws below stay inside these ranges and needn't reach their ends.
Inputs may be any that keep to these rules, and one draw needn't show every extreme that they name: `expert_ids`: among the tokens of one device (128 in a row of a sequence) no expert is named more than 8 times, a bound that some block reaches; a token's two experts differ. `doc_ids`: document numbers never fall along a sequence, every number appears, and one document of each sequence holds exactly 1984 tokens.
All inputs are finite; a program needn't handle non-finite values.
Results may differ from the reference program's by a relative error of at most 0.024.
Values may be sent and summed in bfloat16 or wider, within the bound.
A program may use at most 192 MiB of HBM per device.

```python
import math
import jax
import jax.numpy as jnp
import numpy as np
from jax import lax

D = 768
H = 12
HD = 64
FF = 3072
BUCKETS = 32
DOCS = 4
TOK_DEV = 128
SEQUENCE_LENGTH = 2048
SEQS = 8
EXPERTS = 64
CAP = 8


def steps_of(stream_key, shape, cuts, low, top_value):
    factor_of = 1.0
    for axis_at, blocks in cuts:
        heights = jax.random.uniform(jax.random.fold_in(jax.random.fold_in(stream_key, 6), axis_at), (blocks,), jnp.float32, low / len(cuts), top_value / len(cuts))
        factor_of = factor_of * jnp.repeat(jnp.exp(heights), shape[axis_at] // blocks).reshape((-1,) + (1,) * (len(shape) - 1 - axis_at))
    return factor_of


def profile(number_of, total, most, lean):
    loads = [(1 << 20) // math.isqrt(standing ** lean) + 1 for standing in range(2, number_of + 1)]
    spare, given = total - most - (number_of - 1), [1] * (number_of - 1)
    while spare > 0:
        movable = [i for i in range(number_of - 1) if given[i] < most]
        pool, budget = sum([loads[i] for i in movable]), spare
        for i in movable:
            more = min(most - given[i], max(1, budget * loads[i] // pool), spare)
            given[i] = given[i] + more
            spare = spare - more
    return np.array([most] + given)


def ragged_sizes(key, amount, total, limit, skew):
    if amount == 2:
        one = jax.random.randint(key, (), max(1, total - limit), min(limit, total - 1) + 1)
        return jnp.stack([one, total - one])
    tallies = jnp.asarray(profile(amount, total, limit, skew), jnp.int32)
    couples = (amount - 1) // 2
    source_of, sink = tallies[1:1 + 2 * couples:2], tallies[2:2 + 2 * couples:2]
    room = jnp.minimum(source_of - 1, limit - sink)
    passed = jax.random.randint(jax.random.fold_in(key, 1), (couples,), 0, 1 << 20) % (room + 1)
    tallies = tallies.at[1:1 + 2 * couples:2].set(source_of - passed).at[2:2 + 2 * couples:2].set(sink + passed)
    return tallies[jax.random.permutation(jax.random.fold_in(key, 2), amount)]


def assign_block(stream_key, own, number, rows, number_of, top, reach, skew):
    ranking = jax.random.permutation(stream_key, number_of)
    crowded, usual = portions_of(number_of, rows * top, reach, skew, True), portions_of(number_of, rows * top, reach, skew, False)
    places = jnp.arange(number_of)

    def named(sizes, rotation):
        used = int((sizes > 0).sum())
        fixed = max(1, used // 4)
        passed = fixed + (places - fixed + rotation * (used - fixed)) % max(1, number_of - fixed)
        return jnp.zeros((number_of,), jnp.int32).at[ranking[jnp.where(places < fixed, places, passed)]].set(jnp.asarray(sizes, jnp.int32))

    sizes = jnp.where(number % 4 == 0, named(crowded, number // 4), named(usual, number - number // 4 - 1))
    mixed = jax.random.permutation(jax.random.fold_in(own, 3), number_of)
    source_of, receiver = mixed[0:number_of // 2 * 2:2], mixed[1:number_of // 2 * 2:2]
    room = jnp.minimum(sizes[source_of] - 1, reach - sizes[receiver]) // 2
    room = jnp.where((source_of == ranking[0]) | (receiver == ranking[0]) | (sizes[receiver] == 0), 0, jnp.maximum(room, 0))
    passed = jax.random.randint(jax.random.fold_in(own, 4), (number_of // 2,), 0, 1 << 20) % (room + 1)
    sizes = sizes.at[source_of].add(-passed).at[receiver].add(passed)
    items = jnp.searchsorted(jnp.cumsum(sizes), jnp.arange(rows * top), side="right").astype(jnp.int32)
    table = items.reshape(top, rows).T
    table = table[jax.random.permutation(jax.random.fold_in(own, 1), rows)]
    rotation = jax.random.randint(jax.random.fold_in(own, 2), (rows, 1), 0, top)
    return jnp.take_along_axis(table, (jnp.arange(top)[None, :] + rotation) % top, axis=1)


def portions_of(count, total, bound, lean, full):
    weights = [(1 << 20) // math.isqrt(rank ** lean) + 1 for rank in range(1, count + 1)]
    largest = bound if full else min(bound, max(-(-total // count), total * weights[0] // sum(weights)))
    least = 1 if total - largest >= count - 1 else 0
    holding, spare = [largest] + [least] * (count - 1), total - largest - least * (count - 1)
    while spare > 0:
        movable = [i for i in range(1, count) if holding[i] < largest] or [i for i in range(1, count) if holding[i] < bound]
        mass, left = sum([weights[i] for i in movable]), spare
        for i in movable:
            extra = min(bound - holding[i], max(1, left * weights[i] // mass), spare)
            holding[i] = holding[i] + extra
            spare = spare - extra
    return np.array(holding)


def bell_draw(own_key, shape, spread, reach, pieces=(), held_as=jnp.bfloat16):
    level = steps_of(own_key, shape, pieces, -0.22, 0.18) if pieces else 1.0
    drawn = jax.random.normal(own_key, shape, jnp.float32) * spread * level
    return jnp.minimum(jnp.maximum(drawn, -reach), reach).astype(held_as)


def setup_inputs(seed: int = 0) -> dict:
    splits = jax.random.split(jax.random.key(seed), 13)
    tokens = bell_draw(splits[0], (SEQS, SEQUENCE_LENGTH, D), 1.0, 6.0, ((0, 8), (1, 16)))
    gain_attn = jnp.clip(1.0 + 0.1 * jax.random.normal(splits[1], (D,), jnp.float32), 0.5, 1.5).astype(jnp.bfloat16)
    w_qkv = bell_draw(splits[2], (D, 3 * D), D ** -0.5, 0.21875, ((0, 128),))
    w_attn_out = bell_draw(splits[3], (D, D), (D // 64) ** -0.5, 1.75, ((0, 128),))
    rel_table = bell_draw(splits[4], (BUCKETS, H), 1.0, 4.0)
    gain_moe = jnp.clip(1.0 + 0.1 * jax.random.normal(splits[5], (D,), jnp.float32), 0.5, 1.5).astype(jnp.bfloat16)
    w_in = bell_draw(splits[6], (2 * EXPERTS, D, FF // 2), D ** -0.5, 0.21875, ((0, 128),))
    w_out = bell_draw(splits[7], (2 * EXPERTS, FF // 2, D), FF ** -0.5, 0.109375, ((0, 128),))
    expert_ids_keys = jax.random.split(jax.random.fold_in(splits[8], 1), SEQS * SEQUENCE_LENGTH // TOK_DEV)
    expert_ids_turns = jax.random.permutation(jax.random.fold_in(splits[8], 3), SEQS * SEQUENCE_LENGTH // TOK_DEV)
    expert_ids = jax.vmap(lambda own, number: assign_block(jax.random.fold_in(splits[8], 2), own, number, TOK_DEV, EXPERTS, 2, CAP, 2))(expert_ids_keys, expert_ids_turns).reshape((SEQS, SEQUENCE_LENGTH, 2))
    gate_values = jnp.clip(0.25 + 0.75 * jax.random.uniform(splits[9], (SEQS, SEQUENCE_LENGTH, 2), jnp.float32) ** steps_of(splits[9], (SEQS, SEQUENCE_LENGTH, 2), ((0, 8), (1, 16)), -0.2, 0.2), 0.25, 1.0)
    doc_ids = jax.vmap(lambda own: jnp.searchsorted(jnp.cumsum(ragged_sizes(own, DOCS, SEQUENCE_LENGTH, SEQUENCE_LENGTH - TOK_DEV // 2, 0)), jnp.arange(SEQUENCE_LENGTH), side="right"))(jax.random.split(splits[10], SEQS)).reshape((SEQS, SEQUENCE_LENGTH)).astype(jnp.int32)
    cotangent = bell_draw(splits[11], (SEQS, SEQUENCE_LENGTH, D), 1.0, 6.0, ((0, 8), (1, 16)))
    return dict(tokens=tokens, gain_attn=gain_attn, w_qkv=w_qkv, w_attn_out=w_attn_out, rel_table=rel_table, gain_moe=gain_moe, w_in=w_in, w_out=w_out, expert_ids=expert_ids, gate_values=gate_values, doc_ids=doc_ids, cotangent=cotangent)


norm_eps = 1e-06
bucket_edges = np.concatenate([np.arange(1, 17), np.ceil(16.0 * 8.0 ** (np.arange(1, 16) / 16.0))]).astype(np.int32)
largest_scores = lax.Precision.HIGHEST

@jax.custom_vjp
def low(v):
    return lax.optimization_barrier(v.astype(jnp.bfloat16)).astype(jnp.float32)

@jax.custom_vjp
def reduced_backward(v):
    return v

def low_keep(v):
    return (low(v), None)

def low_pass(kept, grad):
    return (grad,)

def back_keep(v):
    return (v, None)

def back_low(kept, grad):
    return (low(grad),)
low.defvjp(low_keep, low_pass)
reduced_backward.defvjp(back_keep, back_low)

def scale_rows(values, gain):
    return values * lax.rsqrt(lax.optimization_barrier(jnp.mean(values * values, axis=-1, keepdims=True)) + norm_eps) * gain

def bucket_index(distance):
    return lax.optimization_barrier(jnp.sum((distance[..., None] >= jnp.asarray(bucket_edges)).astype(jnp.int32), axis=-1))

def attend(normed, doc_row, qkv_weight, bias_table):
    qkv_all = reduced_backward(low(jnp.dot(normed, qkv_weight, precision=largest_scores)))
    queries = qkv_all[:, :D].reshape(SEQUENCE_LENGTH, H, HD)
    key_heads = qkv_all[:, D:2 * D].reshape(SEQUENCE_LENGTH, H, HD)
    value_heads = qkv_all[:, 2 * D:].reshape(SEQUENCE_LENGTH, H, HD)
    block_rows = min(512, SEQUENCE_LENGTH)
    key_pos = jnp.arange(SEQUENCE_LENGTH, dtype=jnp.int32)

    def one_block(block_start):
        query_block = lax.dynamic_slice_in_dim(queries, block_start, block_rows, 0)
        query_pos = block_start + jnp.arange(block_rows, dtype=jnp.int32)
        query_docs = lax.dynamic_slice_in_dim(doc_row, block_start, block_rows, 0)
        distance = query_pos[:, None] - key_pos[None, :]
        scores = jnp.einsum('qhd,khd->hqk', query_block, key_heads, precision=largest_scores) * 0.125
        scores = scores + jnp.transpose(jnp.take(bias_table, bucket_index(distance), axis=0), (2, 0, 1))
        scores = reduced_backward(scores)
        allowed = (distance >= 0) & (query_docs[:, None] == doc_row[None, :])
        scores = jnp.where(allowed[None], scores, -1e+30)
        weights_soft = jax.nn.softmax(scores, axis=-1)
        mixed_out = jnp.einsum('hqk,khd->qhd', low(weights_soft), value_heads, precision=largest_scores)
        return mixed_out.reshape(block_rows, D)
    starts = jnp.arange(SEQUENCE_LENGTH // block_rows, dtype=jnp.int32) * block_rows
    return lax.map(jax.checkpoint(one_block), starts).reshape(SEQUENCE_LENGTH, D)

def reference(tokens, gain_attn, w_qkv, w_attn_out, rel_table, gain_moe, w_in, w_out, expert_ids, gate_values, doc_ids, cotangent):
    blocks = SEQS * SEQUENCE_LENGTH // TOK_DEV
    route_ids = expert_ids.reshape(blocks, TOK_DEV * 2).astype(jnp.int32)
    route_marks = (route_ids[:, :, None] == jnp.arange(EXPERTS, dtype=jnp.int32)[None, None, :]).astype(jnp.int32)
    earlier = jnp.cumsum(route_marks, axis=1) - route_marks
    slot_of = lax.optimization_barrier(jnp.sum(earlier * route_marks, axis=2))
    slot_place = (jnp.arange(blocks, dtype=jnp.int32)[:, None] * CAP + slot_of).reshape(-1).astype(jnp.int32)
    flat_ids = route_ids.reshape(-1)
    token_of = (jnp.arange(blocks * TOK_DEV * 2, dtype=jnp.int32) // 2).astype(jnp.int32)
    slot_token = jnp.zeros((EXPERTS, blocks * CAP), jnp.int32).at[flat_ids, slot_place].set(token_of)

    def forward(inputs, gain_one, qkv_weight, attention_weight, bias_table, gain_two, in_weight, out_weight, gate_float):
        normed = low(scale_rows(inputs, gain_one))
        mixed_all = lax.map(lambda pair_args: attend(pair_args[0], pair_args[1], qkv_weight, bias_table), (normed, doc_ids))
        attention_values = reduced_backward(low(mixed_all))
        residual_branch = reduced_backward(jnp.einsum('tqp,pf->tqf', attention_values, attention_weight, precision=largest_scores))
        middle = inputs + residual_branch
        moe_in = low(scale_rows(middle, gain_two)).reshape(SEQS * SEQUENCE_LENGTH, D)
        gate_slot = jnp.zeros((EXPERTS, blocks * CAP), jnp.float32).at[flat_ids, slot_place].set(gate_float.reshape(-1))
        in_full = jnp.transpose(in_weight.reshape(EXPERTS, 2, D, FF // 2), (0, 2, 1, 3)).reshape(EXPERTS, D, FF)
        out_full = out_weight.reshape(EXPERTS, FF, D)

        def expert(triple):
            first_w, second_w, rows_index = triple
            rows_in = jnp.take(moe_in, rows_index, axis=0)
            pre_act = reduced_backward(jnp.dot(rows_in, first_w, precision=largest_scores))
            hidden = low(jax.nn.gelu(pre_act))
            return reduced_backward(low(jnp.dot(hidden, second_w, precision=largest_scores)))
        expert_outs = lax.map(jax.checkpoint(expert), (in_full, out_full, slot_token))
        weighted = (expert_outs * gate_slot[:, :, None]).reshape(-1, D)
        moe_sum = jnp.zeros((SEQS * SEQUENCE_LENGTH, D), jnp.float32).at[slot_token.reshape(-1)].add(weighted)
        return middle + moe_sum.reshape(SEQS, SEQUENCE_LENGTH, D)
    result, pullback = jax.vjp(forward, tokens.astype(jnp.float32), gain_attn.astype(jnp.float32), w_qkv.astype(jnp.float32), w_attn_out.astype(jnp.float32), rel_table.astype(jnp.float32), gain_moe.astype(jnp.float32), w_in.astype(jnp.float32), w_out.astype(jnp.float32), gate_values.astype(jnp.float32))
    gradients = pullback(cotangent.astype(jnp.float32))
    return (result.astype(jnp.bfloat16), gradients[0].astype(jnp.bfloat16), gradients[8], gradients[1], gradients[2], gradients[3], gradients[4], gradients[5], gradients[6], gradients[7])
```

```python
import functools

import jax
import jax.numpy as jnp
import numpy as np
from jax import lax
from jax.experimental import pallas as pl
from jax.experimental.pallas import tpu as pltpu
from jax.sharding import Mesh
from jax.sharding import PartitionSpec as P

D = 768
H = 12
HD = 64
BUCKETS = 32
GROUPS = 4
GH = H // GROUPS
GW = GH * HD
TOK = 128
CTX = ("ctx_0", "ctx_1")
EXP = ("exp_0", "exp_1")
AXES = ("ctx_0", "ctx_1", "exp_0", "exp_1")
MESH = pl.DeviceIdType.MESH
ANY = pl.BlockSpec(memory_space=pl.ANY)
BF = jnp.bfloat16
F32 = jnp.float32

norm_eps = 1e-06
bucket_edges = [int(e) for e in np.concatenate(
    [np.arange(1, 17), np.ceil(16.0 * 8.0 ** (np.arange(1, 16) / 16.0))]
).astype(np.int32)]
masked = -1e30


def scale_rows(values, gain):
    return values * lax.rsqrt(jnp.mean(values * values, axis=-1, keepdims=True) + norm_eps) * gain


def place():
    return tuple(lax.axis_index(a) for a in AXES)


def chip_of(z, x, y):
    return (z * 4 + x) * 4 + y


def chip_peer(i, z, x, y):
    return (z + i // 16) % 4, (x + (i // 4) % 4) % 4, (y + i % 4) % 4


def loop(first, last, body):
    lax.fori_loop(first, last, lambda i, carry: (body(i), carry)[1], 0)


def signal(device):
    pl.semaphore_signal(
        pltpu.get_barrier_semaphore(), inc=1, device_id=device, device_id_type=MESH
    )


def arrive(count):
    pl.semaphore_wait(pltpu.get_barrier_semaphore(), count)


def push(src, dst, send, recv, device):
    pltpu.make_async_remote_copy(
        src_ref=src, dst_ref=dst, send_sem=send, recv_sem=recv, device_id=device, device_id_type=MESH
    ).start()


def keep(src, dst, sem):
    pltpu.make_async_copy(src, dst, sem).start()


def wait_bytes(ref, sem):
    pltpu.make_async_copy(ref, ref, sem).wait()


def comm_call(kernel, outs, scratch, collective_id, name):
    return pl.pallas_call(
        kernel,
        out_shape=outs,
        in_specs=None,
        out_specs=jax.tree.map(lambda _: ANY, outs),
        scratch_shapes=scratch,
        compiler_params=pltpu.CompilerParams(
            collective_id=collective_id, has_side_effects=True, vmem_limit_bytes=32 * 2**20
        ),
        name=name,
    )


def run_comm(kernel, args, outs, scratch, collective_id, name):
    return pl.pallas_call(
        kernel,
        out_shape=outs,
        in_specs=[ANY] * len(args),
        out_specs=jax.tree.map(lambda _: ANY, outs),
        scratch_shapes=scratch,
        compiler_params=pltpu.CompilerParams(
            collective_id=collective_id, has_side_effects=True, vmem_limit_bytes=32 * 2**20
        ),
        name=name,
    )(*args)


DMA = pltpu.SemaphoreType.DMA


def start_kernel(tok, wmsg, rows, tok_all, w_all, rows_all, send, recv, core_recv):
    z, x, y, c = place()
    me = chip_of(z, x, y)
    sib = (z, x, y, 1 - c)

    def greet(i):
        signal((*chip_peer(i, z, x, y), c))

    loop(1, 64, greet)
    signal(sib)
    arrive(64)
    for k in range(1, 4):
        push(tok, tok_all.at[z], send.at[0], recv.at[0], ((z + k) % 4, x, y, c))
    keep(tok, tok_all.at[z], recv.at[0])

    def weights(i):
        there = chip_peer(i, z, x, y)
        push(wmsg.at[there[0]], w_all.at[me, c], send.at[1], recv.at[1], (*there, c))

    loop(1, 64, weights)
    keep(wmsg.at[z], w_all.at[me, c], recv.at[1])

    def routes(i):
        there = chip_peer(i, z, x, y)
        push(rows.at[chip_of(*there)], rows_all.at[c, me], send.at[2], recv.at[2], (*there, c))

    loop(1, 64, routes)
    keep(rows.at[me], rows_all.at[c, me], recv.at[2])
    wait_bytes(w_all.at[:, c], recv.at[1])
    push(w_all.at[:, c], w_all.at[:, c], send.at[3], core_recv.at[0], sib)
    wait_bytes(rows_all.at[c], recv.at[2])
    push(rows_all.at[c], rows_all.at[c], send.at[4], core_recv.at[1], sib)
    wait_bytes(tok_all, recv.at[0])
    wait_bytes(w_all.at[:, 1 - c], core_recv.at[0])
    wait_bytes(rows_all.at[1 - c], core_recv.at[1])
    wait_bytes(tok_all.at[pl.ds(0, 3)], send.at[0])
    wait_bytes(w_all.at[pl.ds(0, 63), c], send.at[1])
    wait_bytes(rows_all.at[c, pl.ds(0, 63)], send.at[2])
    wait_bytes(w_all.at[:, c], send.at[3])
    wait_bytes(rows_all.at[c], send.at[4])


def start_exchange(tok, wmsg, rows):
    return run_comm(
        start_kernel,
        (tok, wmsg, rows),
        (
            jax.ShapeDtypeStruct((4, TOK, D), BF),
            jax.ShapeDtypeStruct((64, 2, 8, 3 * GW), BF),
            jax.ShapeDtypeStruct((2, 64, 8, D), BF),
        ),
        [DMA((5,)), DMA((3,)), DMA((2,))],
        0,
        "start_exchange",
    )


def dispatch_kernel(rows, rows_all, send, recv, core_recv):
    z, x, y, c = place()
    me = chip_of(z, x, y)
    sib = (z, x, y, 1 - c)

    def greet(i):
        signal((*chip_peer(i, z, x, y), c))

    loop(1, 64, greet)
    signal(sib)
    arrive(64)

    def routes(i):
        there = chip_peer(i, z, x, y)
        push(rows.at[chip_of(*there)], rows_all.at[c, me], send.at[0], recv.at[0], (*there, c))

    loop(1, 64, routes)
    keep(rows.at[me], rows_all.at[c, me], recv.at[0])
    wait_bytes(rows_all.at[c], recv.at[0])
    push(rows_all.at[c], rows_all.at[c], send.at[1], core_recv, sib)
    wait_bytes(rows_all.at[1 - c], core_recv)
    wait_bytes(rows_all.at[c, pl.ds(0, 63)], send.at[0])
    wait_bytes(rows_all.at[c], send.at[1])


def dispatch(rows):
    return run_comm(
        dispatch_kernel,
        (rows,),
        jax.ShapeDtypeStruct((2, 64, 8, D), BF),
        [DMA((2,)), DMA((1,)), DMA],
        1,
        "dispatch",
    )


def home_kernel(halves, home, own, other, total, send, recv, core_recv, own_sem):
    z, x, y, c = place()
    me = chip_of(z, x, y)
    sib = (z, x, y, 1 - c)

    def greet(i):
        signal((*chip_peer(i, z, x, y), c))

    loop(1, 64, greet)
    signal(sib)
    arrive(64)
    push(halves.at[1 - c], other, send.at[0], core_recv, sib)
    keep(halves.at[c], own, own_sem)
    wait_bytes(own, own_sem)
    wait_bytes(other, core_recv)

    def both(i):
        there = chip_peer(i, z, x, y)
        at = chip_of(*there)
        total[at] = (own[at].astype(F32) + other[at].astype(F32)).astype(BF)
        push(total.at[at], home.at[me], send.at[1], recv.at[0], (*there, c))

    loop(1, 64, both)
    total[me] = (own[me].astype(F32) + other[me].astype(F32)).astype(BF)
    keep(total.at[me], home.at[me], recv.at[0])
    wait_bytes(home, recv.at[0])
    wait_bytes(total.at[pl.ds(0, 63)], send.at[1])
    wait_bytes(other, send.at[0])


def go_home(halves, collective_id, name):
    rows = pltpu.VMEM((64, 8, D), BF)
    return run_comm(
        home_kernel,
        (halves,),
        jax.ShapeDtypeStruct((64, 8, D), BF),
        [rows, rows, rows, DMA((2,)), DMA((1,)), DMA, DMA],
        collective_id,
        name,
    )


def z_kernel(blocks, out, send, recv):
    z, x, y, c = place()
    for k in range(1, 4):
        signal(((z + k) % 4, x, y, c))
    arrive(3)
    for k in range(1, 4):
        there = (z + k) % 4
        push(blocks.at[there], out.at[z], send, recv, (there, x, y, c))
    keep(blocks.at[z], out.at[z], recv)
    wait_bytes(out, recv)
    wait_bytes(out.at[pl.ds(0, 3)], send)


def z_exchange(blocks, collective_id, name):
    return run_comm(
        z_kernel,
        (blocks,),
        jax.ShapeDtypeStruct(blocks.shape, blocks.dtype),
        [DMA, DMA],
        collective_id,
        name,
    )


def kv_kernel(kv, kv_all, send, recv):
    z, x, y, c = place()
    for k in range(1, 4):
        signal((z, (x + k) % 4, y, c))
    arrive(3)
    for k in range(1, 4):
        for b in range(4):
            push(kv.at[b], kv_all.at[b, x], send, recv, (z, (x + k) % 4, y, c))
    for b in range(4):
        keep(kv.at[b], kv_all.at[b, x], recv)
    wait_bytes(kv_all, recv)
    wait_bytes(kv_all.at[pl.ds(0, 3)], send)


def kv_gather(kv):
    return run_comm(
        kv_kernel,
        (kv,),
        jax.ShapeDtypeStruct((4, 4, TOK, 2 * GW), BF),
        [DMA, DMA],
        2,
        "kv_gather",
    )


def kv_back_kernel(dkv, branch, parts, branch_all, send, recv):
    z, x, y, c = place()
    for k in range(1, 4):
        signal((z, (x + k) % 4, y, c))
        signal(((z + k) % 4, x, y, c))
    arrive(6)
    for k in range(1, 4):
        there = (x + k) % 4
        for b in range(4):
            push(dkv.at[b, there], parts.at[x, b], send.at[0], recv.at[0], (z, there, y, c))
    for k in range(1, 4):
        push(branch, branch_all.at[z], send.at[1], recv.at[1], ((z + k) % 4, x, y, c))
    for b in range(4):
        keep(dkv.at[b, x], parts.at[x, b], recv.at[0])
    keep(branch, branch_all.at[z], recv.at[1])
    wait_bytes(parts, recv.at[0])
    wait_bytes(branch_all, recv.at[1])
    wait_bytes(parts.at[pl.ds(0, 3)], send.at[0])
    wait_bytes(branch_all.at[pl.ds(0, 3)], send.at[1])


def kv_back(dkv, branch):
    return run_comm(
        kv_back_kernel,
        (dkv, branch),
        (
            jax.ShapeDtypeStruct((4, 4, TOK, 2 * GW), BF),
            jax.ShapeDtypeStruct((4, TOK, D), BF),
        ),
        [DMA((2,)), DMA((2,))],
        3,
        "kv_back",
    )


def device_of(d):
    return d // 32, (d // 8) % 4, (d // 2) % 4, d % 2


def sums_kernel(
    qkv, att, small, qkv_out, att_out, small_out,
    qkv_in, att_in, small_in, qkv_sum, att_sum, small_sum, send, recv, out_sem,
):
    z, x, y, c = place()
    p = x * 8 + y * 2 + c
    me = z * 32 + p

    def peer(i):
        return (z, (x + i // 8) % 4, (y + (i // 2) % 4) % 4, (c + i % 2) % 2)

    loop(1, 32, lambda i: signal(peer(i)))
    source = me // 4

    def greet(k):
        from_me = (k == z) & (source == p)

        @pl.when(jnp.logical_not(from_me))
        def _():
            signal((k, source // 8, (source // 2) % 4, source % 2))

    loop(0, 4, greet)
    arrive(31 + 4 - jnp.where(source == p, 1, 0))

    def out(i):
        there = peer(i)
        q = there[1] * 8 + there[2] * 2 + there[3]
        push(qkv.at[q], qkv_in.at[p], send.at[0], recv.at[0], there)
        push(att.at[q], att_in.at[p], send.at[1], recv.at[1], there)
        push(small.at[q], small_in.at[p], send.at[2], recv.at[2], there)

    loop(1, 32, out)
    keep(qkv.at[p], qkv_in.at[p], recv.at[0])
    keep(att.at[p], att_in.at[p], recv.at[1])
    keep(small.at[p], small_in.at[p], recv.at[2])
    wait_bytes(qkv_in, recv.at[0])
    total = qkv_in[0].astype(F32)
    for q in range(1, 32):
        total = total + qkv_in[q].astype(F32)
    for k in range(4):
        qkv_sum[k, 0:6, :] = total[6 * k : 6 * k + 6]
        qkv_sum[k, 6:8, :] = jnp.zeros((2, 3 * GW), F32)
    wait_bytes(small_in, recv.at[2])
    small_total = small_in[0]
    for q in range(1, 32):
        small_total = small_total + small_in[q]
    small_sum[...] = small_total

    def final(k):
        d = 4 * p + k
        there = device_of(d)

        @pl.when(d != me)
        def _():
            push(qkv_sum.at[k], qkv_out.at[z], send.at[3], recv.at[3], there)
            push(small_sum, small_out.at[z], send.at[4], recv.at[4], there)

        @pl.when(d == me)
        def _():
            keep(qkv_sum.at[k], qkv_out.at[z], recv.at[3])
            keep(small_sum, small_out.at[z], recv.at[4])

    loop(0, 4, final)
    wait_bytes(att_in, recv.at[1])
    att_total = att_in[0].astype(F32)
    for q in range(1, 32):
        att_total = att_total + att_in[q].astype(F32)
    att_sum[...] = att_total
    keep(att_sum, att_out, out_sem)
    wait_bytes(att_sum, out_sem)
    wait_bytes(qkv_out, recv.at[3])
    wait_bytes(small_out, recv.at[4])
    wait_bytes(qkv_in.at[pl.ds(0, 31)], send.at[0])
    wait_bytes(att_in.at[pl.ds(0, 31)], send.at[1])
    wait_bytes(small_in.at[pl.ds(0, 31)], send.at[2])

    def sent(k):
        @pl.when(4 * p + k != me)
        def _():
            wait_bytes(qkv_sum.at[0], send.at[3])
            wait_bytes(small_sum, send.at[4])

    loop(0, 4, sent)


def weight_sums(qkv, att, small):
    return run_comm(
        sums_kernel,
        (qkv, att, small),
        (
            jax.ShapeDtypeStruct((4, 8, 3 * GW), F32),
            jax.ShapeDtypeStruct((8, D), F32),
            jax.ShapeDtypeStruct((4, 8, 128), F32),
        ),
        [
            pltpu.VMEM((32, 24, 3 * GW), BF),
            pltpu.VMEM((32, 8, D), BF),
            pltpu.VMEM((32, 8, 128), F32),
            pltpu.VMEM((4, 8, 3 * GW), F32),
            pltpu.VMEM((8, D), F32),
            pltpu.VMEM((8, 128), F32),
            DMA((5,)),
            DMA((5,)),
            DMA,
        ],
        4,
        "weight_sums",
    )


NT = (((1,), (1,)), ((), ()))
NN = (((1,), (0,)), ((), ()))
TN = (((0,), (0,)), ((), ()))


def dot(a, b, dims):
    return lax.dot_general(a, b, dims, preferred_element_type=F32)


def near_distance(dist):
    a = lax.broadcasted_iota(jnp.int32, (TOK, TOK), 0)
    b = lax.broadcasted_iota(jnp.int32, (TOK, TOK), 1)
    return dist * TOK + a - b


def table_kind(zq, zk, x, kx):
    return jnp.clip((zq - zk) * 4 + x - kx + 1, 0, 3)


def attn_forward_kernel(pos, tab, q, kv, qd, kd, out, p_out, bias, v_s, s_s):
    h = pl.program_id(0)
    x = pos[0]

    @pl.when(h == 0)
    def _():
        v_s[...] = kv[:, GW:]

    for dist in range(2):
        n = near_distance(dist)
        acc = jnp.full((TOK, TOK), tab[0, h], F32)
        for k, edge in enumerate(bucket_edges):
            acc = jnp.where(n >= edge, tab[k + 1, h], acc)
        bias[1 + dist] = jnp.where(n >= 0, acc, masked)
    bias[0] = jnp.full((TOK, TOK), masked, F32)
    far = tab[BUCKETS - 1, h]
    bias[3] = jnp.full((TOK, TOK), far, F32)
    head_cols = lax.broadcasted_iota(jnp.int32, (1, GW), 1) // HD == h
    for zk in range(4):
        qm = jnp.where(head_cols, q[zk * TOK :, :] * 0.125, 0.0).astype(BF)
        s_s[zk * TOK :, zk * 512 : (zk + 1) * 512] = dot(qm, kv[zk * 512 : (zk + 1) * 512, :GW], NT)
    for zq in range(4):
        rows = pl.ds(zq * TOK, TOK)
        docs = qd[rows, :]
        top = None
        for zk in range(zq + 1):
            for kx in range(4):
                cols = pl.ds((zk * 4 + kx) * TOK, TOK)
                s = s_s[rows, cols]
                if zk < zq - 1:
                    s = s + far
                else:
                    s = s + bias[table_kind(zq, zk, x, kx)]
                s = jnp.where(docs == kd[:, cols], s, masked)
                s_s[rows, cols] = s
                top = s if top is None else jnp.maximum(top, s)
        top = jnp.max(top, axis=1, keepdims=True)
        total = jnp.zeros((TOK, TOK), F32)
        for kb in range(4 * (zq + 1)):
            cols = pl.ds(kb * TOK, TOK)
            e = jnp.exp(s_s[rows, cols] - top)
            s_s[rows, cols] = e
            total = total + e
        inv = 1.0 / jnp.sum(total, axis=1, keepdims=True)
        for kb in range(4 * (zq + 1)):
            cols = pl.ds(kb * TOK, TOK)
            p_out[0, rows, cols] = (s_s[rows, cols] * inv).astype(BF)
        width = (zq + 1) * 512
        o = dot(p_out[0, rows, :width], v_s[:width, :], NN).astype(BF)

        @pl.when(h == 0)
        def _():
            out[rows, :] = o

        @pl.when(h > 0)
        def _():
            out[rows, :] = jnp.where(head_cols, o, out[rows, :])


def whole(shape):
    return pl.BlockSpec(shape, lambda h: (0,) * len(shape))


def attn_forward(pos, tab, q, kv, qd, kd):
    smem = pl.BlockSpec(memory_space=pltpu.SMEM)
    return pl.pallas_call(
        attn_forward_kernel,
        grid=(GH,),
        out_shape=(
            jax.ShapeDtypeStruct((512, GW), BF),
            jax.ShapeDtypeStruct((GH, 512, 2048), BF),
        ),
        in_specs=[
            smem, smem, whole((512, GW)), whole((2048, 2 * GW)), whole((512, 1)), whole((1, 2048)),
        ],
        out_specs=(whole((512, GW)), pl.BlockSpec((1, 512, 2048), lambda h: (h, 0, 0))),
        scratch_shapes=[
            pltpu.VMEM((4, TOK, TOK), F32),
            pltpu.VMEM((2048, GW), BF),
            pltpu.VMEM((512, 2048), F32),
        ],
        compiler_params=pltpu.CompilerParams(
            dimension_semantics=("arbitrary",), vmem_limit_bytes=40 * 2**20
        ),
        name="attn_forward",
    )(pos, tab, q, kv, qd, kd)


def attn_backward_kernel(pos, p, q, kv, do, dq, dkv, tab, v_s, dk_s, dv_s, dp_s, ds_s, near):
    h = pl.program_id(0)
    x = pos[0]

    @pl.when(h == 0)
    def _():
        v_s[...] = kv[:, GW:]

    head_cols = lax.broadcasted_iota(jnp.int32, (1, GW), 1) // HD == h
    for zk in range(4):
        dm = jnp.where(head_cols, do[zk * TOK :, :], 0.0).astype(BF)
        cols = pl.ds(zk * 512, 512)
        dp_s[zk * TOK :, cols] = dot(dm, v_s[cols, :], NT)
        dv = dot(p[0, zk * TOK :, cols], dm, TN)

        @pl.when(h == 0)
        def _():
            dv_s[cols, :] = dv

        @pl.when(h > 0)
        def _():
            dv_s[cols, :] += dv

    near[...] = jnp.zeros_like(near)
    for zq in range(4):
        rows = pl.ds(zq * TOK, TOK)
        acc = jnp.zeros((TOK, TOK), F32)
        for kb in range(4 * (zq + 1)):
            cols = pl.ds(kb * TOK, TOK)
            acc = acc + p[0, rows, cols].astype(F32) * dp_s[rows, cols]
        delta = jnp.sum(acc, axis=1, keepdims=True)
        far = jnp.zeros((TOK, TOK), F32)
        for zk in range(zq + 1):
            for kx in range(4):
                cols = pl.ds((zk * 4 + kx) * TOK, TOK)
                ds = (p[0, rows, cols].astype(F32) * (dp_s[rows, cols] - delta)).astype(BF)
                ds_s[rows, cols] = ds
                if zk < zq - 1:
                    far = far + ds.astype(F32)
                else:
                    near[table_kind(zq, zk, x, kx)] += ds.astype(F32)
        near[3] += far
        width = (zq + 1) * 512
        o = (dot(ds_s[rows, :width], kv[:width, :GW], NN) * 0.125).astype(BF)

        @pl.when(h == 0)
        def _():
            dq[rows, :] = o

        @pl.when(h > 0)
        def _():
            dq[rows, :] = jnp.where(head_cols, o, dq[rows, :])

    for zk in range(4):
        qm = jnp.where(head_cols, q[zk * TOK :, :] * 0.125, 0.0).astype(BF)
        cols = pl.ds(zk * 512, 512)
        dk = dot(ds_s[zk * TOK :, cols], qm, TN)

        @pl.when(h == 0)
        def _():
            dk_s[cols, :] = dk

        @pl.when(h > 0)
        def _():
            dk_s[cols, :] += dk

    for dist in range(2):
        n = near_distance(dist)
        held = near[1 + dist]
        bounds = [-(10**6)] + bucket_edges + [10**6]
        for b in range(BUCKETS):
            low, high = bounds[b], bounds[b + 1]
            if high <= dist * TOK - TOK + 1 or low > dist * TOK + TOK - 1:
                if dist == 0:
                    tab[0, b : b + 1, :] = jnp.zeros((1, TOK), F32)
                continue
            part = jnp.sum(jnp.where((n >= low) & (n < high), held, 0.0), axis=0, keepdims=True)
            if dist == 0:
                tab[0, b : b + 1, :] = part
            else:
                tab[0, b : b + 1, :] += part
    tab[0, BUCKETS - 1 :, :] += jnp.sum(near[3], axis=0, keepdims=True)

    @pl.when(h == GH - 1)
    def _():
        dkv[:, :GW] = dk_s[...].astype(BF)
        dkv[:, GW:] = dv_s[...].astype(BF)


def attn_backward(pos, p, q, kv, do):
    smem = pl.BlockSpec(memory_space=pltpu.SMEM)
    return pl.pallas_call(
        attn_backward_kernel,
        grid=(GH,),
        out_shape=(
            jax.ShapeDtypeStruct((512, GW), BF),
            jax.ShapeDtypeStruct((2048, 2 * GW), BF),
            jax.ShapeDtypeStruct((GH, BUCKETS, TOK), F32),
        ),
        in_specs=[
            smem,
            pl.BlockSpec((1, 512, 2048), lambda h: (h, 0, 0)),
            whole((512, GW)), whole((2048, 2 * GW)), whole((512, GW)),
        ],
        out_specs=(
            whole((512, GW)),
            whole((2048, 2 * GW)),
            pl.BlockSpec((1, BUCKETS, TOK), lambda h: (h, 0, 0)),
        ),
        scratch_shapes=[
            pltpu.VMEM((2048, GW), BF),
            pltpu.VMEM((2048, GW), F32),
            pltpu.VMEM((2048, GW), F32),
            pltpu.VMEM((512, 2048), F32),
            pltpu.VMEM((512, 2048), BF),
            pltpu.VMEM((4, TOK, TOK), F32),
        ],
        compiler_params=pltpu.CompilerParams(
            dimension_semantics=("arbitrary",), vmem_limit_bytes=48 * 2**20
        ),
        name="attn_backward",
    )(pos, p, q, kv, do)


def per_device(
    tokens,
    gain_attn,
    w_qkv,
    w_attn_out,
    rel_table,
    gain_moe,
    w_in,
    w_out,
    expert_ids,
    gate_values,
    doc_ids,
    cotangent,
):
    z, x, y, c = place()
    experts = 64
    capacity = 8
    slots = experts * capacity
    own_tokens = tokens.reshape(TOK, D)
    grad_bf = cotangent.reshape(TOK, D)
    grad_out = grad_bf.astype(F32)

    route = expert_ids.reshape(TOK * 2)
    marks = (route[:, None] == jnp.arange(experts, dtype=jnp.int32)[None, :]).astype(jnp.int32)
    earlier = jnp.cumsum(marks, axis=0) - marks
    slot = route * capacity + jnp.sum(earlier * marks, axis=1)
    slot_pair = slot.reshape(TOK, 2)
    gates = gate_values.reshape(TOK, 2)
    slot_ids = jnp.arange(slots, dtype=jnp.int32)
    pick_0 = slot_pair[:, 0][:, None] == slot_ids[None, :]
    pick_1 = slot_pair[:, 1][:, None] == slot_ids[None, :]
    pick = (pick_0 | pick_1).astype(BF)
    gate_of = jnp.where(pick_0, gates[:, :1], 0.0) + jnp.where(pick_1, gates[:, 1:], 0.0)
    gate_slot = jnp.sum(gate_of, axis=0)
    d_eo = (dot(pick, grad_bf, TN) * gate_slot[:, None]).astype(BF).reshape(experts, capacity, D)

    slab = w_qkv.reshape(6, 3, GROUPS, GW).transpose(2, 0, 1, 3).reshape(GROUPS, 6, 3 * GW)
    notes = jnp.concatenate(
        [
            gain_attn, gain_moe, jnp.zeros((116,), BF),
            doc_ids.reshape(TOK).astype(BF), jnp.zeros((3 * GW - 256,), BF),
        ]
    )
    notes = jnp.concatenate([notes[None], jnp.zeros((1, 3 * GW), BF)], axis=0)
    message = jnp.concatenate([slab, jnp.broadcast_to(notes, (GROUPS, 2, 3 * GW))], axis=1)
    attention_weight = lax.all_gather(w_attn_out, AXES, axis=0, tiled=True)
    tok_all, w_all, d_eo_all = start_exchange(own_tokens, message, d_eo)

    weight = w_all[:, :, :6, :].reshape(D, 3 * GW)
    gain_one = w_all[:, :, 6, 0:6].reshape(D).astype(F32)
    gain_two = w_all[:, :, 6, 6:12].reshape(D).astype(F32)
    doc_rows = w_all[:, :, 6, 128:256].reshape(16, 4, 2, TOK)
    doc_rows = lax.dynamic_slice(doc_rows, (0, y, c, 0), (16, 1, 1, TOK)).reshape(16, TOK).astype(F32)
    key_docs = doc_rows.reshape(1, 2048)
    query_docs = lax.dynamic_slice(doc_rows.reshape(4, 4, TOK), (0, x, 0), (4, 1, TOK)).reshape(512, 1)

    inputs_all = tok_all.reshape(512, D).astype(F32)
    normed = scale_rows(inputs_all, gain_one).astype(BF)
    qkv = dot(normed, weight, NN).astype(BF)
    queries = qkv[:, :GW]
    kv_all = kv_gather(qkv[:, GW:].reshape(4, TOK, 2 * GW)).reshape(2048, 2 * GW)
    table = lax.dynamic_slice(rel_table, (0, z * GH), (BUCKETS, GH)).astype(F32)
    pos = jnp.full((1,), x, jnp.int32)
    attn_part, probs = attn_forward(pos, table, queries, kv_all, query_docs, key_docs)
    attn = z_exchange(attn_part.reshape(4, TOK, GW), 5, "attn_exchange")
    attn = attn.transpose(1, 0, 2).reshape(TOK, D)

    inputs = own_tokens.astype(F32)
    middle = inputs + dot(attn, attention_weight, NN)
    moe_float, norm_two_back = jax.vjp(scale_rows, middle, gain_two)
    moe_in = moe_float.astype(BF)
    send_rows = dot(pick, moe_in, TN).astype(BF).reshape(experts, capacity, D)
    rows = dispatch(send_rows).reshape(-1, D)
    first_half = w_in[0]
    second_half = w_out[0]
    d_rows = d_eo_all.reshape(-1, D)
    hidden_grad = dot(d_rows, second_half, NT)
    pre_act = dot(rows, first_half, NN)
    gelu_vals, gelu_back = jax.vjp(jax.nn.gelu, pre_act)
    hidden = gelu_vals.astype(BF)
    act_grad = gelu_back(hidden_grad)[0].astype(BF)
    in_halves = dot(act_grad, first_half, NT).astype(BF).reshape(2, experts, capacity, D)
    home = go_home(in_halves, 6, "home_grads").reshape(slots, D)
    moe_in_grad = dot(pick, home, NN)
    middle_part, gain_two_grad = norm_two_back(moe_in_grad)
    middle_grad = grad_out + middle_part
    branch = middle_grad.astype(BF)
    d_attn = dot(branch, attention_weight, NT).astype(BF)
    d_attn = d_attn.reshape(TOK, GROUPS, GW).transpose(1, 0, 2)
    d_attn = z_exchange(d_attn, 7, "d_attn_exchange").reshape(512, GW)

    d_q, d_kv, table_part = attn_backward(pos, probs, queries, kv_all, d_attn)
    kv_parts, branch_all = kv_back(d_kv.reshape(4, 4, TOK, 2 * GW), branch)
    d_kv = jnp.sum(kv_parts.astype(F32), axis=0).astype(BF).reshape(512, 2 * GW)
    d_qkv = jnp.concatenate([d_q, d_kv], axis=1)
    normed_part = dot(d_qkv, weight, NT).astype(BF).reshape(4, TOK, D)
    normed_part = z_exchange(normed_part, 8, "normed_grads")
    normed_grad = jnp.sum(normed_part.astype(F32), axis=0)
    _, norm_one_back = jax.vjp(scale_rows, inputs, gain_one)
    input_part, gain_one_grad = norm_one_back(normed_grad)
    input_grad = middle_grad + input_part

    out_halves = dot(hidden, second_half, NN).astype(BF).reshape(2, experts, capacity, D)
    expert_out = go_home(out_halves, 9, "home_outputs").reshape(slots, D)
    both = jnp.concatenate([pick_0, pick_1], axis=0).astype(BF)
    picked = dot(both, expert_out, NN).reshape(2, TOK, D)
    block_out = middle + gates[:, :1] * picked[0] + gates[:, 1:] * picked[1]
    gate_grad = jnp.sum(picked * grad_out[None], axis=2).T
    expert_out_grad = dot(hidden, d_rows, TN)[None]
    expert_in_grad = dot(rows, act_grad, TN)[None]

    qkv_part = dot(normed, d_qkv, TN).astype(BF).reshape(32, 24, 3 * GW)
    att_part = dot(attn_part, branch_all.reshape(512, D), TN).astype(BF).reshape(32, 6, D)
    att_part = jnp.pad(att_part, ((0, 0), (0, 2), (0, 0)))
    table_sum = jnp.sum(table_part, axis=2).reshape(1, GH * BUCKETS)
    small = jnp.stack(
        [
            jnp.pad(gain_one_grad.reshape(32, 24), ((0, 0), (0, 104))),
            jnp.pad(gain_two_grad.reshape(32, 24), ((0, 0), (0, 104))),
            jnp.broadcast_to(jnp.pad(table_sum, ((0, 0), (0, 128 - GH * BUCKETS))), (32, 128)),
        ],
        axis=1,
    )
    small = jnp.pad(small, ((0, 0), (0, 5), (0, 0)))
    qkv_sum, att_sum, small_sum = weight_sums(qkv_part, att_part, small)
    qkv_grad = qkv_sum[:, :6, :].reshape(GROUPS, 6, 3, GW).transpose(1, 2, 0, 3).reshape(6, 3 * D)
    attn_out_grad = att_sum[:6]
    place_in = (y * 2 + c) % 4
    gains = lax.dynamic_slice(jnp.sum(small_sum[:, :2, :], axis=0), (0, place_in * 6), (2, 6))
    table_grad = (
        small_sum[:, 2, : GH * BUCKETS].reshape(GROUPS * GH, BUCKETS).T
    )
    return (
        block_out.reshape(1, TOK, D).astype(BF),
        input_grad.reshape(1, TOK, D).astype(BF),
        gate_grad.reshape(1, TOK, 2),
        gains[0],
        qkv_grad,
        attn_out_grad,
        table_grad,
        gains[1],
        expert_in_grad,
        expert_out_grad,
    )


def solution(mesh):
    torus = Mesh(mesh.devices.reshape(4, 4, 4, 2), AXES)
    in_specs = (
        P(EXP, CTX, None),
        P(AXES),
        P(AXES, None),
        P(AXES, None),
        P(),
        P(AXES),
        P(AXES, None, None),
        P(AXES, None, None),
        P(EXP, CTX, None),
        P(EXP, CTX, None),
        P(EXP, CTX),
        P(EXP, CTX, None),
    )
    out_specs = (
        P(EXP, CTX, None),
        P(EXP, CTX, None),
        P(EXP, CTX, None),
        P(AXES),
        P(AXES, None),
        P(AXES, None),
        P(),
        P(AXES),
        P(AXES, None, None),
        P(AXES, None, None),
    )
    return jax.shard_map(
        per_device, mesh=torus, in_specs=in_specs, out_specs=out_specs, check_vma=False
    )
```

```python
import functools

import jax
import jax.numpy as jnp
import numpy as np
from jax import lax
from jax.experimental import pallas as pl
from jax.experimental.pallas import tpu as pltpu
from jax.sharding import Mesh
from jax.sharding import PartitionSpec as P

D = 768
H = 12
HD = 64
BUCKETS = 32
GROUPS = 4
GH = H // GROUPS
GW = GH * HD
TOK = 128
CTX = ("ctx_0", "ctx_1")
EXP = ("exp_0", "exp_1")
AXES = ("ctx_0", "ctx_1", "exp_0", "exp_1")
MESH = pl.DeviceIdType.MESH
ANY = pl.BlockSpec(memory_space=pl.ANY)
BF = jnp.bfloat16
F32 = jnp.float32

norm_eps = 1e-06
bucket_edges = [int(e) for e in np.concatenate(
    [np.arange(1, 17), np.ceil(16.0 * 8.0 ** (np.arange(1, 16) / 16.0))]
).astype(np.int32)]
masked = -1e30


def scale_rows(values, gain):
    return values * lax.rsqrt(jnp.mean(values * values, axis=-1, keepdims=True) + norm_eps) * gain


def place():
    return tuple(lax.axis_index(a) for a in AXES)


def chip_of(z, x, y):
    return (z * 4 + x) * 4 + y


def chip_peer(i, z, x, y):
    return (z + i // 16) % 4, (x + (i // 4) % 4) % 4, (y + i % 4) % 4


def loop(first, last, body):
    lax.fori_loop(first, last, lambda i, carry: (body(i), carry)[1], 0)


def signal(device):
    pl.semaphore_signal(
        pltpu.get_barrier_semaphore(), inc=1, device_id=device, device_id_type=MESH
    )


def arrive(count):
    pl.semaphore_wait(pltpu.get_barrier_semaphore(), count)


def push(src, dst, send, recv, device):
    pltpu.make_async_remote_copy(
        src_ref=src, dst_ref=dst, send_sem=send, recv_sem=recv, device_id=device, device_id_type=MESH
    ).start()


def keep(src, dst, sem):
    pltpu.make_async_copy(src, dst, sem).start()


def wait_bytes(ref, sem):
    pltpu.make_async_copy(ref, ref, sem).wait()


def comm_call(kernel, outs, scratch, collective_id, name):
    return pl.pallas_call(
        kernel,
        out_shape=outs,
        in_specs=None,
        out_specs=jax.tree.map(lambda _: ANY, outs),
        scratch_shapes=scratch,
        compiler_params=pltpu.CompilerParams(
            collective_id=collective_id, has_side_effects=True, vmem_limit_bytes=32 * 2**20
        ),
        name=name,
    )


def run_comm(kernel, args, outs, scratch, collective_id, name):
    return pl.pallas_call(
        kernel,
        out_shape=outs,
        in_specs=[ANY] * len(args),
        out_specs=jax.tree.map(lambda _: ANY, outs),
        scratch_shapes=scratch,
        compiler_params=pltpu.CompilerParams(
            collective_id=collective_id, has_side_effects=True, vmem_limit_bytes=32 * 2**20
        ),
        name=name,
    )(*args)


DMA = pltpu.SemaphoreType.DMA


def half_peer(i, z, x, y, c):
    return (z + i // 8) % 4, (x + (i // 2) % 4) % 4, c + 2 * ((y // 2 + i % 2) % 2), y % 2


def block_of(z, x, y):
    return pl.multiple_of((y % 2) * 512 + ((z * 4 + x) * 2 + y // 2) * 16, 16)


def greet_chips(z, x, y, c):
    loop(1, 32, lambda i: signal(half_peer(i, z, x, y, c)))

    @pl.when(y % 2 != c)
    def _():
        signal(half_peer(0, z, x, y, c))

    signal((z, x, y, 1 - c))
    return 32 + jnp.where(y % 2 == c, 0, 1)


def to_chips(z, x, y, c, source, target, send, recv):
    def one(i):
        there = half_peer(i, z, x, y, c)
        push(source(there), target, send, recv, there)

    loop(1, 32, one)
    first = half_peer(0, z, x, y, c)

    @pl.when(y % 2 == c)
    def _():
        keep(source(first), target, recv)

    @pl.when(y % 2 != c)
    def _():
        push(source(first), target, send, recv, first)


def sent_to_chips(rows, y, c, send):
    wait_bytes(rows.at[pl.ds(0, 496)], send)

    @pl.when(y % 2 != c)
    def _():
        wait_bytes(rows.at[pl.ds(0, 16)], send)


def start_kernel(
    tok, wmsg, rows, tok_all, w_all, rows_all,
    wm, wo, xs, xo, send, recv, core_recv, own,
):
    z, x, y, c = place()
    sib = (z, x, y, 1 - c)
    mine = pl.ds(pl.multiple_of(c * 512, 512), 512)
    theirs = pl.ds(pl.multiple_of((1 - c) * 512, 512), 512)
    keep(wmsg, wm, own.at[0])
    keep(rows.at[mine], xs, own.at[1])
    expected = greet_chips(z, x, y, c)
    for k in range(1, 4):
        signal(((z + k) % 4, x, y, c))
    arrive(expected + 3)
    push(wmsg, wo, send.at[0], core_recv.at[0], sib)
    push(rows.at[theirs], xo, send.at[1], core_recv.at[1], sib)
    for k in range(1, 4):
        push(tok, tok_all.at[z], send.at[2], recv.at[0], ((z + k) % 4, x, y, c))
    keep(tok, tok_all.at[z], recv.at[0])
    wait_bytes(wm, own.at[0])
    wait_bytes(wo, core_recv.at[0])
    wm[...] = wm[...] + wo[...]
    half = z * 8 + x * 2 + y // 2
    to_chips(
        z, x, y, c, lambda there: wm.at[there[0]], w_all.at[half, y % 2], send.at[3], recv.at[1]
    )
    wait_bytes(xs, own.at[1])
    wait_bytes(xo, core_recv.at[1])
    xs[...] = xs[...] + xo[...]
    me = block_of(z, x, y)
    to_chips(
        z, x, y, c,
        lambda there: xs.at[pl.ds(pl.multiple_of(block_of(*there[:3]) - c * 512, 16), 16)],
        rows_all.at[pl.ds(me, 16)], send.at[4], recv.at[2],
    )
    wait_bytes(w_all.at[:, c], recv.at[1])
    push(w_all.at[:, c], w_all.at[:, c], send.at[5], core_recv.at[2], sib)
    wait_bytes(rows_all.at[mine], recv.at[2])
    push(rows_all.at[mine], rows_all.at[mine], send.at[6], core_recv.at[3], sib)
    wait_bytes(tok_all, recv.at[0])
    wait_bytes(w_all.at[:, 1 - c], core_recv.at[2])
    wait_bytes(rows_all.at[theirs], core_recv.at[3])
    wait_bytes(wo, send.at[0])
    wait_bytes(xo, send.at[1])
    wait_bytes(tok_all.at[pl.ds(0, 3)], send.at[2])
    wait_bytes(w_all.at[pl.ds(0, 31), c], send.at[3])

    @pl.when(y % 2 != c)
    def _():
        wait_bytes(w_all.at[0, c], send.at[3])

    sent_to_chips(rows_all, y, c, send.at[4])
    wait_bytes(w_all.at[:, c], send.at[5])
    wait_bytes(rows_all.at[mine], send.at[6])


def start_exchange(tok, wmsg, rows):
    return run_comm(
        start_kernel,
        (tok, wmsg, rows),
        (
            jax.ShapeDtypeStruct((4, TOK, D), BF),
            jax.ShapeDtypeStruct((32, 2, 16, 3 * GW), BF),
            jax.ShapeDtypeStruct((1024, D), BF),
        ),
        [
            pltpu.VMEM((4, 16, 3 * GW), BF),
            pltpu.VMEM((4, 16, 3 * GW), BF),
            pltpu.VMEM((512, D), BF),
            pltpu.VMEM((512, D), BF),
            DMA((7,)),
            DMA((3,)),
            DMA((4,)),
            DMA((2,)),
        ],
        0,
        "start_exchange",
    )


FH = 1536
WIDE = 256


def experts_kernel(
    x16, d_rows, w_in, w_out, home_in, home_out, g_in, g_out,
    xs, xo, rows, dv, w1, w2, dh, hidden, dact, in_h, out_h, in_o, out_o, stage_out, stage_in,
    send, recv, core_recv, own, staged,
):
    z, x, y, c = place()
    sib = (z, x, y, 1 - c)
    at_mine = pl.multiple_of(c * 512, 512)
    at_theirs = pl.multiple_of((1 - c) * 512, 512)
    mine, theirs = pl.ds(at_mine, 512), pl.ds(at_theirs, 512)
    me = block_of(z, x, y)
    keep(x16.at[mine], xs, own.at[0])
    keep(d_rows, dv, own.at[1])
    keep(w_out, w2, own.at[2])
    keep(w_in, w1, own.at[3])
    expected = greet_chips(z, x, y, c)
    arrive(expected)
    push(x16.at[theirs], xo, send.at[0], core_recv.at[0], sib)
    wait_bytes(xs, own.at[0])
    wait_bytes(xo, core_recv.at[0])
    xs[...] = xs[...] + xo[...]
    to_chips(
        z, x, y, c,
        lambda there: xs.at[pl.ds(pl.multiple_of(block_of(*there[:3]) - c * 512, 16), 16)],
        rows.at[pl.ds(me, 16)], send.at[1], recv.at[0],
    )
    wait_bytes(dv, own.at[1])
    wait_bytes(w2, own.at[2])

    def hidden_grads(n):
        cols = pl.ds(pl.multiple_of(n * WIDE, WIDE), WIDE)
        dh[:, cols] = dot(dv[...], w2[cols, :], NT)

    loop(0, FH // WIDE, hidden_grads)
    wait_bytes(w1, own.at[3])
    wait_bytes(rows.at[mine], recv.at[0])
    push(rows.at[mine], rows.at[mine], send.at[2], core_recv.at[1], sib)

    def activate(at):
        part = pl.ds(at, 512)

        def one(n):
            cols = pl.ds(pl.multiple_of(n * WIDE, WIDE), WIDE)
            a = dot(rows[part, :], w1[:, cols], NN)
            square = a * a
            t = jnp.tanh(0.7978845608028654 * (a + 0.044715 * (square * a)))
            cdf = 0.5 * (1.0 + t)
            hidden[part, cols] = (a * cdf).astype(BF)
            slope = cdf + 0.5 * a * (1.0 - t * t) * (
                0.7978845608028654 * (1.0 + 0.134145 * square)
            )
            dact[part, cols] = (slope * dh[part, cols]).astype(BF)

        loop(0, FH // WIDE, one)

    def in_half(at):
        part = pl.ds(at, 512)

        def one(n):
            cols = pl.ds(pl.multiple_of(n * WIDE, WIDE), WIDE)
            in_h[part, cols] = dot(dact[part, :], w1[cols, :], NT).astype(BF)

        loop(0, D // WIDE, one)

    def out_half(at):
        part = pl.ds(at, 512)

        def one(n):
            cols = pl.ds(pl.multiple_of(n * WIDE, WIDE), WIDE)
            out_h[part, cols] = dot(hidden[part, :], w2[:, cols], NN).astype(BF)

        loop(0, D // WIDE, one)

    activate(at_mine)
    wait_bytes(rows.at[theirs], core_recv.at[1])
    activate(at_theirs)
    in_half(at_theirs)
    push(in_h.at[theirs], in_o, send.at[3], core_recv.at[2], sib)
    in_half(at_mine)
    wait_bytes(in_o, core_recv.at[2])
    in_o[...] = (in_o[...].astype(F32) + in_h[mine, :].astype(F32)).astype(BF)
    to_chips(
        z, x, y, c,
        lambda there: in_o.at[pl.ds(pl.multiple_of(block_of(*there[:3]) - c * 512, 16), 16)],
        home_in.at[pl.ds(me, 16)], send.at[4], recv.at[1],
    )
    out_half(at_theirs)
    push(out_h.at[theirs], out_o, send.at[5], core_recv.at[3], sib)
    out_half(at_mine)
    wait_bytes(out_o, core_recv.at[3])
    out_o[...] = (out_o[...].astype(F32) + out_h[mine, :].astype(F32)).astype(BF)
    to_chips(
        z, x, y, c,
        lambda there: out_o.at[pl.ds(pl.multiple_of(block_of(*there[:3]) - c * 512, 16), 16)],
        home_out.at[pl.ds(me, 16)], send.at[6], recv.at[2],
    )

    def out_grads(n):
        cols = pl.ds(pl.multiple_of(n * WIDE, WIDE), WIDE)
        slot = n % 2

        @pl.when(n >= 2)
        def _():
            wait_bytes(stage_out.at[slot], staged.at[slot])

        stage_out[slot] = dot(hidden[:, cols], dv[...], TN)
        keep(stage_out.at[slot], g_out.at[cols], staged.at[slot])

    loop(0, FH // WIDE, out_grads)
    wait_bytes(home_in.at[mine], recv.at[1])
    push(home_in.at[mine], home_in.at[mine], send.at[7], core_recv.at[4], sib)

    def in_grads(n):
        cols = pl.ds(pl.multiple_of(n * WIDE, WIDE), WIDE)
        slot = n % 2

        @pl.when(n >= 2)
        def _():
            wait_bytes(stage_in.at[slot], staged.at[2 + slot])

        stage_in[slot] = dot(rows[:, cols], dact[...], TN)
        keep(stage_in.at[slot], g_in.at[cols], staged.at[2 + slot])

    loop(0, D // WIDE, in_grads)
    wait_bytes(home_out.at[mine], recv.at[2])
    push(home_out.at[mine], home_out.at[mine], send.at[8], core_recv.at[5], sib)
    for slot in range(2):
        wait_bytes(stage_out.at[slot], staged.at[slot])
        wait_bytes(stage_in.at[slot], staged.at[2 + slot])
    wait_bytes(xo, send.at[0])
    sent_to_chips(rows, y, c, send.at[1])
    wait_bytes(rows.at[mine], send.at[2])
    wait_bytes(in_o, send.at[3])
    sent_to_chips(home_in, y, c, send.at[4])
    wait_bytes(out_o, send.at[5])
    sent_to_chips(home_out, y, c, send.at[6])
    wait_bytes(home_in.at[theirs], core_recv.at[4])
    wait_bytes(home_out.at[theirs], core_recv.at[5])
    wait_bytes(home_in.at[mine], send.at[7])
    wait_bytes(home_out.at[mine], send.at[8])


def run_experts(x16, d_rows, w_in, w_out):
    whole_rows = pltpu.VMEM((1024, D), BF)
    half_rows = pltpu.VMEM((512, D), BF)
    hid = pltpu.VMEM((1024, FH), BF)
    return pl.pallas_call(
        experts_kernel,
        out_shape=(
            jax.ShapeDtypeStruct((1024, D), BF),
            jax.ShapeDtypeStruct((1024, D), BF),
            jax.ShapeDtypeStruct((D, FH), F32),
            jax.ShapeDtypeStruct((FH, D), F32),
        ),
        in_specs=[ANY] * 4,
        out_specs=(ANY,) * 4,
        scratch_shapes=[
            half_rows, half_rows, whole_rows, whole_rows,
            pltpu.VMEM((D, FH), BF), pltpu.VMEM((FH, D), BF), pltpu.VMEM((1024, FH), F32),
            hid, hid, whole_rows, whole_rows, half_rows, half_rows,
            pltpu.VMEM((2, WIDE, D), F32), pltpu.VMEM((2, WIDE, FH), F32),
            DMA((9,)), DMA((3,)), DMA((6,)), DMA((4,)), DMA((4,)),
        ],
        compiler_params=pltpu.CompilerParams(
            collective_id=1, has_side_effects=True, vmem_limit_bytes=48 * 2**20
        ),
        name="experts",
    )(x16, d_rows, w_in, w_out)


def z_kernel(blocks, out, send, recv):
    z, x, y, c = place()
    for k in range(1, 4):
        signal(((z + k) % 4, x, y, c))
    arrive(3)
    for k in range(1, 4):
        there = (z + k) % 4
        push(blocks.at[there], out.at[z], send, recv, (there, x, y, c))
    keep(blocks.at[z], out.at[z], recv)
    wait_bytes(out, recv)
    wait_bytes(out.at[pl.ds(0, 3)], send)


def z_exchange(blocks, collective_id, name):
    return run_comm(
        z_kernel,
        (blocks,),
        jax.ShapeDtypeStruct(blocks.shape, blocks.dtype),
        [DMA, DMA],
        collective_id,
        name,
    )


def kv_kernel(kv, kv_all, send, recv):
    z, x, y, c = place()
    for k in range(1, 4):
        signal((z, (x + k) % 4, y, c))
    arrive(3)
    for k in range(1, 4):
        for b in range(4):
            push(kv.at[b], kv_all.at[b, x], send, recv, (z, (x + k) % 4, y, c))
    for b in range(4):
        keep(kv.at[b], kv_all.at[b, x], recv)
    wait_bytes(kv_all, recv)
    wait_bytes(kv_all.at[pl.ds(0, 3)], send)


def kv_gather(kv):
    return run_comm(
        kv_kernel,
        (kv,),
        jax.ShapeDtypeStruct((4, 4, TOK, 2 * GW), BF),
        [DMA, DMA],
        2,
        "kv_gather",
    )


def kv_back_kernel(dkv, branch, parts, branch_all, send, recv):
    z, x, y, c = place()
    for k in range(1, 4):
        signal((z, (x + k) % 4, y, c))
        signal(((z + k) % 4, x, y, c))
    arrive(6)
    for k in range(1, 4):
        there = (x + k) % 4
        for b in range(4):
            push(dkv.at[b, there], parts.at[x, b], send.at[0], recv.at[0], (z, there, y, c))
    for k in range(1, 4):
        push(branch, branch_all.at[z], send.at[1], recv.at[1], ((z + k) % 4, x, y, c))
    for b in range(4):
        keep(dkv.at[b, x], parts.at[x, b], recv.at[0])
    keep(branch, branch_all.at[z], recv.at[1])
    wait_bytes(parts, recv.at[0])
    wait_bytes(branch_all, recv.at[1])
    wait_bytes(parts.at[pl.ds(0, 3)], send.at[0])
    wait_bytes(branch_all.at[pl.ds(0, 3)], send.at[1])


def kv_back(dkv, branch):
    return run_comm(
        kv_back_kernel,
        (dkv, branch),
        (
            jax.ShapeDtypeStruct((4, 4, TOK, 2 * GW), BF),
            jax.ShapeDtypeStruct((4, TOK, D), BF),
        ),
        [DMA((2,)), DMA((2,))],
        3,
        "kv_back",
    )


def device_of(d):
    return d // 32, (d // 8) % 4, (d // 2) % 4, d % 2


def sums_kernel(
    qkv, att, small, qkv_out, att_out, small_out,
    qkv_in, att_in, small_in, qkv_sum, att_sum, small_sum, send, recv, out_sem,
):
    z, x, y, c = place()
    p = x * 8 + y * 2 + c
    me = z * 32 + p

    def peer(i):
        return (z, (x + i // 8) % 4, (y + (i // 2) % 4) % 4, (c + i % 2) % 2)

    loop(1, 32, lambda i: signal(peer(i)))
    source = me // 4

    def greet(k):
        from_me = (k == z) & (source == p)

        @pl.when(jnp.logical_not(from_me))
        def _():
            signal((k, source // 8, (source // 2) % 4, source % 2))

    loop(0, 4, greet)
    arrive(31 + 4 - jnp.where(source == p, 1, 0))

    def out(i):
        there = peer(i)
        q = there[1] * 8 + there[2] * 2 + there[3]
        push(qkv.at[q], qkv_in.at[p], send.at[0], recv.at[0], there)
        push(att.at[q], att_in.at[p], send.at[1], recv.at[1], there)
        push(small.at[q], small_in.at[p], send.at[2], recv.at[2], there)

    loop(1, 32, out)
    keep(qkv.at[p], qkv_in.at[p], recv.at[0])
    keep(att.at[p], att_in.at[p], recv.at[1])
    keep(small.at[p], small_in.at[p], recv.at[2])
    wait_bytes(qkv_in, recv.at[0])
    total = qkv_in[0].astype(F32)
    for q in range(1, 32):
        total = total + qkv_in[q].astype(F32)
    for k in range(4):
        qkv_sum[k, 0:6, :] = total[6 * k : 6 * k + 6]
        qkv_sum[k, 6:8, :] = jnp.zeros((2, 3 * GW), F32)
    wait_bytes(small_in, recv.at[2])
    small_total = small_in[0]
    for q in range(1, 32):
        small_total = small_total + small_in[q]
    small_sum[...] = small_total

    def final(k):
        d = 4 * p + k
        there = device_of(d)

        @pl.when(d != me)
        def _():
            push(qkv_sum.at[k], qkv_out.at[z], send.at[3], recv.at[3], there)
            push(small_sum, small_out.at[z], send.at[4], recv.at[4], there)

        @pl.when(d == me)
        def _():
            keep(qkv_sum.at[k], qkv_out.at[z], recv.at[3])
            keep(small_sum, small_out.at[z], recv.at[4])

    loop(0, 4, final)
    wait_bytes(att_in, recv.at[1])
    att_total = att_in[0].astype(F32)
    for q in range(1, 32):
        att_total = att_total + att_in[q].astype(F32)
    att_sum[...] = att_total
    keep(att_sum, att_out, out_sem)
    wait_bytes(att_sum, out_sem)
    wait_bytes(qkv_out, recv.at[3])
    wait_bytes(small_out, recv.at[4])
    wait_bytes(qkv_in.at[pl.ds(0, 31)], send.at[0])
    wait_bytes(att_in.at[pl.ds(0, 31)], send.at[1])
    wait_bytes(small_in.at[pl.ds(0, 31)], send.at[2])

    def sent(k):
        @pl.when(4 * p + k != me)
        def _():
            wait_bytes(qkv_sum.at[0], send.at[3])
            wait_bytes(small_sum, send.at[4])

    loop(0, 4, sent)


def weight_sums(qkv, att, small):
    return run_comm(
        sums_kernel,
        (qkv, att, small),
        (
            jax.ShapeDtypeStruct((4, 8, 3 * GW), F32),
            jax.ShapeDtypeStruct((8, D), F32),
            jax.ShapeDtypeStruct((4, 8, 128), F32),
        ),
        [
            pltpu.VMEM((32, 24, 3 * GW), BF),
            pltpu.VMEM((32, 8, D), BF),
            pltpu.VMEM((32, 8, 128), F32),
            pltpu.VMEM((4, 8, 3 * GW), F32),
            pltpu.VMEM((8, D), F32),
            pltpu.VMEM((8, 128), F32),
            DMA((5,)),
            DMA((5,)),
            DMA,
        ],
        4,
        "weight_sums",
    )


NT = (((1,), (1,)), ((), ()))
NN = (((1,), (0,)), ((), ()))
TN = (((0,), (0,)), ((), ()))


def dot(a, b, dims):
    return lax.dot_general(a, b, dims, preferred_element_type=F32)


def near_distance(dist):
    a = lax.broadcasted_iota(jnp.int32, (TOK, TOK), 0)
    b = lax.broadcasted_iota(jnp.int32, (TOK, TOK), 1)
    return dist * TOK + a - b


def table_kind(zq, zk, x, kx):
    return jnp.clip((zq - zk) * 4 + x - kx + 1, 0, 3)


def attn_forward_kernel(pos, tab, q, kv, qd, kd, out, p_out, bias, v_s, s_s):
    h = pl.program_id(0)
    x = pos[0]

    @pl.when(h == 0)
    def _():
        v_s[...] = kv[:, GW:]

    for dist in range(2):
        n = near_distance(dist)
        acc = jnp.full((TOK, TOK), tab[0, h], F32)
        for k, edge in enumerate(bucket_edges):
            acc = jnp.where(n >= edge, tab[k + 1, h], acc)
        bias[1 + dist] = jnp.where(n >= 0, acc, masked)
    bias[0] = jnp.full((TOK, TOK), masked, F32)
    far = tab[BUCKETS - 1, h]
    bias[3] = jnp.full((TOK, TOK), far, F32)
    head_cols = lax.broadcasted_iota(jnp.int32, (1, GW), 1) // HD == h
    for zk in range(4):
        qm = jnp.where(head_cols, q[zk * TOK :, :] * 0.125, 0.0).astype(BF)
        s_s[zk * TOK :, zk * 512 : (zk + 1) * 512] = dot(qm, kv[zk * 512 : (zk + 1) * 512, :GW], NT)
    for zq in range(4):
        rows = pl.ds(zq * TOK, TOK)
        docs = qd[rows, :]
        top = None
        for zk in range(zq + 1):
            for kx in range(4):
                cols = pl.ds((zk * 4 + kx) * TOK, TOK)
                s = s_s[rows, cols]
                if zk < zq - 1:
                    s = s + far
                else:
                    s = s + bias[table_kind(zq, zk, x, kx)]
                s = jnp.where(docs == kd[:, cols], s, masked)
                s_s[rows, cols] = s
                top = s if top is None else jnp.maximum(top, s)
        top = jnp.max(top, axis=1, keepdims=True)
        total = jnp.zeros((TOK, TOK), F32)
        for kb in range(4 * (zq + 1)):
            cols = pl.ds(kb * TOK, TOK)
            e = jnp.exp(s_s[rows, cols] - top)
            s_s[rows, cols] = e
            total = total + e
        inv = 1.0 / jnp.sum(total, axis=1, keepdims=True)
        for kb in range(4 * (zq + 1)):
            cols = pl.ds(kb * TOK, TOK)
            p_out[0, rows, cols] = (s_s[rows, cols] * inv).astype(BF)
        width = (zq + 1) * 512
        o = dot(p_out[0, rows, :width], v_s[:width, :], NN).astype(BF)

        @pl.when(h == 0)
        def _():
            out[rows, :] = o

        @pl.when(h > 0)
        def _():
            out[rows, :] = jnp.where(head_cols, o, out[rows, :])


def whole(shape):
    return pl.BlockSpec(shape, lambda h: (0,) * len(shape))


def attn_forward(pos, tab, q, kv, qd, kd):
    smem = pl.BlockSpec(memory_space=pltpu.SMEM)
    return pl.pallas_call(
        attn_forward_kernel,
        grid=(GH,),
        out_shape=(
            jax.ShapeDtypeStruct((512, GW), BF),
            jax.ShapeDtypeStruct((GH, 512, 2048), BF),
        ),
        in_specs=[
            smem, smem, whole((512, GW)), whole((2048, 2 * GW)), whole((512, 1)), whole((1, 2048)),
        ],
        out_specs=(whole((512, GW)), pl.BlockSpec((1, 512, 2048), lambda h: (h, 0, 0))),
        scratch_shapes=[
            pltpu.VMEM((4, TOK, TOK), F32),
            pltpu.VMEM((2048, GW), BF),
            pltpu.VMEM((512, 2048), F32),
        ],
        compiler_params=pltpu.CompilerParams(
            dimension_semantics=("arbitrary",), vmem_limit_bytes=40 * 2**20
        ),
        name="attn_forward",
    )(pos, tab, q, kv, qd, kd)


def attn_backward_kernel(pos, p, q, kv, do, dq, dkv, tab, v_s, dk_s, dv_s, dp_s, ds_s, near):
    h = pl.program_id(0)
    x = pos[0]

    @pl.when(h == 0)
    def _():
        v_s[...] = kv[:, GW:]

    head_cols = lax.broadcasted_iota(jnp.int32, (1, GW), 1) // HD == h
    for zk in range(4):
        dm = jnp.where(head_cols, do[zk * TOK :, :], 0.0).astype(BF)
        cols = pl.ds(zk * 512, 512)
        dp_s[zk * TOK :, cols] = dot(dm, v_s[cols, :], NT)
        dv = dot(p[0, zk * TOK :, cols], dm, TN)

        @pl.when(h == 0)
        def _():
            dv_s[cols, :] = dv

        @pl.when(h > 0)
        def _():
            dv_s[cols, :] += dv

    near[...] = jnp.zeros_like(near)
    for zq in range(4):
        rows = pl.ds(zq * TOK, TOK)
        acc = jnp.zeros((TOK, TOK), F32)
        for kb in range(4 * (zq + 1)):
            cols = pl.ds(kb * TOK, TOK)
            acc = acc + p[0, rows, cols].astype(F32) * dp_s[rows, cols]
        delta = jnp.sum(acc, axis=1, keepdims=True)
        far = jnp.zeros((TOK, TOK), F32)
        for zk in range(zq + 1):
            for kx in range(4):
                cols = pl.ds((zk * 4 + kx) * TOK, TOK)
                ds = (p[0, rows, cols].astype(F32) * (dp_s[rows, cols] - delta)).astype(BF)
                ds_s[rows, cols] = ds
                if zk < zq - 1:
                    far = far + ds.astype(F32)
                else:
                    near[table_kind(zq, zk, x, kx)] += ds.astype(F32)
        near[3] += far
        width = (zq + 1) * 512
        o = (dot(ds_s[rows, :width], kv[:width, :GW], NN) * 0.125).astype(BF)

        @pl.when(h == 0)
        def _():
            dq[rows, :] = o

        @pl.when(h > 0)
        def _():
            dq[rows, :] = jnp.where(head_cols, o, dq[rows, :])

    for zk in range(4):
        qm = jnp.where(head_cols, q[zk * TOK :, :] * 0.125, 0.0).astype(BF)
        cols = pl.ds(zk * 512, 512)
        dk = dot(ds_s[zk * TOK :, cols], qm, TN)

        @pl.when(h == 0)
        def _():
            dk_s[cols, :] = dk

        @pl.when(h > 0)
        def _():
            dk_s[cols, :] += dk

    for dist in range(2):
        n = near_distance(dist)
        held = near[1 + dist]
        bounds = [-(10**6)] + bucket_edges + [10**6]
        for b in range(BUCKETS):
            low, high = bounds[b], bounds[b + 1]
            if high <= dist * TOK - TOK + 1 or low > dist * TOK + TOK - 1:
                if dist == 0:
                    tab[0, b : b + 1, :] = jnp.zeros((1, TOK), F32)
                continue
            part = jnp.sum(jnp.where((n >= low) & (n < high), held, 0.0), axis=0, keepdims=True)
            if dist == 0:
                tab[0, b : b + 1, :] = part
            else:
                tab[0, b : b + 1, :] += part
    tab[0, BUCKETS - 1 :, :] += jnp.sum(near[3], axis=0, keepdims=True)

    @pl.when(h == GH - 1)
    def _():
        dkv[:, :GW] = dk_s[...].astype(BF)
        dkv[:, GW:] = dv_s[...].astype(BF)


def attn_backward(pos, p, q, kv, do):
    smem = pl.BlockSpec(memory_space=pltpu.SMEM)
    return pl.pallas_call(
        attn_backward_kernel,
        grid=(GH,),
        out_shape=(
            jax.ShapeDtypeStruct((512, GW), BF),
            jax.ShapeDtypeStruct((2048, 2 * GW), BF),
            jax.ShapeDtypeStruct((GH, BUCKETS, TOK), F32),
        ),
        in_specs=[
            smem,
            pl.BlockSpec((1, 512, 2048), lambda h: (h, 0, 0)),
            whole((512, GW)), whole((2048, 2 * GW)), whole((512, GW)),
        ],
        out_specs=(
            whole((512, GW)),
            whole((2048, 2 * GW)),
            pl.BlockSpec((1, BUCKETS, TOK), lambda h: (h, 0, 0)),
        ),
        scratch_shapes=[
            pltpu.VMEM((2048, GW), BF),
            pltpu.VMEM((2048, GW), F32),
            pltpu.VMEM((2048, GW), F32),
            pltpu.VMEM((512, 2048), F32),
            pltpu.VMEM((512, 2048), BF),
            pltpu.VMEM((4, TOK, TOK), F32),
        ],
        compiler_params=pltpu.CompilerParams(
            dimension_semantics=("arbitrary",), vmem_limit_bytes=48 * 2**20
        ),
        name="attn_backward",
    )(pos, p, q, kv, do)


def per_device(
    tokens,
    gain_attn,
    w_qkv,
    w_attn_out,
    rel_table,
    gain_moe,
    w_in,
    w_out,
    expert_ids,
    gate_values,
    doc_ids,
    cotangent,
):
    z, x, y, c = place()
    experts = 64
    capacity = 8
    slots = 2 * experts * capacity
    own_tokens = tokens.reshape(TOK, D)
    grad_bf = cotangent.reshape(TOK, D)
    grad_out = grad_bf.astype(F32)

    route = expert_ids.reshape(TOK * 2)
    marks = (route[:, None] == jnp.arange(experts, dtype=jnp.int32)[None, :]).astype(jnp.int32)
    earlier = jnp.cumsum(marks, axis=0) - marks
    block = (route % 2) * 32 + (route // 4) * 2 + (route % 4) // 2
    slot = block * 16 + c * capacity + jnp.sum(earlier * marks, axis=1)
    slot_pair = slot.reshape(TOK, 2)
    gates = gate_values.reshape(TOK, 2)
    slot_ids = jnp.arange(slots, dtype=jnp.int32)
    pick_0 = slot_pair[:, 0][:, None] == slot_ids[None, :]
    pick_1 = slot_pair[:, 1][:, None] == slot_ids[None, :]
    pick = (pick_0 | pick_1).astype(BF)
    gate_of = jnp.where(pick_0, gates[:, :1], 0.0) + jnp.where(pick_1, gates[:, 1:], 0.0)
    gate_slot = jnp.sum(gate_of, axis=0)
    d_eo = (dot(pick, grad_bf, TN) * gate_slot[:, None]).astype(BF)

    slab = w_qkv.reshape(6, 3, GROUPS, GW).transpose(2, 0, 1, 3).reshape(GROUPS, 6, 3 * GW)
    notes = jnp.concatenate(
        [
            gain_attn, gain_moe, jnp.zeros((116,), BF),
            doc_ids.reshape(TOK).astype(BF), jnp.zeros((3 * GW - 256,), BF),
        ]
    )
    notes = jnp.broadcast_to(notes, (GROUPS, 1, 3 * GW))
    nothing = jnp.zeros((GROUPS, 6, 3 * GW), BF)
    message = jnp.where(
        c == 0,
        jnp.concatenate([slab, nothing, notes, nothing[:, :3]], axis=1),
        jnp.concatenate([nothing, slab, nothing[:, :1], notes, nothing[:, :2]], axis=1),
    )
    attention_weight = lax.all_gather(w_attn_out, AXES, axis=0, tiled=True)
    tok_all, w_all, d_eo_all = start_exchange(own_tokens, message, d_eo)

    weight = w_all[:, :, :12, :].reshape(D, 3 * GW)
    gain_one = w_all[:, :, 12:14, 0:6].reshape(D).astype(F32)
    gain_two = w_all[:, :, 12:14, 6:12].reshape(D).astype(F32)
    doc_rows = w_all[:, :, 12:14, 128:256].reshape(16, 4, 2, TOK)
    doc_rows = lax.dynamic_slice(doc_rows, (0, y, c, 0), (16, 1, 1, TOK)).reshape(16, TOK).astype(F32)
    key_docs = doc_rows.reshape(1, 2048)
    query_docs = lax.dynamic_slice(doc_rows.reshape(4, 4, TOK), (0, x, 0), (4, 1, TOK)).reshape(512, 1)

    inputs_all = tok_all.reshape(512, D).astype(F32)
    normed = scale_rows(inputs_all, gain_one).astype(BF)
    qkv = dot(normed, weight, NN).astype(BF)
    queries = qkv[:, :GW]
    kv_all = kv_gather(qkv[:, GW:].reshape(4, TOK, 2 * GW)).reshape(2048, 2 * GW)
    table = lax.dynamic_slice(rel_table, (0, z * GH), (BUCKETS, GH)).astype(F32)
    pos = jnp.full((1,), x, jnp.int32)
    attn_part, probs = attn_forward(pos, table, queries, kv_all, query_docs, key_docs)
    attn = z_exchange(attn_part.reshape(4, TOK, GW), 5, "attn_exchange")
    attn = attn.transpose(1, 0, 2).reshape(TOK, D)

    inputs = own_tokens.astype(F32)
    middle = inputs + dot(attn, attention_weight, NN)
    moe_float, norm_two_back = jax.vjp(scale_rows, middle, gain_two)
    moe_in = moe_float.astype(BF)
    send_rows = dot(pick, moe_in, TN).astype(BF)
    home, expert_out, expert_in_grad, expert_out_grad = run_experts(
        send_rows, d_eo_all, w_in[0], w_out[0]
    )
    moe_in_grad = dot(pick, home, NN)
    middle_part, gain_two_grad = norm_two_back(moe_in_grad)
    middle_grad = grad_out + middle_part
    branch = middle_grad.astype(BF)
    d_attn = dot(branch, attention_weight, NT).astype(BF)
    d_attn = d_attn.reshape(TOK, GROUPS, GW).transpose(1, 0, 2)
    d_attn = z_exchange(d_attn, 7, "d_attn_exchange").reshape(512, GW)

    d_q, d_kv, table_part = attn_backward(pos, probs, queries, kv_all, d_attn)
    kv_parts, branch_all = kv_back(d_kv.reshape(4, 4, TOK, 2 * GW), branch)
    d_kv = jnp.sum(kv_parts.astype(F32), axis=0).astype(BF).reshape(512, 2 * GW)
    d_qkv = jnp.concatenate([d_q, d_kv], axis=1)
    normed_part = dot(d_qkv, weight, NT).astype(BF).reshape(4, TOK, D)
    normed_part = z_exchange(normed_part, 8, "normed_grads")
    normed_grad = jnp.sum(normed_part.astype(F32), axis=0)
    _, norm_one_back = jax.vjp(scale_rows, inputs, gain_one)
    input_part, gain_one_grad = norm_one_back(normed_grad)
    input_grad = middle_grad + input_part

    both = jnp.concatenate([pick_0, pick_1], axis=0).astype(BF)
    picked = dot(both, expert_out, NN).reshape(2, TOK, D)
    block_out = middle + gates[:, :1] * picked[0] + gates[:, 1:] * picked[1]
    gate_grad = jnp.sum(picked * grad_out[None], axis=2).T

    qkv_part = dot(normed, d_qkv, TN).astype(BF).reshape(32, 24, 3 * GW)
    att_part = dot(attn_part, branch_all.reshape(512, D), TN).astype(BF).reshape(32, 6, D)
    att_part = jnp.pad(att_part, ((0, 0), (0, 2), (0, 0)))
    table_sum = jnp.sum(table_part, axis=2).reshape(1, GH * BUCKETS)
    small = jnp.stack(
        [
            jnp.pad(gain_one_grad.reshape(32, 24), ((0, 0), (0, 104))),
            jnp.pad(gain_two_grad.reshape(32, 24), ((0, 0), (0, 104))),
            jnp.broadcast_to(jnp.pad(table_sum, ((0, 0), (0, 128 - GH * BUCKETS))), (32, 128)),
        ],
        axis=1,
    )
    small = jnp.pad(small, ((0, 0), (0, 5), (0, 0)))
    qkv_sum, att_sum, small_sum = weight_sums(qkv_part, att_part, small)
    qkv_grad = qkv_sum[:, :6, :].reshape(GROUPS, 6, 3, GW).transpose(1, 2, 0, 3).reshape(6, 3 * D)
    attn_out_grad = att_sum[:6]
    place_in = (y * 2 + c) % 4
    gains = lax.dynamic_slice(jnp.sum(small_sum[:, :2, :], axis=0), (0, place_in * 6), (2, 6))
    table_grad = (
        small_sum[:, 2, : GH * BUCKETS].reshape(GROUPS * GH, BUCKETS).T
    )
    return (
        block_out.reshape(1, TOK, D).astype(BF),
        input_grad.reshape(1, TOK, D).astype(BF),
        gate_grad.reshape(1, TOK, 2),
        gains[0],
        qkv_grad,
        attn_out_grad,
        table_grad,
        gains[1],
        expert_in_grad[None],
        expert_out_grad[None],
    )


def solution(mesh):
    torus = Mesh(mesh.devices.reshape(4, 4, 4, 2), AXES)
    in_specs = (
        P(EXP, CTX, None),
        P(AXES),
        P(AXES, None),
        P(AXES, None),
        P(),
        P(AXES),
        P(AXES, None, None),
        P(AXES, None, None),
        P(EXP, CTX, None),
        P(EXP, CTX, None),
        P(EXP, CTX),
        P(EXP, CTX, None),
    )
    out_specs = (
        P(EXP, CTX, None),
        P(EXP, CTX, None),
        P(EXP, CTX, None),
        P(AXES),
        P(AXES, None),
        P(AXES, None),
        P(),
        P(AXES),
        P(AXES, None, None),
        P(AXES, None, None),
    )
    return jax.shard_map(
        per_device, mesh=torus, in_specs=in_specs, out_specs=out_specs, check_vma=False
    )
```

```python
import functools

import jax
import jax.numpy as jnp
import numpy as np
from jax import lax
from jax.experimental import pallas as pl
from jax.experimental.pallas import tpu as pltpu
from jax.sharding import Mesh
from jax.sharding import PartitionSpec as P

D = 768
H = 12
HD = 64
BUCKETS = 32
GROUPS = 4
GH = H // GROUPS
GW = GH * HD
TOK = 128
CTX = ("ctx_0", "ctx_1")
EXP = ("exp_0", "exp_1")
AXES = ("ctx_0", "ctx_1", "exp_0", "exp_1")
MESH = pl.DeviceIdType.MESH
ANY = pl.BlockSpec(memory_space=pl.ANY)
BF = jnp.bfloat16
F32 = jnp.float32

norm_eps = 1e-06
bucket_edges = [int(e) for e in np.concatenate(
    [np.arange(1, 17), np.ceil(16.0 * 8.0 ** (np.arange(1, 16) / 16.0))]
).astype(np.int32)]
masked = -1e30


def scale_rows(values, gain):
    return values * lax.rsqrt(jnp.mean(values * values, axis=-1, keepdims=True) + norm_eps) * gain


def place():
    return tuple(lax.axis_index(a) for a in AXES)


def chip_of(z, x, y):
    return (z * 4 + x) * 4 + y


def chip_peer(i, z, x, y):
    return (z + i // 16) % 4, (x + (i // 4) % 4) % 4, (y + i % 4) % 4


def loop(first, last, body):
    lax.fori_loop(first, last, lambda i, carry: (body(i), carry)[1], 0)


def signal(device):
    pl.semaphore_signal(
        pltpu.get_barrier_semaphore(), inc=1, device_id=device, device_id_type=MESH
    )


def arrive(count):
    pl.semaphore_wait(pltpu.get_barrier_semaphore(), count)


def push(src, dst, send, recv, device):
    pltpu.make_async_remote_copy(
        src_ref=src, dst_ref=dst, send_sem=send, recv_sem=recv, device_id=device, device_id_type=MESH
    ).start()


def keep(src, dst, sem):
    pltpu.make_async_copy(src, dst, sem).start()


def wait_bytes(ref, sem):
    pltpu.make_async_copy(ref, ref, sem).wait()


def comm_call(kernel, outs, scratch, collective_id, name):
    return pl.pallas_call(
        kernel,
        out_shape=outs,
        in_specs=None,
        out_specs=jax.tree.map(lambda _: ANY, outs),
        scratch_shapes=scratch,
        compiler_params=pltpu.CompilerParams(
            collective_id=collective_id, has_side_effects=True, vmem_limit_bytes=32 * 2**20
        ),
        name=name,
    )


def run_comm(kernel, args, outs, scratch, collective_id, name):
    return pl.pallas_call(
        kernel,
        out_shape=outs,
        in_specs=[ANY] * len(args),
        out_specs=jax.tree.map(lambda _: ANY, outs),
        scratch_shapes=scratch,
        compiler_params=pltpu.CompilerParams(
            collective_id=collective_id, has_side_effects=True, vmem_limit_bytes=32 * 2**20
        ),
        name=name,
    )(*args)


DMA = pltpu.SemaphoreType.DMA


def half_peer(i, z, x, y, c):
    return (z + i // 8) % 4, (x + (i // 2) % 4) % 4, c + 2 * ((y // 2 + i % 2) % 2), y % 2


def block_of(z, x, y):
    return pl.multiple_of((y % 2) * 512 + ((z * 4 + x) * 2 + y // 2) * 16, 16)


def greet_chips(z, x, y, c):
    loop(1, 32, lambda i: signal(half_peer(i, z, x, y, c)))

    @pl.when(y % 2 != c)
    def _():
        signal(half_peer(0, z, x, y, c))

    signal((z, x, y, 1 - c))
    return 32 + jnp.where(y % 2 == c, 0, 1)


def to_chips(z, x, y, c, source, target, send, recv):
    def one(i):
        there = half_peer(i, z, x, y, c)
        push(source(there), target, send, recv, there)

    loop(1, 32, one)
    first = half_peer(0, z, x, y, c)

    @pl.when(y % 2 == c)
    def _():
        keep(source(first), target, recv)

    @pl.when(y % 2 != c)
    def _():
        push(source(first), target, send, recv, first)


def sent_to_chips(rows, y, c, send):
    wait_bytes(rows.at[pl.ds(0, 496)], send)

    @pl.when(y % 2 != c)
    def _():
        wait_bytes(rows.at[pl.ds(0, 16)], send)


def start_kernel(tok, wmsg, tok_all, w_all, wm, wo, send, recv, core_recv, own):
    z, x, y, c = place()
    sib = (z, x, y, 1 - c)
    keep(wmsg, wm, own)
    expected = greet_chips(z, x, y, c)
    for k in range(1, 4):
        signal(((z + k) % 4, x, y, c))
    arrive(expected + 3)
    push(wmsg, wo, send.at[0], core_recv.at[0], sib)
    for k in range(1, 4):
        push(tok, tok_all.at[z], send.at[1], recv.at[0], ((z + k) % 4, x, y, c))
    keep(tok, tok_all.at[z], recv.at[0])
    wait_bytes(wm, own)
    wait_bytes(wo, core_recv.at[0])
    wm[...] = wm[...] + wo[...]
    half = z * 8 + x * 2 + y // 2
    to_chips(
        z, x, y, c, lambda there: wm.at[there[0]], w_all.at[half, y % 2], send.at[2], recv.at[1]
    )
    wait_bytes(w_all.at[:, c], recv.at[1])
    push(w_all.at[:, c], w_all.at[:, c], send.at[3], core_recv.at[1], sib)
    wait_bytes(tok_all, recv.at[0])
    wait_bytes(w_all.at[:, 1 - c], core_recv.at[1])
    wait_bytes(wo, send.at[0])
    wait_bytes(tok_all.at[pl.ds(0, 3)], send.at[1])
    wait_bytes(w_all.at[pl.ds(0, 31), c], send.at[2])

    @pl.when(y % 2 != c)
    def _():
        wait_bytes(w_all.at[0, c], send.at[2])

    wait_bytes(w_all.at[:, c], send.at[3])


def start_exchange(tok, wmsg):
    return run_comm(
        start_kernel,
        (tok, wmsg),
        (
            jax.ShapeDtypeStruct((4, TOK, D), BF),
            jax.ShapeDtypeStruct((32, 2, 16, 3 * GW), BF),
        ),
        [
            pltpu.VMEM((4, 16, 3 * GW), BF),
            pltpu.VMEM((4, 16, 3 * GW), BF),
            DMA((4,)),
            DMA((2,)),
            DMA((2,)),
            DMA,
        ],
        0,
        "start_exchange",
    )


FH = 1536
WIDE = 256


def experts_kernel(
    x16, d_rows, w_in, w_out, home_in, home_out, g_in, g_out,
    xs, xo, rows, dv, w1, w2, dh, hidden, dact, in_h, out_h, in_o, out_o, stage_out, stage_in,
    send, recv, core_recv, own, staged,
):
    z, x, y, c = place()
    sib = (z, x, y, 1 - c)
    at_mine = pl.multiple_of(c * 512, 512)
    at_theirs = pl.multiple_of((1 - c) * 512, 512)
    mine, theirs = pl.ds(at_mine, 512), pl.ds(at_theirs, 512)
    me = block_of(z, x, y)
    keep(x16.at[mine], xs, own.at[0])
    keep(d_rows, dv, own.at[1])
    keep(w_out, w2, own.at[2])
    keep(w_in, w1, own.at[3])
    expected = greet_chips(z, x, y, c)
    arrive(expected)
    push(x16.at[theirs], xo, send.at[0], core_recv.at[0], sib)
    wait_bytes(xs, own.at[0])
    wait_bytes(xo, core_recv.at[0])
    xs[...] = xs[...] + xo[...]
    to_chips(
        z, x, y, c,
        lambda there: xs.at[pl.ds(pl.multiple_of(block_of(*there[:3]) - c * 512, 16), 16)],
        rows.at[pl.ds(me, 16)], send.at[1], recv.at[0],
    )
    wait_bytes(dv, own.at[1])
    wait_bytes(w2, own.at[2])

    def hidden_grads(n):
        cols = pl.ds(pl.multiple_of(n * WIDE, WIDE), WIDE)
        dh[:, cols] = dot(dv[...], w2[cols, :], NT)

    loop(0, FH // WIDE, hidden_grads)
    wait_bytes(w1, own.at[3])
    wait_bytes(rows.at[mine], recv.at[0])
    push(rows.at[mine], rows.at[mine], send.at[2], core_recv.at[1], sib)

    def activate(at):
        part = pl.ds(at, 512)

        def one(n):
            cols = pl.ds(pl.multiple_of(n * WIDE, WIDE), WIDE)
            a = dot(rows[part, :], w1[:, cols], NN)
            square = a * a
            t = jnp.tanh(0.7978845608028654 * (a + 0.044715 * (square * a)))
            cdf = 0.5 * (1.0 + t)
            hidden[part, cols] = (a * cdf).astype(BF)
            slope = cdf + 0.5 * a * (1.0 - t * t) * (
                0.7978845608028654 * (1.0 + 0.134145 * square)
            )
            dact[part, cols] = (slope * dh[part, cols]).astype(BF)

        loop(0, FH // WIDE, one)

    def in_half(at):
        part = pl.ds(at, 512)

        def one(n):
            cols = pl.ds(pl.multiple_of(n * WIDE, WIDE), WIDE)
            in_h[part, cols] = dot(dact[part, :], w1[cols, :], NT).astype(BF)

        loop(0, D // WIDE, one)

    def out_half(at):
        part = pl.ds(at, 512)

        def one(n):
            cols = pl.ds(pl.multiple_of(n * WIDE, WIDE), WIDE)
            out_h[part, cols] = dot(hidden[part, :], w2[:, cols], NN).astype(BF)

        loop(0, D // WIDE, one)

    activate(at_mine)
    wait_bytes(rows.at[theirs], core_recv.at[1])
    activate(at_theirs)
    in_half(at_theirs)
    push(in_h.at[theirs], in_o, send.at[3], core_recv.at[2], sib)
    in_half(at_mine)
    wait_bytes(in_o, core_recv.at[2])
    in_o[...] = (in_o[...].astype(F32) + in_h[mine, :].astype(F32)).astype(BF)
    to_chips(
        z, x, y, c,
        lambda there: in_o.at[pl.ds(pl.multiple_of(block_of(*there[:3]) - c * 512, 16), 16)],
        home_in.at[pl.ds(me, 16)], send.at[4], recv.at[1],
    )
    out_half(at_theirs)
    push(out_h.at[theirs], out_o, send.at[5], core_recv.at[3], sib)
    out_half(at_mine)
    wait_bytes(out_o, core_recv.at[3])
    out_o[...] = (out_o[...].astype(F32) + out_h[mine, :].astype(F32)).astype(BF)
    to_chips(
        z, x, y, c,
        lambda there: out_o.at[pl.ds(pl.multiple_of(block_of(*there[:3]) - c * 512, 16), 16)],
        home_out.at[pl.ds(me, 16)], send.at[6], recv.at[2],
    )

    def out_grads(n):
        cols = pl.ds(pl.multiple_of(n * WIDE, WIDE), WIDE)
        slot = n % 2

        @pl.when(n >= 2)
        def _():
            wait_bytes(stage_out.at[slot], staged.at[slot])

        stage_out[slot] = dot(hidden[:, cols], dv[...], TN)
        keep(stage_out.at[slot], g_out.at[cols], staged.at[slot])

    loop(0, FH // WIDE, out_grads)
    wait_bytes(home_in.at[mine], recv.at[1])
    push(home_in.at[mine], home_in.at[mine], send.at[7], core_recv.at[4], sib)

    def in_grads(n):
        cols = pl.ds(pl.multiple_of(n * WIDE, WIDE), WIDE)
        slot = n % 2

        @pl.when(n >= 2)
        def _():
            wait_bytes(stage_in.at[slot], staged.at[2 + slot])

        stage_in[slot] = dot(rows[:, cols], dact[...], TN)
        keep(stage_in.at[slot], g_in.at[cols], staged.at[2 + slot])

    loop(0, D // WIDE, in_grads)
    wait_bytes(home_out.at[mine], recv.at[2])
    push(home_out.at[mine], home_out.at[mine], send.at[8], core_recv.at[5], sib)
    for slot in range(2):
        wait_bytes(stage_out.at[slot], staged.at[slot])
        wait_bytes(stage_in.at[slot], staged.at[2 + slot])
    wait_bytes(xo, send.at[0])
    sent_to_chips(rows, y, c, send.at[1])
    wait_bytes(rows.at[mine], send.at[2])
    wait_bytes(in_o, send.at[3])
    sent_to_chips(home_in, y, c, send.at[4])
    wait_bytes(out_o, send.at[5])
    sent_to_chips(home_out, y, c, send.at[6])
    wait_bytes(home_in.at[theirs], core_recv.at[4])
    wait_bytes(home_out.at[theirs], core_recv.at[5])
    wait_bytes(home_in.at[mine], send.at[7])
    wait_bytes(home_out.at[mine], send.at[8])


def run_experts(x16, d_rows, w_in, w_out):
    whole_rows = pltpu.VMEM((1024, D), BF)
    half_rows = pltpu.VMEM((512, D), BF)
    hid = pltpu.VMEM((1024, FH), BF)
    return pl.pallas_call(
        experts_kernel,
        out_shape=(
            jax.ShapeDtypeStruct((1024, D), BF),
            jax.ShapeDtypeStruct((1024, D), BF),
            jax.ShapeDtypeStruct((D, FH), F32),
            jax.ShapeDtypeStruct((FH, D), F32),
        ),
        in_specs=[ANY] * 4,
        out_specs=(ANY,) * 4,
        scratch_shapes=[
            half_rows, half_rows, whole_rows, whole_rows,
            pltpu.VMEM((D, FH), BF), pltpu.VMEM((FH, D), BF), pltpu.VMEM((1024, FH), F32),
            hid, hid, whole_rows, whole_rows, half_rows, half_rows,
            pltpu.VMEM((2, WIDE, D), F32), pltpu.VMEM((2, WIDE, FH), F32),
            DMA((9,)), DMA((3,)), DMA((6,)), DMA((4,)), DMA((4,)),
        ],
        compiler_params=pltpu.CompilerParams(
            collective_id=1, has_side_effects=True, vmem_limit_bytes=48 * 2**20
        ),
        name="experts",
    )(x16, d_rows, w_in, w_out)


def z_kernel(blocks, out, send, recv):
    z, x, y, c = place()
    for k in range(1, 4):
        signal(((z + k) % 4, x, y, c))
    arrive(3)
    for k in range(1, 4):
        there = (z + k) % 4
        push(blocks.at[there], out.at[z], send, recv, (there, x, y, c))
    keep(blocks.at[z], out.at[z], recv)
    wait_bytes(out, recv)
    wait_bytes(out.at[pl.ds(0, 3)], send)


def z_exchange(blocks, collective_id, name):
    return run_comm(
        z_kernel,
        (blocks,),
        jax.ShapeDtypeStruct(blocks.shape, blocks.dtype),
        [DMA, DMA],
        collective_id,
        name,
    )


def device_of(d):
    return d // 32, (d // 8) % 4, (d // 2) % 4, d % 2


def sums_kernel(
    qkv, att, small, qkv_out, att_out, small_out,
    qkv_in, att_in, small_in, qkv_sum, att_sum, small_sum, send, recv, out_sem,
):
    z, x, y, c = place()
    p = x * 8 + y * 2 + c
    me = z * 32 + p

    def peer(i):
        return (z, (x + i // 8) % 4, (y + (i // 2) % 4) % 4, (c + i % 2) % 2)

    loop(1, 32, lambda i: signal(peer(i)))
    source = me // 4

    def greet(k):
        from_me = (k == z) & (source == p)

        @pl.when(jnp.logical_not(from_me))
        def _():
            signal((k, source // 8, (source // 2) % 4, source % 2))

    loop(0, 4, greet)
    arrive(31 + 4 - jnp.where(source == p, 1, 0))

    def out(i):
        there = peer(i)
        q = there[1] * 8 + there[2] * 2 + there[3]
        push(qkv.at[q], qkv_in.at[p], send.at[0], recv.at[0], there)
        push(att.at[q], att_in.at[p], send.at[1], recv.at[1], there)
        push(small.at[q], small_in.at[p], send.at[2], recv.at[2], there)

    loop(1, 32, out)
    keep(qkv.at[p], qkv_in.at[p], recv.at[0])
    keep(att.at[p], att_in.at[p], recv.at[1])
    keep(small.at[p], small_in.at[p], recv.at[2])
    wait_bytes(qkv_in, recv.at[0])
    total = qkv_in[0].astype(F32)
    for q in range(1, 32):
        total = total + qkv_in[q].astype(F32)
    for k in range(4):
        qkv_sum[k, 0:6, :] = total[6 * k : 6 * k + 6]
        qkv_sum[k, 6:8, :] = jnp.zeros((2, 3 * GW), F32)
    wait_bytes(small_in, recv.at[2])
    small_total = small_in[0]
    for q in range(1, 32):
        small_total = small_total + small_in[q]
    small_sum[...] = small_total

    def final(k):
        d = 4 * p + k
        there = device_of(d)

        @pl.when(d != me)
        def _():
            push(qkv_sum.at[k], qkv_out.at[z], send.at[3], recv.at[3], there)
            push(small_sum, small_out.at[z], send.at[4], recv.at[4], there)

        @pl.when(d == me)
        def _():
            keep(qkv_sum.at[k], qkv_out.at[z], recv.at[3])
            keep(small_sum, small_out.at[z], recv.at[4])

    loop(0, 4, final)
    wait_bytes(att_in, recv.at[1])
    att_total = att_in[0].astype(F32)
    for q in range(1, 32):
        att_total = att_total + att_in[q].astype(F32)
    att_sum[...] = att_total
    keep(att_sum, att_out, out_sem)
    wait_bytes(att_sum, out_sem)
    wait_bytes(qkv_out, recv.at[3])
    wait_bytes(small_out, recv.at[4])
    wait_bytes(qkv_in.at[pl.ds(0, 31)], send.at[0])
    wait_bytes(att_in.at[pl.ds(0, 31)], send.at[1])
    wait_bytes(small_in.at[pl.ds(0, 31)], send.at[2])

    def sent(k):
        @pl.when(4 * p + k != me)
        def _():
            wait_bytes(qkv_sum.at[0], send.at[3])
            wait_bytes(small_sum, send.at[4])

    loop(0, 4, sent)


def weight_sums(qkv, att, small):
    return run_comm(
        sums_kernel,
        (qkv, att, small),
        (
            jax.ShapeDtypeStruct((4, 8, 3 * GW), F32),
            jax.ShapeDtypeStruct((8, D), F32),
            jax.ShapeDtypeStruct((4, 8, 128), F32),
        ),
        [
            pltpu.VMEM((32, 24, 3 * GW), BF),
            pltpu.VMEM((32, 8, D), BF),
            pltpu.VMEM((32, 8, 128), F32),
            pltpu.VMEM((4, 8, 3 * GW), F32),
            pltpu.VMEM((8, D), F32),
            pltpu.VMEM((8, 128), F32),
            DMA((5,)),
            DMA((5,)),
            DMA,
        ],
        4,
        "weight_sums",
    )


NT = (((1,), (1,)), ((), ()))
NN = (((1,), (0,)), ((), ()))
TN = (((0,), (0,)), ((), ()))


def dot(a, b, dims):
    return lax.dot_general(a, b, dims, preferred_element_type=F32)


def near_distance(dist):
    a = lax.broadcasted_iota(jnp.int32, (TOK, TOK), 0)
    b = lax.broadcasted_iota(jnp.int32, (TOK, TOK), 1)
    return dist * TOK + a - b


def table_kind(zq, zk, x, kx):
    return jnp.clip((zq - zk) * 4 + x - kx + 1, 0, 3)


def block_cols(zk, kx):
    return pl.ds(pl.multiple_of((zk * 4 + kx) * TOK, TOK), TOK)


VMEM = pl.BlockSpec(memory_space=pltpu.VMEM)
SMEM = pl.BlockSpec(memory_space=pltpu.SMEM)


def attn_forward_kernel(
    tab, q, kv, qd, kd, d_eo, wa,
    attn_all, part, p_out, kv_out, d_rows, wa_all,
    kv_s, v_s, qm, bias, s_s, p_s, xs, xo, wm, wo,
    send, recv, kv_recv, core_recv, own,
):
    z, x, y, c = place()
    sib = (z, x, y, 1 - c)
    mine = pl.ds(pl.multiple_of(c * 512, 512), 512)
    theirs = pl.ds(pl.multiple_of((1 - c) * 512, 512), 512)
    keep(d_eo.at[mine], xs, own.at[0])
    expected = greet_chips(z, x, y, c)
    for k in range(1, 4):
        signal(((z + k) % 4, x, y, c))
        signal((z, (x + k) % 4, y, c))
    arrive(expected + 6)
    for k in range(1, 4):
        for b in range(4):
            push(
                kv.at[b], kv_s.at[block_cols(b, x)], send.at[0], kv_recv.at[4 - k],
                (z, (x + k) % 4, y, c),
            )
    for b in range(4):
        keep(kv.at[b], kv_s.at[block_cols(b, x)], kv_recv.at[0])
    push(wa, wo, send.at[1], core_recv.at[0], sib)
    push(d_eo.at[theirs], xo, send.at[2], core_recv.at[1], sib)
    for h in range(GH):
        head_cols = lax.broadcasted_iota(jnp.int32, (1, GW), 1) // HD == h
        qm[h] = jnp.where(head_cols, q[...] * 0.125, 0.0).astype(BF)
    wait_bytes(wo, core_recv.at[0])
    wm[...] = wa[...] + wo[...]
    half = z * 8 + x * 2 + y // 2
    to_chips(z, x, y, c, lambda there: wm, wa_all.at[half, y % 2], send.at[3], recv.at[0])
    wait_bytes(xs, own.at[0])
    wait_bytes(xo, core_recv.at[1])
    xs[...] = xs[...] + xo[...]
    me = block_of(z, x, y)
    to_chips(
        z, x, y, c,
        lambda there: xs.at[pl.ds(pl.multiple_of(block_of(*there[:3]) - c * 512, 16), 16)],
        d_rows.at[pl.ds(me, 16)], send.at[4], recv.at[1],
    )

    def tables(h):
        for dist in range(2):
            n = near_distance(dist)
            acc = jnp.full((TOK, TOK), tab[0, h], F32)
            for k, edge in enumerate(bucket_edges):
                acc = jnp.where(n >= edge, tab[k + 1, h], acc)
            bias[h, 1 + dist] = jnp.where(n >= 0, acc, masked)
        bias[h, 0] = jnp.full((TOK, TOK), masked, F32)
        bias[h, 3] = jnp.full((TOK, TOK), tab[BUCKETS - 1, h], F32)

    loop(0, GH, tables)
    for k in range(4):
        kx = (x + k) % 4
        if k == 0:
            for b in range(4):
                wait_bytes(kv_s.at[block_cols(b, kx)], kv_recv.at[0])
        else:
            wait_bytes(kv_s.at[pl.ds(0, 512)], kv_recv.at[k])
        for b in range(4):
            cols = block_cols(b, kx)
            v_s[cols, :] = kv_s[cols, GW:]
            for h in range(GH):
                s_s[h, b * TOK :, cols] = dot(qm[h, b * TOK :, :], kv_s[cols, :GW], NT)
    keep(kv_s, kv_out, own.at[1])
    wait_bytes(wa_all.at[:, c], recv.at[0])
    push(wa_all.at[:, c], wa_all.at[:, c], send.at[5], core_recv.at[2], sib)

    def head(h):
        head_cols = lax.broadcasted_iota(jnp.int32, (1, GW), 1) // HD == h
        far = tab[BUCKETS - 1, h]
        for zq in range(4):
            rows = pl.ds(zq * TOK, TOK)
            docs = qd[rows, :]
            top = None
            for zk in range(zq + 1):
                for kx in range(4):
                    cols = pl.ds((zk * 4 + kx) * TOK, TOK)
                    s = s_s[h, rows, cols]
                    if zk < zq - 1:
                        s = s + far
                    else:
                        s = s + bias[h, table_kind(zq, zk, x, kx)]
                    s = jnp.where(docs == kd[:, cols], s, masked)
                    s_s[h, rows, cols] = s
                    top = s if top is None else jnp.maximum(top, s)
            top = jnp.max(top, axis=1, keepdims=True)
            total = jnp.zeros((TOK, TOK), F32)
            for kb in range(4 * (zq + 1)):
                cols = pl.ds(kb * TOK, TOK)
                e = jnp.exp(s_s[h, rows, cols] - top)
                s_s[h, rows, cols] = e
                total = total + e
            inv = 1.0 / jnp.sum(total, axis=1, keepdims=True)
            for kb in range(4 * (zq + 1)):
                cols = pl.ds(kb * TOK, TOK)
                p_s[h, rows, cols] = (s_s[h, rows, cols] * inv).astype(BF)
            width = (zq + 1) * 512
            o = dot(p_s[h, rows, :width], v_s[:width, :], NN).astype(BF)

            @pl.when(h == 0)
            def _():
                part[rows, :] = o

            @pl.when(h > 0)
            def _():
                part[rows, :] = jnp.where(head_cols, o, part[rows, :])

    loop(0, GH, head)
    for k in range(1, 4):
        there = (z + k) % 4
        push(
            part.at[pl.ds(pl.multiple_of(there * TOK, TOK), TOK)], attn_all.at[z],
            send.at[6], recv.at[2], (there, x, y, c),
        )
    keep(part.at[pl.ds(pl.multiple_of(z * TOK, TOK), TOK)], attn_all.at[z], recv.at[2])
    keep(p_s, p_out, own.at[2])
    wait_bytes(d_rows.at[mine], recv.at[1])
    push(d_rows.at[mine], d_rows.at[mine], send.at[7], core_recv.at[3], sib)
    wait_bytes(attn_all, recv.at[2])
    wait_bytes(wa_all.at[:, 1 - c], core_recv.at[2])
    wait_bytes(d_rows.at[theirs], core_recv.at[3])
    wait_bytes(kv_s, own.at[1])
    wait_bytes(p_s, own.at[2])
    wait_bytes(kv_s.at[pl.ds(0, 1536)], send.at[0])
    wait_bytes(wo, send.at[1])
    wait_bytes(xo, send.at[2])
    wait_bytes(wa_all.at[pl.ds(0, 31), c], send.at[3])

    @pl.when(y % 2 != c)
    def _():
        wait_bytes(wa_all.at[0, c], send.at[3])

    sent_to_chips(d_rows, y, c, send.at[4])
    wait_bytes(wa_all.at[:, c], send.at[5])
    wait_bytes(attn_all.at[pl.ds(0, 3)], send.at[6])
    wait_bytes(d_rows.at[mine], send.at[7])


def attn_forward(tab, q, kv, qd, kd, d_eo, wa):
    probs = (GH, 512, 2048)
    return pl.pallas_call(
        attn_forward_kernel,
        out_shape=(
            jax.ShapeDtypeStruct((4, TOK, GW), BF),
            jax.ShapeDtypeStruct((512, GW), BF),
            jax.ShapeDtypeStruct(probs, BF),
            jax.ShapeDtypeStruct((2048, 2 * GW), BF),
            jax.ShapeDtypeStruct((1024, D), BF),
            jax.ShapeDtypeStruct((32, 2, 16, D), BF),
        ),
        in_specs=[SMEM, VMEM, VMEM, VMEM, VMEM, ANY, VMEM],
        out_specs=(ANY, VMEM, ANY, ANY, ANY, ANY),
        scratch_shapes=[
            pltpu.VMEM((2048, 2 * GW), BF),
            pltpu.VMEM((2048, GW), BF),
            pltpu.VMEM((GH, 512, GW), BF),
            pltpu.VMEM((GH, 4, TOK, TOK), F32),
            pltpu.VMEM(probs, F32),
            pltpu.VMEM(probs, BF),
            pltpu.VMEM((512, D), BF),
            pltpu.VMEM((512, D), BF),
            pltpu.VMEM((16, D), BF),
            pltpu.VMEM((16, D), BF),
            DMA((8,)),
            DMA((3,)),
            DMA((4,)),
            DMA((4,)),
            DMA((3,)),
        ],
        compiler_params=pltpu.CompilerParams(
            collective_id=2, has_side_effects=True, vmem_limit_bytes=44 * 2**20
        ),
        name="attn_forward",
    )(tab, q, kv, qd, kd, d_eo, wa)


def attn_backward_kernel(
    p, q, kv, d_attn, branch, dq, tab, parts, branch_all,
    p_s, v_s, do_s, dm, qm, dp_s, ds_s, near, messages,
    send, recv, own,
):
    z, x, y, c = place()
    keep(p, p_s, own)
    for k in range(1, 4):
        signal(((z + k) % 4, x, y, c))
        signal((z, (x + k) % 4, y, c))
    arrive(6)
    for k in range(1, 4):
        there = (z + k) % 4
        push(d_attn.at[there], do_s.at[z], send.at[0], recv.at[0], (there, x, y, c))
    keep(d_attn.at[z], do_s.at[z], recv.at[0])
    for k in range(1, 4):
        push(branch, branch_all.at[z], send.at[1], recv.at[1], ((z + k) % 4, x, y, c))
    keep(branch, branch_all.at[z], recv.at[1])
    v_s[...] = kv[:, GW:]
    for h in range(GH):
        head_cols = lax.broadcasted_iota(jnp.int32, (1, GW), 1) // HD == h
        qm[h] = jnp.where(head_cols, q[...] * 0.125, 0.0).astype(BF)
    wait_bytes(do_s, recv.at[0])
    for h in range(GH):
        head_cols = lax.broadcasted_iota(jnp.int32, (1, GW), 1) // HD == h
        for b in range(4):
            dm[h, b * TOK : (b + 1) * TOK, :] = jnp.where(head_cols, do_s[b], 0.0).astype(BF)
    wait_bytes(p_s, own)

    def key_sums(left, right, first):
        for k in (1, 2, 3, 0):
            kx = (x + k) % 4
            for b in range(4):
                cols = block_cols(b, kx)
                total = None
                for h in range(GH):
                    one = dot(left[h, b * TOK :, cols], right[h, b * TOK :, :], TN)
                    total = one if total is None else total + one
                side = GW * (b % 2)
                messages[k, first + b // 2, :, side : side + GW] = total.astype(BF)
            for m in range(first, first + 2):
                if k:
                    push(
                        messages.at[k, m], parts.at[x, m], send.at[2], recv.at[2],
                        (z, kx, y, c),
                    )
                else:
                    keep(messages.at[k, m], parts.at[x, m], recv.at[2])

    key_sums(p_s, dm, 0)

    def head(h):
        head_cols = lax.broadcasted_iota(jnp.int32, (1, GW), 1) // HD == h
        for zk in range(4):
            cols = pl.ds(zk * 512, 512)
            dp_s[zk * TOK :, cols] = dot(dm[h, zk * TOK :, :], v_s[cols, :], NT)
        near[...] = jnp.zeros_like(near)
        for zq in range(4):
            rows = pl.ds(zq * TOK, TOK)
            acc = jnp.zeros((TOK, TOK), F32)
            for kb in range(4 * (zq + 1)):
                cols = pl.ds(kb * TOK, TOK)
                acc = acc + p_s[h, rows, cols].astype(F32) * dp_s[rows, cols]
            delta = jnp.sum(acc, axis=1, keepdims=True)
            far = jnp.zeros((TOK, TOK), F32)
            for zk in range(zq + 1):
                for kx in range(4):
                    cols = pl.ds((zk * 4 + kx) * TOK, TOK)
                    ds = (p_s[h, rows, cols].astype(F32) * (dp_s[rows, cols] - delta)).astype(BF)
                    ds_s[h, rows, cols] = ds
                    if zk < zq - 1:
                        far = far + ds.astype(F32)
                    else:
                        near[table_kind(zq, zk, x, kx)] += ds.astype(F32)
            near[3] += far
            width = (zq + 1) * 512
            o = (dot(ds_s[h, rows, :width], kv[:width, :GW], NN) * 0.125).astype(BF)

            @pl.when(h == 0)
            def _():
                dq[rows, :] = o

            @pl.when(h > 0)
            def _():
                dq[rows, :] = jnp.where(head_cols, o, dq[rows, :])

        for dist in range(2):
            n = near_distance(dist)
            held = near[1 + dist]
            bounds = [-(10**6)] + bucket_edges + [10**6]
            for b in range(BUCKETS):
                low, high = bounds[b], bounds[b + 1]
                if high <= dist * TOK - TOK + 1 or low > dist * TOK + TOK - 1:
                    if dist == 0:
                        tab[h, b : b + 1, :] = jnp.zeros((1, TOK), F32)
                    continue
                inside = jnp.sum(
                    jnp.where((n >= low) & (n < high), held, 0.0), axis=0, keepdims=True
                )
                if dist == 0:
                    tab[h, b : b + 1, :] = inside
                else:
                    tab[h, b : b + 1, :] += inside
        tab[h, BUCKETS - 1 :, :] += jnp.sum(near[3], axis=0, keepdims=True)

    loop(0, GH, head)
    key_sums(ds_s, qm, 2)
    wait_bytes(parts, recv.at[2])
    wait_bytes(branch_all, recv.at[1])
    wait_bytes(do_s.at[pl.ds(0, 3)], send.at[0])
    wait_bytes(branch_all.at[pl.ds(0, 3)], send.at[1])
    wait_bytes(parts.at[pl.ds(0, 3)], send.at[2])


def attn_backward(p, q, kv, d_attn, branch):
    probs = (GH, 512, 2048)
    return pl.pallas_call(
        attn_backward_kernel,
        out_shape=(
            jax.ShapeDtypeStruct((512, GW), BF),
            jax.ShapeDtypeStruct((GH, BUCKETS, TOK), F32),
            jax.ShapeDtypeStruct((4, 4, TOK, 2 * GW), BF),
            jax.ShapeDtypeStruct((4, TOK, D), BF),
        ),
        in_specs=[ANY, VMEM, VMEM, VMEM, VMEM],
        out_specs=(VMEM, VMEM, ANY, ANY),
        scratch_shapes=[
            pltpu.VMEM(probs, BF),
            pltpu.VMEM((2048, GW), BF),
            pltpu.VMEM((4, TOK, GW), BF),
            pltpu.VMEM((GH, 512, GW), BF),
            pltpu.VMEM((GH, 512, GW), BF),
            pltpu.VMEM((512, 2048), F32),
            pltpu.VMEM(probs, BF),
            pltpu.VMEM((4, TOK, TOK), F32),
            pltpu.VMEM((4, 4, TOK, 2 * GW), BF),
            DMA((3,)),
            DMA((3,)),
            DMA,
        ],
        compiler_params=pltpu.CompilerParams(
            collective_id=3, has_side_effects=True, vmem_limit_bytes=44 * 2**20
        ),
        name="attn_backward",
    )(p, q, kv, d_attn, branch)


def per_device(
    tokens,
    gain_attn,
    w_qkv,
    w_attn_out,
    rel_table,
    gain_moe,
    w_in,
    w_out,
    expert_ids,
    gate_values,
    doc_ids,
    cotangent,
):
    z, x, y, c = place()
    experts = 64
    capacity = 8
    slots = 2 * experts * capacity
    own_tokens = tokens.reshape(TOK, D)
    grad_bf = cotangent.reshape(TOK, D)
    grad_out = grad_bf.astype(F32)

    route = expert_ids.reshape(TOK * 2)
    marks = (route[:, None] == jnp.arange(experts, dtype=jnp.int32)[None, :]).astype(jnp.int32)
    earlier = jnp.cumsum(marks, axis=0) - marks
    block = (route % 2) * 32 + (route // 4) * 2 + (route % 4) // 2
    slot = block * 16 + c * capacity + jnp.sum(earlier * marks, axis=1)
    slot_pair = slot.reshape(TOK, 2)
    gates = gate_values.reshape(TOK, 2)
    slot_ids = jnp.arange(slots, dtype=jnp.int32)
    pick_0 = slot_pair[:, 0][:, None] == slot_ids[None, :]
    pick_1 = slot_pair[:, 1][:, None] == slot_ids[None, :]
    pick = (pick_0 | pick_1).astype(BF)
    gate_of = jnp.where(pick_0, gates[:, :1], 0.0) + jnp.where(pick_1, gates[:, 1:], 0.0)
    gate_slot = jnp.sum(gate_of, axis=0)
    d_eo = (dot(pick, grad_bf, TN) * gate_slot[:, None]).astype(BF)

    slab = w_qkv.reshape(6, 3, GROUPS, GW).transpose(2, 0, 1, 3).reshape(GROUPS, 6, 3 * GW)
    notes = jnp.concatenate(
        [
            gain_attn, gain_moe, jnp.zeros((116,), BF),
            doc_ids.reshape(TOK).astype(BF), jnp.zeros((3 * GW - 256,), BF),
        ]
    )
    notes = jnp.broadcast_to(notes, (GROUPS, 1, 3 * GW))
    nothing = jnp.zeros((GROUPS, 6, 3 * GW), BF)
    message = jnp.where(
        c == 0,
        jnp.concatenate([slab, nothing, notes, nothing[:, :3]], axis=1),
        jnp.concatenate([nothing, slab, nothing[:, :1], notes, nothing[:, :2]], axis=1),
    )
    zero_rows = jnp.zeros((6, D), BF)
    out_slab = jnp.where(
        c == 0,
        jnp.concatenate([w_attn_out, zero_rows, zero_rows[:4]], axis=0),
        jnp.concatenate([zero_rows, w_attn_out, zero_rows[:4]], axis=0),
    )
    tok_all, w_all = start_exchange(own_tokens, message)

    weight = w_all[:, :, :12, :].reshape(D, 3 * GW)
    gain_one = w_all[:, :, 12:14, 0:6].reshape(D).astype(F32)
    gain_two = w_all[:, :, 12:14, 6:12].reshape(D).astype(F32)
    doc_rows = w_all[:, :, 12:14, 128:256].reshape(16, 4, 2, TOK)
    doc_rows = lax.dynamic_slice(doc_rows, (0, y, c, 0), (16, 1, 1, TOK)).reshape(16, TOK).astype(F32)
    key_docs = doc_rows.reshape(1, 2048)
    query_docs = lax.dynamic_slice(doc_rows.reshape(4, 4, TOK), (0, x, 0), (4, 1, TOK)).reshape(512, 1)

    inputs_all = tok_all.reshape(512, D).astype(F32)
    normed = scale_rows(inputs_all, gain_one).astype(BF)
    qkv = dot(normed, weight, NN).astype(BF)
    queries = qkv[:, :GW]
    table = lax.dynamic_slice(rel_table, (0, z * GH), (BUCKETS, GH)).astype(F32)
    attn, attn_part, probs, kv_all, d_eo_all, out_weights = attn_forward(
        table, queries, qkv[:, GW:].reshape(4, TOK, 2 * GW), query_docs, key_docs, d_eo, out_slab
    )
    attn = attn.transpose(1, 0, 2).reshape(TOK, D)
    attention_weight = out_weights[:, :, :12, :].reshape(D, D)

    inputs = own_tokens.astype(F32)
    middle = inputs + dot(attn, attention_weight, NN)
    moe_float, norm_two_back = jax.vjp(scale_rows, middle, gain_two)
    moe_in = moe_float.astype(BF)
    send_rows = dot(pick, moe_in, TN).astype(BF)
    home, expert_out, expert_in_grad, expert_out_grad = run_experts(
        send_rows, d_eo_all, w_in[0], w_out[0]
    )
    moe_in_grad = dot(pick, home, NN)
    middle_part, gain_two_grad = norm_two_back(moe_in_grad)
    middle_grad = grad_out + middle_part
    branch = middle_grad.astype(BF)
    d_attn = dot(branch, attention_weight, NT).astype(BF)
    d_attn = d_attn.reshape(TOK, GROUPS, GW).transpose(1, 0, 2)

    d_q, table_part, kv_parts, branch_all = attn_backward(probs, queries, kv_all, d_attn, branch)
    d_kv = jnp.sum(kv_parts.astype(F32), axis=0).astype(BF)
    d_kv = d_kv.reshape(2, 2, TOK, 2, GW).transpose(0, 1, 3, 2, 4).reshape(2, 512, GW)
    d_kv = jnp.concatenate([d_kv[1], d_kv[0]], axis=1)
    d_qkv = jnp.concatenate([d_q, d_kv], axis=1)
    normed_part = dot(d_qkv, weight, NT).astype(BF).reshape(4, TOK, D)
    normed_part = z_exchange(normed_part, 8, "normed_grads")
    normed_grad = jnp.sum(normed_part.astype(F32), axis=0)
    _, norm_one_back = jax.vjp(scale_rows, inputs, gain_one)
    input_part, gain_one_grad = norm_one_back(normed_grad)
    input_grad = middle_grad + input_part

    both = jnp.concatenate([pick_0, pick_1], axis=0).astype(BF)
    picked = dot(both, expert_out, NN).reshape(2, TOK, D)
    block_out = middle + gates[:, :1] * picked[0] + gates[:, 1:] * picked[1]
    gate_grad = jnp.sum(picked * grad_out[None], axis=2).T

    qkv_part = dot(normed, d_qkv, TN).astype(BF).reshape(32, 24, 3 * GW)
    att_part = dot(attn_part, branch_all.reshape(512, D), TN).astype(BF).reshape(32, 6, D)
    att_part = jnp.pad(att_part, ((0, 0), (0, 2), (0, 0)))
    table_sum = jnp.sum(table_part, axis=2).reshape(1, GH * BUCKETS)
    small = jnp.stack(
        [
            jnp.pad(gain_one_grad.reshape(32, 24), ((0, 0), (0, 104))),
            jnp.pad(gain_two_grad.reshape(32, 24), ((0, 0), (0, 104))),
            jnp.broadcast_to(jnp.pad(table_sum, ((0, 0), (0, 128 - GH * BUCKETS))), (32, 128)),
        ],
        axis=1,
    )
    small = jnp.pad(small, ((0, 0), (0, 5), (0, 0)))
    qkv_sum, att_sum, small_sum = weight_sums(qkv_part, att_part, small)
    qkv_grad = qkv_sum[:, :6, :].reshape(GROUPS, 6, 3, GW).transpose(1, 2, 0, 3).reshape(6, 3 * D)
    attn_out_grad = att_sum[:6]
    place_in = (y * 2 + c) % 4
    gains = lax.dynamic_slice(jnp.sum(small_sum[:, :2, :], axis=0), (0, place_in * 6), (2, 6))
    table_grad = (
        small_sum[:, 2, : GH * BUCKETS].reshape(GROUPS * GH, BUCKETS).T
    )
    return (
        block_out.reshape(1, TOK, D).astype(BF),
        input_grad.reshape(1, TOK, D).astype(BF),
        gate_grad.reshape(1, TOK, 2),
        gains[0],
        qkv_grad,
        attn_out_grad,
        table_grad,
        gains[1],
        expert_in_grad[None],
        expert_out_grad[None],
    )


def solution(mesh):
    torus = Mesh(mesh.devices.reshape(4, 4, 4, 2), AXES)
    in_specs = (
        P(EXP, CTX, None),
        P(AXES),
        P(AXES, None),
        P(AXES, None),
        P(),
        P(AXES),
        P(AXES, None, None),
        P(AXES, None, None),
        P(EXP, CTX, None),
        P(EXP, CTX, None),
        P(EXP, CTX),
        P(EXP, CTX, None),
    )
    out_specs = (
        P(EXP, CTX, None),
        P(EXP, CTX, None),
        P(EXP, CTX, None),
        P(AXES),
        P(AXES, None),
        P(AXES, None),
        P(),
        P(AXES),
        P(AXES, None, None),
        P(AXES, None, None),
    )
    return jax.shard_map(
        per_device, mesh=torus, in_specs=in_specs, out_specs=out_specs, check_vma=False
    )
```

```python
import functools

import jax
import jax.numpy as jnp
import numpy as np
from jax import lax
from jax.experimental import pallas as pl
from jax.experimental.pallas import tpu as pltpu
from jax.sharding import Mesh
from jax.sharding import PartitionSpec as P

D = 768
H = 12
HD = 64
BUCKETS = 32
GROUPS = 4
GH = H // GROUPS
GW = GH * HD
TOK = 128
CTX = ("ctx_0", "ctx_1")
EXP = ("exp_0", "exp_1")
AXES = ("ctx_0", "ctx_1", "exp_0", "exp_1")
MESH = pl.DeviceIdType.MESH
ANY = pl.BlockSpec(memory_space=pl.ANY)
BF = jnp.bfloat16
F32 = jnp.float32

norm_eps = 1e-06
bucket_edges = [int(e) for e in np.concatenate(
    [np.arange(1, 17), np.ceil(16.0 * 8.0 ** (np.arange(1, 16) / 16.0))]
).astype(np.int32)]
masked = -1e30


def scale_rows(values, gain):
    return values * lax.rsqrt(jnp.mean(values * values, axis=-1, keepdims=True) + norm_eps) * gain


def place():
    return tuple(lax.axis_index(a) for a in AXES)


def chip_of(z, x, y):
    return (z * 4 + x) * 4 + y


def chip_peer(i, z, x, y):
    return (z + i // 16) % 4, (x + (i // 4) % 4) % 4, (y + i % 4) % 4


def loop(first, last, body):
    lax.fori_loop(first, last, lambda i, carry: (body(i), carry)[1], 0)


def signal(device):
    pl.semaphore_signal(
        pltpu.get_barrier_semaphore(), inc=1, device_id=device, device_id_type=MESH
    )


def arrive(count):
    pl.semaphore_wait(pltpu.get_barrier_semaphore(), count)


def push(src, dst, send, recv, device):
    pltpu.make_async_remote_copy(
        src_ref=src, dst_ref=dst, send_sem=send, recv_sem=recv, device_id=device, device_id_type=MESH
    ).start()


def keep(src, dst, sem):
    pltpu.make_async_copy(src, dst, sem).start()


def wait_bytes(ref, sem):
    pltpu.make_async_copy(ref, ref, sem).wait()


def comm_call(kernel, outs, scratch, collective_id, name):
    return pl.pallas_call(
        kernel,
        out_shape=outs,
        in_specs=None,
        out_specs=jax.tree.map(lambda _: ANY, outs),
        scratch_shapes=scratch,
        compiler_params=pltpu.CompilerParams(
            collective_id=collective_id, has_side_effects=True, vmem_limit_bytes=32 * 2**20
        ),
        name=name,
    )


def run_comm(kernel, args, outs, scratch, collective_id, name):
    return pl.pallas_call(
        kernel,
        out_shape=outs,
        in_specs=[ANY] * len(args),
        out_specs=jax.tree.map(lambda _: ANY, outs),
        scratch_shapes=scratch,
        compiler_params=pltpu.CompilerParams(
            collective_id=collective_id, has_side_effects=True, vmem_limit_bytes=32 * 2**20
        ),
        name=name,
    )(*args)


DMA = pltpu.SemaphoreType.DMA


def half_peer(i, z, x, y, c):
    return (z + i // 8) % 4, (x + (i // 2) % 4) % 4, c + 2 * ((y // 2 + i % 2) % 2), y % 2


def block_of(z, x, y):
    return pl.multiple_of((y % 2) * 512 + ((z * 4 + x) * 2 + y // 2) * 16, 16)


def greet_chips(z, x, y, c):
    loop(1, 32, lambda i: signal(half_peer(i, z, x, y, c)))

    @pl.when(y % 2 != c)
    def _():
        signal(half_peer(0, z, x, y, c))

    signal((z, x, y, 1 - c))
    return 32 + jnp.where(y % 2 == c, 0, 1)


def to_chips(z, x, y, c, source, target, send, recv):
    def one(i):
        there = half_peer(i, z, x, y, c)
        push(source(there), target, send, recv, there)

    loop(1, 32, one)
    first = half_peer(0, z, x, y, c)

    @pl.when(y % 2 == c)
    def _():
        keep(source(first), target, recv)

    @pl.when(y % 2 != c)
    def _():
        push(source(first), target, send, recv, first)


def sent_to_chips(rows, y, c, send):
    wait_bytes(rows.at[pl.ds(0, 496)], send)

    @pl.when(y % 2 != c)
    def _():
        wait_bytes(rows.at[pl.ds(0, 16)], send)


def start_kernel(tok, wmsg, tok_all, w_all, wm, wo, send, recv, core_recv, own):
    z, x, y, c = place()
    sib = (z, x, y, 1 - c)
    keep(wmsg, wm, own)
    expected = greet_chips(z, x, y, c)
    for k in range(1, 4):
        signal(((z + k) % 4, x, y, c))
    arrive(expected + 3)
    push(wmsg, wo, send.at[0], core_recv.at[0], sib)
    for k in range(1, 4):
        push(tok, tok_all.at[z], send.at[1], recv.at[0], ((z + k) % 4, x, y, c))
    keep(tok, tok_all.at[z], recv.at[0])
    wait_bytes(wm, own)
    wait_bytes(wo, core_recv.at[0])
    wm[...] = wm[...] + wo[...]
    half = z * 8 + x * 2 + y // 2
    to_chips(
        z, x, y, c, lambda there: wm.at[there[0]], w_all.at[half, y % 2], send.at[2], recv.at[1]
    )
    wait_bytes(w_all.at[:, c], recv.at[1])
    push(w_all.at[:, c], w_all.at[:, c], send.at[3], core_recv.at[1], sib)
    wait_bytes(tok_all, recv.at[0])
    wait_bytes(w_all.at[:, 1 - c], core_recv.at[1])
    wait_bytes(wo, send.at[0])
    wait_bytes(tok_all.at[pl.ds(0, 3)], send.at[1])
    wait_bytes(w_all.at[pl.ds(0, 31), c], send.at[2])

    @pl.when(y % 2 != c)
    def _():
        wait_bytes(w_all.at[0, c], send.at[2])

    wait_bytes(w_all.at[:, c], send.at[3])


def start_exchange(tok, wmsg):
    return run_comm(
        start_kernel,
        (tok, wmsg),
        (
            jax.ShapeDtypeStruct((4, TOK, D), BF),
            jax.ShapeDtypeStruct((32, 2, 16, 3 * GW), BF),
        ),
        [
            pltpu.VMEM((4, 16, 3 * GW), BF),
            pltpu.VMEM((4, 16, 3 * GW), BF),
            DMA((4,)),
            DMA((2,)),
            DMA((2,)),
            DMA,
        ],
        0,
        "start_exchange",
    )


FH = 1536
WIDE = 256


def experts_kernel(
    x16, d_eo, w_in, w_out, home_in, home_out, g_in, g_out,
    xs, xo, es, eo, rows, dv, w1, w2, slope, hidden, dact, in_h, out_h, in_o, out_o, stage_out, stage_in,
    send, recv, core_recv, own, staged,
):
    z, x, y, c = place()
    sib = (z, x, y, 1 - c)
    at_mine = pl.multiple_of(c * 512, 512)
    at_theirs = pl.multiple_of((1 - c) * 512, 512)
    mine, theirs = pl.ds(at_mine, 512), pl.ds(at_theirs, 512)
    me = block_of(z, x, y)
    keep(x16.at[mine], xs, own.at[0])
    keep(d_eo.at[mine], es, own.at[1])
    keep(w_out, w2, own.at[2])
    keep(w_in, w1, own.at[3])
    expected = greet_chips(z, x, y, c)
    arrive(expected)
    push(x16.at[theirs], xo, send.at[0], core_recv.at[0], sib)
    push(d_eo.at[theirs], eo, send.at[9], core_recv.at[6], sib)
    wait_bytes(xs, own.at[0])
    wait_bytes(xo, core_recv.at[0])
    xs[...] = xs[...] + xo[...]
    to_chips(
        z, x, y, c,
        lambda there: xs.at[pl.ds(pl.multiple_of(block_of(*there[:3]) - c * 512, 16), 16)],
        rows.at[pl.ds(me, 16)], send.at[1], recv.at[0],
    )
    wait_bytes(es, own.at[1])
    wait_bytes(eo, core_recv.at[6])
    es[...] = es[...] + eo[...]
    to_chips(
        z, x, y, c,
        lambda there: es.at[pl.ds(pl.multiple_of(block_of(*there[:3]) - c * 512, 16), 16)],
        dv.at[pl.ds(me, 16)], send.at[10], recv.at[3],
    )
    wait_bytes(w1, own.at[3])
    wait_bytes(w2, own.at[2])
    wait_bytes(rows.at[mine], recv.at[0])
    push(rows.at[mine], rows.at[mine], send.at[2], core_recv.at[1], sib)

    def activate(at):
        part = pl.ds(at, 512)

        def one(n):
            cols = pl.ds(pl.multiple_of(n * WIDE, WIDE), WIDE)
            a = dot(rows[part, :], w1[:, cols], NN)
            square = a * a
            t = jnp.tanh(0.7978845608028654 * (a + 0.044715 * (square * a)))
            cdf = 0.5 * (1.0 + t)
            hidden[part, cols] = (a * cdf).astype(BF)
            slope[part, cols] = cdf + 0.5 * a * (1.0 - t * t) * (
                0.7978845608028654 * (1.0 + 0.134145 * square)
            )

        loop(0, FH // WIDE, one)

    def act_grads(at):
        part = pl.ds(at, 512)

        def one(n):
            cols = pl.ds(pl.multiple_of(n * WIDE, WIDE), WIDE)
            d_hidden = dot(dv[part, :], w2[cols, :], NT)
            dact[part, cols] = (slope[part, cols] * d_hidden).astype(BF)

        loop(0, FH // WIDE, one)

    def in_half(at):
        part = pl.ds(at, 512)

        def one(n):
            cols = pl.ds(pl.multiple_of(n * WIDE, WIDE), WIDE)
            in_h[part, cols] = dot(dact[part, :], w1[cols, :], NT).astype(BF)

        loop(0, D // WIDE, one)

    def out_half(at):
        part = pl.ds(at, 512)

        def one(n):
            cols = pl.ds(pl.multiple_of(n * WIDE, WIDE), WIDE)
            out_h[part, cols] = dot(hidden[part, :], w2[:, cols], NN).astype(BF)

        loop(0, D // WIDE, one)

    activate(at_mine)
    wait_bytes(dv.at[mine], recv.at[3])
    push(dv.at[mine], dv.at[mine], send.at[11], core_recv.at[7], sib)
    wait_bytes(rows.at[theirs], core_recv.at[1])
    activate(at_theirs)
    wait_bytes(dv.at[theirs], core_recv.at[7])
    act_grads(at_theirs)
    in_half(at_theirs)
    push(in_h.at[theirs], in_o, send.at[3], core_recv.at[2], sib)
    act_grads(at_mine)
    in_half(at_mine)
    wait_bytes(in_o, core_recv.at[2])
    in_o[...] = (in_o[...].astype(F32) + in_h[mine, :].astype(F32)).astype(BF)
    to_chips(
        z, x, y, c,
        lambda there: in_o.at[pl.ds(pl.multiple_of(block_of(*there[:3]) - c * 512, 16), 16)],
        home_in.at[pl.ds(me, 16)], send.at[4], recv.at[1],
    )
    out_half(at_theirs)
    push(out_h.at[theirs], out_o, send.at[5], core_recv.at[3], sib)
    out_half(at_mine)
    wait_bytes(out_o, core_recv.at[3])
    out_o[...] = (out_o[...].astype(F32) + out_h[mine, :].astype(F32)).astype(BF)
    to_chips(
        z, x, y, c,
        lambda there: out_o.at[pl.ds(pl.multiple_of(block_of(*there[:3]) - c * 512, 16), 16)],
        home_out.at[pl.ds(me, 16)], send.at[6], recv.at[2],
    )

    def out_grads(n):
        cols = pl.ds(pl.multiple_of(n * WIDE, WIDE), WIDE)
        slot = n % 2

        @pl.when(n >= 2)
        def _():
            wait_bytes(stage_out.at[slot], staged.at[slot])

        stage_out[slot] = dot(hidden[:, cols], dv[...], TN)
        keep(stage_out.at[slot], g_out.at[cols], staged.at[slot])

    loop(0, FH // WIDE, out_grads)
    wait_bytes(home_in.at[mine], recv.at[1])
    push(home_in.at[mine], home_in.at[mine], send.at[7], core_recv.at[4], sib)

    def in_grads(n):
        cols = pl.ds(pl.multiple_of(n * WIDE, WIDE), WIDE)
        slot = n % 2

        @pl.when(n >= 2)
        def _():
            wait_bytes(stage_in.at[slot], staged.at[2 + slot])

        stage_in[slot] = dot(rows[:, cols], dact[...], TN)
        keep(stage_in.at[slot], g_in.at[cols], staged.at[2 + slot])

    loop(0, D // WIDE, in_grads)
    wait_bytes(home_out.at[mine], recv.at[2])
    push(home_out.at[mine], home_out.at[mine], send.at[8], core_recv.at[5], sib)
    for slot in range(2):
        wait_bytes(stage_out.at[slot], staged.at[slot])
        wait_bytes(stage_in.at[slot], staged.at[2 + slot])
    wait_bytes(xo, send.at[0])
    sent_to_chips(rows, y, c, send.at[1])
    wait_bytes(rows.at[mine], send.at[2])
    wait_bytes(in_o, send.at[3])
    sent_to_chips(home_in, y, c, send.at[4])
    wait_bytes(out_o, send.at[5])
    sent_to_chips(home_out, y, c, send.at[6])
    wait_bytes(home_in.at[theirs], core_recv.at[4])
    wait_bytes(home_out.at[theirs], core_recv.at[5])
    wait_bytes(home_in.at[mine], send.at[7])
    wait_bytes(home_out.at[mine], send.at[8])
    wait_bytes(eo, send.at[9])
    sent_to_chips(dv, y, c, send.at[10])
    wait_bytes(dv.at[mine], send.at[11])


def run_experts(x16, d_eo, w_in, w_out):
    whole_rows = pltpu.VMEM((1024, D), BF)
    half_rows = pltpu.VMEM((512, D), BF)
    hid = pltpu.VMEM((1024, FH), BF)
    return pl.pallas_call(
        experts_kernel,
        out_shape=(
            jax.ShapeDtypeStruct((1024, D), BF),
            jax.ShapeDtypeStruct((1024, D), BF),
            jax.ShapeDtypeStruct((D, FH), F32),
            jax.ShapeDtypeStruct((FH, D), F32),
        ),
        in_specs=[ANY] * 4,
        out_specs=(ANY,) * 4,
        scratch_shapes=[
            half_rows, half_rows, half_rows, half_rows, whole_rows, whole_rows,
            pltpu.VMEM((D, FH), BF), pltpu.VMEM((FH, D), BF), pltpu.VMEM((1024, FH), F32),
            hid, hid, whole_rows, whole_rows, half_rows, half_rows,
            pltpu.VMEM((2, WIDE, D), F32), pltpu.VMEM((2, WIDE, FH), F32),
            DMA((12,)), DMA((4,)), DMA((8,)), DMA((4,)), DMA((4,)),
        ],
        compiler_params=pltpu.CompilerParams(
            collective_id=1, has_side_effects=True, vmem_limit_bytes=48 * 2**20
        ),
        name="experts",
    )(x16, d_eo, w_in, w_out)


def z_kernel(blocks, out, send, recv):
    z, x, y, c = place()
    for k in range(1, 4):
        signal(((z + k) % 4, x, y, c))
    arrive(3)
    for k in range(1, 4):
        there = (z + k) % 4
        push(blocks.at[there], out.at[z], send, recv, (there, x, y, c))
    keep(blocks.at[z], out.at[z], recv)
    wait_bytes(out, recv)
    wait_bytes(out.at[pl.ds(0, 3)], send)


def z_exchange(blocks, collective_id, name):
    return run_comm(
        z_kernel,
        (blocks,),
        jax.ShapeDtypeStruct(blocks.shape, blocks.dtype),
        [DMA, DMA],
        collective_id,
        name,
    )


def device_of(d):
    return d // 32, (d // 8) % 4, (d // 2) % 4, d % 2


def finish_kernel(
    normed, qkv, att, small, tok, gain, d_middle,
    input_grad, qkv_out, att_out, small_out,
    normed_in, q_own, q_sib, q_in, a_own, a_sib, a_in, s_own, s_sib, s_tot, s_in,
    qkv_sum, att_sum, s_sum, send, recv, core_recv, own,
):
    z, x, y, c = place()
    sib = (z, x, y, 1 - c)
    p16 = x * 4 + y
    p = p16 * 2 + c
    me = z * 32 + p
    source = me // 4

    def peer(i):
        return z, (x + i // 4) % 4, (y + i % 4) % 4, c

    keep(qkv.at[:, c], q_own, own.at[0])
    keep(att.at[:, c], a_own, own.at[1])
    loop(1, 16, lambda i: signal(peer(i)))
    for k in range(1, 4):
        signal(((z + k) % 4, x, y, c))
    signal(sib)

    def greet(k):
        @pl.when(jnp.logical_not((k == z) & (source == p)))
        def _():
            signal((k, source // 8, (source // 2) % 4, source % 2))

    loop(0, 4, greet)
    arrive(15 + 3 + 1 + 4 - jnp.where(source == p, 1, 0))
    for k in range(1, 4):
        there = (z + k) % 4
        push(normed.at[there], normed_in.at[z], send.at[0], recv.at[0], (there, x, y, c))
    keep(normed.at[z], normed_in.at[z], recv.at[0])
    push(qkv.at[:, 1 - c], q_sib, send.at[1], core_recv.at[0], sib)
    push(att.at[:, 1 - c], a_sib, send.at[2], core_recv.at[1], sib)
    wait_bytes(q_own, own.at[0])
    wait_bytes(q_sib, core_recv.at[0])

    def qkv_blocks(i):
        there = peer(i)
        j = there[1] * 4 + there[2]
        q_own[j] = (q_own[j].astype(F32) + q_sib[j].astype(F32)).astype(BF)
        push(q_own.at[j], q_in.at[p16], send.at[3], recv.at[1], there)

    loop(1, 16, qkv_blocks)
    q_own[p16] = (q_own[p16].astype(F32) + q_sib[p16].astype(F32)).astype(BF)
    keep(q_own.at[p16], q_in.at[p16], recv.at[1])
    wait_bytes(a_own, own.at[1])
    wait_bytes(a_sib, core_recv.at[1])

    def att_blocks(i):
        there = peer(i)
        j = there[1] * 4 + there[2]
        a_own[j] = (a_own[j].astype(F32) + a_sib[j].astype(F32)).astype(BF)
        push(a_own.at[j], a_in.at[p16], send.at[4], recv.at[2], there)

    loop(1, 16, att_blocks)
    a_own[p16] = (a_own[p16].astype(F32) + a_sib[p16].astype(F32)).astype(BF)
    keep(a_own.at[p16], a_in.at[p16], recv.at[2])

    wait_bytes(normed_in, recv.at[0])
    d_normed = normed_in[0].astype(F32)
    for k in range(1, 4):
        d_normed = d_normed + normed_in[k].astype(F32)
    v = tok[...].astype(F32)
    r = lax.rsqrt(jnp.mean(v * v, axis=1, keepdims=True) + norm_eps)
    unit = v * r
    s_own[...] = small[...]
    s_own[0:1, :] = jnp.sum(d_normed * unit, axis=0, keepdims=True)
    push(s_own, s_sib, send.at[5], core_recv.at[2], sib)
    d_unit = d_normed * gain[...]
    d_in = r * (d_unit - unit * jnp.mean(d_unit * unit, axis=1, keepdims=True))
    input_grad[...] = (d_middle[...] + d_in).astype(BF)
    wait_bytes(s_sib, core_recv.at[2])
    s_tot[...] = s_own[...] + s_sib[...]
    loop(1, 16, lambda i: push(s_tot, s_in.at[p16], send.at[6], recv.at[3], peer(i)))
    keep(s_tot, s_in.at[p16], recv.at[3])

    wait_bytes(q_in, recv.at[1])
    total = q_in[0].astype(F32)
    for q in range(1, 16):
        total = total + q_in[q].astype(F32)
    for k in range(4):
        qkv_sum[k, 0:6, :] = total[6 * k : 6 * k + 6]
        qkv_sum[k, 6:8, :] = jnp.zeros((2, 3 * GW), F32)

    def final(k):
        d = 4 * p + k

        @pl.when(d != me)
        def _():
            push(qkv_sum.at[k], qkv_out.at[z], send.at[7], recv.at[4], device_of(d))

        @pl.when(d == me)
        def _():
            keep(qkv_sum.at[k], qkv_out.at[z], recv.at[4])

    loop(0, 4, final)
    wait_bytes(a_in, recv.at[2])
    att_total = a_in[0].astype(F32)
    for q in range(1, 16):
        att_total = att_total + a_in[q].astype(F32)
    att_sum[...] = att_total
    keep(att_sum, att_out, own.at[2])
    wait_bytes(s_in, recv.at[3])
    s_total = s_in[0]
    for q in range(1, 16):
        s_total = s_total + s_in[q]
    s_sum[...] = s_total
    for k in range(1, 4):
        push(s_sum, small_out.at[z], send.at[8], recv.at[5], ((z + k) % 4, x, y, c))
    keep(s_sum, small_out.at[z], recv.at[5])
    wait_bytes(att_sum, own.at[2])
    wait_bytes(qkv_out, recv.at[4])
    wait_bytes(small_out, recv.at[5])
    wait_bytes(normed_in.at[pl.ds(0, 3)], send.at[0])
    wait_bytes(q_sib, send.at[1])
    wait_bytes(a_sib, send.at[2])
    wait_bytes(q_in.at[pl.ds(0, 15)], send.at[3])
    wait_bytes(a_in.at[pl.ds(0, 15)], send.at[4])
    wait_bytes(s_own, send.at[5])
    wait_bytes(s_in.at[pl.ds(0, 15)], send.at[6])

    def sent(k):
        @pl.when(4 * p + k != me)
        def _():
            wait_bytes(qkv_sum.at[0], send.at[7])

    loop(0, 4, sent)
    wait_bytes(small_out.at[pl.ds(0, 3)], send.at[8])


def finish(normed, qkv, att, small, tok, gain, d_middle):
    return pl.pallas_call(
        finish_kernel,
        out_shape=(
            jax.ShapeDtypeStruct((TOK, D), BF),
            jax.ShapeDtypeStruct((4, 8, 3 * GW), F32),
            jax.ShapeDtypeStruct((8, D), F32),
            jax.ShapeDtypeStruct((4, 8, D), F32),
        ),
        in_specs=[ANY, ANY, ANY] + [pl.BlockSpec(memory_space=pltpu.VMEM)] * 4,
        out_specs=(pl.BlockSpec(memory_space=pltpu.VMEM), ANY, ANY, ANY),
        scratch_shapes=[
            pltpu.VMEM((4, TOK, D), BF),
            pltpu.VMEM((16, 24, 3 * GW), BF),
            pltpu.VMEM((16, 24, 3 * GW), BF),
            pltpu.VMEM((16, 24, 3 * GW), BF),
            pltpu.VMEM((16, 8, D), BF),
            pltpu.VMEM((16, 8, D), BF),
            pltpu.VMEM((16, 8, D), BF),
            pltpu.VMEM((8, D), F32),
            pltpu.VMEM((8, D), F32),
            pltpu.VMEM((8, D), F32),
            pltpu.VMEM((16, 8, D), F32),
            pltpu.VMEM((4, 8, 3 * GW), F32),
            pltpu.VMEM((8, D), F32),
            pltpu.VMEM((8, D), F32),
            DMA((9,)),
            DMA((6,)),
            DMA((3,)),
            DMA((3,)),
        ],
        compiler_params=pltpu.CompilerParams(
            collective_id=4, has_side_effects=True, vmem_limit_bytes=32 * 2**20
        ),
        name="finish",
    )(normed, qkv, att, small, tok, gain, d_middle)


NT = (((1,), (1,)), ((), ()))
NN = (((1,), (0,)), ((), ()))
TN = (((0,), (0,)), ((), ()))


def dot(a, b, dims):
    return lax.dot_general(a, b, dims, preferred_element_type=F32)


def near_distance(dist):
    a = lax.broadcasted_iota(jnp.int32, (TOK, TOK), 0)
    b = lax.broadcasted_iota(jnp.int32, (TOK, TOK), 1)
    return dist * TOK + a - b


def table_kind(zq, zk, x, kx):
    return jnp.clip((zq - zk) * 4 + x - kx + 1, 0, 3)


def block_cols(zk, kx):
    return pl.ds(pl.multiple_of((zk * 4 + kx) * TOK, TOK), TOK)


VMEM = pl.BlockSpec(memory_space=pltpu.VMEM)
SMEM = pl.BlockSpec(memory_space=pltpu.SMEM)


def attn_forward_kernel(
    tab, q, kv, qd, kd, wa,
    attn_all, part, p_out, kv_out, wa_all,
    kv_s, v_s, qm, bias, s_s, p_s, wm, wo,
    send, recv, kv_recv, core_recv, own,
):
    z, x, y, c = place()
    sib = (z, x, y, 1 - c)
    expected = greet_chips(z, x, y, c)
    for k in range(1, 4):
        signal(((z + k) % 4, x, y, c))
        signal((z, (x + k) % 4, y, c))
    arrive(expected + 6)
    for k in range(1, 4):
        for b in range(4):
            push(
                kv.at[b], kv_s.at[block_cols(b, x)], send.at[0], kv_recv.at[4 - k],
                (z, (x + k) % 4, y, c),
            )
    for b in range(4):
        keep(kv.at[b], kv_s.at[block_cols(b, x)], kv_recv.at[0])
    push(wa, wo, send.at[1], core_recv.at[0], sib)
    for h in range(GH):
        head_cols = lax.broadcasted_iota(jnp.int32, (1, GW), 1) // HD == h
        qm[h] = jnp.where(head_cols, q[...] * 0.125, 0.0).astype(BF)
    wait_bytes(wo, core_recv.at[0])
    wm[...] = wa[...] + wo[...]

    def tables(h):
        for dist in range(2):
            n = near_distance(dist)
            acc = jnp.full((TOK, TOK), tab[0, h], F32)
            for k, edge in enumerate(bucket_edges):
                acc = jnp.where(n >= edge, tab[k + 1, h], acc)
            bias[h, 1 + dist] = jnp.where(n >= 0, acc, masked)
        bias[h, 0] = jnp.full((TOK, TOK), masked, F32)
        bias[h, 3] = jnp.full((TOK, TOK), tab[BUCKETS - 1, h], F32)

    loop(0, GH, tables)
    for k in range(4):
        kx = (x + k) % 4
        if k == 0:
            for b in range(4):
                wait_bytes(kv_s.at[block_cols(b, kx)], kv_recv.at[0])
        else:
            wait_bytes(kv_s.at[pl.ds(0, 512)], kv_recv.at[k])
        for b in range(4):
            cols = block_cols(b, kx)
            v_s[cols, :] = kv_s[cols, GW:]
            for h in range(GH):
                s_s[h, b * TOK :, cols] = dot(qm[h, b * TOK :, :], kv_s[cols, :GW], NT)
    keep(kv_s, kv_out, own.at[1])
    half = z * 8 + x * 2 + y // 2
    to_chips(z, x, y, c, lambda there: wm, wa_all.at[half, y % 2], send.at[3], recv.at[0])

    def head(h):
        head_cols = lax.broadcasted_iota(jnp.int32, (1, GW), 1) // HD == h
        far = tab[BUCKETS - 1, h]
        for zq in range(4):
            rows = pl.ds(zq * TOK, TOK)
            docs = qd[rows, :]
            top = None
            for zk in range(zq + 1):
                for kx in range(4):
                    cols = pl.ds((zk * 4 + kx) * TOK, TOK)
                    s = s_s[h, rows, cols]
                    if zk < zq - 1:
                        s = s + far
                    else:
                        s = s + bias[h, table_kind(zq, zk, x, kx)]
                    s = jnp.where(docs == kd[:, cols], s, masked)
                    s_s[h, rows, cols] = s
                    top = s if top is None else jnp.maximum(top, s)
            top = jnp.max(top, axis=1, keepdims=True)
            total = jnp.zeros((TOK, TOK), F32)
            for kb in range(4 * (zq + 1)):
                cols = pl.ds(kb * TOK, TOK)
                e = jnp.exp(s_s[h, rows, cols] - top)
                s_s[h, rows, cols] = e
                total = total + e
            inv = 1.0 / jnp.sum(total, axis=1, keepdims=True)
            for kb in range(4 * (zq + 1)):
                cols = pl.ds(kb * TOK, TOK)
                p_s[h, rows, cols] = (s_s[h, rows, cols] * inv).astype(BF)
            width = (zq + 1) * 512
            o = dot(p_s[h, rows, :width], v_s[:width, :], NN).astype(BF)

            @pl.when(h == 0)
            def _():
                part[rows, :] = o

            @pl.when(h > 0)
            def _():
                part[rows, :] = jnp.where(head_cols, o, part[rows, :])

    loop(0, GH, head)
    for k in range(1, 4):
        there = (z + k) % 4
        push(
            part.at[pl.ds(pl.multiple_of(there * TOK, TOK), TOK)], attn_all.at[z],
            send.at[6], recv.at[2], (there, x, y, c),
        )
    keep(part.at[pl.ds(pl.multiple_of(z * TOK, TOK), TOK)], attn_all.at[z], recv.at[2])
    keep(p_s, p_out, own.at[2])
    wait_bytes(wa_all.at[:, c], recv.at[0])
    push(wa_all.at[:, c], wa_all.at[:, c], send.at[5], core_recv.at[2], sib)
    wait_bytes(attn_all, recv.at[2])
    wait_bytes(wa_all.at[:, 1 - c], core_recv.at[2])
    wait_bytes(kv_s, own.at[1])
    wait_bytes(p_s, own.at[2])
    wait_bytes(kv_s.at[pl.ds(0, 1536)], send.at[0])
    wait_bytes(wo, send.at[1])
    wait_bytes(wa_all.at[pl.ds(0, 31), c], send.at[3])

    @pl.when(y % 2 != c)
    def _():
        wait_bytes(wa_all.at[0, c], send.at[3])

    wait_bytes(wa_all.at[:, c], send.at[5])
    wait_bytes(attn_all.at[pl.ds(0, 3)], send.at[6])


def attn_forward(tab, q, kv, qd, kd, wa):
    probs = (GH, 512, 2048)
    return pl.pallas_call(
        attn_forward_kernel,
        out_shape=(
            jax.ShapeDtypeStruct((4, TOK, GW), BF),
            jax.ShapeDtypeStruct((512, GW), BF),
            jax.ShapeDtypeStruct(probs, BF),
            jax.ShapeDtypeStruct((2048, 2 * GW), BF),
            jax.ShapeDtypeStruct((32, 2, 16, D), BF),
        ),
        in_specs=[SMEM, VMEM, VMEM, VMEM, VMEM, VMEM],
        out_specs=(ANY, VMEM, ANY, ANY, ANY),
        scratch_shapes=[
            pltpu.VMEM((2048, 2 * GW), BF),
            pltpu.VMEM((2048, GW), BF),
            pltpu.VMEM((GH, 512, GW), BF),
            pltpu.VMEM((GH, 4, TOK, TOK), F32),
            pltpu.VMEM(probs, F32),
            pltpu.VMEM(probs, BF),
            pltpu.VMEM((16, D), BF),
            pltpu.VMEM((16, D), BF),
            DMA((8,)),
            DMA((3,)),
            DMA((4,)),
            DMA((4,)),
            DMA((3,)),
        ],
        compiler_params=pltpu.CompilerParams(
            collective_id=2, has_side_effects=True, vmem_limit_bytes=44 * 2**20
        ),
        name="attn_forward",
    )(tab, q, kv, qd, kd, wa)


def attn_backward_kernel(
    p, q, kv, d_attn, branch, dq, tab, parts, branch_all,
    p_s, v_s, do_s, dm, qm, dp_s, ds_s, near, messages,
    send, recv, own,
):
    z, x, y, c = place()
    keep(p, p_s, own)
    for k in range(1, 4):
        signal(((z + k) % 4, x, y, c))
        signal((z, (x + k) % 4, y, c))
    arrive(6)
    for k in range(1, 4):
        there = (z + k) % 4
        push(d_attn.at[there], do_s.at[z], send.at[0], recv.at[0], (there, x, y, c))
    keep(d_attn.at[z], do_s.at[z], recv.at[0])
    for k in range(1, 4):
        push(branch, branch_all.at[z], send.at[1], recv.at[1], ((z + k) % 4, x, y, c))
    keep(branch, branch_all.at[z], recv.at[1])
    v_s[...] = kv[:, GW:]
    for h in range(GH):
        head_cols = lax.broadcasted_iota(jnp.int32, (1, GW), 1) // HD == h
        qm[h] = jnp.where(head_cols, q[...] * 0.125, 0.0).astype(BF)
    wait_bytes(do_s, recv.at[0])
    for h in range(GH):
        head_cols = lax.broadcasted_iota(jnp.int32, (1, GW), 1) // HD == h
        for b in range(4):
            dm[h, b * TOK : (b + 1) * TOK, :] = jnp.where(head_cols, do_s[b], 0.0).astype(BF)
    wait_bytes(p_s, own)

    def key_sums(left, right, first):
        for k in (1, 2, 3, 0):
            kx = (x + k) % 4
            for b in range(4):
                cols = block_cols(b, kx)
                total = None
                for h in range(GH):
                    one = dot(left[h, b * TOK :, cols], right[h, b * TOK :, :], TN)
                    total = one if total is None else total + one
                side = GW * (b % 2)
                messages[k, first + b // 2, :, side : side + GW] = total.astype(BF)
            for m in range(first, first + 2):
                if k:
                    push(
                        messages.at[k, m], parts.at[x, m], send.at[2], recv.at[2],
                        (z, kx, y, c),
                    )
                else:
                    keep(messages.at[k, m], parts.at[x, m], recv.at[2])

    key_sums(p_s, dm, 0)

    def head(h):
        head_cols = lax.broadcasted_iota(jnp.int32, (1, GW), 1) // HD == h
        for zk in range(4):
            cols = pl.ds(zk * 512, 512)
            dp_s[zk * TOK :, cols] = dot(dm[h, zk * TOK :, :], v_s[cols, :], NT)
        near[...] = jnp.zeros_like(near)
        for zq in range(4):
            rows = pl.ds(zq * TOK, TOK)
            acc = jnp.zeros((TOK, TOK), F32)
            for kb in range(4 * (zq + 1)):
                cols = pl.ds(kb * TOK, TOK)
                acc = acc + p_s[h, rows, cols].astype(F32) * dp_s[rows, cols]
            delta = jnp.sum(acc, axis=1, keepdims=True)
            far = jnp.zeros((TOK, TOK), F32)
            for zk in range(zq + 1):
                for kx in range(4):
                    cols = pl.ds((zk * 4 + kx) * TOK, TOK)
                    ds = (p_s[h, rows, cols].astype(F32) * (dp_s[rows, cols] - delta)).astype(BF)
                    ds_s[h, rows, cols] = ds
                    if zk < zq - 1:
                        far = far + ds.astype(F32)
                    else:
                        near[table_kind(zq, zk, x, kx)] += ds.astype(F32)
            near[3] += far
            width = (zq + 1) * 512
            o = (dot(ds_s[h, rows, :width], kv[:width, :GW], NN) * 0.125).astype(BF)

            @pl.when(h == 0)
            def _():
                dq[rows, :] = o

            @pl.when(h > 0)
            def _():
                dq[rows, :] = jnp.where(head_cols, o, dq[rows, :])

        for dist in range(2):
            n = near_distance(dist)
            held = near[1 + dist]
            bounds = [-(10**6)] + bucket_edges + [10**6]
            for b in range(BUCKETS):
                low, high = bounds[b], bounds[b + 1]
                if high <= dist * TOK - TOK + 1 or low > dist * TOK + TOK - 1:
                    if dist == 0:
                        tab[h, b : b + 1, :] = jnp.zeros((1, TOK), F32)
                    continue
                inside = jnp.sum(
                    jnp.where((n >= low) & (n < high), held, 0.0), axis=0, keepdims=True
                )
                if dist == 0:
                    tab[h, b : b + 1, :] = inside
                else:
                    tab[h, b : b + 1, :] += inside
        tab[h, BUCKETS - 1 :, :] += jnp.sum(near[3], axis=0, keepdims=True)

    loop(0, GH, head)
    key_sums(ds_s, qm, 2)
    wait_bytes(parts, recv.at[2])
    wait_bytes(branch_all, recv.at[1])
    wait_bytes(do_s.at[pl.ds(0, 3)], send.at[0])
    wait_bytes(branch_all.at[pl.ds(0, 3)], send.at[1])
    wait_bytes(parts.at[pl.ds(0, 3)], send.at[2])


def attn_backward(p, q, kv, d_attn, branch):
    probs = (GH, 512, 2048)
    return pl.pallas_call(
        attn_backward_kernel,
        out_shape=(
            jax.ShapeDtypeStruct((512, GW), BF),
            jax.ShapeDtypeStruct((GH, BUCKETS, TOK), F32),
            jax.ShapeDtypeStruct((4, 4, TOK, 2 * GW), BF),
            jax.ShapeDtypeStruct((4, TOK, D), BF),
        ),
        in_specs=[ANY, VMEM, VMEM, VMEM, VMEM],
        out_specs=(VMEM, VMEM, ANY, ANY),
        scratch_shapes=[
            pltpu.VMEM(probs, BF),
            pltpu.VMEM((2048, GW), BF),
            pltpu.VMEM((4, TOK, GW), BF),
            pltpu.VMEM((GH, 512, GW), BF),
            pltpu.VMEM((GH, 512, GW), BF),
            pltpu.VMEM((512, 2048), F32),
            pltpu.VMEM(probs, BF),
            pltpu.VMEM((4, TOK, TOK), F32),
            pltpu.VMEM((4, 4, TOK, 2 * GW), BF),
            DMA((3,)),
            DMA((3,)),
            DMA,
        ],
        compiler_params=pltpu.CompilerParams(
            collective_id=3, has_side_effects=True, vmem_limit_bytes=44 * 2**20
        ),
        name="attn_backward",
    )(p, q, kv, d_attn, branch)


def per_device(
    tokens,
    gain_attn,
    w_qkv,
    w_attn_out,
    rel_table,
    gain_moe,
    w_in,
    w_out,
    expert_ids,
    gate_values,
    doc_ids,
    cotangent,
):
    z, x, y, c = place()
    experts = 64
    capacity = 8
    slots = 2 * experts * capacity
    own_tokens = tokens.reshape(TOK, D)
    grad_bf = cotangent.reshape(TOK, D)
    grad_out = grad_bf.astype(F32)

    route = expert_ids.reshape(TOK * 2)
    marks = (route[:, None] == jnp.arange(experts, dtype=jnp.int32)[None, :]).astype(jnp.int32)
    earlier = jnp.cumsum(marks, axis=0) - marks
    block = (route % 2) * 32 + (route // 4) * 2 + (route % 4) // 2
    slot = block * 16 + c * capacity + jnp.sum(earlier * marks, axis=1)
    slot_pair = slot.reshape(TOK, 2)
    gates = gate_values.reshape(TOK, 2)
    slot_ids = jnp.arange(slots, dtype=jnp.int32)
    pick_0 = slot_pair[:, 0][:, None] == slot_ids[None, :]
    pick_1 = slot_pair[:, 1][:, None] == slot_ids[None, :]
    pick = (pick_0 | pick_1).astype(BF)
    gate_of = jnp.where(pick_0, gates[:, :1], 0.0) + jnp.where(pick_1, gates[:, 1:], 0.0)
    gate_slot = jnp.sum(gate_of, axis=0)
    d_eo = (dot(pick, grad_bf, TN) * gate_slot[:, None]).astype(BF)

    slab = w_qkv.reshape(6, 3, GROUPS, GW).transpose(2, 0, 1, 3).reshape(GROUPS, 6, 3 * GW)
    notes = jnp.concatenate(
        [
            gain_attn, gain_moe, jnp.zeros((116,), BF),
            doc_ids.reshape(TOK).astype(BF), jnp.zeros((3 * GW - 256,), BF),
        ]
    )
    notes = jnp.broadcast_to(notes, (GROUPS, 1, 3 * GW))
    nothing = jnp.zeros((GROUPS, 6, 3 * GW), BF)
    message = jnp.where(
        c == 0,
        jnp.concatenate([slab, nothing, notes, nothing[:, :3]], axis=1),
        jnp.concatenate([nothing, slab, nothing[:, :1], notes, nothing[:, :2]], axis=1),
    )
    zero_rows = jnp.zeros((6, D), BF)
    out_slab = jnp.where(
        c == 0,
        jnp.concatenate([w_attn_out, zero_rows, zero_rows[:4]], axis=0),
        jnp.concatenate([zero_rows, w_attn_out, zero_rows[:4]], axis=0),
    )
    tok_all, w_all = start_exchange(own_tokens, message)

    weight = w_all[:, :, :12, :].reshape(D, 3 * GW)
    gain_one = w_all[:, :, 12:14, 0:6].reshape(D).astype(F32)
    gain_two = w_all[:, :, 12:14, 6:12].reshape(D).astype(F32)
    doc_rows = w_all[:, :, 12:14, 128:256].reshape(16, 4, 2, TOK)
    doc_rows = lax.dynamic_slice(doc_rows, (0, y, c, 0), (16, 1, 1, TOK)).reshape(16, TOK).astype(F32)
    key_docs = doc_rows.reshape(1, 2048)
    query_docs = lax.dynamic_slice(doc_rows.reshape(4, 4, TOK), (0, x, 0), (4, 1, TOK)).reshape(512, 1)

    inputs_all = tok_all.reshape(512, D).astype(F32)
    normed = scale_rows(inputs_all, gain_one).astype(BF)
    qkv = dot(normed, weight, NN).astype(BF)
    queries = qkv[:, :GW]
    table = lax.dynamic_slice(rel_table, (0, z * GH), (BUCKETS, GH)).astype(F32)
    attn, attn_part, probs, kv_all, out_weights = attn_forward(
        table, queries, qkv[:, GW:].reshape(4, TOK, 2 * GW), query_docs, key_docs, out_slab
    )
    attn = attn.transpose(1, 0, 2).reshape(TOK, D)
    attention_weight = out_weights[:, :, :12, :].reshape(D, D)

    inputs = own_tokens.astype(F32)
    middle = inputs + dot(attn, attention_weight, NN)
    moe_float, norm_two_back = jax.vjp(scale_rows, middle, gain_two)
    moe_in = moe_float.astype(BF)
    send_rows = dot(pick, moe_in, TN).astype(BF)
    home, expert_out, expert_in_grad, expert_out_grad = run_experts(
        send_rows, d_eo, w_in[0], w_out[0]
    )
    moe_in_grad = dot(pick, home, NN)
    middle_part, gain_two_grad = norm_two_back(moe_in_grad)
    middle_grad = grad_out + middle_part
    branch = middle_grad.astype(BF)
    d_attn = dot(branch, attention_weight, NT).astype(BF)
    d_attn = d_attn.reshape(TOK, GROUPS, GW).transpose(1, 0, 2)

    d_q, table_part, kv_parts, branch_all = attn_backward(probs, queries, kv_all, d_attn, branch)
    d_kv = jnp.sum(kv_parts.astype(F32), axis=0).astype(BF)
    d_kv = d_kv.reshape(2, 2, TOK, 2, GW).transpose(0, 1, 3, 2, 4).reshape(2, 512, GW)
    d_kv = jnp.concatenate([d_kv[1], d_kv[0]], axis=1)
    d_qkv = jnp.concatenate([d_q, d_kv], axis=1)
    normed_part = dot(d_qkv, weight, NT).astype(BF).reshape(4, TOK, D)
    both = jnp.concatenate([pick_0, pick_1], axis=0).astype(BF)
    picked = dot(both, expert_out, NN).reshape(2, TOK, D)
    block_out = middle + gates[:, :1] * picked[0] + gates[:, 1:] * picked[1]
    gate_grad = jnp.sum(picked * grad_out[None], axis=2).T

    qkv_part = dot(normed, d_qkv, TN).astype(BF).reshape(16, 2, 24, 3 * GW)
    att_part = dot(attn_part, branch_all.reshape(512, D), TN).astype(BF).reshape(16, 2, 6, D)
    att_part = jnp.pad(att_part, ((0, 0), (0, 0), (0, 2), (0, 0)))
    table_sum = jnp.sum(table_part, axis=2).reshape(1, GH * BUCKETS)
    small = jnp.concatenate(
        [
            jnp.zeros((1, D), F32),
            gain_two_grad.reshape(1, D),
            jnp.pad(table_sum, ((0, 0), (0, D - GH * BUCKETS))),
            jnp.zeros((5, D), F32),
        ]
    )
    input_grad, qkv_sum, att_sum, small_sum = finish(
        normed_part, qkv_part, att_part, small, own_tokens, gain_one.reshape(1, D), middle_grad
    )
    qkv_grad = qkv_sum[:, :6, :].reshape(GROUPS, 6, 3, GW).transpose(1, 2, 0, 3).reshape(6, 3 * D)
    attn_out_grad = att_sum[:6]
    place_in = chip_of(z, x, y) * 2 + c
    gains = lax.dynamic_slice(jnp.sum(small_sum[:, :2, :], axis=0), (0, place_in * 6), (2, 6))
    table_grad = small_sum[:, 2, : GH * BUCKETS].reshape(GROUPS * GH, BUCKETS).T
    return (
        block_out.reshape(1, TOK, D).astype(BF),
        input_grad.reshape(1, TOK, D),
        gate_grad.reshape(1, TOK, 2),
        gains[0],
        qkv_grad,
        attn_out_grad,
        table_grad,
        gains[1],
        expert_in_grad[None],
        expert_out_grad[None],
    )


def solution(mesh):
    torus = Mesh(mesh.devices.reshape(4, 4, 4, 2), AXES)
    in_specs = (
        P(EXP, CTX, None),
        P(AXES),
        P(AXES, None),
        P(AXES, None),
        P(),
        P(AXES),
        P(AXES, None, None),
        P(AXES, None, None),
        P(EXP, CTX, None),
        P(EXP, CTX, None),
        P(EXP, CTX),
        P(EXP, CTX, None),
    )
    out_specs = (
        P(EXP, CTX, None),
        P(EXP, CTX, None),
        P(EXP, CTX, None),
        P(AXES),
        P(AXES, None),
        P(AXES, None),
        P(),
        P(AXES),
        P(AXES, None, None),
        P(AXES, None, None),
    )
    return jax.shard_map(
        per_device, mesh=torus, in_specs=in_specs, out_specs=out_specs, check_vma=False
    )
```

```python
import functools

import jax
import jax.numpy as jnp
import numpy as np
from jax import lax
from jax.experimental import pallas as pl
from jax.experimental.pallas import tpu as pltpu
from jax.sharding import Mesh
from jax.sharding import PartitionSpec as P

D = 768
H = 12
HD = 64
BUCKETS = 32
GROUPS = 4
GH = H // GROUPS
GW = GH * HD
TOK = 128
CTX = ("ctx_0", "ctx_1")
EXP = ("exp_0", "exp_1")
AXES = ("ctx_0", "ctx_1", "exp_0", "exp_1")
MESH = pl.DeviceIdType.MESH
ANY = pl.BlockSpec(memory_space=pl.ANY)
BF = jnp.bfloat16
F32 = jnp.float32

norm_eps = 1e-06
bucket_edges = [int(e) for e in np.concatenate(
    [np.arange(1, 17), np.ceil(16.0 * 8.0 ** (np.arange(1, 16) / 16.0))]
).astype(np.int32)]
masked = -1e30


def scale_rows(values, gain):
    return values * lax.rsqrt(jnp.mean(values * values, axis=-1, keepdims=True) + norm_eps) * gain


def place():
    return tuple(lax.axis_index(a) for a in AXES)


def chip_of(z, x, y):
    return (z * 4 + x) * 4 + y


def chip_peer(i, z, x, y):
    return (z + i // 16) % 4, (x + (i // 4) % 4) % 4, (y + i % 4) % 4


def loop(first, last, body):
    lax.fori_loop(first, last, lambda i, carry: (body(i), carry)[1], 0)


def signal(device):
    pl.semaphore_signal(
        pltpu.get_barrier_semaphore(), inc=1, device_id=device, device_id_type=MESH
    )


def arrive(count):
    pl.semaphore_wait(pltpu.get_barrier_semaphore(), count)


def push(src, dst, send, recv, device):
    pltpu.make_async_remote_copy(
        src_ref=src, dst_ref=dst, send_sem=send, recv_sem=recv, device_id=device, device_id_type=MESH
    ).start()


def keep(src, dst, sem):
    pltpu.make_async_copy(src, dst, sem).start()


def wait_bytes(ref, sem):
    pltpu.make_async_copy(ref, ref, sem).wait()


def comm_call(kernel, outs, scratch, collective_id, name):
    return pl.pallas_call(
        kernel,
        out_shape=outs,
        in_specs=None,
        out_specs=jax.tree.map(lambda _: ANY, outs),
        scratch_shapes=scratch,
        compiler_params=pltpu.CompilerParams(
            collective_id=collective_id, has_side_effects=True, vmem_limit_bytes=32 * 2**20
        ),
        name=name,
    )


def run_comm(kernel, args, outs, scratch, collective_id, name):
    return pl.pallas_call(
        kernel,
        out_shape=outs,
        in_specs=[ANY] * len(args),
        out_specs=jax.tree.map(lambda _: ANY, outs),
        scratch_shapes=scratch,
        compiler_params=pltpu.CompilerParams(
            collective_id=collective_id, has_side_effects=True, vmem_limit_bytes=32 * 2**20
        ),
        name=name,
    )(*args)


DMA = pltpu.SemaphoreType.DMA


def half_peer(i, z, x, y, c):
    return (z + i // 8) % 4, (x + (i // 2) % 4) % 4, c + 2 * ((y // 2 + i % 2) % 2), y % 2


def block_of(z, x, y):
    return pl.multiple_of((y % 2) * 512 + ((z * 4 + x) * 2 + y // 2) * 16, 16)


def greet_chips(z, x, y, c):
    loop(1, 32, lambda i: signal(half_peer(i, z, x, y, c)))

    @pl.when(y % 2 != c)
    def _():
        signal(half_peer(0, z, x, y, c))

    signal((z, x, y, 1 - c))
    return 32 + jnp.where(y % 2 == c, 0, 1)


def to_chips(z, x, y, c, source, target, send, recv):
    def one(i):
        there = half_peer(i, z, x, y, c)
        push(source(there), target, send, recv, there)

    loop(1, 32, one)
    first = half_peer(0, z, x, y, c)

    @pl.when(y % 2 == c)
    def _():
        keep(source(first), target, recv)

    @pl.when(y % 2 != c)
    def _():
        push(source(first), target, send, recv, first)


def sent_to_chips(rows, y, c, send):
    wait_bytes(rows.at[pl.ds(0, 496)], send)

    @pl.when(y % 2 != c)
    def _():
        wait_bytes(rows.at[pl.ds(0, 16)], send)


def start_kernel(tok, wmsg, tok_all, w_all, wm, wo, send, recv, core_recv, own):
    z, x, y, c = place()
    sib = (z, x, y, 1 - c)
    keep(wmsg, wm, own)
    expected = greet_chips(z, x, y, c)
    for k in range(1, 4):
        signal(((z + k) % 4, x, y, c))
    arrive(expected + 3)
    push(wmsg, wo, send.at[0], core_recv.at[0], sib)
    for k in range(1, 4):
        push(tok, tok_all.at[z], send.at[1], recv.at[0], ((z + k) % 4, x, y, c))
    keep(tok, tok_all.at[z], recv.at[0])
    wait_bytes(wm, own)
    wait_bytes(wo, core_recv.at[0])
    wm[...] = wm[...] + wo[...]
    half = z * 8 + x * 2 + y // 2
    to_chips(
        z, x, y, c, lambda there: wm.at[there[0]], w_all.at[half, y % 2], send.at[2], recv.at[1]
    )
    wait_bytes(w_all.at[:, c], recv.at[1])
    push(w_all.at[:, c], w_all.at[:, c], send.at[3], core_recv.at[1], sib)
    wait_bytes(tok_all, recv.at[0])
    wait_bytes(w_all.at[:, 1 - c], core_recv.at[1])
    wait_bytes(wo, send.at[0])
    wait_bytes(tok_all.at[pl.ds(0, 3)], send.at[1])
    wait_bytes(w_all.at[pl.ds(0, 31), c], send.at[2])

    @pl.when(y % 2 != c)
    def _():
        wait_bytes(w_all.at[0, c], send.at[2])

    wait_bytes(w_all.at[:, c], send.at[3])


def start_exchange(tok, wmsg):
    return run_comm(
        start_kernel,
        (tok, wmsg),
        (
            jax.ShapeDtypeStruct((4, TOK, D), BF),
            jax.ShapeDtypeStruct((32, 2, 16, 3 * GW), BF),
        ),
        [
            pltpu.VMEM((4, 16, 3 * GW), BF),
            pltpu.VMEM((4, 16, 3 * GW), BF),
            DMA((4,)),
            DMA((2,)),
            DMA((2,)),
            DMA,
        ],
        0,
        "start_exchange",
    )


FH = 1536
WIDE = 256


def experts_kernel(
    x16, d_rows, w_in, w_out, home_in, home_out, g_in, g_out,
    xs, xo, rows, dv, w1, w2, dh, hidden, dact, in_h, out_h, in_o, out_o, stage_out, stage_in,
    send, recv, core_recv, own, staged,
):
    z, x, y, c = place()
    sib = (z, x, y, 1 - c)
    at_mine = pl.multiple_of(c * 512, 512)
    at_theirs = pl.multiple_of((1 - c) * 512, 512)
    mine, theirs = pl.ds(at_mine, 512), pl.ds(at_theirs, 512)
    me = block_of(z, x, y)
    keep(x16.at[mine], xs, own.at[0])
    keep(d_rows, dv, own.at[1])
    keep(w_out, w2, own.at[2])
    keep(w_in, w1, own.at[3])
    expected = greet_chips(z, x, y, c)
    arrive(expected)
    push(x16.at[theirs], xo, send.at[0], core_recv.at[0], sib)
    wait_bytes(xs, own.at[0])
    wait_bytes(xo, core_recv.at[0])
    xs[...] = xs[...] + xo[...]
    to_chips(
        z, x, y, c,
        lambda there: xs.at[pl.ds(pl.multiple_of(block_of(*there[:3]) - c * 512, 16), 16)],
        rows.at[pl.ds(me, 16)], send.at[1], recv.at[0],
    )
    wait_bytes(dv, own.at[1])
    wait_bytes(w2, own.at[2])

    def hidden_grads(n):
        cols = pl.ds(pl.multiple_of(n * WIDE, WIDE), WIDE)
        dh[:, cols] = dot(dv[...], w2[cols, :], NT)

    loop(0, FH // WIDE, hidden_grads)
    wait_bytes(w1, own.at[3])
    wait_bytes(rows.at[mine], recv.at[0])
    push(rows.at[mine], rows.at[mine], send.at[2], core_recv.at[1], sib)

    def activate(at):
        part = pl.ds(at, 512)

        def one(n):
            cols = pl.ds(pl.multiple_of(n * WIDE, WIDE), WIDE)
            a = dot(rows[part, :], w1[:, cols], NN)
            square = a * a
            t = jnp.tanh(0.7978845608028654 * (a + 0.044715 * (square * a)))
            cdf = 0.5 * (1.0 + t)
            hidden[part, cols] = (a * cdf).astype(BF)
            slope = cdf + 0.5 * a * (1.0 - t * t) * (
                0.7978845608028654 * (1.0 + 0.134145 * square)
            )
            dact[part, cols] = (slope * dh[part, cols]).astype(BF)

        loop(0, FH // WIDE, one)

    def in_half(at):
        part = pl.ds(at, 512)

        def one(n):
            cols = pl.ds(pl.multiple_of(n * WIDE, WIDE), WIDE)
            in_h[part, cols] = dot(dact[part, :], w1[cols, :], NT).astype(BF)

        loop(0, D // WIDE, one)

    def out_half(at):
        part = pl.ds(at, 512)

        def one(n):
            cols = pl.ds(pl.multiple_of(n * WIDE, WIDE), WIDE)
            out_h[part, cols] = dot(hidden[part, :], w2[:, cols], NN).astype(BF)

        loop(0, D // WIDE, one)

    activate(at_mine)
    wait_bytes(rows.at[theirs], core_recv.at[1])
    activate(at_theirs)
    in_half(at_theirs)
    push(in_h.at[theirs], in_o, send.at[3], core_recv.at[2], sib)
    in_half(at_mine)
    wait_bytes(in_o, core_recv.at[2])
    in_o[...] = (in_o[...].astype(F32) + in_h[mine, :].astype(F32)).astype(BF)
    to_chips(
        z, x, y, c,
        lambda there: in_o.at[pl.ds(pl.multiple_of(block_of(*there[:3]) - c * 512, 16), 16)],
        home_in.at[pl.ds(me, 16)], send.at[4], recv.at[1],
    )
    out_half(at_theirs)
    push(out_h.at[theirs], out_o, send.at[5], core_recv.at[3], sib)
    out_half(at_mine)
    wait_bytes(out_o, core_recv.at[3])
    out_o[...] = (out_o[...].astype(F32) + out_h[mine, :].astype(F32)).astype(BF)
    to_chips(
        z, x, y, c,
        lambda there: out_o.at[pl.ds(pl.multiple_of(block_of(*there[:3]) - c * 512, 16), 16)],
        home_out.at[pl.ds(me, 16)], send.at[6], recv.at[2],
    )

    def out_grads(n):
        cols = pl.ds(pl.multiple_of(n * WIDE, WIDE), WIDE)
        slot = n % 2

        @pl.when(n >= 2)
        def _():
            wait_bytes(stage_out.at[slot], staged.at[slot])

        stage_out[slot] = dot(hidden[:, cols], dv[...], TN)
        keep(stage_out.at[slot], g_out.at[cols], staged.at[slot])

    loop(0, FH // WIDE, out_grads)
    wait_bytes(home_in.at[mine], recv.at[1])
    push(home_in.at[mine], home_in.at[mine], send.at[7], core_recv.at[4], sib)

    def in_grads(n):
        cols = pl.ds(pl.multiple_of(n * WIDE, WIDE), WIDE)
        slot = n % 2

        @pl.when(n >= 2)
        def _():
            wait_bytes(stage_in.at[slot], staged.at[2 + slot])

        stage_in[slot] = dot(rows[:, cols], dact[...], TN)
        keep(stage_in.at[slot], g_in.at[cols], staged.at[2 + slot])

    loop(0, D // WIDE, in_grads)
    wait_bytes(home_out.at[mine], recv.at[2])
    push(home_out.at[mine], home_out.at[mine], send.at[8], core_recv.at[5], sib)
    for slot in range(2):
        wait_bytes(stage_out.at[slot], staged.at[slot])
        wait_bytes(stage_in.at[slot], staged.at[2 + slot])
    wait_bytes(xo, send.at[0])
    sent_to_chips(rows, y, c, send.at[1])
    wait_bytes(rows.at[mine], send.at[2])
    wait_bytes(in_o, send.at[3])
    sent_to_chips(home_in, y, c, send.at[4])
    wait_bytes(out_o, send.at[5])
    sent_to_chips(home_out, y, c, send.at[6])
    wait_bytes(home_in.at[theirs], core_recv.at[4])
    wait_bytes(home_out.at[theirs], core_recv.at[5])
    wait_bytes(home_in.at[mine], send.at[7])
    wait_bytes(home_out.at[mine], send.at[8])


def run_experts(x16, d_rows, w_in, w_out):
    whole_rows = pltpu.VMEM((1024, D), BF)
    half_rows = pltpu.VMEM((512, D), BF)
    hid = pltpu.VMEM((1024, FH), BF)
    return pl.pallas_call(
        experts_kernel,
        out_shape=(
            jax.ShapeDtypeStruct((1024, D), BF),
            jax.ShapeDtypeStruct((1024, D), BF),
            jax.ShapeDtypeStruct((D, FH), F32),
            jax.ShapeDtypeStruct((FH, D), F32),
        ),
        in_specs=[ANY] * 4,
        out_specs=(ANY,) * 4,
        scratch_shapes=[
            half_rows, half_rows, whole_rows, whole_rows,
            pltpu.VMEM((D, FH), BF), pltpu.VMEM((FH, D), BF), pltpu.VMEM((1024, FH), F32),
            hid, hid, whole_rows, whole_rows, half_rows, half_rows,
            pltpu.VMEM((2, WIDE, D), F32), pltpu.VMEM((2, WIDE, FH), F32),
            DMA((9,)), DMA((3,)), DMA((6,)), DMA((4,)), DMA((4,)),
        ],
        compiler_params=pltpu.CompilerParams(
            collective_id=1, has_side_effects=True, vmem_limit_bytes=48 * 2**20
        ),
        name="experts",
    )(x16, d_rows, w_in, w_out)


def device_of(d):
    return d // 32, (d // 8) % 4, (d // 2) % 4, d % 2


NT = (((1,), (1,)), ((), ()))
NN = (((1,), (0,)), ((), ()))
TN = (((0,), (0,)), ((), ()))


def dot(a, b, dims):
    return lax.dot_general(a, b, dims, preferred_element_type=F32)


def near_distance(dist):
    a = lax.broadcasted_iota(jnp.int32, (TOK, TOK), 0)
    b = lax.broadcasted_iota(jnp.int32, (TOK, TOK), 1)
    return dist * TOK + a - b


def table_kind(zq, zk, x, kx):
    return jnp.clip((zq - zk) * 4 + x - kx + 1, 0, 3)


def block_cols(zk, kx):
    return pl.ds(pl.multiple_of((zk * 4 + kx) * TOK, TOK), TOK)


VMEM = pl.BlockSpec(memory_space=pltpu.VMEM)
SMEM = pl.BlockSpec(memory_space=pltpu.SMEM)


def attn_forward_kernel(
    tab, q, kv, qd, kd, wa, d_eo,
    attn_all, part, p_out, kv_out, wa_all, d_rows,
    kv_s, v_s, qm, bias, s_s, p_s, wm, wo, xo,
    send, recv, kv_recv, core_recv, own,
):
    z, x, y, c = place()
    sib = (z, x, y, 1 - c)
    mine = pl.ds(pl.multiple_of(c * 512, 512), 512)
    theirs = pl.ds(pl.multiple_of((1 - c) * 512, 512), 512)
    expected = greet_chips(z, x, y, c)
    for k in range(1, 4):
        signal(((z + k) % 4, x, y, c))
        signal((z, (x + k) % 4, y, c))
    arrive(expected + 6)
    for k in range(1, 4):
        for b in range(4):
            push(
                kv.at[b], kv_s.at[block_cols(b, x)], send.at[0], kv_recv.at[4 - k],
                (z, (x + k) % 4, y, c),
            )
    for b in range(4):
        keep(kv.at[b], kv_s.at[block_cols(b, x)], kv_recv.at[0])
    push(wa, wo, send.at[1], core_recv.at[0], sib)
    push(d_eo.at[theirs], xo, send.at[2], core_recv.at[1], sib)
    for h in range(GH):
        head_cols = lax.broadcasted_iota(jnp.int32, (1, GW), 1) // HD == h
        qm[h] = jnp.where(head_cols, q[...] * 0.125, 0.0).astype(BF)
    wait_bytes(wo, core_recv.at[0])
    wm[...] = wa[...] + wo[...]
    wait_bytes(xo, core_recv.at[1])
    xo[...] = xo[...] + d_eo[mine, :]

    def tables(h):
        for dist in range(2):
            n = near_distance(dist)
            acc = jnp.full((TOK, TOK), tab[0, h], F32)
            for k, edge in enumerate(bucket_edges):
                acc = jnp.where(n >= edge, tab[k + 1, h], acc)
            bias[h, 1 + dist] = jnp.where(n >= 0, acc, masked)
        bias[h, 0] = jnp.full((TOK, TOK), masked, F32)
        bias[h, 3] = jnp.full((TOK, TOK), tab[BUCKETS - 1, h], F32)

    loop(0, GH, tables)
    for k in range(4):
        kx = (x + k) % 4
        if k == 0:
            for b in range(4):
                wait_bytes(kv_s.at[block_cols(b, kx)], kv_recv.at[0])
        else:
            wait_bytes(kv_s.at[pl.ds(0, 512)], kv_recv.at[k])
        for b in range(4):
            cols = block_cols(b, kx)
            v_s[cols, :] = kv_s[cols, GW:]
            for h in range(GH):
                s_s[h, b * TOK :, cols] = dot(qm[h, b * TOK :, :], kv_s[cols, :GW], NT)
    keep(kv_s, kv_out, own.at[1])
    half = z * 8 + x * 2 + y // 2
    to_chips(z, x, y, c, lambda there: wm, wa_all.at[half, y % 2], send.at[3], recv.at[0])
    me = block_of(z, x, y)
    to_chips(
        z, x, y, c,
        lambda there: xo.at[pl.ds(pl.multiple_of(block_of(*there[:3]) - c * 512, 16), 16)],
        d_rows.at[pl.ds(me, 16)], send.at[4], recv.at[1],
    )

    def head(h):
        head_cols = lax.broadcasted_iota(jnp.int32, (1, GW), 1) // HD == h
        far = tab[BUCKETS - 1, h]
        for zq in range(4):
            rows = pl.ds(zq * TOK, TOK)
            docs = qd[rows, :]
            top = None
            for zk in range(zq + 1):
                for kx in range(4):
                    cols = pl.ds((zk * 4 + kx) * TOK, TOK)
                    s = s_s[h, rows, cols]
                    if zk < zq - 1:
                        s = s + far
                    else:
                        s = s + bias[h, table_kind(zq, zk, x, kx)]
                    s = jnp.where(docs == kd[:, cols], s, masked)
                    s_s[h, rows, cols] = s
                    top = s if top is None else jnp.maximum(top, s)
            top = jnp.max(top, axis=1, keepdims=True)
            total = jnp.zeros((TOK, TOK), F32)
            for kb in range(4 * (zq + 1)):
                cols = pl.ds(kb * TOK, TOK)
                e = jnp.exp(s_s[h, rows, cols] - top)
                s_s[h, rows, cols] = e
                total = total + e
            inv = 1.0 / jnp.sum(total, axis=1, keepdims=True)
            for kb in range(4 * (zq + 1)):
                cols = pl.ds(kb * TOK, TOK)
                p_s[h, rows, cols] = (s_s[h, rows, cols] * inv).astype(BF)
            width = (zq + 1) * 512
            o = dot(p_s[h, rows, :width], v_s[:width, :], NN).astype(BF)

            @pl.when(h == 0)
            def _():
                part[rows, :] = o

            @pl.when(h > 0)
            def _():
                part[rows, :] = jnp.where(head_cols, o, part[rows, :])

    loop(0, GH, head)
    for k in range(1, 4):
        there = (z + k) % 4
        push(
            part.at[pl.ds(pl.multiple_of(there * TOK, TOK), TOK)], attn_all.at[z],
            send.at[6], recv.at[2], (there, x, y, c),
        )
    keep(part.at[pl.ds(pl.multiple_of(z * TOK, TOK), TOK)], attn_all.at[z], recv.at[2])
    keep(p_s, p_out, own.at[2])
    wait_bytes(wa_all.at[:, c], recv.at[0])
    push(wa_all.at[:, c], wa_all.at[:, c], send.at[5], core_recv.at[2], sib)
    wait_bytes(d_rows.at[mine], recv.at[1])
    push(d_rows.at[mine], d_rows.at[mine], send.at[7], core_recv.at[3], sib)
    wait_bytes(attn_all, recv.at[2])
    wait_bytes(wa_all.at[:, 1 - c], core_recv.at[2])
    wait_bytes(d_rows.at[theirs], core_recv.at[3])
    wait_bytes(kv_s, own.at[1])
    wait_bytes(p_s, own.at[2])
    wait_bytes(kv_s.at[pl.ds(0, 1536)], send.at[0])
    wait_bytes(wo, send.at[1])
    wait_bytes(wa_all.at[pl.ds(0, 31), c], send.at[3])

    @pl.when(y % 2 != c)
    def _():
        wait_bytes(wa_all.at[0, c], send.at[3])

    wait_bytes(wa_all.at[:, c], send.at[5])
    wait_bytes(attn_all.at[pl.ds(0, 3)], send.at[6])
    wait_bytes(xo, send.at[2])
    sent_to_chips(d_rows, y, c, send.at[4])
    wait_bytes(d_rows.at[mine], send.at[7])


def attn_forward(tab, q, kv, qd, kd, wa, d_eo):
    probs = (GH, 512, 2048)
    return pl.pallas_call(
        attn_forward_kernel,
        out_shape=(
            jax.ShapeDtypeStruct((4, TOK, GW), BF),
            jax.ShapeDtypeStruct((512, GW), BF),
            jax.ShapeDtypeStruct(probs, BF),
            jax.ShapeDtypeStruct((2048, 2 * GW), BF),
            jax.ShapeDtypeStruct((32, 2, 16, D), BF),
            jax.ShapeDtypeStruct((1024, D), BF),
        ),
        in_specs=[SMEM] + [VMEM] * 6,
        out_specs=(ANY, VMEM, ANY, ANY, ANY, ANY),
        scratch_shapes=[
            pltpu.VMEM((2048, 2 * GW), BF),
            pltpu.VMEM((2048, GW), BF),
            pltpu.VMEM((GH, 512, GW), BF),
            pltpu.VMEM((GH, 4, TOK, TOK), F32),
            pltpu.VMEM(probs, F32),
            pltpu.VMEM(probs, BF),
            pltpu.VMEM((16, D), BF),
            pltpu.VMEM((16, D), BF),
            pltpu.VMEM((512, D), BF),
            DMA((8,)),
            DMA((3,)),
            DMA((4,)),
            DMA((4,)),
            DMA((3,)),
        ],
        compiler_params=pltpu.CompilerParams(
            collective_id=2, has_side_effects=True, vmem_limit_bytes=44 * 2**20
        ),
        name="attn_forward",
    )(tab, q, kv, qd, kd, wa, d_eo)


def attn_backward_kernel(
    p, q, kv, d_attn, branch, weight, normed, attn_part, small, tok, gain, d_middle,
    input_grad, qkv_out, att_out, small_out,
    p_s, v_s, do_s, dm, qm, dp_s, ds_s, near, messages, parts, branch_all, dq, tab,
    d_qkv, n_part, normed_in, att_f, q_blk, q_sib, q_tot, q_in, a_blk, a_sib, a_tot, a_in,
    s_own, s_sib, s_tot, s_in, qkv_sum, att_sum, s_sum, send, recv, core_recv, own,
):
    z, x, y, c = place()
    sib = (z, x, y, 1 - c)
    p16 = x * 4 + y
    p32 = p16 * 2 + c
    me = z * 32 + p32
    source = me // 4

    def peer(i):
        return z, (x + i // 4) % 4, (y + i % 4) % 4, c

    keep(p, p_s, own.at[0])
    loop(1, 16, lambda i: signal(peer(i)))
    for k in range(1, 4):
        signal(((z + k) % 4, x, y, c))
    signal(sib)

    def greet(k):
        @pl.when(jnp.logical_not((k == z) & (source == p32)))
        def _():
            signal((k, source // 8, (source // 2) % 4, source % 2))

    loop(0, 4, greet)
    arrive(15 + 3 + 1 + 4 - jnp.where(source == p32, 1, 0))
    for k in range(1, 4):
        there = (z + k) % 4
        push(d_attn.at[there], do_s.at[z], send.at[0], recv.at[0], (there, x, y, c))
    keep(d_attn.at[z], do_s.at[z], recv.at[0])
    z_rows = pl.ds(pl.multiple_of(z * TOK, TOK), TOK)
    for k in range(1, 4):
        push(branch, branch_all.at[z_rows], send.at[1], recv.at[1], ((z + k) % 4, x, y, c))
    keep(branch, branch_all.at[z_rows], recv.at[1])
    v_s[...] = kv[:, GW:]
    for h in range(GH):
        head_cols = lax.broadcasted_iota(jnp.int32, (1, GW), 1) // HD == h
        qm[h] = jnp.where(head_cols, q[...] * 0.125, 0.0).astype(BF)
    wait_bytes(do_s, recv.at[0])
    for h in range(GH):
        head_cols = lax.broadcasted_iota(jnp.int32, (1, GW), 1) // HD == h
        for b in range(4):
            dm[h, b * TOK : (b + 1) * TOK, :] = jnp.where(head_cols, do_s[b], 0.0).astype(BF)
    wait_bytes(p_s, own.at[0])

    def key_sums(left, right, first):
        for k in (1, 2, 3, 0):
            kx = (x + k) % 4
            for b in range(4):
                cols = block_cols(b, kx)
                total = None
                for h in range(GH):
                    one = dot(left[h, b * TOK :, cols], right[h, b * TOK :, :], TN)
                    total = one if total is None else total + one
                side = GW * (b % 2)
                messages[k, first + b // 2, :, side : side + GW] = total.astype(BF)
            for m in range(first, first + 2):
                if k:
                    push(
                        messages.at[k, m], parts.at[x, m], send.at[2], recv.at[2],
                        (z, kx, y, c),
                    )
                else:
                    keep(messages.at[k, m], parts.at[x, m], recv.at[2])

    key_sums(p_s, dm, 0)

    def head(h):
        head_cols = lax.broadcasted_iota(jnp.int32, (1, GW), 1) // HD == h
        for zk in range(4):
            cols = pl.ds(zk * 512, 512)
            dp_s[zk * TOK :, cols] = dot(dm[h, zk * TOK :, :], v_s[cols, :], NT)
        near[...] = jnp.zeros_like(near)
        for zq in range(4):
            rows = pl.ds(zq * TOK, TOK)
            acc = jnp.zeros((TOK, TOK), F32)
            for kb in range(4 * (zq + 1)):
                cols = pl.ds(kb * TOK, TOK)
                acc = acc + p_s[h, rows, cols].astype(F32) * dp_s[rows, cols]
            delta = jnp.sum(acc, axis=1, keepdims=True)
            far = jnp.zeros((TOK, TOK), F32)
            for zk in range(zq + 1):
                for kx in range(4):
                    cols = pl.ds((zk * 4 + kx) * TOK, TOK)
                    ds = (p_s[h, rows, cols].astype(F32) * (dp_s[rows, cols] - delta)).astype(BF)
                    ds_s[h, rows, cols] = ds
                    if zk < zq - 1:
                        far = far + ds.astype(F32)
                    else:
                        near[table_kind(zq, zk, x, kx)] += ds.astype(F32)
            near[3] += far
            width = (zq + 1) * 512
            o = (dot(ds_s[h, rows, :width], kv[:width, :GW], NN) * 0.125).astype(BF)

            @pl.when(h == 0)
            def _():
                dq[rows, :] = o

            @pl.when(h > 0)
            def _():
                dq[rows, :] = jnp.where(head_cols, o, dq[rows, :])

        for dist in range(2):
            n = near_distance(dist)
            held = near[1 + dist]
            bounds = [-(10**6)] + bucket_edges + [10**6]
            for b in range(BUCKETS):
                low, high = bounds[b], bounds[b + 1]
                if high <= dist * TOK - TOK + 1 or low > dist * TOK + TOK - 1:
                    if dist == 0:
                        tab[h, b : b + 1, :] = jnp.zeros((1, TOK), F32)
                    continue
                inside = jnp.sum(
                    jnp.where((n >= low) & (n < high), held, 0.0), axis=0, keepdims=True
                )
                if dist == 0:
                    tab[h, b : b + 1, :] = inside
                else:
                    tab[h, b : b + 1, :] += inside
        tab[h, BUCKETS - 1 :, :] += jnp.sum(near[3], axis=0, keepdims=True)

    loop(0, GH, head)
    key_sums(ds_s, qm, 2)

    wait_bytes(branch_all, recv.at[1])
    att_f[0:GW, :] = dot(attn_part[...], branch_all[...], TN)
    att_f[GW:, :] = jnp.zeros((8, D), F32)
    for j in range(32):
        a_blk[j // 2, j % 2] = att_f[6 * j : 6 * j + 8, :].astype(BF)
    push(a_blk.at[:, 1 - c], a_sib, send.at[4], core_recv.at[1], sib)
    s_own[...] = small[...]
    for h in range(GH):
        s_own[2:3, BUCKETS * h : BUCKETS * (h + 1)] = jnp.sum(tab[h].T, axis=0, keepdims=True)

    wait_bytes(parts, recv.at[2])
    d_qkv[:, :GW] = dq[...]
    for b in range(4):
        rows = slice(b * TOK, (b + 1) * TOK)
        side = GW * (b % 2)
        for m, at in ((2 + b // 2, GW), (b // 2, 2 * GW)):
            total = parts[0, m, :, side : side + GW].astype(F32)
            for k in range(1, 4):
                total = total + parts[k, m, :, side : side + GW].astype(F32)
            d_qkv[rows, at : at + GW] = total.astype(BF)
    n_part[...] = dot(d_qkv[...], weight[...], NT).astype(BF)
    for k in range(1, 4):
        there = (z + k) % 4
        push(
            n_part.at[pl.ds(pl.multiple_of(there * TOK, TOK), TOK)], normed_in.at[z],
            send.at[3], recv.at[3], (there, x, y, c),
        )
    keep(n_part.at[z_rows], normed_in.at[z], recv.at[3])
    total = dot(normed[...], d_qkv[...], TN)
    for j in range(32):
        q_blk[j // 2, j % 2] = total[24 * j : 24 * j + 24].astype(BF)
    push(q_blk.at[:, 1 - c], q_sib, send.at[5], core_recv.at[0], sib)
    wait_bytes(a_sib, core_recv.at[1])

    def att_blocks(i):
        there = peer(i)
        j = there[1] * 4 + there[2]
        a_tot[j] = (a_blk[j, c].astype(F32) + a_sib[j].astype(F32)).astype(BF)
        push(a_tot.at[j], a_in.at[p16], send.at[6], recv.at[4], there)

    loop(1, 16, att_blocks)
    a_tot[p16] = (a_blk[p16, c].astype(F32) + a_sib[p16].astype(F32)).astype(BF)
    keep(a_tot.at[p16], a_in.at[p16], recv.at[4])
    wait_bytes(q_sib, core_recv.at[0])

    def qkv_blocks(i):
        there = peer(i)
        j = there[1] * 4 + there[2]
        q_tot[j] = (q_blk[j, c].astype(F32) + q_sib[j].astype(F32)).astype(BF)
        push(q_tot.at[j], q_in.at[p16], send.at[7], recv.at[5], there)

    loop(1, 16, qkv_blocks)
    q_tot[p16] = (q_blk[p16, c].astype(F32) + q_sib[p16].astype(F32)).astype(BF)
    keep(q_tot.at[p16], q_in.at[p16], recv.at[5])

    wait_bytes(normed_in, recv.at[3])
    d_normed = normed_in[0].astype(F32)
    for k in range(1, 4):
        d_normed = d_normed + normed_in[k].astype(F32)
    v = tok[...].astype(F32)
    r = lax.rsqrt(jnp.mean(v * v, axis=1, keepdims=True) + norm_eps)
    unit = v * r
    s_own[0:1, :] = jnp.sum(d_normed * unit, axis=0, keepdims=True)
    push(s_own, s_sib, send.at[8], core_recv.at[2], sib)
    d_unit = d_normed * gain[...]
    d_in = r * (d_unit - unit * jnp.mean(d_unit * unit, axis=1, keepdims=True))
    input_grad[...] = (d_middle[...] + d_in).astype(BF)
    wait_bytes(s_sib, core_recv.at[2])
    s_tot[...] = s_own[...] + s_sib[...]
    loop(1, 16, lambda i: push(s_tot, s_in.at[p16], send.at[9], recv.at[6], peer(i)))
    keep(s_tot, s_in.at[p16], recv.at[6])

    wait_bytes(q_in, recv.at[5])
    q_total = q_in[0].astype(F32)
    for k in range(1, 16):
        q_total = q_total + q_in[k].astype(F32)
    for k in range(4):
        qkv_sum[k, 0:6, :] = q_total[6 * k : 6 * k + 6]
        qkv_sum[k, 6:8, :] = jnp.zeros((2, 3 * GW), F32)

    def final(k):
        d = 4 * p32 + k

        @pl.when(d != me)
        def _():
            push(qkv_sum.at[k], qkv_out.at[z], send.at[10], recv.at[7], device_of(d))

        @pl.when(d == me)
        def _():
            keep(qkv_sum.at[k], qkv_out.at[z], recv.at[7])

    loop(0, 4, final)
    wait_bytes(a_in, recv.at[4])
    a_total = a_in[0].astype(F32)
    for k in range(1, 16):
        a_total = a_total + a_in[k].astype(F32)
    att_sum[...] = a_total
    keep(att_sum, att_out, own.at[1])
    wait_bytes(s_in, recv.at[6])
    s_total = s_in[0]
    for k in range(1, 16):
        s_total = s_total + s_in[k]
    s_sum[...] = s_total
    for k in range(1, 4):
        push(s_sum, small_out.at[z], send.at[11], recv.at[8], ((z + k) % 4, x, y, c))
    keep(s_sum, small_out.at[z], recv.at[8])
    wait_bytes(att_sum, own.at[1])
    wait_bytes(qkv_out, recv.at[7])
    wait_bytes(small_out, recv.at[8])
    wait_bytes(do_s.at[pl.ds(0, 3)], send.at[0])
    wait_bytes(branch_all.at[pl.ds(0, 3 * TOK)], send.at[1])
    wait_bytes(parts.at[pl.ds(0, 3)], send.at[2])
    wait_bytes(normed_in.at[pl.ds(0, 3)], send.at[3])
    wait_bytes(a_sib, send.at[4])
    wait_bytes(q_sib, send.at[5])
    wait_bytes(a_in.at[pl.ds(0, 15)], send.at[6])
    wait_bytes(q_in.at[pl.ds(0, 15)], send.at[7])
    wait_bytes(s_own, send.at[8])
    wait_bytes(s_in.at[pl.ds(0, 15)], send.at[9])

    def sent(k):
        @pl.when(4 * p32 + k != me)
        def _():
            wait_bytes(qkv_sum.at[0], send.at[10])

    loop(0, 4, sent)
    wait_bytes(small_out.at[pl.ds(0, 3)], send.at[11])


def attn_backward(p, *rest):
    probs = (GH, 512, 2048)
    vm = pltpu.VMEM
    return pl.pallas_call(
        attn_backward_kernel,
        out_shape=(
            jax.ShapeDtypeStruct((TOK, D), BF),
            jax.ShapeDtypeStruct((4, 8, 3 * GW), F32),
            jax.ShapeDtypeStruct((8, D), F32),
            jax.ShapeDtypeStruct((4, 8, D), F32),
        ),
        in_specs=[ANY] + [VMEM] * len(rest),
        out_specs=(VMEM, ANY, ANY, ANY),
        scratch_shapes=[
            vm(probs, BF), vm((2048, GW), BF), vm((4, TOK, GW), BF), vm((GH, 512, GW), BF),
            vm((GH, 512, GW), BF), vm((512, 2048), F32), vm(probs, BF), vm((4, TOK, TOK), F32),
            vm((4, 4, TOK, 2 * GW), BF), vm((4, 4, TOK, 2 * GW), BF), vm((512, D), BF),
            vm((512, GW), BF), vm((GH, BUCKETS, TOK), F32),
            vm((512, 3 * GW), BF), vm((512, D), BF), vm((4, TOK, D), BF), vm((GW + 8, D), F32),
            vm((16, 2, 24, 3 * GW), BF), vm((16, 24, 3 * GW), BF),
            vm((16, 24, 3 * GW), BF), vm((16, 24, 3 * GW), BF),
            vm((16, 2, 8, D), BF), vm((16, 8, D), BF), vm((16, 8, D), BF), vm((16, 8, D), BF),
            vm((8, D), F32), vm((8, D), F32), vm((8, D), F32), vm((16, 8, D), F32),
            vm((4, 8, 3 * GW), F32), vm((8, D), F32), vm((8, D), F32),
            DMA((12,)), DMA((9,)), DMA((3,)), DMA((2,)),
        ],
        compiler_params=pltpu.CompilerParams(
            collective_id=3, has_side_effects=True, vmem_limit_bytes=52 * 2**20
        ),
        name="attn_backward",
    )(p, *rest)


def per_device(
    tokens,
    gain_attn,
    w_qkv,
    w_attn_out,
    rel_table,
    gain_moe,
    w_in,
    w_out,
    expert_ids,
    gate_values,
    doc_ids,
    cotangent,
):
    z, x, y, c = place()
    experts = 64
    capacity = 8
    slots = 2 * experts * capacity
    own_tokens = tokens.reshape(TOK, D)
    grad_bf = cotangent.reshape(TOK, D)
    grad_out = grad_bf.astype(F32)

    routes = expert_ids.reshape(TOK, 2)
    gates = gate_values.reshape(TOK, 2)
    expert_list = jnp.arange(experts, dtype=jnp.int32)[None, :]
    marks = jnp.concatenate(
        [(routes[:, :1] == expert_list), (routes[:, 1:] == expert_list)], axis=1
    ).astype(BF)
    lower = jnp.tril(jnp.ones((TOK, TOK), BF), -1)
    earlier = dot(lower, marks, NN)
    marks = marks.astype(F32)
    firsts = jnp.sum(marks[:, :experts], axis=0, keepdims=True)
    rank_0 = jnp.sum(earlier[:, :experts] * marks[:, :experts], axis=1)
    rank_1 = jnp.sum((earlier[:, experts:] + firsts) * marks[:, experts:], axis=1)
    blocks = (routes % 2) * 32 + (routes // 4) * 2 + (routes % 4) // 2
    places = blocks * 16 + c * capacity + jnp.stack([rank_0, rank_1], axis=1).astype(jnp.int32)
    slot_ids = jnp.arange(slots, dtype=jnp.int32)[None, :]
    picks = jnp.concatenate(
        [(places[:, :1] == slot_ids), (places[:, 1:] == slot_ids)], axis=0
    ).astype(BF)
    gated = jnp.concatenate([gates[:, :1] * grad_out, gates[:, 1:] * grad_out], axis=0).astype(BF)
    d_eo = dot(picks, gated, TN).astype(BF)

    slab = w_qkv.reshape(6, 3, GROUPS, GW).transpose(2, 0, 1, 3).reshape(GROUPS, 6, 3 * GW)
    notes = jnp.concatenate(
        [
            gain_attn, gain_moe, jnp.zeros((116,), BF),
            doc_ids.reshape(TOK).astype(BF), jnp.zeros((3 * GW - 256,), BF),
        ]
    )
    notes = jnp.broadcast_to(notes, (GROUPS, 1, 3 * GW))
    nothing = jnp.zeros((GROUPS, 6, 3 * GW), BF)
    message = jnp.where(
        c == 0,
        jnp.concatenate([slab, nothing, notes, nothing[:, :3]], axis=1),
        jnp.concatenate([nothing, slab, nothing[:, :1], notes, nothing[:, :2]], axis=1),
    )
    zero_rows = jnp.zeros((6, D), BF)
    out_slab = jnp.where(
        c == 0,
        jnp.concatenate([w_attn_out, zero_rows, zero_rows[:4]], axis=0),
        jnp.concatenate([zero_rows, w_attn_out, zero_rows[:4]], axis=0),
    )
    tok_all, w_all = start_exchange(own_tokens, message)

    weight = w_all[:, :, :12, :].reshape(D, 3 * GW)
    gain_one = w_all[:, :, 12:14, 0:6].reshape(D).astype(F32)
    gain_two = w_all[:, :, 12:14, 6:12].reshape(D).astype(F32)
    doc_rows = w_all[:, :, 12:14, 128:256].reshape(16, 4, 2, TOK)
    doc_rows = lax.dynamic_slice(doc_rows, (0, y, c, 0), (16, 1, 1, TOK)).reshape(16, TOK).astype(F32)
    key_docs = doc_rows.reshape(1, 2048)
    query_docs = lax.dynamic_slice(doc_rows.reshape(4, 4, TOK), (0, x, 0), (4, 1, TOK)).reshape(512, 1)

    inputs_all = tok_all.reshape(512, D).astype(F32)
    normed = scale_rows(inputs_all, gain_one).astype(BF)
    qkv = dot(normed, weight, NN).astype(BF)
    queries = qkv[:, :GW]
    table = lax.dynamic_slice(rel_table, (0, z * GH), (BUCKETS, GH)).astype(F32)
    attn, attn_part, probs, kv_all, out_weights, d_eo_all = attn_forward(
        table, queries, qkv[:, GW:].reshape(4, TOK, 2 * GW), query_docs, key_docs, out_slab, d_eo
    )
    attn = attn.transpose(1, 0, 2).reshape(TOK, D)
    attention_weight = out_weights[:, :, :12, :].reshape(D, D)

    inputs = own_tokens.astype(F32)
    middle = inputs + dot(attn, attention_weight, NN)
    moe_float, norm_two_back = jax.vjp(scale_rows, middle, gain_two)
    moe_in = moe_float.astype(BF)
    send_rows = dot(picks, jnp.concatenate([moe_in, moe_in], axis=0), TN).astype(BF)
    home, expert_out, expert_in_grad, expert_out_grad = run_experts(
        send_rows, d_eo_all, w_in[0], w_out[0]
    )
    home_picked = dot(picks, home, NN)
    moe_in_grad = home_picked[:TOK] + home_picked[TOK:]
    middle_part, gain_two_grad = norm_two_back(moe_in_grad)
    middle_grad = grad_out + middle_part
    branch = middle_grad.astype(BF)
    d_attn = dot(branch, attention_weight, NT).astype(BF)
    d_attn = d_attn.reshape(TOK, GROUPS, GW).transpose(1, 0, 2)

    small = jnp.concatenate(
        [jnp.zeros((1, D), F32), gain_two_grad.reshape(1, D), jnp.zeros((6, D), F32)]
    )
    input_grad, qkv_sum, att_sum, small_sum = attn_backward(
        probs, queries, kv_all, d_attn, branch, weight, normed, attn_part, small, own_tokens,
        gain_one.reshape(1, D), middle_grad,
    )

    picked = dot(picks, expert_out, NN).reshape(2, TOK, D)
    block_out = middle + gates[:, :1] * picked[0] + gates[:, 1:] * picked[1]
    gate_grad = jnp.sum(picked * grad_out[None], axis=2).T

    qkv_grad = qkv_sum[:, :6, :].reshape(GROUPS, 6, 3, GW).transpose(1, 2, 0, 3).reshape(6, 3 * D)
    attn_out_grad = att_sum[:6]
    place_in = chip_of(z, x, y) * 2 + c
    gains = lax.dynamic_slice(jnp.sum(small_sum[:, :2, :], axis=0), (0, place_in * 6), (2, 6))
    table_grad = small_sum[:, 2, : GH * BUCKETS].reshape(GROUPS * GH, BUCKETS).T
    return (
        block_out.reshape(1, TOK, D).astype(BF),
        input_grad.reshape(1, TOK, D),
        gate_grad.reshape(1, TOK, 2),
        gains[0],
        qkv_grad,
        attn_out_grad,
        table_grad,
        gains[1],
        expert_in_grad[None],
        expert_out_grad[None],
    )


def solution(mesh):
    torus = Mesh(mesh.devices.reshape(4, 4, 4, 2), AXES)
    in_specs = (
        P(EXP, CTX, None),
        P(AXES),
        P(AXES, None),
        P(AXES, None),
        P(),
        P(AXES),
        P(AXES, None, None),
        P(AXES, None, None),
        P(EXP, CTX, None),
        P(EXP, CTX, None),
        P(EXP, CTX),
        P(EXP, CTX, None),
    )
    out_specs = (
        P(EXP, CTX, None),
        P(EXP, CTX, None),
        P(EXP, CTX, None),
        P(AXES),
        P(AXES, None),
        P(AXES, None),
        P(),
        P(AXES),
        P(AXES, None, None),
        P(AXES, None, None),
    )
    return jax.shard_map(
        per_device, mesh=torus, in_specs=in_specs, out_specs=out_specs, check_vma=False
    )
```

```python
import functools

import jax
import jax.numpy as jnp
import numpy as np
from jax import lax
from jax.experimental import pallas as pl
from jax.experimental.pallas import tpu as pltpu
from jax.sharding import Mesh
from jax.sharding import PartitionSpec as P

D = 768
H = 12
HD = 64
BUCKETS = 32
GROUPS = 4
GH = H // GROUPS
GW = GH * HD
TOK = 128
CTX = ("ctx_0", "ctx_1")
EXP = ("exp_0", "exp_1")
AXES = ("ctx_0", "ctx_1", "exp_0", "exp_1")
MESH = pl.DeviceIdType.MESH
ANY = pl.BlockSpec(memory_space=pl.ANY)
BF = jnp.bfloat16
F32 = jnp.float32

norm_eps = 1e-06
bucket_edges = [int(e) for e in np.concatenate(
    [np.arange(1, 17), np.ceil(16.0 * 8.0 ** (np.arange(1, 16) / 16.0))]
).astype(np.int32)]
masked = -1e30


def scale_rows(values, gain):
    return values * lax.rsqrt(jnp.mean(values * values, axis=-1, keepdims=True) + norm_eps) * gain


def place():
    return tuple(lax.axis_index(a) for a in AXES)


def chip_of(z, x, y):
    return (z * 4 + x) * 4 + y


def chip_peer(i, z, x, y):
    return (z + i // 16) % 4, (x + (i // 4) % 4) % 4, (y + i % 4) % 4


def loop(first, last, body):
    lax.fori_loop(first, last, lambda i, carry: (body(i), carry)[1], 0)


def signal(device):
    pl.semaphore_signal(
        pltpu.get_barrier_semaphore(), inc=1, device_id=device, device_id_type=MESH
    )


def arrive(count):
    pl.semaphore_wait(pltpu.get_barrier_semaphore(), count)


def push(src, dst, send, recv, device):
    pltpu.make_async_remote_copy(
        src_ref=src, dst_ref=dst, send_sem=send, recv_sem=recv, device_id=device, device_id_type=MESH
    ).start()


def keep(src, dst, sem):
    pltpu.make_async_copy(src, dst, sem).start()


def wait_bytes(ref, sem):
    pltpu.make_async_copy(ref, ref, sem).wait()


def comm_call(kernel, outs, scratch, collective_id, name):
    return pl.pallas_call(
        kernel,
        out_shape=outs,
        in_specs=None,
        out_specs=jax.tree.map(lambda _: ANY, outs),
        scratch_shapes=scratch,
        compiler_params=pltpu.CompilerParams(
            collective_id=collective_id, has_side_effects=True, vmem_limit_bytes=32 * 2**20
        ),
        name=name,
    )


def run_comm(kernel, args, outs, scratch, collective_id, name):
    return pl.pallas_call(
        kernel,
        out_shape=outs,
        in_specs=[ANY] * len(args),
        out_specs=jax.tree.map(lambda _: ANY, outs),
        scratch_shapes=scratch,
        compiler_params=pltpu.CompilerParams(
            collective_id=collective_id, has_side_effects=True, vmem_limit_bytes=32 * 2**20
        ),
        name=name,
    )(*args)


DMA = pltpu.SemaphoreType.DMA


def half_peer(i, z, x, y, c):
    return (z + i // 8) % 4, (x + (i // 2) % 4) % 4, c + 2 * ((y // 2 + i % 2) % 2), y % 2


def block_of(z, x, y):
    return pl.multiple_of((y % 2) * 512 + ((z * 4 + x) * 2 + y // 2) * 16, 16)


def greet_chips(z, x, y, c):
    loop(1, 32, lambda i: signal(half_peer(i, z, x, y, c)))

    @pl.when(y % 2 != c)
    def _():
        signal(half_peer(0, z, x, y, c))

    signal((z, x, y, 1 - c))
    return 32 + jnp.where(y % 2 == c, 0, 1)


def to_chips(z, x, y, c, source, target, send, recv):
    def one(i):
        there = half_peer(i, z, x, y, c)
        push(source(there), target, send, recv, there)

    loop(1, 32, one)
    first = half_peer(0, z, x, y, c)

    @pl.when(y % 2 == c)
    def _():
        keep(source(first), target, recv)

    @pl.when(y % 2 != c)
    def _():
        push(source(first), target, send, recv, first)


def sent_to_chips(rows, y, c, send):
    wait_bytes(rows.at[pl.ds(0, 496)], send)

    @pl.when(y % 2 != c)
    def _():
        wait_bytes(rows.at[pl.ds(0, 16)], send)


FH = 1536
WIDE = 256


def experts_kernel(
    x16, d_rows, w_in, w_out, home_in, home_out, g_in, g_out,
    xs, xo, rows, dv, w1, w2, dh, hidden, dact, in_h, out_h, in_o, out_o, stage_out, stage_in,
    send, recv, core_recv, own, staged,
):
    z, x, y, c = place()
    sib = (z, x, y, 1 - c)
    at_mine = pl.multiple_of(c * 512, 512)
    at_theirs = pl.multiple_of((1 - c) * 512, 512)
    mine, theirs = pl.ds(at_mine, 512), pl.ds(at_theirs, 512)
    me = block_of(z, x, y)
    keep(x16.at[mine], xs, own.at[0])
    keep(d_rows, dv, own.at[1])
    keep(w_out, w2, own.at[2])
    keep(w_in, w1, own.at[3])
    expected = greet_chips(z, x, y, c)
    arrive(expected)
    push(x16.at[theirs], xo, send.at[0], core_recv.at[0], sib)
    wait_bytes(xs, own.at[0])
    wait_bytes(xo, core_recv.at[0])
    xs[...] = xs[...] + xo[...]
    to_chips(
        z, x, y, c,
        lambda there: xs.at[pl.ds(pl.multiple_of(block_of(*there[:3]) - c * 512, 16), 16)],
        rows.at[pl.ds(me, 16)], send.at[1], recv.at[0],
    )
    wait_bytes(dv, own.at[1])
    wait_bytes(w2, own.at[2])

    def hidden_grads(n):
        cols = pl.ds(pl.multiple_of(n * WIDE, WIDE), WIDE)
        dh[:, cols] = dot(dv[...], w2[cols, :], NT)

    loop(0, FH // WIDE, hidden_grads)
    wait_bytes(w1, own.at[3])
    wait_bytes(rows.at[mine], recv.at[0])
    push(rows.at[mine], rows.at[mine], send.at[2], core_recv.at[1], sib)

    def activate(at):
        part = pl.ds(at, 512)

        def one(n):
            cols = pl.ds(pl.multiple_of(n * WIDE, WIDE), WIDE)
            a = dot(rows[part, :], w1[:, cols], NN)
            square = a * a
            t = jnp.tanh(0.7978845608028654 * (a + 0.044715 * (square * a)))
            cdf = 0.5 * (1.0 + t)
            hidden[part, cols] = (a * cdf).astype(BF)
            slope = cdf + 0.5 * a * (1.0 - t * t) * (
                0.7978845608028654 * (1.0 + 0.134145 * square)
            )
            dact[part, cols] = (slope * dh[part, cols]).astype(BF)

        loop(0, FH // WIDE, one)

    def in_half(at):
        part = pl.ds(at, 512)

        def one(n):
            cols = pl.ds(pl.multiple_of(n * WIDE, WIDE), WIDE)
            in_h[part, cols] = dot(dact[part, :], w1[cols, :], NT).astype(BF)

        loop(0, D // WIDE, one)

    def out_half(at):
        part = pl.ds(at, 512)

        def one(n):
            cols = pl.ds(pl.multiple_of(n * WIDE, WIDE), WIDE)
            out_h[part, cols] = dot(hidden[part, :], w2[:, cols], NN).astype(BF)

        loop(0, D // WIDE, one)

    activate(at_mine)
    wait_bytes(rows.at[theirs], core_recv.at[1])
    activate(at_theirs)
    in_half(at_theirs)
    push(in_h.at[theirs], in_o, send.at[3], core_recv.at[2], sib)
    in_half(at_mine)
    wait_bytes(in_o, core_recv.at[2])
    in_o[...] = (in_o[...].astype(F32) + in_h[mine, :].astype(F32)).astype(BF)
    to_chips(
        z, x, y, c,
        lambda there: in_o.at[pl.ds(pl.multiple_of(block_of(*there[:3]) - c * 512, 16), 16)],
        home_in.at[pl.ds(me, 16)], send.at[4], recv.at[1],
    )
    out_half(at_theirs)
    push(out_h.at[theirs], out_o, send.at[5], core_recv.at[3], sib)
    out_half(at_mine)
    wait_bytes(out_o, core_recv.at[3])
    out_o[...] = (out_o[...].astype(F32) + out_h[mine, :].astype(F32)).astype(BF)
    to_chips(
        z, x, y, c,
        lambda there: out_o.at[pl.ds(pl.multiple_of(block_of(*there[:3]) - c * 512, 16), 16)],
        home_out.at[pl.ds(me, 16)], send.at[6], recv.at[2],
    )

    def out_grads(n):
        cols = pl.ds(pl.multiple_of(n * WIDE, WIDE), WIDE)
        slot = n % 2

        @pl.when(n >= 2)
        def _():
            wait_bytes(stage_out.at[slot], staged.at[slot])

        stage_out[slot] = dot(hidden[:, cols], dv[...], TN)
        keep(stage_out.at[slot], g_out.at[cols], staged.at[slot])

    loop(0, FH // WIDE, out_grads)
    wait_bytes(home_in.at[mine], recv.at[1])
    push(home_in.at[mine], home_in.at[mine], send.at[7], core_recv.at[4], sib)

    def in_grads(n):
        cols = pl.ds(pl.multiple_of(n * WIDE, WIDE), WIDE)
        slot = n % 2

        @pl.when(n >= 2)
        def _():
            wait_bytes(stage_in.at[slot], staged.at[2 + slot])

        stage_in[slot] = dot(rows[:, cols], dact[...], TN)
        keep(stage_in.at[slot], g_in.at[cols], staged.at[2 + slot])

    loop(0, D // WIDE, in_grads)
    wait_bytes(home_out.at[mine], recv.at[2])
    push(home_out.at[mine], home_out.at[mine], send.at[8], core_recv.at[5], sib)
    for slot in range(2):
        wait_bytes(stage_out.at[slot], staged.at[slot])
        wait_bytes(stage_in.at[slot], staged.at[2 + slot])
    wait_bytes(xo, send.at[0])
    sent_to_chips(rows, y, c, send.at[1])
    wait_bytes(rows.at[mine], send.at[2])
    wait_bytes(in_o, send.at[3])
    sent_to_chips(home_in, y, c, send.at[4])
    wait_bytes(out_o, send.at[5])
    sent_to_chips(home_out, y, c, send.at[6])
    wait_bytes(home_in.at[theirs], core_recv.at[4])
    wait_bytes(home_out.at[theirs], core_recv.at[5])
    wait_bytes(home_in.at[mine], send.at[7])
    wait_bytes(home_out.at[mine], send.at[8])


def run_experts(x16, d_rows, w_in, w_out):
    whole_rows = pltpu.VMEM((1024, D), BF)
    half_rows = pltpu.VMEM((512, D), BF)
    hid = pltpu.VMEM((1024, FH), BF)
    return pl.pallas_call(
        experts_kernel,
        out_shape=(
            jax.ShapeDtypeStruct((1024, D), BF),
            jax.ShapeDtypeStruct((1024, D), BF),
            jax.ShapeDtypeStruct((D, FH), F32),
            jax.ShapeDtypeStruct((FH, D), F32),
        ),
        in_specs=[ANY] * 4,
        out_specs=(ANY,) * 4,
        scratch_shapes=[
            half_rows, half_rows, whole_rows, whole_rows,
            pltpu.VMEM((D, FH), BF), pltpu.VMEM((FH, D), BF), pltpu.VMEM((1024, FH), F32),
            hid, hid, whole_rows, whole_rows, half_rows, half_rows,
            pltpu.VMEM((2, WIDE, D), F32), pltpu.VMEM((2, WIDE, FH), F32),
            DMA((9,)), DMA((3,)), DMA((6,)), DMA((4,)), DMA((4,)),
        ],
        compiler_params=pltpu.CompilerParams(
            collective_id=1, has_side_effects=True, vmem_limit_bytes=48 * 2**20
        ),
        name="experts",
    )(x16, d_rows, w_in, w_out)


def device_of(d):
    return d // 32, (d // 8) % 4, (d // 2) % 4, d % 2


NT = (((1,), (1,)), ((), ()))
NN = (((1,), (0,)), ((), ()))
TN = (((0,), (0,)), ((), ()))


def dot(a, b, dims):
    return lax.dot_general(a, b, dims, preferred_element_type=F32)


def near_distance(dist):
    a = lax.broadcasted_iota(jnp.int32, (TOK, TOK), 0)
    b = lax.broadcasted_iota(jnp.int32, (TOK, TOK), 1)
    return dist * TOK + a - b


def table_kind(zq, zk, x, kx):
    return jnp.clip((zq - zk) * 4 + x - kx + 1, 0, 3)


def block_cols(zk, kx):
    return pl.ds(pl.multiple_of((zk * 4 + kx) * TOK, TOK), TOK)


VMEM = pl.BlockSpec(memory_space=pltpu.VMEM)
SMEM = pl.BlockSpec(memory_space=pltpu.SMEM)


def attn_forward_kernel(
    tab, tok, wmsg, wa, d_eo,
    attn_all, part, p_out, kv_out, wa_all, d_rows, normed, weight, q, gains,
    wm, wo, w_s, tok_s, select, picker, qd, kd,
    kv, kv_s, v_s, qm, bias, s_s, p_s, xo,
    send, recv, kv_recv, core_recv, own,
):
    z, x, y, c = place()
    sib = (z, x, y, 1 - c)
    mine = pl.ds(pl.multiple_of(c * 512, 512), 512)
    theirs = pl.ds(pl.multiple_of((1 - c) * 512, 512), 512)
    me = block_of(z, x, y)
    keep(wa, wa_all.at[z, x, y, c], own.at[0])
    expected = greet_chips(z, x, y, c)
    for k in range(1, 4):
        signal(((z + k) % 4, x, y, c))
        signal((z, (x + k) % 4, y, c))
        signal((z, x, (y + k) % 4, c))
    arrive(expected + 9)
    push(wmsg, wo, send.at[0], core_recv.at[0], sib)
    for k in range(1, 4):
        push(tok, tok_s.at[z], send.at[1], recv.at[0], ((z + k) % 4, x, y, c))
    keep(tok, tok_s.at[z], recv.at[0])
    push(d_eo.at[theirs], xo, send.at[2], core_recv.at[1], sib)
    wait_bytes(wo, core_recv.at[0])
    wm[...] = wmsg[...] + wo[...]
    to_chips(
        z, x, y, c, lambda there: wm.at[there[0]], w_s.at[pl.ds(me, 16)], send.at[3], recv.at[1]
    )
    for k in range(1, 4):
        push(wa, wa_all.at[z, x, y, c], send.at[4], recv.at[2], ((z + k) % 4, x, y, c))

    row = lax.broadcasted_iota(jnp.int32, (1, 1024), 1)
    r, half, at = row & 15, row >> 9, (row >> 4) & 31
    row_z, row_x, row_y = at >> 3, (at >> 1) & 3, (at & 1) * 2 + half
    feature = jnp.where(r < 12, (row_z * 16 + row_x * 4 + row_y) * 12 + r, -1)
    select[...] = jnp.where(
        lax.broadcasted_iota(jnp.int32, (D, 1024), 0) == feature, 1.0, 0.0
    ).astype(BF)
    j = lax.broadcasted_iota(jnp.int32, (32, 1024), 0)
    gain_rows = (j < 4) & (r >> 1 == 6 + (j >> 1)) & (row_z >> 1 == j & 1)
    notes = (r == 12 + c) & (row_y == y)
    key_rows = (j >= 8) & (row_z * 4 + row_x == j - 8)
    query_rows = (j >= 24) & (row_z == j - 24) & (row_x == x)
    picker[...] = jnp.where(gain_rows | (notes & (key_rows | query_rows)), 1.0, 0.0).astype(BF)
    xo_ready = core_recv.at[1]

    def tables(h):
        for dist in range(2):
            n = near_distance(dist)
            acc = jnp.full((TOK, TOK), tab[0, h], F32)
            for k, edge in enumerate(bucket_edges):
                acc = jnp.where(n >= edge, tab[k + 1, h], acc)
            bias[h, 1 + dist] = jnp.where(n >= 0, acc, masked)
        bias[h, 0] = jnp.full((TOK, TOK), masked, F32)
        bias[h, 3] = jnp.full((TOK, TOK), tab[BUCKETS - 1, h], F32)

    loop(0, GH, tables)
    wait_bytes(xo, xo_ready)
    xo[...] = xo[...] + d_eo[mine, :]
    wait_bytes(w_s.at[mine], recv.at[1])
    push(w_s.at[mine], w_s.at[mine], send.at[5], core_recv.at[2], sib)
    wait_bytes(wa_all.at[z, x, y, c], own.at[0])
    wait_bytes(wa_all.at[pl.ds(0, 3), x, y, c], recv.at[2])
    for k in range(1, 4):
        push(
            wa_all.at[:, x, y, c], wa_all.at[:, x, y, c], send.at[6], recv.at[3],
            (z, (x + k) % 4, y, c),
        )
    wait_bytes(w_s.at[theirs], core_recv.at[2])
    picked = dot(picker[...], w_s[...], NN)
    gain = jnp.concatenate([picked[0:1, :384], picked[1:2, :384]], axis=1)
    gains[0:1, :] = gain
    gains[1:2, :] = jnp.concatenate([picked[2:3, :384], picked[3:4, :384]], axis=1)
    gains[2:8, :] = jnp.zeros((6, D), F32)
    kd[...] = picked[8:24, 384:512]
    qd[...] = picked[24:32, 384:512].T
    weight[...] = dot(select[...], w_s[...], NN).astype(BF)
    wait_bytes(tok_s, recv.at[0])
    for b in range(4):
        v = tok_s[b].astype(F32)
        normed[b * TOK : (b + 1) * TOK, :] = scale_rows(v, gain).astype(BF)
    qkv = dot(normed[...], weight[...], NN).astype(BF)
    q[...] = qkv[:, :GW]
    for b in range(4):
        kv[b] = qkv[b * TOK : (b + 1) * TOK, GW:]
    for k in range(1, 4):
        for b in range(4):
            push(
                kv.at[b], kv_s.at[block_cols(b, x)], send.at[7], kv_recv.at[4 - k],
                (z, (x + k) % 4, y, c),
            )
    for b in range(4):
        keep(kv.at[b], kv_s.at[block_cols(b, x)], kv_recv.at[0])
    wait_bytes(wa_all.at[:, pl.ds(0, 3), y, c], recv.at[3])
    for k in range(1, 4):
        push(
            wa_all.at[:, :, y, c], wa_all.at[:, :, y, c], send.at[8], recv.at[4],
            (z, x, (y + k) % 4, c),
        )
    for h in range(GH):
        head_cols = lax.broadcasted_iota(jnp.int32, (1, GW), 1) // HD == h
        qm[h] = jnp.where(head_cols, q[...] * 0.125, 0.0).astype(BF)
    for k in range(4):
        kx = (x + k) % 4
        if k == 0:
            for b in range(4):
                wait_bytes(kv_s.at[block_cols(b, kx)], kv_recv.at[0])
        else:
            wait_bytes(kv_s.at[pl.ds(0, 512)], kv_recv.at[k])
        for b in range(4):
            cols = block_cols(b, kx)
            v_s[cols, :] = kv_s[cols, GW:]
            for h in range(GH):
                s_s[h, b * TOK :, cols] = dot(qm[h, b * TOK :, :], kv_s[cols, :GW], NT)
    keep(kv_s, kv_out, own.at[1])
    to_chips(
        z, x, y, c,
        lambda there: xo.at[pl.ds(pl.multiple_of(block_of(*there[:3]) - c * 512, 16), 16)],
        d_rows.at[pl.ds(me, 16)], send.at[9], recv.at[5],
    )
    wait_bytes(wa_all.at[:, :, pl.ds(0, 3), c], recv.at[4])
    push(wa_all.at[:, :, :, c], wa_all.at[:, :, :, c], send.at[10], core_recv.at[3], sib)

    def head(h):
        head_cols = lax.broadcasted_iota(jnp.int32, (1, GW), 1) // HD == h
        far = tab[BUCKETS - 1, h]
        for zq in range(4):
            rows = pl.ds(zq * TOK, TOK)
            docs = qd[:, zq : zq + 1]
            top = None
            for zk in range(zq + 1):
                for kx in range(4):
                    cols = pl.ds((zk * 4 + kx) * TOK, TOK)
                    s = s_s[h, rows, cols]
                    if zk < zq - 1:
                        s = s + far
                    else:
                        s = s + bias[h, table_kind(zq, zk, x, kx)]
                    kb = zk * 4 + kx
                    s = jnp.where(docs == kd[kb : kb + 1, :], s, masked)
                    s_s[h, rows, cols] = s
                    top = s if top is None else jnp.maximum(top, s)
            top = jnp.max(top, axis=1, keepdims=True)
            total = jnp.zeros((TOK, TOK), F32)
            for kb in range(4 * (zq + 1)):
                cols = pl.ds(kb * TOK, TOK)
                e = jnp.exp(s_s[h, rows, cols] - top)
                s_s[h, rows, cols] = e
                total = total + e
            inv = 1.0 / jnp.sum(total, axis=1, keepdims=True)
            for kb in range(4 * (zq + 1)):
                cols = pl.ds(kb * TOK, TOK)
                p_s[h, rows, cols] = (s_s[h, rows, cols] * inv).astype(BF)
            width = (zq + 1) * 512
            o = dot(p_s[h, rows, :width], v_s[:width, :], NN).astype(BF)

            @pl.when(h == 0)
            def _():
                part[rows, :] = o

            @pl.when(h > 0)
            def _():
                part[rows, :] = jnp.where(head_cols, o, part[rows, :])

    loop(0, GH, head)
    for k in range(1, 4):
        there = (z + k) % 4
        push(
            part.at[pl.ds(pl.multiple_of(there * TOK, TOK), TOK)], attn_all.at[z],
            send.at[11], recv.at[6], (there, x, y, c),
        )
    keep(part.at[pl.ds(pl.multiple_of(z * TOK, TOK), TOK)], attn_all.at[z], recv.at[6])
    keep(p_s, p_out, own.at[2])
    wait_bytes(d_rows.at[mine], recv.at[5])
    push(d_rows.at[mine], d_rows.at[mine], send.at[12], core_recv.at[4], sib)
    wait_bytes(attn_all, recv.at[6])
    wait_bytes(wa_all.at[:, :, :, 1 - c], core_recv.at[3])
    wait_bytes(d_rows.at[theirs], core_recv.at[4])
    wait_bytes(kv_s, own.at[1])
    wait_bytes(p_s, own.at[2])
    wait_bytes(wo, send.at[0])
    wait_bytes(tok_s.at[pl.ds(0, 3)], send.at[1])
    wait_bytes(xo, send.at[2])
    sent_to_chips(w_s, y, c, send.at[3])
    wait_bytes(wa_all.at[pl.ds(0, 3), x, y, c], send.at[4])
    wait_bytes(w_s.at[mine], send.at[5])
    wait_bytes(wa_all.at[:, pl.ds(0, 3), y, c], send.at[6])
    wait_bytes(kv_s.at[pl.ds(0, 1536)], send.at[7])
    wait_bytes(wa_all.at[:, :, pl.ds(0, 3), c], send.at[8])
    sent_to_chips(d_rows, y, c, send.at[9])
    wait_bytes(wa_all.at[:, :, :, c], send.at[10])
    wait_bytes(attn_all.at[pl.ds(0, 3)], send.at[11])
    wait_bytes(d_rows.at[mine], send.at[12])


def attn_forward(tab, tok, wmsg, wa, d_eo):
    probs = (GH, 512, 2048)
    vm = pltpu.VMEM
    return pl.pallas_call(
        attn_forward_kernel,
        out_shape=(
            jax.ShapeDtypeStruct((4, TOK, GW), BF),
            jax.ShapeDtypeStruct((512, GW), BF),
            jax.ShapeDtypeStruct(probs, BF),
            jax.ShapeDtypeStruct((2048, 2 * GW), BF),
            jax.ShapeDtypeStruct((4, 4, 4, 2, 8, D), BF),
            jax.ShapeDtypeStruct((1024, D), BF),
            jax.ShapeDtypeStruct((512, D), BF),
            jax.ShapeDtypeStruct((D, 3 * GW), BF),
            jax.ShapeDtypeStruct((512, GW), BF),
            jax.ShapeDtypeStruct((8, D), F32),
        ),
        in_specs=[SMEM, VMEM, VMEM, VMEM, VMEM],
        out_specs=(ANY, VMEM, ANY, ANY, ANY, ANY, VMEM, VMEM, VMEM, VMEM),
        scratch_shapes=[
            vm((4, 16, 3 * GW), BF), vm((4, 16, 3 * GW), BF), vm((1024, 3 * GW), BF),
            vm((4, TOK, D), BF), vm((D, 1024), BF), vm((32, 1024), BF),
            vm((TOK, 8), F32), vm((16, TOK), F32),
            vm((4, TOK, 2 * GW), BF), vm((2048, 2 * GW), BF), vm((2048, GW), BF),
            vm((GH, 512, GW), BF), vm((GH, 4, TOK, TOK), F32), vm(probs, F32), vm(probs, BF),
            vm((512, D), BF),
            DMA((13,)), DMA((7,)), DMA((4,)), DMA((5,)), DMA((3,)),
        ],
        compiler_params=pltpu.CompilerParams(
            collective_id=2, has_side_effects=True, vmem_limit_bytes=48 * 2**20
        ),
        name="attn_forward",
    )(tab, tok, wmsg, wa, d_eo)


def attn_backward_kernel(
    p, q, kv, d_attn, branch, weight, normed, attn_part, small, tok, gain, d_middle,
    input_grad, qkv_out, att_out, small_out,
    p_s, v_s, do_s, dm, qm, dp_s, ds_s, near, messages, parts, branch_all, dq, tab,
    d_qkv, n_part, normed_in, att_f, q_blk, q_sib, q_tot, q_in, a_blk, a_sib, a_tot, a_in,
    s_own, s_sib, s_tot, s_in, qkv_sum, att_sum, s_sum, send, recv, core_recv, own,
):
    z, x, y, c = place()
    sib = (z, x, y, 1 - c)
    p16 = x * 4 + y
    p32 = p16 * 2 + c
    me = z * 32 + p32
    source = me // 4

    def peer(i):
        return z, (x + i // 4) % 4, (y + i % 4) % 4, c

    keep(p, p_s, own.at[0])
    loop(1, 16, lambda i: signal(peer(i)))
    for k in range(1, 4):
        signal(((z + k) % 4, x, y, c))
    signal(sib)

    def greet(k):
        @pl.when(jnp.logical_not((k == z) & (source == p32)))
        def _():
            signal((k, source // 8, (source // 2) % 4, source % 2))

    loop(0, 4, greet)
    v_s[...] = kv[:, GW:]
    for h in range(GH):
        head_cols = lax.broadcasted_iota(jnp.int32, (1, GW), 1) // HD == h
        qm[h] = jnp.where(head_cols, q[...] * 0.125, 0.0).astype(BF)
    arrive(15 + 3 + 1 + 4 - jnp.where(source == p32, 1, 0))
    for k in range(1, 4):
        there = (z + k) % 4
        push(d_attn.at[there], do_s.at[z], send.at[0], recv.at[0], (there, x, y, c))
    keep(d_attn.at[z], do_s.at[z], recv.at[0])
    z_rows = pl.ds(pl.multiple_of(z * TOK, TOK), TOK)
    for k in range(1, 4):
        push(branch, branch_all.at[z_rows], send.at[1], recv.at[1], ((z + k) % 4, x, y, c))
    keep(branch, branch_all.at[z_rows], recv.at[1])
    wait_bytes(do_s, recv.at[0])
    for h in range(GH):
        head_cols = lax.broadcasted_iota(jnp.int32, (1, GW), 1) // HD == h
        for b in range(4):
            dm[h, b * TOK : (b + 1) * TOK, :] = jnp.where(head_cols, do_s[b], 0.0).astype(BF)
    wait_bytes(p_s, own.at[0])

    def key_sums(left, right, first):
        for k in (1, 2, 3, 0):
            kx = (x + k) % 4
            for b in range(4):
                cols = block_cols(b, kx)
                total = None
                for h in range(GH):
                    one = dot(left[h, b * TOK :, cols], right[h, b * TOK :, :], TN)
                    total = one if total is None else total + one
                side = GW * (b % 2)
                messages[k, first + b // 2, :, side : side + GW] = total.astype(BF)
            for m in range(first, first + 2):
                if k:
                    push(
                        messages.at[k, m], parts.at[x, m], send.at[2], recv.at[2],
                        (z, kx, y, c),
                    )
                else:
                    keep(messages.at[k, m], parts.at[x, m], recv.at[2])

    key_sums(p_s, dm, 0)

    def head(h):
        head_cols = lax.broadcasted_iota(jnp.int32, (1, GW), 1) // HD == h
        for zk in range(4):
            cols = pl.ds(zk * 512, 512)
            dp_s[zk * TOK :, cols] = dot(dm[h, zk * TOK :, :], v_s[cols, :], NT)
        near[...] = jnp.zeros_like(near)
        for zq in range(4):
            rows = pl.ds(zq * TOK, TOK)
            acc = jnp.zeros((TOK, TOK), F32)
            for kb in range(4 * (zq + 1)):
                cols = pl.ds(kb * TOK, TOK)
                acc = acc + p_s[h, rows, cols].astype(F32) * dp_s[rows, cols]
            delta = jnp.sum(acc, axis=1, keepdims=True)
            far = jnp.zeros((TOK, TOK), F32)
            for zk in range(zq + 1):
                for kx in range(4):
                    cols = pl.ds((zk * 4 + kx) * TOK, TOK)
                    ds = (p_s[h, rows, cols].astype(F32) * (dp_s[rows, cols] - delta)).astype(BF)
                    ds_s[h, rows, cols] = ds
                    if zk < zq - 1:
                        far = far + ds.astype(F32)
                    else:
                        near[table_kind(zq, zk, x, kx)] += ds.astype(F32)
            near[3] += far
            width = (zq + 1) * 512
            o = (dot(ds_s[h, rows, :width], kv[:width, :GW], NN) * 0.125).astype(BF)

            @pl.when(h == 0)
            def _():
                dq[rows, :] = o

            @pl.when(h > 0)
            def _():
                dq[rows, :] = jnp.where(head_cols, o, dq[rows, :])

        for dist in range(2):
            n = near_distance(dist)
            held = near[1 + dist]
            bounds = [-(10**6)] + bucket_edges + [10**6]
            for b in range(BUCKETS):
                low, high = bounds[b], bounds[b + 1]
                if high <= dist * TOK - TOK + 1 or low > dist * TOK + TOK - 1:
                    if dist == 0:
                        tab[h, b : b + 1, :] = jnp.zeros((1, TOK), F32)
                    continue
                inside = jnp.sum(
                    jnp.where((n >= low) & (n < high), held, 0.0), axis=0, keepdims=True
                )
                if dist == 0:
                    tab[h, b : b + 1, :] = inside
                else:
                    tab[h, b : b + 1, :] += inside
        tab[h, BUCKETS - 1 :, :] += jnp.sum(near[3], axis=0, keepdims=True)

    loop(0, GH, head)
    key_sums(ds_s, qm, 2)

    wait_bytes(branch_all, recv.at[1])
    att_f[0:GW, :] = dot(attn_part[...], branch_all[...], TN)
    att_f[GW:, :] = jnp.zeros((8, D), F32)
    for j in range(32):
        a_blk[j // 2, j % 2] = att_f[6 * j : 6 * j + 8, :].astype(BF)
    push(a_blk.at[:, 1 - c], a_sib, send.at[4], core_recv.at[1], sib)
    s_own[...] = small[...]
    for h in range(GH):
        s_own[2:3, BUCKETS * h : BUCKETS * (h + 1)] = jnp.sum(tab[h].T, axis=0, keepdims=True)

    wait_bytes(parts, recv.at[2])
    d_qkv[:, :GW] = dq[...]
    for b in range(4):
        rows = slice(b * TOK, (b + 1) * TOK)
        side = GW * (b % 2)
        for m, at in ((2 + b // 2, GW), (b // 2, 2 * GW)):
            total = parts[0, m, :, side : side + GW].astype(F32)
            for k in range(1, 4):
                total = total + parts[k, m, :, side : side + GW].astype(F32)
            d_qkv[rows, at : at + GW] = total.astype(BF)
    n_part[...] = dot(d_qkv[...], weight[...], NT).astype(BF)
    for k in range(1, 4):
        there = (z + k) % 4
        push(
            n_part.at[pl.ds(pl.multiple_of(there * TOK, TOK), TOK)], normed_in.at[z],
            send.at[3], recv.at[3], (there, x, y, c),
        )
    keep(n_part.at[z_rows], normed_in.at[z], recv.at[3])
    total = dot(normed[...], d_qkv[...], TN)
    for j in range(32):
        q_blk[j // 2, j % 2] = total[24 * j : 24 * j + 24].astype(BF)
    push(q_blk.at[:, 1 - c], q_sib, send.at[5], core_recv.at[0], sib)
    wait_bytes(a_sib, core_recv.at[1])

    def att_blocks(i):
        there = peer(i)
        j = there[1] * 4 + there[2]
        a_tot[j] = (a_blk[j, c].astype(F32) + a_sib[j].astype(F32)).astype(BF)
        push(a_tot.at[j], a_in.at[p16], send.at[6], recv.at[4], there)

    loop(1, 16, att_blocks)
    a_tot[p16] = (a_blk[p16, c].astype(F32) + a_sib[p16].astype(F32)).astype(BF)
    keep(a_tot.at[p16], a_in.at[p16], recv.at[4])
    wait_bytes(q_sib, core_recv.at[0])

    def qkv_blocks(i):
        there = peer(i)
        j = there[1] * 4 + there[2]
        q_tot[j] = (q_blk[j, c].astype(F32) + q_sib[j].astype(F32)).astype(BF)
        push(q_tot.at[j], q_in.at[p16], send.at[7], recv.at[5], there)

    loop(1, 16, qkv_blocks)
    q_tot[p16] = (q_blk[p16, c].astype(F32) + q_sib[p16].astype(F32)).astype(BF)
    keep(q_tot.at[p16], q_in.at[p16], recv.at[5])

    wait_bytes(normed_in, recv.at[3])
    d_normed = normed_in[0].astype(F32)
    for k in range(1, 4):
        d_normed = d_normed + normed_in[k].astype(F32)
    v = tok[...].astype(F32)
    r = lax.rsqrt(jnp.mean(v * v, axis=1, keepdims=True) + norm_eps)
    unit = v * r
    s_own[0:1, :] = jnp.sum(d_normed * unit, axis=0, keepdims=True)
    push(s_own, s_sib, send.at[8], core_recv.at[2], sib)
    d_unit = d_normed * gain[...]
    d_in = r * (d_unit - unit * jnp.mean(d_unit * unit, axis=1, keepdims=True))
    input_grad[...] = (d_middle[...] + d_in).astype(BF)
    wait_bytes(s_sib, core_recv.at[2])
    s_tot[...] = s_own[...] + s_sib[...]
    loop(1, 16, lambda i: push(s_tot, s_in.at[p16], send.at[9], recv.at[6], peer(i)))
    keep(s_tot, s_in.at[p16], recv.at[6])

    wait_bytes(q_in, recv.at[5])
    q_total = q_in[0].astype(F32)
    for k in range(1, 16):
        q_total = q_total + q_in[k].astype(F32)
    for k in range(4):
        qkv_sum[k, 0:6, :] = q_total[6 * k : 6 * k + 6]
        qkv_sum[k, 6:8, :] = jnp.zeros((2, 3 * GW), F32)

    def final(k):
        d = 4 * p32 + k

        @pl.when(d != me)
        def _():
            push(qkv_sum.at[k], qkv_out.at[z], send.at[10], recv.at[7], device_of(d))

        @pl.when(d == me)
        def _():
            keep(qkv_sum.at[k], qkv_out.at[z], recv.at[7])

    loop(0, 4, final)
    wait_bytes(a_in, recv.at[4])
    a_total = a_in[0].astype(F32)
    for k in range(1, 16):
        a_total = a_total + a_in[k].astype(F32)
    att_sum[...] = a_total
    keep(att_sum, att_out, own.at[1])
    wait_bytes(s_in, recv.at[6])
    s_total = s_in[0]
    for k in range(1, 16):
        s_total = s_total + s_in[k]
    s_sum[...] = s_total
    for k in range(1, 4):
        push(s_sum, small_out.at[z], send.at[11], recv.at[8], ((z + k) % 4, x, y, c))
    keep(s_sum, small_out.at[z], recv.at[8])
    wait_bytes(att_sum, own.at[1])
    wait_bytes(qkv_out, recv.at[7])
    wait_bytes(small_out, recv.at[8])
    wait_bytes(do_s.at[pl.ds(0, 3)], send.at[0])
    wait_bytes(branch_all.at[pl.ds(0, 3 * TOK)], send.at[1])
    wait_bytes(parts.at[pl.ds(0, 3)], send.at[2])
    wait_bytes(normed_in.at[pl.ds(0, 3)], send.at[3])
    wait_bytes(a_sib, send.at[4])
    wait_bytes(q_sib, send.at[5])
    wait_bytes(a_in.at[pl.ds(0, 15)], send.at[6])
    wait_bytes(q_in.at[pl.ds(0, 15)], send.at[7])
    wait_bytes(s_own, send.at[8])
    wait_bytes(s_in.at[pl.ds(0, 15)], send.at[9])

    def sent(k):
        @pl.when(4 * p32 + k != me)
        def _():
            wait_bytes(qkv_sum.at[0], send.at[10])

    loop(0, 4, sent)
    wait_bytes(small_out.at[pl.ds(0, 3)], send.at[11])


def attn_backward(p, *rest):
    probs = (GH, 512, 2048)
    vm = pltpu.VMEM
    return pl.pallas_call(
        attn_backward_kernel,
        out_shape=(
            jax.ShapeDtypeStruct((TOK, D), BF),
            jax.ShapeDtypeStruct((4, 8, 3 * GW), F32),
            jax.ShapeDtypeStruct((8, D), F32),
            jax.ShapeDtypeStruct((4, 8, D), F32),
        ),
        in_specs=[ANY] + [VMEM] * len(rest),
        out_specs=(VMEM, ANY, ANY, ANY),
        scratch_shapes=[
            vm(probs, BF), vm((2048, GW), BF), vm((4, TOK, GW), BF), vm((GH, 512, GW), BF),
            vm((GH, 512, GW), BF), vm((512, 2048), F32), vm(probs, BF), vm((4, TOK, TOK), F32),
            vm((4, 4, TOK, 2 * GW), BF), vm((4, 4, TOK, 2 * GW), BF), vm((512, D), BF),
            vm((512, GW), BF), vm((GH, BUCKETS, TOK), F32),
            vm((512, 3 * GW), BF), vm((512, D), BF), vm((4, TOK, D), BF), vm((GW + 8, D), F32),
            vm((16, 2, 24, 3 * GW), BF), vm((16, 24, 3 * GW), BF),
            vm((16, 24, 3 * GW), BF), vm((16, 24, 3 * GW), BF),
            vm((16, 2, 8, D), BF), vm((16, 8, D), BF), vm((16, 8, D), BF), vm((16, 8, D), BF),
            vm((8, D), F32), vm((8, D), F32), vm((8, D), F32), vm((16, 8, D), F32),
            vm((4, 8, 3 * GW), F32), vm((8, D), F32), vm((8, D), F32),
            DMA((12,)), DMA((9,)), DMA((3,)), DMA((2,)),
        ],
        compiler_params=pltpu.CompilerParams(
            collective_id=3, has_side_effects=True, vmem_limit_bytes=52 * 2**20
        ),
        name="attn_backward",
    )(p, *rest)


def per_device(
    tokens,
    gain_attn,
    w_qkv,
    w_attn_out,
    rel_table,
    gain_moe,
    w_in,
    w_out,
    expert_ids,
    gate_values,
    doc_ids,
    cotangent,
):
    z, x, y, c = place()
    experts = 64
    capacity = 8
    slots = 2 * experts * capacity
    own_tokens = tokens.reshape(TOK, D)
    grad_bf = cotangent.reshape(TOK, D)
    grad_out = grad_bf.astype(F32)

    routes = expert_ids.reshape(TOK, 2)
    gates = gate_values.reshape(TOK, 2)
    expert_list = jnp.arange(experts, dtype=jnp.int32)[None, :]
    marks = jnp.concatenate(
        [(routes[:, :1] == expert_list), (routes[:, 1:] == expert_list)], axis=1
    ).astype(BF)
    lower = jnp.tril(jnp.ones((TOK, TOK), BF), -1)
    earlier = dot(lower, marks, NN)
    marks = marks.astype(F32)
    firsts = jnp.sum(marks[:, :experts], axis=0, keepdims=True)
    rank_0 = jnp.sum(earlier[:, :experts] * marks[:, :experts], axis=1)
    rank_1 = jnp.sum((earlier[:, experts:] + firsts) * marks[:, experts:], axis=1)
    blocks = (routes % 2) * 32 + (routes // 4) * 2 + (routes % 4) // 2
    places = blocks * 16 + c * capacity + jnp.stack([rank_0, rank_1], axis=1).astype(jnp.int32)
    slot_ids = jnp.arange(slots, dtype=jnp.int32)[None, :]
    picks = jnp.concatenate(
        [(places[:, :1] == slot_ids), (places[:, 1:] == slot_ids)], axis=0
    ).astype(BF)
    gated = jnp.concatenate([gates[:, :1] * grad_out, gates[:, 1:] * grad_out], axis=0).astype(BF)
    d_eo = dot(picks, gated, TN).astype(BF)

    slab = w_qkv.reshape(6, 3, GROUPS, GW).transpose(2, 0, 1, 3).reshape(GROUPS, 6, 3 * GW)
    place_in = chip_of(z, x, y) * 2 + c
    among = (place_in % 64) * 6
    row_one = lax.dynamic_update_slice(jnp.zeros((3 * GW,), BF), gain_attn, (among,))
    row_one = lax.dynamic_update_slice(row_one, doc_ids.reshape(TOK).astype(BF), (384,))
    row_two = lax.dynamic_update_slice(jnp.zeros((3 * GW,), BF), gain_moe, (among,))
    note_one = jnp.broadcast_to(row_one, (GROUPS, 1, 3 * GW))
    note_two = jnp.broadcast_to(row_two, (GROUPS, 1, 3 * GW))
    nothing = jnp.zeros((GROUPS, 6, 3 * GW), BF)
    none = nothing[:, :1]
    message = jnp.where(
        c == 0,
        jnp.concatenate([slab, nothing, note_one, none, note_two, none], axis=1),
        jnp.concatenate([nothing, slab, none, note_one, none, note_two], axis=1),
    )
    out_slab = jnp.concatenate([w_attn_out, jnp.zeros((2, D), BF)], axis=0)
    table = lax.dynamic_slice(rel_table, (0, z * GH), (BUCKETS, GH)).astype(F32)
    (
        attn, attn_part, probs, kv_all, out_weights, d_eo_all, normed, weight, queries, gain_rows,
    ) = attn_forward(table, own_tokens, message, out_slab, d_eo)
    gain_one, gain_two = gain_rows[0], gain_rows[1]
    attn = attn.transpose(1, 0, 2).reshape(TOK, D)
    attention_weight = out_weights[:, :, :, :, :6, :].reshape(D, D)

    inputs = own_tokens.astype(F32)
    middle = inputs + dot(attn, attention_weight, NN)
    moe_float, norm_two_back = jax.vjp(scale_rows, middle, gain_two)
    moe_in = moe_float.astype(BF)
    send_rows = dot(picks, jnp.concatenate([moe_in, moe_in], axis=0), TN).astype(BF)
    home, expert_out, expert_in_grad, expert_out_grad = run_experts(
        send_rows, d_eo_all, w_in[0], w_out[0]
    )
    home_picked = dot(picks, home, NN)
    moe_in_grad = home_picked[:TOK] + home_picked[TOK:]
    middle_part, gain_two_grad = norm_two_back(moe_in_grad)
    middle_grad = grad_out + middle_part
    branch = middle_grad.astype(BF)
    d_attn = dot(branch, attention_weight, NT).astype(BF)
    d_attn = d_attn.reshape(TOK, GROUPS, GW).transpose(1, 0, 2)

    small = jnp.concatenate(
        [jnp.zeros((1, D), F32), gain_two_grad.reshape(1, D), jnp.zeros((6, D), F32)]
    )
    input_grad, qkv_sum, att_sum, small_sum = attn_backward(
        probs, queries, kv_all, d_attn, branch, weight, normed, attn_part, small, own_tokens,
        gain_one.reshape(1, D), middle_grad,
    )

    picked = dot(picks, expert_out, NN).reshape(2, TOK, D)
    block_out = middle + gates[:, :1] * picked[0] + gates[:, 1:] * picked[1]
    gate_grad = jnp.sum(picked * grad_out[None], axis=2).T

    qkv_grad = qkv_sum[:, :6, :].reshape(GROUPS, 6, 3, GW).transpose(1, 2, 0, 3).reshape(6, 3 * D)
    attn_out_grad = att_sum[:6]
    gains = lax.dynamic_slice(jnp.sum(small_sum[:, :2, :], axis=0), (0, place_in * 6), (2, 6))
    table_grad = small_sum[:, 2, : GH * BUCKETS].reshape(GROUPS * GH, BUCKETS).T
    return (
        block_out.reshape(1, TOK, D).astype(BF),
        input_grad.reshape(1, TOK, D),
        gate_grad.reshape(1, TOK, 2),
        gains[0],
        qkv_grad,
        attn_out_grad,
        table_grad,
        gains[1],
        expert_in_grad[None],
        expert_out_grad[None],
    )


def solution(mesh):
    torus = Mesh(mesh.devices.reshape(4, 4, 4, 2), AXES)
    in_specs = (
        P(EXP, CTX, None),
        P(AXES),
        P(AXES, None),
        P(AXES, None),
        P(),
        P(AXES),
        P(AXES, None, None),
        P(AXES, None, None),
        P(EXP, CTX, None),
        P(EXP, CTX, None),
        P(EXP, CTX),
        P(EXP, CTX, None),
    )
    out_specs = (
        P(EXP, CTX, None),
        P(EXP, CTX, None),
        P(EXP, CTX, None),
        P(AXES),
        P(AXES, None),
        P(AXES, None),
        P(),
        P(AXES),
        P(AXES, None, None),
        P(AXES, None, None),
    )
    return jax.shard_map(
        per_device, mesh=torus, in_specs=in_specs, out_specs=out_specs, check_vma=False
    )
```

```python
import functools

import jax
import jax.numpy as jnp
import numpy as np
from jax import lax
from jax.experimental import pallas as pl
from jax.experimental.pallas import tpu as pltpu
from jax.sharding import Mesh
from jax.sharding import PartitionSpec as P

D = 768
H = 12
HD = 64
BUCKETS = 32
GROUPS = 4
GH = H // GROUPS
GW = GH * HD
TOK = 128
CTX = ("ctx_0", "ctx_1")
EXP = ("exp_0", "exp_1")
AXES = ("ctx_0", "ctx_1", "exp_0", "exp_1")
MESH = pl.DeviceIdType.MESH
ANY = pl.BlockSpec(memory_space=pl.ANY)
BF = jnp.bfloat16
F32 = jnp.float32

norm_eps = 1e-06
bucket_edges = [int(e) for e in np.concatenate(
    [np.arange(1, 17), np.ceil(16.0 * 8.0 ** (np.arange(1, 16) / 16.0))]
).astype(np.int32)]
masked = -1e30


def scale_rows(values, gain):
    return values * lax.rsqrt(jnp.mean(values * values, axis=-1, keepdims=True) + norm_eps) * gain


def place():
    return tuple(lax.axis_index(a) for a in AXES)


def chip_of(z, x, y):
    return (z * 4 + x) * 4 + y


def chip_peer(i, z, x, y):
    return (z + i // 16) % 4, (x + (i // 4) % 4) % 4, (y + i % 4) % 4


def loop(first, last, body):
    lax.fori_loop(first, last, lambda i, carry: (body(i), carry)[1], 0)


def signal(device):
    pl.semaphore_signal(
        pltpu.get_barrier_semaphore(), inc=1, device_id=device, device_id_type=MESH
    )


def arrive(count):
    pl.semaphore_wait(pltpu.get_barrier_semaphore(), count)


def push(src, dst, send, recv, device):
    pltpu.make_async_remote_copy(
        src_ref=src, dst_ref=dst, send_sem=send, recv_sem=recv, device_id=device, device_id_type=MESH
    ).start()


def keep(src, dst, sem):
    pltpu.make_async_copy(src, dst, sem).start()


def wait_bytes(ref, sem):
    pltpu.make_async_copy(ref, ref, sem).wait()


def comm_call(kernel, outs, scratch, collective_id, name):
    return pl.pallas_call(
        kernel,
        out_shape=outs,
        in_specs=None,
        out_specs=jax.tree.map(lambda _: ANY, outs),
        scratch_shapes=scratch,
        compiler_params=pltpu.CompilerParams(
            collective_id=collective_id, has_side_effects=True, vmem_limit_bytes=32 * 2**20
        ),
        name=name,
    )


def run_comm(kernel, args, outs, scratch, collective_id, name):
    return pl.pallas_call(
        kernel,
        out_shape=outs,
        in_specs=[ANY] * len(args),
        out_specs=jax.tree.map(lambda _: ANY, outs),
        scratch_shapes=scratch,
        compiler_params=pltpu.CompilerParams(
            collective_id=collective_id, has_side_effects=True, vmem_limit_bytes=32 * 2**20
        ),
        name=name,
    )(*args)


DMA = pltpu.SemaphoreType.DMA


def half_peer(i, z, x, y, c):
    return (z + i // 8) % 4, (x + (i // 2) % 4) % 4, c + 2 * ((y // 2 + i % 2) % 2), y % 2


def block_of(z, x, y):
    return pl.multiple_of((y % 2) * 512 + ((z * 4 + x) * 2 + y // 2) * 16, 16)


def greet_chips(z, x, y, c):
    loop(1, 32, lambda i: signal(half_peer(i, z, x, y, c)))

    @pl.when(y % 2 != c)
    def _():
        signal(half_peer(0, z, x, y, c))

    signal((z, x, y, 1 - c))
    return 32 + jnp.where(y % 2 == c, 0, 1)


def to_chips(z, x, y, c, source, target, send, recv):
    def one(i):
        there = half_peer(i, z, x, y, c)
        push(source(there), target, send, recv, there)

    loop(1, 32, one)
    first = half_peer(0, z, x, y, c)

    @pl.when(y % 2 == c)
    def _():
        keep(source(first), target, recv)

    @pl.when(y % 2 != c)
    def _():
        push(source(first), target, send, recv, first)


def sent_to_chips(rows, y, c, send):
    wait_bytes(rows.at[pl.ds(0, 496)], send)

    @pl.when(y % 2 != c)
    def _():
        wait_bytes(rows.at[pl.ds(0, 16)], send)


FH = 1536
WIDE = 256


def experts_kernel(
    x16, d_rows, w_in, w_out, home_in, home_out, g_in, g_out,
    xs, xo, rows, dv, w1, w2, dh, hidden, dact, in_h, out_h, in_o, out_o, stage_out, stage_in,
    send, recv, core_recv, own, staged,
):
    z, x, y, c = place()
    sib = (z, x, y, 1 - c)
    at_mine = pl.multiple_of(c * 512, 512)
    at_theirs = pl.multiple_of((1 - c) * 512, 512)
    mine, theirs = pl.ds(at_mine, 512), pl.ds(at_theirs, 512)
    me = block_of(z, x, y)
    keep(x16.at[mine], xs, own.at[0])
    keep(d_rows, dv, own.at[1])
    keep(w_out, w2, own.at[2])
    keep(w_in, w1, own.at[3])
    expected = greet_chips(z, x, y, c)
    arrive(expected)
    push(x16.at[theirs], xo, send.at[0], core_recv.at[0], sib)
    wait_bytes(xs, own.at[0])
    wait_bytes(xo, core_recv.at[0])
    xs[...] = xs[...] + xo[...]
    to_chips(
        z, x, y, c,
        lambda there: xs.at[pl.ds(pl.multiple_of(block_of(*there[:3]) - c * 512, 16), 16)],
        rows.at[pl.ds(me, 16)], send.at[1], recv.at[0],
    )
    wait_bytes(dv, own.at[1])
    wait_bytes(w2, own.at[2])

    def hidden_grads(n):
        cols = pl.ds(pl.multiple_of(n * WIDE, WIDE), WIDE)
        dh[:, cols] = dot(dv[...], w2[cols, :], NT)

    loop(0, FH // WIDE, hidden_grads)
    wait_bytes(w1, own.at[3])
    wait_bytes(rows.at[mine], recv.at[0])
    push(rows.at[mine], rows.at[mine], send.at[2], core_recv.at[1], sib)

    def activate(at):
        part = pl.ds(at, 512)

        def one(n):
            cols = pl.ds(pl.multiple_of(n * WIDE, WIDE), WIDE)
            a = dot(rows[part, :], w1[:, cols], NN)
            square = a * a
            t = jnp.tanh(0.7978845608028654 * (a + 0.044715 * (square * a)))
            cdf = 0.5 * (1.0 + t)
            hidden[part, cols] = (a * cdf).astype(BF)
            slope = cdf + 0.5 * a * (1.0 - t * t) * (
                0.7978845608028654 * (1.0 + 0.134145 * square)
            )
            dact[part, cols] = (slope * dh[part, cols]).astype(BF)

        loop(0, FH // WIDE, one)

    def in_half(at):
        part = pl.ds(at, 512)

        def one(n):
            cols = pl.ds(pl.multiple_of(n * WIDE, WIDE), WIDE)
            in_h[part, cols] = dot(dact[part, :], w1[cols, :], NT).astype(BF)

        loop(0, D // WIDE, one)

    def out_half(at):
        part = pl.ds(at, 512)

        def one(n):
            cols = pl.ds(pl.multiple_of(n * WIDE, WIDE), WIDE)
            out_h[part, cols] = dot(hidden[part, :], w2[:, cols], NN).astype(BF)

        loop(0, D // WIDE, one)

    activate(at_mine)
    wait_bytes(rows.at[theirs], core_recv.at[1])
    activate(at_theirs)
    in_half(at_theirs)
    push(in_h.at[theirs], in_o, send.at[3], core_recv.at[2], sib)
    in_half(at_mine)
    wait_bytes(in_o, core_recv.at[2])
    in_o[...] = (in_o[...].astype(F32) + in_h[mine, :].astype(F32)).astype(BF)
    to_chips(
        z, x, y, c,
        lambda there: in_o.at[pl.ds(pl.multiple_of(block_of(*there[:3]) - c * 512, 16), 16)],
        home_in.at[pl.ds(me, 16)], send.at[4], recv.at[1],
    )
    out_half(at_theirs)
    push(out_h.at[theirs], out_o, send.at[5], core_recv.at[3], sib)
    out_half(at_mine)
    wait_bytes(out_o, core_recv.at[3])
    out_o[...] = (out_o[...].astype(F32) + out_h[mine, :].astype(F32)).astype(BF)
    to_chips(
        z, x, y, c,
        lambda there: out_o.at[pl.ds(pl.multiple_of(block_of(*there[:3]) - c * 512, 16), 16)],
        home_out.at[pl.ds(me, 16)], send.at[6], recv.at[2],
    )

    def out_grads(n):
        cols = pl.ds(pl.multiple_of(n * WIDE, WIDE), WIDE)
        slot = n % 2

        @pl.when(n >= 2)
        def _():
            wait_bytes(stage_out.at[slot], staged.at[slot])

        stage_out[slot] = dot(hidden[:, cols], dv[...], TN)
        keep(stage_out.at[slot], g_out.at[cols], staged.at[slot])

    loop(0, FH // WIDE, out_grads)
    wait_bytes(home_in.at[mine], recv.at[1])
    push(home_in.at[mine], home_in.at[mine], send.at[7], core_recv.at[4], sib)

    def in_grads(n):
        cols = pl.ds(pl.multiple_of(n * WIDE, WIDE), WIDE)
        slot = n % 2

        @pl.when(n >= 2)
        def _():
            wait_bytes(stage_in.at[slot], staged.at[2 + slot])

        stage_in[slot] = dot(rows[:, cols], dact[...], TN)
        keep(stage_in.at[slot], g_in.at[cols], staged.at[2 + slot])

    loop(0, D // WIDE, in_grads)
    wait_bytes(home_out.at[mine], recv.at[2])
    push(home_out.at[mine], home_out.at[mine], send.at[8], core_recv.at[5], sib)
    for slot in range(2):
        wait_bytes(stage_out.at[slot], staged.at[slot])
        wait_bytes(stage_in.at[slot], staged.at[2 + slot])
    wait_bytes(xo, send.at[0])
    sent_to_chips(rows, y, c, send.at[1])
    wait_bytes(rows.at[mine], send.at[2])
    wait_bytes(in_o, send.at[3])
    sent_to_chips(home_in, y, c, send.at[4])
    wait_bytes(out_o, send.at[5])
    sent_to_chips(home_out, y, c, send.at[6])
    wait_bytes(home_in.at[theirs], core_recv.at[4])
    wait_bytes(home_out.at[theirs], core_recv.at[5])
    wait_bytes(home_in.at[mine], send.at[7])
    wait_bytes(home_out.at[mine], send.at[8])


def run_experts(x16, d_rows, w_in, w_out):
    whole_rows = pltpu.VMEM((1024, D), BF)
    half_rows = pltpu.VMEM((512, D), BF)
    hid = pltpu.VMEM((1024, FH), BF)
    return pl.pallas_call(
        experts_kernel,
        out_shape=(
            jax.ShapeDtypeStruct((1024, D), BF),
            jax.ShapeDtypeStruct((1024, D), BF),
            jax.ShapeDtypeStruct((D, FH), F32),
            jax.ShapeDtypeStruct((FH, D), F32),
        ),
        in_specs=[ANY] * 4,
        out_specs=(ANY,) * 4,
        scratch_shapes=[
            half_rows, half_rows, whole_rows, whole_rows,
            pltpu.VMEM((D, FH), BF), pltpu.VMEM((FH, D), BF), pltpu.VMEM((1024, FH), F32),
            hid, hid, whole_rows, whole_rows, half_rows, half_rows,
            pltpu.VMEM((2, WIDE, D), F32), pltpu.VMEM((2, WIDE, FH), F32),
            DMA((9,)), DMA((3,)), DMA((6,)), DMA((4,)), DMA((4,)),
        ],
        compiler_params=pltpu.CompilerParams(
            collective_id=1, has_side_effects=True, vmem_limit_bytes=48 * 2**20
        ),
        name="experts",
    )(x16, d_rows, w_in, w_out)


def device_of(d):
    return d // 32, (d // 8) % 4, (d // 2) % 4, d % 2


NT = (((1,), (1,)), ((), ()))
NN = (((1,), (0,)), ((), ()))
TN = (((0,), (0,)), ((), ()))


def dot(a, b, dims):
    return lax.dot_general(a, b, dims, preferred_element_type=F32)


def near_distance(dist):
    a = lax.broadcasted_iota(jnp.int32, (TOK, TOK), 0)
    b = lax.broadcasted_iota(jnp.int32, (TOK, TOK), 1)
    return dist * TOK + a - b


def table_kind(zq, zk, x, kx):
    return jnp.clip((zq - zk) * 4 + x - kx + 1, 0, 3)


def block_cols(zk, kx):
    return pl.ds(pl.multiple_of((zk * 4 + kx) * TOK, TOK), TOK)


VMEM = pl.BlockSpec(memory_space=pltpu.VMEM)
SMEM = pl.BlockSpec(memory_space=pltpu.SMEM)


def attn_forward_kernel(
    tab, tok, wmsg, wa, d_eo,
    attn_all, part, p_out, kv_out, wa_all, d_rows, normed, weight, q, gains,
    wm, wo, w_s, tok_s, select, picker, qd, kd,
    kv, kv_s, v_s, qm, bias, s_s, p_s, xo,
    send, recv, kv_recv, core_recv, own,
):
    z, x, y, c = place()
    sib = (z, x, y, 1 - c)
    mine = pl.ds(pl.multiple_of(c * 512, 512), 512)
    theirs = pl.ds(pl.multiple_of((1 - c) * 512, 512), 512)
    me = block_of(z, x, y)
    keep(wa, wa_all.at[z, x, y, c], own.at[0])
    expected = greet_chips(z, x, y, c)
    for k in range(1, 4):
        signal(((z + k) % 4, x, y, c))
        signal((z, (x + k) % 4, y, c))
        signal((z, x, (y + k) % 4, c))
    arrive(expected + 9)
    push(wmsg, wo, send.at[0], core_recv.at[0], sib)
    for k in range(1, 4):
        push(tok, tok_s.at[z], send.at[1], recv.at[0], ((z + k) % 4, x, y, c))
    keep(tok, tok_s.at[z], recv.at[0])
    push(d_eo.at[theirs], xo, send.at[2], core_recv.at[1], sib)
    wait_bytes(wo, core_recv.at[0])
    wm[...] = wmsg[...] + wo[...]
    to_chips(
        z, x, y, c, lambda there: wm.at[there[0]], w_s.at[pl.ds(me, 16)], send.at[3], recv.at[1]
    )
    for k in range(1, 4):
        push(wa, wa_all.at[z, x, y, c], send.at[4], recv.at[2], ((z + k) % 4, x, y, c))
    wait_bytes(xo, core_recv.at[1])
    xo[...] = xo[...] + d_eo[mine, :]
    to_chips(
        z, x, y, c,
        lambda there: xo.at[pl.ds(pl.multiple_of(block_of(*there[:3]) - c * 512, 16), 16)],
        d_rows.at[pl.ds(me, 16)], send.at[9], recv.at[5],
    )

    row = lax.broadcasted_iota(jnp.int32, (1, 1024), 1)
    r, half, at = row & 15, row >> 9, (row >> 4) & 31
    row_z, row_x, row_y = at >> 3, (at >> 1) & 3, (at & 1) * 2 + half
    feature = jnp.where(r < 12, (row_z * 16 + row_x * 4 + row_y) * 12 + r, -1)
    select[...] = jnp.where(
        lax.broadcasted_iota(jnp.int32, (D, 1024), 0) == feature, 1.0, 0.0
    ).astype(BF)
    j = lax.broadcasted_iota(jnp.int32, (32, 1024), 0)
    gain_rows = (j < 4) & (r >> 1 == 6 + (j >> 1)) & (row_z >> 1 == j & 1)
    notes = (r == 12 + c) & (row_y == y)
    key_rows = (j >= 8) & (row_z * 4 + row_x == j - 8)
    query_rows = (j >= 24) & (row_z == j - 24) & (row_x == x)
    picker[...] = jnp.where(gain_rows | (notes & (key_rows | query_rows)), 1.0, 0.0).astype(BF)

    def tables(h):
        for dist in range(2):
            n = near_distance(dist)
            acc = jnp.full((TOK, TOK), tab[0, h], F32)
            for k, edge in enumerate(bucket_edges):
                acc = jnp.where(n >= edge, tab[k + 1, h], acc)
            bias[h, 1 + dist] = jnp.where(n >= 0, acc, masked)
        bias[h, 0] = jnp.full((TOK, TOK), masked, F32)
        bias[h, 3] = jnp.full((TOK, TOK), tab[BUCKETS - 1, h], F32)

    loop(0, GH, tables)
    wait_bytes(w_s.at[mine], recv.at[1])
    push(w_s.at[mine], w_s.at[mine], send.at[5], core_recv.at[2], sib)
    wait_bytes(wa_all.at[z, x, y, c], own.at[0])
    wait_bytes(wa_all.at[pl.ds(0, 3), x, y, c], recv.at[2])
    for k in range(1, 4):
        push(
            wa_all.at[:, x, y, c], wa_all.at[:, x, y, c], send.at[6], recv.at[3],
            (z, (x + k) % 4, y, c),
        )
    wait_bytes(w_s.at[theirs], core_recv.at[2])
    picked = dot(picker[...], w_s[...], NN)
    gain = jnp.concatenate([picked[0:1, :384], picked[1:2, :384]], axis=1)
    gains[0:1, :] = gain
    gains[1:2, :] = jnp.concatenate([picked[2:3, :384], picked[3:4, :384]], axis=1)
    gains[2:8, :] = jnp.zeros((6, D), F32)
    kd[...] = picked[8:24, 384:512]
    qd[...] = picked[24:32, 384:512].T
    weight[...] = dot(select[...], w_s[...], NN).astype(BF)
    wait_bytes(tok_s, recv.at[0])
    for b in range(4):
        v = tok_s[b].astype(F32)
        normed[b * TOK : (b + 1) * TOK, :] = scale_rows(v, gain).astype(BF)
    qkv = dot(normed[...], weight[...], NN).astype(BF)
    q[...] = qkv[:, :GW]
    for b in range(4):
        kv[b] = qkv[b * TOK : (b + 1) * TOK, GW:]
    for k in range(1, 4):
        for b in range(4):
            push(
                kv.at[b], kv_s.at[block_cols(b, x)], send.at[7], kv_recv.at[4 - k],
                (z, (x + k) % 4, y, c),
            )
    for b in range(4):
        keep(kv.at[b], kv_s.at[block_cols(b, x)], kv_recv.at[0])
    wait_bytes(wa_all.at[:, pl.ds(0, 3), y, c], recv.at[3])
    for k in range(1, 4):
        push(
            wa_all.at[:, :, y, c], wa_all.at[:, :, y, c], send.at[8], recv.at[4],
            (z, x, (y + k) % 4, c),
        )
    for h in range(GH):
        head_cols = lax.broadcasted_iota(jnp.int32, (1, GW), 1) // HD == h
        qm[h] = jnp.where(head_cols, q[...] * 0.125, 0.0).astype(BF)
    for k in range(4):
        kx = (x + k) % 4
        if k == 0:
            for b in range(4):
                wait_bytes(kv_s.at[block_cols(b, kx)], kv_recv.at[0])
        else:
            wait_bytes(kv_s.at[pl.ds(0, 512)], kv_recv.at[k])
        for b in range(4):
            cols = block_cols(b, kx)
            v_s[cols, :] = kv_s[cols, GW:]
            for h in range(GH):
                s_s[h, b * TOK :, cols] = dot(qm[h, b * TOK :, :], kv_s[cols, :GW], NT)
    keep(kv_s, kv_out, own.at[1])
    wait_bytes(d_rows.at[mine], recv.at[5])
    push(d_rows.at[mine], d_rows.at[mine], send.at[12], core_recv.at[4], sib)
    wait_bytes(wa_all.at[:, :, pl.ds(0, 3), c], recv.at[4])
    push(wa_all.at[:, :, :, c], wa_all.at[:, :, :, c], send.at[10], core_recv.at[3], sib)

    def head(h):
        head_cols = lax.broadcasted_iota(jnp.int32, (1, GW), 1) // HD == h
        far = tab[BUCKETS - 1, h]
        for zq in range(4):
            rows = pl.ds(zq * TOK, TOK)
            docs = qd[:, zq : zq + 1]
            top = None
            for zk in range(zq + 1):
                for kx in range(4):
                    cols = pl.ds((zk * 4 + kx) * TOK, TOK)
                    s = s_s[h, rows, cols]
                    if zk < zq - 1:
                        s = s + far
                    else:
                        s = s + bias[h, table_kind(zq, zk, x, kx)]
                    kb = zk * 4 + kx
                    s = jnp.where(docs == kd[kb : kb + 1, :], s, masked)
                    s_s[h, rows, cols] = s
                    top = s if top is None else jnp.maximum(top, s)
            top = jnp.max(top, axis=1, keepdims=True)
            total = jnp.zeros((TOK, TOK), F32)
            for kb in range(4 * (zq + 1)):
                cols = pl.ds(kb * TOK, TOK)
                e = jnp.exp(s_s[h, rows, cols] - top)
                s_s[h, rows, cols] = e
                total = total + e
            inv = 1.0 / jnp.sum(total, axis=1, keepdims=True)
            for kb in range(4 * (zq + 1)):
                cols = pl.ds(kb * TOK, TOK)
                p_s[h, rows, cols] = (s_s[h, rows, cols] * inv).astype(BF)
            width = (zq + 1) * 512
            o = dot(p_s[h, rows, :width], v_s[:width, :], NN).astype(BF)

            @pl.when(h == 0)
            def _():
                part[rows, :] = o

            @pl.when(h > 0)
            def _():
                part[rows, :] = jnp.where(head_cols, o, part[rows, :])

    loop(0, GH, head)
    for k in range(1, 4):
        there = (z + k) % 4
        push(
            part.at[pl.ds(pl.multiple_of(there * TOK, TOK), TOK)], attn_all.at[z],
            send.at[11], recv.at[6], (there, x, y, c),
        )
    keep(part.at[pl.ds(pl.multiple_of(z * TOK, TOK), TOK)], attn_all.at[z], recv.at[6])
    keep(p_s, p_out, own.at[2])
    wait_bytes(attn_all, recv.at[6])
    wait_bytes(wa_all.at[:, :, :, 1 - c], core_recv.at[3])
    wait_bytes(d_rows.at[theirs], core_recv.at[4])
    wait_bytes(kv_s, own.at[1])
    wait_bytes(p_s, own.at[2])
    wait_bytes(wo, send.at[0])
    wait_bytes(tok_s.at[pl.ds(0, 3)], send.at[1])
    wait_bytes(xo, send.at[2])
    sent_to_chips(w_s, y, c, send.at[3])
    wait_bytes(wa_all.at[pl.ds(0, 3), x, y, c], send.at[4])
    wait_bytes(w_s.at[mine], send.at[5])
    wait_bytes(wa_all.at[:, pl.ds(0, 3), y, c], send.at[6])
    wait_bytes(kv_s.at[pl.ds(0, 1536)], send.at[7])
    wait_bytes(wa_all.at[:, :, pl.ds(0, 3), c], send.at[8])
    sent_to_chips(d_rows, y, c, send.at[9])
    wait_bytes(wa_all.at[:, :, :, c], send.at[10])
    wait_bytes(attn_all.at[pl.ds(0, 3)], send.at[11])
    wait_bytes(d_rows.at[mine], send.at[12])


def attn_forward(tab, tok, wmsg, wa, d_eo):
    probs = (GH, 512, 2048)
    vm = pltpu.VMEM
    return pl.pallas_call(
        attn_forward_kernel,
        out_shape=(
            jax.ShapeDtypeStruct((4, TOK, GW), BF),
            jax.ShapeDtypeStruct((512, GW), BF),
            jax.ShapeDtypeStruct(probs, BF),
            jax.ShapeDtypeStruct((2048, 2 * GW), BF),
            jax.ShapeDtypeStruct((4, 4, 4, 2, 8, D), BF),
            jax.ShapeDtypeStruct((1024, D), BF),
            jax.ShapeDtypeStruct((512, D), BF),
            jax.ShapeDtypeStruct((D, 3 * GW), BF),
            jax.ShapeDtypeStruct((512, GW), BF),
            jax.ShapeDtypeStruct((8, D), F32),
        ),
        in_specs=[SMEM, VMEM, VMEM, VMEM, VMEM],
        out_specs=(ANY, VMEM, ANY, ANY, ANY, ANY, VMEM, VMEM, VMEM, VMEM),
        scratch_shapes=[
            vm((4, 16, 3 * GW), BF), vm((4, 16, 3 * GW), BF), vm((1024, 3 * GW), BF),
            vm((4, TOK, D), BF), vm((D, 1024), BF), vm((32, 1024), BF),
            vm((TOK, 8), F32), vm((16, TOK), F32),
            vm((4, TOK, 2 * GW), BF), vm((2048, 2 * GW), BF), vm((2048, GW), BF),
            vm((GH, 512, GW), BF), vm((GH, 4, TOK, TOK), F32), vm(probs, F32), vm(probs, BF),
            vm((512, D), BF),
            DMA((13,)), DMA((7,)), DMA((4,)), DMA((5,)), DMA((3,)),
        ],
        compiler_params=pltpu.CompilerParams(
            collective_id=2, has_side_effects=True, vmem_limit_bytes=48 * 2**20
        ),
        name="attn_forward",
    )(tab, tok, wmsg, wa, d_eo)


def attn_backward_kernel(
    p, q, kv, d_attn, branch, weight, normed, attn_part, small, tok, gain, d_middle,
    input_grad, qkv_out, att_out, small_out,
    p_s, v_s, do_s, dm, qm, dp_s, ds_s, near, messages, parts, branch_all, dq, tab,
    d_qkv, n_part, normed_in, att_f, q_blk, q_sib, q_tot, q_in, a_blk, a_sib, a_tot, a_in,
    s_own, s_sib, s_tot, s_in, qkv_sum, att_sum, s_sum, send, recv, core_recv, own,
):
    z, x, y, c = place()
    sib = (z, x, y, 1 - c)
    p16 = x * 4 + y
    p32 = p16 * 2 + c
    me = z * 32 + p32
    source = me // 4

    def peer(i):
        return z, (x + i // 4) % 4, (y + i % 4) % 4, c

    keep(p, p_s, own.at[0])
    loop(1, 16, lambda i: signal(peer(i)))
    for k in range(1, 4):
        signal(((z + k) % 4, x, y, c))
    signal(sib)

    def greet(k):
        @pl.when(jnp.logical_not((k == z) & (source == p32)))
        def _():
            signal((k, source // 8, (source // 2) % 4, source % 2))

    loop(0, 4, greet)
    v_s[...] = kv[:, GW:]
    for h in range(GH):
        head_cols = lax.broadcasted_iota(jnp.int32, (1, GW), 1) // HD == h
        qm[h] = jnp.where(head_cols, q[...] * 0.125, 0.0).astype(BF)
    arrive(15 + 3 + 1 + 4 - jnp.where(source == p32, 1, 0))
    for k in range(1, 4):
        there = (z + k) % 4
        push(d_attn.at[there], do_s.at[z], send.at[0], recv.at[0], (there, x, y, c))
    keep(d_attn.at[z], do_s.at[z], recv.at[0])
    z_rows = pl.ds(pl.multiple_of(z * TOK, TOK), TOK)
    for k in range(1, 4):
        push(branch, branch_all.at[z_rows], send.at[1], recv.at[1], ((z + k) % 4, x, y, c))
    keep(branch, branch_all.at[z_rows], recv.at[1])
    wait_bytes(do_s, recv.at[0])
    for h in range(GH):
        head_cols = lax.broadcasted_iota(jnp.int32, (1, GW), 1) // HD == h
        for b in range(4):
            dm[h, b * TOK : (b + 1) * TOK, :] = jnp.where(head_cols, do_s[b], 0.0).astype(BF)
    wait_bytes(p_s, own.at[0])

    def key_sums(left, right, m, pair):
        for k in (1, 2, 3, 0):
            kx = (x + k) % 4
            for b in (2 * pair, 2 * pair + 1):
                cols = block_cols(b, kx)
                total = None
                for h in range(GH):
                    one = dot(left[h, b * TOK :, cols], right[h, b * TOK :, :], TN)
                    total = one if total is None else total + one
                side = GW * (b % 2)
                messages[k, m, :, side : side + GW] = total.astype(BF)
            if k:
                push(messages.at[k, m], parts.at[x, m], send.at[2], recv.at[2], (z, kx, y, c))
            else:
                keep(messages.at[k, m], parts.at[x, m], recv.at[2])

    key_sums(p_s, dm, 0, 0)
    key_sums(p_s, dm, 1, 1)
    near[...] = jnp.zeros_like(near)

    def score_grads(zq):
        rows = pl.ds(zq * TOK, TOK)
        width = (zq + 1) * 512

        def head(h):
            head_cols = lax.broadcasted_iota(jnp.int32, (1, GW), 1) // HD == h
            dp_s[:, :width] = dot(dm[h, rows, :], v_s[:width, :], NT)
            acc = jnp.zeros((TOK, TOK), F32)
            for kb in range(4 * (zq + 1)):
                cols = pl.ds(kb * TOK, TOK)
                acc = acc + p_s[h, rows, cols].astype(F32) * dp_s[:, cols]
            delta = jnp.sum(acc, axis=1, keepdims=True)
            far = jnp.zeros((TOK, TOK), F32)
            for zk in range(zq + 1):
                for kx in range(4):
                    cols = pl.ds((zk * 4 + kx) * TOK, TOK)
                    ds = (p_s[h, rows, cols].astype(F32) * (dp_s[:, cols] - delta)).astype(BF)
                    ds_s[h, rows, cols] = ds
                    if zk < zq - 1:
                        far = far + ds.astype(F32)
                    else:
                        near[h, table_kind(zq, zk, x, kx)] += ds.astype(F32)
            if zq > 1:
                near[h, 3] += far
            o = (dot(ds_s[h, rows, :width], kv[:width, :GW], NN) * 0.125).astype(BF)

            @pl.when(h == 0)
            def _():
                dq[rows, :] = o

            @pl.when(h > 0)
            def _():
                dq[rows, :] = jnp.where(head_cols, o, dq[rows, :])

        loop(0, GH, head)

    score_grads(3)
    score_grads(2)
    key_sums(ds_s, qm, 3, 1)
    score_grads(1)
    score_grads(0)
    key_sums(ds_s, qm, 2, 0)

    def bucket_sums(h):
        for dist in range(2):
            n = near_distance(dist)
            held = near[h, 1 + dist]
            bounds = [-(10**6)] + bucket_edges + [10**6]
            for b in range(BUCKETS):
                low, high = bounds[b], bounds[b + 1]
                if high <= dist * TOK - TOK + 1 or low > dist * TOK + TOK - 1:
                    if dist == 0:
                        tab[h, b : b + 1, :] = jnp.zeros((1, TOK), F32)
                    continue
                inside = jnp.sum(
                    jnp.where((n >= low) & (n < high), held, 0.0), axis=0, keepdims=True
                )
                if dist == 0:
                    tab[h, b : b + 1, :] = inside
                else:
                    tab[h, b : b + 1, :] += inside
        tab[h, BUCKETS - 1 :, :] += jnp.sum(near[h, 3], axis=0, keepdims=True)

    loop(0, GH, bucket_sums)

    wait_bytes(branch_all, recv.at[1])
    att_f[0:GW, :] = dot(attn_part[...], branch_all[...], TN)
    att_f[GW:, :] = jnp.zeros((8, D), F32)
    for j in range(32):
        a_blk[j // 2, j % 2] = att_f[6 * j : 6 * j + 8, :].astype(BF)
    push(a_blk.at[:, 1 - c], a_sib, send.at[4], core_recv.at[1], sib)
    s_own[...] = small[...]
    for h in range(GH):
        s_own[2:3, BUCKETS * h : BUCKETS * (h + 1)] = jnp.sum(tab[h].T, axis=0, keepdims=True)

    wait_bytes(a_sib, core_recv.at[1])

    def att_blocks(i):
        there = peer(i)
        j = there[1] * 4 + there[2]
        a_tot[j] = (a_blk[j, c].astype(F32) + a_sib[j].astype(F32)).astype(BF)
        push(a_tot.at[j], a_in.at[p16], send.at[6], recv.at[4], there)

    loop(1, 16, att_blocks)
    a_tot[p16] = (a_blk[p16, c].astype(F32) + a_sib[p16].astype(F32)).astype(BF)
    keep(a_tot.at[p16], a_in.at[p16], recv.at[4])

    wait_bytes(parts, recv.at[2])
    d_qkv[:, :GW] = dq[...]
    for b in range(4):
        rows = slice(b * TOK, (b + 1) * TOK)
        side = GW * (b % 2)
        for m, at in ((2 + b // 2, GW), (b // 2, 2 * GW)):
            total = parts[0, m, :, side : side + GW].astype(F32)
            for k in range(1, 4):
                total = total + parts[k, m, :, side : side + GW].astype(F32)
            d_qkv[rows, at : at + GW] = total.astype(BF)
    d_normed = dot(d_qkv[...], weight[...], NT)
    n_part[...] = d_normed.astype(BF)
    for k in range(1, 4):
        there = (z + k) % 4
        push(
            n_part.at[pl.ds(pl.multiple_of(there * TOK, TOK), TOK)], normed_in.at[z],
            send.at[3], recv.at[3], (there, x, y, c),
        )
    keep(n_part.at[z_rows], normed_in.at[z], recv.at[3])
    along = jnp.sum(d_normed * normed[...].astype(F32), axis=0, keepdims=True)
    s_own[0:1, :] = along / gain[...]
    push(s_own, s_sib, send.at[8], core_recv.at[2], sib)
    total = dot(normed[...], d_qkv[...], TN)
    for j in range(32):
        q_blk[j // 2, j % 2] = total[24 * j : 24 * j + 24].astype(BF)
    push(q_blk.at[:, 1 - c], q_sib, send.at[5], core_recv.at[0], sib)
    wait_bytes(s_sib, core_recv.at[2])
    s_tot[...] = s_own[...] + s_sib[...]
    loop(1, 16, lambda i: push(s_tot, s_in.at[p16], send.at[9], recv.at[6], peer(i)))
    keep(s_tot, s_in.at[p16], recv.at[6])
    wait_bytes(q_sib, core_recv.at[0])

    def qkv_blocks(i):
        there = peer(i)
        j = there[1] * 4 + there[2]
        q_tot[j] = (q_blk[j, c].astype(F32) + q_sib[j].astype(F32)).astype(BF)
        push(q_tot.at[j], q_in.at[p16], send.at[7], recv.at[5], there)

    loop(1, 16, qkv_blocks)
    q_tot[p16] = (q_blk[p16, c].astype(F32) + q_sib[p16].astype(F32)).astype(BF)
    keep(q_tot.at[p16], q_in.at[p16], recv.at[5])

    wait_bytes(s_in, recv.at[6])
    s_total = s_in[0]
    for k in range(1, 16):
        s_total = s_total + s_in[k]
    s_sum[...] = s_total
    for k in range(1, 4):
        push(s_sum, small_out.at[z], send.at[11], recv.at[8], ((z + k) % 4, x, y, c))
    keep(s_sum, small_out.at[z], recv.at[8])
    wait_bytes(q_in, recv.at[5])
    q_total = q_in[0].astype(F32)
    for k in range(1, 16):
        q_total = q_total + q_in[k].astype(F32)
    for k in range(4):
        qkv_sum[k, 0:6, :] = q_total[6 * k : 6 * k + 6]
        qkv_sum[k, 6:8, :] = jnp.zeros((2, 3 * GW), F32)

    def final(k):
        d = 4 * p32 + k

        @pl.when(d != me)
        def _():
            push(qkv_sum.at[k], qkv_out.at[z], send.at[10], recv.at[7], device_of(d))

        @pl.when(d == me)
        def _():
            keep(qkv_sum.at[k], qkv_out.at[z], recv.at[7])

    loop(0, 4, final)
    wait_bytes(a_in, recv.at[4])
    a_total = a_in[0].astype(F32)
    for k in range(1, 16):
        a_total = a_total + a_in[k].astype(F32)
    att_sum[...] = a_total
    keep(att_sum, att_out, own.at[1])
    wait_bytes(normed_in, recv.at[3])
    d_normed = normed_in[0].astype(F32)
    for k in range(1, 4):
        d_normed = d_normed + normed_in[k].astype(F32)
    v = tok[...].astype(F32)
    r = lax.rsqrt(jnp.mean(v * v, axis=1, keepdims=True) + norm_eps)
    unit = v * r
    d_unit = d_normed * gain[...]
    d_in = r * (d_unit - unit * jnp.mean(d_unit * unit, axis=1, keepdims=True))
    input_grad[...] = (d_middle[...] + d_in).astype(BF)

    wait_bytes(att_sum, own.at[1])
    wait_bytes(qkv_out, recv.at[7])
    wait_bytes(small_out, recv.at[8])
    wait_bytes(do_s.at[pl.ds(0, 3)], send.at[0])
    wait_bytes(branch_all.at[pl.ds(0, 3 * TOK)], send.at[1])
    wait_bytes(parts.at[pl.ds(0, 3)], send.at[2])
    wait_bytes(normed_in.at[pl.ds(0, 3)], send.at[3])
    wait_bytes(a_sib, send.at[4])
    wait_bytes(q_sib, send.at[5])
    wait_bytes(a_in.at[pl.ds(0, 15)], send.at[6])
    wait_bytes(q_in.at[pl.ds(0, 15)], send.at[7])
    wait_bytes(s_own, send.at[8])
    wait_bytes(s_in.at[pl.ds(0, 15)], send.at[9])

    def sent(k):
        @pl.when(4 * p32 + k != me)
        def _():
            wait_bytes(qkv_sum.at[0], send.at[10])

    loop(0, 4, sent)
    wait_bytes(small_out.at[pl.ds(0, 3)], send.at[11])


def attn_backward(p, *rest):
    probs = (GH, 512, 2048)
    vm = pltpu.VMEM
    return pl.pallas_call(
        attn_backward_kernel,
        out_shape=(
            jax.ShapeDtypeStruct((TOK, D), BF),
            jax.ShapeDtypeStruct((4, 8, 3 * GW), F32),
            jax.ShapeDtypeStruct((8, D), F32),
            jax.ShapeDtypeStruct((4, 8, D), F32),
        ),
        in_specs=[ANY] + [VMEM] * len(rest),
        out_specs=(VMEM, ANY, ANY, ANY),
        scratch_shapes=[
            vm(probs, BF), vm((2048, GW), BF), vm((4, TOK, GW), BF), vm((GH, 512, GW), BF),
            vm((GH, 512, GW), BF), vm((TOK, 2048), F32), vm(probs, BF), vm((GH, 4, TOK, TOK), F32),
            vm((4, 4, TOK, 2 * GW), BF), vm((4, 4, TOK, 2 * GW), BF), vm((512, D), BF),
            vm((512, GW), BF), vm((GH, BUCKETS, TOK), F32),
            vm((512, 3 * GW), BF), vm((512, D), BF), vm((4, TOK, D), BF), vm((GW + 8, D), F32),
            vm((16, 2, 24, 3 * GW), BF), vm((16, 24, 3 * GW), BF),
            vm((16, 24, 3 * GW), BF), vm((16, 24, 3 * GW), BF),
            vm((16, 2, 8, D), BF), vm((16, 8, D), BF), vm((16, 8, D), BF), vm((16, 8, D), BF),
            vm((8, D), F32), vm((8, D), F32), vm((8, D), F32), vm((16, 8, D), F32),
            vm((4, 8, 3 * GW), F32), vm((8, D), F32), vm((8, D), F32),
            DMA((12,)), DMA((9,)), DMA((3,)), DMA((2,)),
        ],
        compiler_params=pltpu.CompilerParams(
            collective_id=3, has_side_effects=True, vmem_limit_bytes=52 * 2**20
        ),
        name="attn_backward",
    )(p, *rest)


def per_device(
    tokens,
    gain_attn,
    w_qkv,
    w_attn_out,
    rel_table,
    gain_moe,
    w_in,
    w_out,
    expert_ids,
    gate_values,
    doc_ids,
    cotangent,
):
    z, x, y, c = place()
    experts = 64
    capacity = 8
    slots = 2 * experts * capacity
    own_tokens = tokens.reshape(TOK, D)
    grad_bf = cotangent.reshape(TOK, D)
    grad_out = grad_bf.astype(F32)

    routes = expert_ids.reshape(TOK, 2)
    gates = gate_values.reshape(TOK, 2)
    expert_list = jnp.arange(experts, dtype=jnp.int32)[None, :]
    marks = jnp.concatenate(
        [(routes[:, :1] == expert_list), (routes[:, 1:] == expert_list)], axis=1
    ).astype(BF)
    lower = jnp.tril(jnp.ones((TOK, TOK), BF), -1)
    earlier = dot(lower, marks, NN)
    marks = marks.astype(F32)
    firsts = jnp.sum(marks[:, :experts], axis=0, keepdims=True)
    rank_0 = jnp.sum(earlier[:, :experts] * marks[:, :experts], axis=1)
    rank_1 = jnp.sum((earlier[:, experts:] + firsts) * marks[:, experts:], axis=1)
    blocks = (routes % 2) * 32 + (routes // 4) * 2 + (routes % 4) // 2
    places = blocks * 16 + c * capacity + jnp.stack([rank_0, rank_1], axis=1).astype(jnp.int32)
    slot_ids = jnp.arange(slots, dtype=jnp.int32)[None, :]
    picks = jnp.concatenate(
        [(places[:, :1] == slot_ids), (places[:, 1:] == slot_ids)], axis=0
    ).astype(BF)
    gated = jnp.concatenate([gates[:, :1] * grad_out, gates[:, 1:] * grad_out], axis=0).astype(BF)
    d_eo = dot(picks, gated, TN).astype(BF)

    slab = w_qkv.reshape(6, 3, GROUPS, GW).transpose(2, 0, 1, 3).reshape(GROUPS, 6, 3 * GW)
    place_in = chip_of(z, x, y) * 2 + c
    among = (place_in % 64) * 6
    row_one = lax.dynamic_update_slice(jnp.zeros((3 * GW,), BF), gain_attn, (among,))
    row_one = lax.dynamic_update_slice(row_one, doc_ids.reshape(TOK).astype(BF), (384,))
    row_two = lax.dynamic_update_slice(jnp.zeros((3 * GW,), BF), gain_moe, (among,))
    note_one = jnp.broadcast_to(row_one, (GROUPS, 1, 3 * GW))
    note_two = jnp.broadcast_to(row_two, (GROUPS, 1, 3 * GW))
    nothing = jnp.zeros((GROUPS, 6, 3 * GW), BF)
    none = nothing[:, :1]
    message = jnp.where(
        c == 0,
        jnp.concatenate([slab, nothing, note_one, none, note_two, none], axis=1),
        jnp.concatenate([nothing, slab, none, note_one, none, note_two], axis=1),
    )
    out_slab = jnp.concatenate([w_attn_out, jnp.zeros((2, D), BF)], axis=0)
    table = lax.dynamic_slice(rel_table, (0, z * GH), (BUCKETS, GH)).astype(F32)
    (
        attn, attn_part, probs, kv_all, out_weights, d_eo_all, normed, weight, queries, gain_rows,
    ) = attn_forward(table, own_tokens, message, out_slab, d_eo)
    gain_one, gain_two = gain_rows[0], gain_rows[1]
    attn = attn.transpose(1, 0, 2).reshape(TOK, D)
    attention_weight = out_weights[:, :, :, :, :6, :].reshape(D, D)

    inputs = own_tokens.astype(F32)
    middle = inputs + dot(attn, attention_weight, NN)
    moe_float, norm_two_back = jax.vjp(scale_rows, middle, gain_two)
    moe_in = moe_float.astype(BF)
    send_rows = dot(picks, jnp.concatenate([moe_in, moe_in], axis=0), TN).astype(BF)
    home, expert_out, expert_in_grad, expert_out_grad = run_experts(
        send_rows, d_eo_all, w_in[0], w_out[0]
    )
    home_picked = dot(picks, home, NN)
    moe_in_grad = home_picked[:TOK] + home_picked[TOK:]
    middle_part, gain_two_grad = norm_two_back(moe_in_grad)
    middle_grad = grad_out + middle_part
    branch = middle_grad.astype(BF)
    d_attn = dot(branch, attention_weight, NT).astype(BF)
    d_attn = d_attn.reshape(TOK, GROUPS, GW).transpose(1, 0, 2)

    small = jnp.concatenate(
        [jnp.zeros((1, D), F32), gain_two_grad.reshape(1, D), jnp.zeros((6, D), F32)]
    )
    input_grad, qkv_sum, att_sum, small_sum = attn_backward(
        probs, queries, kv_all, d_attn, branch, weight, normed, attn_part, small, own_tokens,
        gain_one.reshape(1, D), middle_grad,
    )

    picked = dot(picks, expert_out, NN).reshape(2, TOK, D)
    block_out = middle + gates[:, :1] * picked[0] + gates[:, 1:] * picked[1]
    gate_grad = jnp.sum(picked * grad_out[None], axis=2).T

    qkv_grad = qkv_sum[:, :6, :].reshape(GROUPS, 6, 3, GW).transpose(1, 2, 0, 3).reshape(6, 3 * D)
    attn_out_grad = att_sum[:6]
    gains = lax.dynamic_slice(jnp.sum(small_sum[:, :2, :], axis=0), (0, place_in * 6), (2, 6))
    table_grad = small_sum[:, 2, : GH * BUCKETS].reshape(GROUPS * GH, BUCKETS).T
    return (
        block_out.reshape(1, TOK, D).astype(BF),
        input_grad.reshape(1, TOK, D),
        gate_grad.reshape(1, TOK, 2),
        gains[0],
        qkv_grad,
        attn_out_grad,
        table_grad,
        gains[1],
        expert_in_grad[None],
        expert_out_grad[None],
    )


def solution(mesh):
    torus = Mesh(mesh.devices.reshape(4, 4, 4, 2), AXES)
    in_specs = (
        P(EXP, CTX, None),
        P(AXES),
        P(AXES, None),
        P(AXES, None),
        P(),
        P(AXES),
        P(AXES, None, None),
        P(AXES, None, None),
        P(EXP, CTX, None),
        P(EXP, CTX, None),
        P(EXP, CTX),
        P(EXP, CTX, None),
    )
    out_specs = (
        P(EXP, CTX, None),
        P(EXP, CTX, None),
        P(EXP, CTX, None),
        P(AXES),
        P(AXES, None),
        P(AXES, None),
        P(),
        P(AXES),
        P(AXES, None, None),
        P(AXES, None, None),
    )
    return jax.shard_map(
        per_device, mesh=torus, in_specs=in_specs, out_specs=out_specs, check_vma=False
    )
```

```python
import functools

import jax
import jax.numpy as jnp
import numpy as np
from jax import lax
from jax.experimental import pallas as pl
from jax.experimental.pallas import tpu as pltpu
from jax.sharding import Mesh
from jax.sharding import PartitionSpec as P

D = 768
H = 12
HD = 64
BUCKETS = 32
GROUPS = 4
GH = H // GROUPS
GW = GH * HD
TOK = 128
CTX = ("ctx_0", "ctx_1")
EXP = ("exp_0", "exp_1")
AXES = ("ctx_0", "ctx_1", "exp_0", "exp_1")
MESH = pl.DeviceIdType.MESH
ANY = pl.BlockSpec(memory_space=pl.ANY)
BF = jnp.bfloat16
F32 = jnp.float32

norm_eps = 1e-06
bucket_edges = [int(e) for e in np.concatenate(
    [np.arange(1, 17), np.ceil(16.0 * 8.0 ** (np.arange(1, 16) / 16.0))]
).astype(np.int32)]
masked = -1e30


def scale_rows(values, gain):
    return values * lax.rsqrt(jnp.mean(values * values, axis=-1, keepdims=True) + norm_eps) * gain


def place():
    return tuple(lax.axis_index(a) for a in AXES)


def chip_of(z, x, y):
    return (z * 4 + x) * 4 + y


def chip_peer(i, z, x, y):
    return (z + i // 16) % 4, (x + (i // 4) % 4) % 4, (y + i % 4) % 4


def loop(first, last, body):
    lax.fori_loop(first, last, lambda i, carry: (body(i), carry)[1], 0)


def signal(device):
    pl.semaphore_signal(
        pltpu.get_barrier_semaphore(), inc=1, device_id=device, device_id_type=MESH
    )


def arrive(count):
    pl.semaphore_wait(pltpu.get_barrier_semaphore(), count)


def push(src, dst, send, recv, device):
    pltpu.make_async_remote_copy(
        src_ref=src, dst_ref=dst, send_sem=send, recv_sem=recv, device_id=device, device_id_type=MESH
    ).start()


def keep(src, dst, sem):
    pltpu.make_async_copy(src, dst, sem).start()


def wait_bytes(ref, sem):
    pltpu.make_async_copy(ref, ref, sem).wait()


def comm_call(kernel, outs, scratch, collective_id, name):
    return pl.pallas_call(
        kernel,
        out_shape=outs,
        in_specs=None,
        out_specs=jax.tree.map(lambda _: ANY, outs),
        scratch_shapes=scratch,
        compiler_params=pltpu.CompilerParams(
            collective_id=collective_id, has_side_effects=True, vmem_limit_bytes=32 * 2**20
        ),
        name=name,
    )


def run_comm(kernel, args, outs, scratch, collective_id, name):
    return pl.pallas_call(
        kernel,
        out_shape=outs,
        in_specs=[ANY] * len(args),
        out_specs=jax.tree.map(lambda _: ANY, outs),
        scratch_shapes=scratch,
        compiler_params=pltpu.CompilerParams(
            collective_id=collective_id, has_side_effects=True, vmem_limit_bytes=32 * 2**20
        ),
        name=name,
    )(*args)


DMA = pltpu.SemaphoreType.DMA


def half_peer(i, z, x, y, c):
    return (z + i // 8) % 4, (x + (i // 2) % 4) % 4, c + 2 * ((y // 2 + i % 2) % 2), y % 2


def block_of(z, x, y):
    return pl.multiple_of((y % 2) * 512 + ((z * 4 + x) * 2 + y // 2) * 16, 16)


def greet_chips(z, x, y, c):
    loop(1, 32, lambda i: signal(half_peer(i, z, x, y, c)))

    @pl.when(y % 2 != c)
    def _():
        signal(half_peer(0, z, x, y, c))

    signal((z, x, y, 1 - c))
    return 32 + jnp.where(y % 2 == c, 0, 1)


def to_chips(z, x, y, c, source, target, send, recv):
    def one(i):
        there = half_peer(i, z, x, y, c)
        push(source(there), target, send, recv, there)

    loop(1, 32, one)
    first = half_peer(0, z, x, y, c)

    @pl.when(y % 2 == c)
    def _():
        keep(source(first), target, recv)

    @pl.when(y % 2 != c)
    def _():
        push(source(first), target, send, recv, first)


def sent_to_chips(rows, y, c, send):
    wait_bytes(rows.at[pl.ds(0, 496)], send)

    @pl.when(y % 2 != c)
    def _():
        wait_bytes(rows.at[pl.ds(0, 16)], send)


FH = 1536
WIDE = 256


def experts_kernel(
    attn, w_proj, tok, gains, picks, d_rows, w_in, w_out,
    home_in, home_out, g_in, g_out, middle,
    x16, xo, rows, dv, w1, w2, dh, hidden, dact, in_h, out_h, in_o, out_o, stage_out, stage_in,
    send, recv, core_recv, own, staged,
):
    z, x, y, c = place()
    sib = (z, x, y, 1 - c)
    at_mine = pl.multiple_of(c * 512, 512)
    at_theirs = pl.multiple_of((1 - c) * 512, 512)
    mine, theirs = pl.ds(at_mine, 512), pl.ds(at_theirs, 512)
    me = block_of(z, x, y)
    keep(d_rows, dv, own.at[1])
    keep(w_out, w2, own.at[2])
    keep(w_in, w1, own.at[3])
    expected = greet_chips(z, x, y, c)
    total = tok[...].astype(F32)
    for k in range(GROUPS):
        total = total + dot(attn[k], w_proj[GW * k : GW * (k + 1), :], NN)
    middle[...] = total
    moe_in = scale_rows(total, gains[1:2, :]).astype(BF)
    for n in range(0, 1024, WIDE):
        x16[n : n + WIDE, :] = (
            dot(picks[:TOK, n : n + WIDE], moe_in, TN) + dot(picks[TOK:, n : n + WIDE], moe_in, TN)
        ).astype(BF)
    arrive(expected)
    push(x16.at[theirs], xo, send.at[0], core_recv.at[0], sib)
    wait_bytes(xo, core_recv.at[0])
    xo[...] = xo[...] + x16[mine, :]
    to_chips(
        z, x, y, c,
        lambda there: xo.at[pl.ds(pl.multiple_of(block_of(*there[:3]) - c * 512, 16), 16)],
        rows.at[pl.ds(me, 16)], send.at[1], recv.at[0],
    )
    wait_bytes(dv, own.at[1])
    wait_bytes(w2, own.at[2])

    def hidden_grads(n):
        cols = pl.ds(pl.multiple_of(n * WIDE, WIDE), WIDE)
        dh[:, cols] = dot(dv[...], w2[cols, :], NT)

    loop(0, FH // WIDE, hidden_grads)
    wait_bytes(w1, own.at[3])
    wait_bytes(rows.at[mine], recv.at[0])
    push(rows.at[mine], rows.at[mine], send.at[2], core_recv.at[1], sib)

    def activate(at):
        part = pl.ds(at, 512)

        def one(n):
            cols = pl.ds(pl.multiple_of(n * WIDE, WIDE), WIDE)
            a = dot(rows[part, :], w1[:, cols], NN)
            square = a * a
            t = jnp.tanh(0.7978845608028654 * (a + 0.044715 * (square * a)))
            cdf = 0.5 * (1.0 + t)
            hidden[part, cols] = (a * cdf).astype(BF)
            slope = cdf + 0.5 * a * (1.0 - t * t) * (
                0.7978845608028654 * (1.0 + 0.134145 * square)
            )
            dact[part, cols] = (slope * dh[part, cols]).astype(BF)

        loop(0, FH // WIDE, one)

    def in_half(at):
        part = pl.ds(at, 512)

        def one(n):
            cols = pl.ds(pl.multiple_of(n * WIDE, WIDE), WIDE)
            in_h[part, cols] = dot(dact[part, :], w1[cols, :], NT).astype(BF)

        loop(0, D // WIDE, one)

    def out_half(at):
        part = pl.ds(at, 512)

        def one(n):
            cols = pl.ds(pl.multiple_of(n * WIDE, WIDE), WIDE)
            out_h[part, cols] = dot(hidden[part, :], w2[:, cols], NN).astype(BF)

        loop(0, D // WIDE, one)

    activate(at_mine)
    wait_bytes(rows.at[theirs], core_recv.at[1])
    activate(at_theirs)
    in_half(at_theirs)
    push(in_h.at[theirs], in_o, send.at[3], core_recv.at[2], sib)
    in_half(at_mine)
    wait_bytes(in_o, core_recv.at[2])
    in_o[...] = (in_o[...].astype(F32) + in_h[mine, :].astype(F32)).astype(BF)
    to_chips(
        z, x, y, c,
        lambda there: in_o.at[pl.ds(pl.multiple_of(block_of(*there[:3]) - c * 512, 16), 16)],
        home_in.at[pl.ds(me, 16)], send.at[4], recv.at[1],
    )
    out_half(at_theirs)
    push(out_h.at[theirs], out_o, send.at[5], core_recv.at[3], sib)
    out_half(at_mine)
    wait_bytes(out_o, core_recv.at[3])
    out_o[...] = (out_o[...].astype(F32) + out_h[mine, :].astype(F32)).astype(BF)
    to_chips(
        z, x, y, c,
        lambda there: out_o.at[pl.ds(pl.multiple_of(block_of(*there[:3]) - c * 512, 16), 16)],
        home_out.at[pl.ds(me, 16)], send.at[6], recv.at[2],
    )

    def out_grads(n):
        cols = pl.ds(pl.multiple_of(n * WIDE, WIDE), WIDE)
        slot = n % 2

        @pl.when(n >= 2)
        def _():
            wait_bytes(stage_out.at[slot], staged.at[slot])

        stage_out[slot] = dot(hidden[:, cols], dv[...], TN)
        keep(stage_out.at[slot], g_out.at[cols], staged.at[slot])

    loop(0, FH // WIDE, out_grads)
    wait_bytes(home_in.at[mine], recv.at[1])
    push(home_in.at[mine], home_in.at[mine], send.at[7], core_recv.at[4], sib)

    def in_grads(n):
        cols = pl.ds(pl.multiple_of(n * WIDE, WIDE), WIDE)
        slot = n % 2

        @pl.when(n >= 2)
        def _():
            wait_bytes(stage_in.at[slot], staged.at[2 + slot])

        stage_in[slot] = dot(rows[:, cols], dact[...], TN)
        keep(stage_in.at[slot], g_in.at[cols], staged.at[2 + slot])

    loop(0, D // WIDE, in_grads)
    wait_bytes(home_out.at[mine], recv.at[2])
    push(home_out.at[mine], home_out.at[mine], send.at[8], core_recv.at[5], sib)
    for slot in range(2):
        wait_bytes(stage_out.at[slot], staged.at[slot])
        wait_bytes(stage_in.at[slot], staged.at[2 + slot])
    wait_bytes(xo, send.at[0])
    sent_to_chips(rows, y, c, send.at[1])
    wait_bytes(rows.at[mine], send.at[2])
    wait_bytes(in_o, send.at[3])
    sent_to_chips(home_in, y, c, send.at[4])
    wait_bytes(out_o, send.at[5])
    sent_to_chips(home_out, y, c, send.at[6])
    wait_bytes(home_in.at[theirs], core_recv.at[4])
    wait_bytes(home_out.at[theirs], core_recv.at[5])
    wait_bytes(home_in.at[mine], send.at[7])
    wait_bytes(home_out.at[mine], send.at[8])


def run_experts(*args):
    whole_rows = pltpu.VMEM((1024, D), BF)
    half_rows = pltpu.VMEM((512, D), BF)
    hid = pltpu.VMEM((1024, FH), BF)
    return pl.pallas_call(
        experts_kernel,
        out_shape=(
            jax.ShapeDtypeStruct((1024, D), BF),
            jax.ShapeDtypeStruct((1024, D), BF),
            jax.ShapeDtypeStruct((D, FH), F32),
            jax.ShapeDtypeStruct((FH, D), F32),
            jax.ShapeDtypeStruct((TOK, D), F32),
        ),
        in_specs=[pl.BlockSpec(memory_space=pltpu.VMEM)] * 5 + [ANY] * 3,
        out_specs=(ANY,) * 4 + (pl.BlockSpec(memory_space=pltpu.VMEM),),
        scratch_shapes=[
            whole_rows, half_rows, whole_rows, whole_rows,
            pltpu.VMEM((D, FH), BF), pltpu.VMEM((FH, D), BF), pltpu.VMEM((1024, FH), F32),
            hid, hid, whole_rows, whole_rows, half_rows, half_rows,
            pltpu.VMEM((2, WIDE, D), F32), pltpu.VMEM((2, WIDE, FH), F32),
            DMA((9,)), DMA((3,)), DMA((6,)), DMA((4,)), DMA((4,)),
        ],
        compiler_params=pltpu.CompilerParams(
            collective_id=1, has_side_effects=True, vmem_limit_bytes=48 * 2**20
        ),
        name="experts",
    )(*args)


def device_of(d):
    return d // 32, (d // 8) % 4, (d // 2) % 4, d % 2


NT = (((1,), (1,)), ((), ()))
NN = (((1,), (0,)), ((), ()))
TN = (((0,), (0,)), ((), ()))


def dot(a, b, dims):
    return lax.dot_general(a, b, dims, preferred_element_type=F32)


def near_distance(dist):
    a = lax.broadcasted_iota(jnp.int32, (TOK, TOK), 0)
    b = lax.broadcasted_iota(jnp.int32, (TOK, TOK), 1)
    return dist * TOK + a - b


def table_kind(zq, zk, x, kx):
    return jnp.clip((zq - zk) * 4 + x - kx + 1, 0, 3)


def block_cols(zk, kx):
    return pl.ds(pl.multiple_of((zk * 4 + kx) * TOK, TOK), TOK)


VMEM = pl.BlockSpec(memory_space=pltpu.VMEM)
SMEM = pl.BlockSpec(memory_space=pltpu.SMEM)


def attn_forward_kernel(
    tab, tok, wmsg, wa, d_eo,
    attn_all, part, p_out, kv_out, wa_all, d_rows, normed, weight, q, gains,
    wm, wo, w_s, tok_s, select, picker, qd, kd,
    kv, kv_s, v_s, qm, bias, s_s, p_s, xo,
    send, recv, kv_recv, core_recv, own,
):
    z, x, y, c = place()
    sib = (z, x, y, 1 - c)
    mine = pl.ds(pl.multiple_of(c * 512, 512), 512)
    theirs = pl.ds(pl.multiple_of((1 - c) * 512, 512), 512)
    me = block_of(z, x, y)
    keep(wa, wa_all.at[z, x, y, c], own.at[0])
    expected = greet_chips(z, x, y, c)
    for k in range(1, 4):
        signal(((z + k) % 4, x, y, c))
        signal((z, (x + k) % 4, y, c))
        signal((z, x, (y + k) % 4, c))
    arrive(expected + 9)
    push(wmsg, wo, send.at[0], core_recv.at[0], sib)
    for k in range(1, 4):
        push(tok, tok_s.at[z], send.at[1], recv.at[0], ((z + k) % 4, x, y, c))
    keep(tok, tok_s.at[z], recv.at[0])
    push(d_eo.at[theirs], xo, send.at[2], core_recv.at[1], sib)
    wait_bytes(wo, core_recv.at[0])
    wm[...] = wmsg[...] + wo[...]
    to_chips(
        z, x, y, c, lambda there: wm.at[there[0]], w_s.at[pl.ds(me, 16)], send.at[3], recv.at[1]
    )
    for k in range(1, 4):
        push(wa, wa_all.at[z, x, y, c], send.at[4], recv.at[2], ((z + k) % 4, x, y, c))

    row = lax.broadcasted_iota(jnp.int32, (1, 1024), 1)
    r, half, at = row & 15, row >> 9, (row >> 4) & 31
    row_z, row_x, row_y = at >> 3, (at >> 1) & 3, (at & 1) * 2 + half
    feature = jnp.where(r < 12, (row_z * 16 + row_x * 4 + row_y) * 12 + r, -1)
    select[...] = jnp.where(
        lax.broadcasted_iota(jnp.int32, (D, 1024), 0) == feature, 1.0, 0.0
    ).astype(BF)
    j = lax.broadcasted_iota(jnp.int32, (32, 1024), 0)
    gain_rows = (j < 4) & (r >> 1 == 6 + (j >> 1)) & (row_z >> 1 == j & 1)
    notes = (r == 12 + c) & (row_y == y)
    key_rows = (j >= 8) & (row_z * 4 + row_x == j - 8)
    query_rows = (j >= 24) & (row_z == j - 24) & (row_x == x)
    picker[...] = jnp.where(gain_rows | (notes & (key_rows | query_rows)), 1.0, 0.0).astype(BF)

    def tables(h):
        for dist in range(2):
            n = near_distance(dist)
            acc = jnp.full((TOK, TOK), tab[0, h], F32)
            for k, edge in enumerate(bucket_edges):
                acc = jnp.where(n >= edge, tab[k + 1, h], acc)
            bias[h, 1 + dist] = jnp.where(n >= 0, acc, masked)
        bias[h, 0] = jnp.full((TOK, TOK), masked, F32)
        bias[h, 3] = jnp.full((TOK, TOK), tab[BUCKETS - 1, h], F32)

    loop(0, GH, tables)
    wait_bytes(xo, core_recv.at[1])
    xo[...] = xo[...] + d_eo[mine, :]
    wait_bytes(w_s.at[mine], recv.at[1])
    push(w_s.at[mine], w_s.at[mine], send.at[5], core_recv.at[2], sib)
    wait_bytes(wa_all.at[z, x, y, c], own.at[0])
    wait_bytes(wa_all.at[pl.ds(0, 3), x, y, c], recv.at[2])
    for k in range(1, 4):
        push(
            wa_all.at[:, x, y, c], wa_all.at[:, x, y, c], send.at[6], recv.at[3],
            (z, (x + k) % 4, y, c),
        )
    wait_bytes(w_s.at[theirs], core_recv.at[2])
    picked = dot(picker[...], w_s[...], NN)
    gain = jnp.concatenate([picked[0:1, :384], picked[1:2, :384]], axis=1)
    gains[0:1, :] = gain
    gains[1:2, :] = jnp.concatenate([picked[2:3, :384], picked[3:4, :384]], axis=1)
    gains[2:8, :] = jnp.zeros((6, D), F32)
    kd[...] = picked[8:24, 384:512]
    qd[...] = picked[24:32, 384:512].T
    weight[...] = dot(select[...], w_s[...], NN).astype(BF)
    wait_bytes(tok_s, recv.at[0])
    for b in range(4):
        v = tok_s[b].astype(F32)
        normed[b * TOK : (b + 1) * TOK, :] = scale_rows(v, gain).astype(BF)
    qkv = dot(normed[...], weight[...], NN).astype(BF)
    q[...] = qkv[:, :GW]
    for b in range(4):
        kv[b] = qkv[b * TOK : (b + 1) * TOK, GW:]
    for k in range(1, 4):
        for b in range(4):
            push(
                kv.at[b], kv_s.at[block_cols(b, x)], send.at[7], kv_recv.at[4 - k],
                (z, (x + k) % 4, y, c),
            )
    for b in range(4):
        keep(kv.at[b], kv_s.at[block_cols(b, x)], kv_recv.at[0])
    wait_bytes(wa_all.at[:, pl.ds(0, 3), y, c], recv.at[3])
    for k in range(1, 4):
        push(
            wa_all.at[:, :, y, c], wa_all.at[:, :, y, c], send.at[8], recv.at[4],
            (z, x, (y + k) % 4, c),
        )
    for h in range(GH):
        head_cols = lax.broadcasted_iota(jnp.int32, (1, GW), 1) // HD == h
        qm[h] = jnp.where(head_cols, q[...] * 0.125, 0.0).astype(BF)
    for k in range(4):
        kx = (x + k) % 4
        if k == 0:
            for b in range(4):
                wait_bytes(kv_s.at[block_cols(b, kx)], kv_recv.at[0])
        else:
            wait_bytes(kv_s.at[pl.ds(0, 512)], kv_recv.at[k])
        for b in range(4):
            cols = block_cols(b, kx)
            v_s[cols, :] = kv_s[cols, GW:]
            for h in range(GH):
                s_s[h, b * TOK :, cols] = dot(qm[h, b * TOK :, :], kv_s[cols, :GW], NT)
    keep(kv_s, kv_out, own.at[1])
    to_chips(
        z, x, y, c,
        lambda there: xo.at[pl.ds(pl.multiple_of(block_of(*there[:3]) - c * 512, 16), 16)],
        d_rows.at[pl.ds(me, 16)], send.at[9], recv.at[5],
    )
    wait_bytes(wa_all.at[:, :, pl.ds(0, 3), c], recv.at[4])
    push(wa_all.at[:, :, :, c], wa_all.at[:, :, :, c], send.at[10], core_recv.at[3], sib)

    def head(h):
        head_cols = lax.broadcasted_iota(jnp.int32, (1, GW), 1) // HD == h
        far = tab[BUCKETS - 1, h]
        for zq in range(4):
            rows = pl.ds(zq * TOK, TOK)
            docs = qd[:, zq : zq + 1]
            top = None
            for zk in range(zq + 1):
                for kx in range(4):
                    cols = pl.ds((zk * 4 + kx) * TOK, TOK)
                    s = s_s[h, rows, cols]
                    if zk < zq - 1:
                        s = s + far
                    else:
                        s = s + bias[h, table_kind(zq, zk, x, kx)]
                    kb = zk * 4 + kx
                    s = jnp.where(docs == kd[kb : kb + 1, :], s, masked)
                    s_s[h, rows, cols] = s
                    top = s if top is None else jnp.maximum(top, s)
            top = jnp.max(top, axis=1, keepdims=True)
            total = jnp.zeros((TOK, TOK), F32)
            for kb in range(4 * (zq + 1)):
                cols = pl.ds(kb * TOK, TOK)
                e = jnp.exp(s_s[h, rows, cols] - top)
                s_s[h, rows, cols] = e
                total = total + e
            inv = 1.0 / jnp.sum(total, axis=1, keepdims=True)
            for kb in range(4 * (zq + 1)):
                cols = pl.ds(kb * TOK, TOK)
                p_s[h, rows, cols] = (s_s[h, rows, cols] * inv).astype(BF)
            width = (zq + 1) * 512
            o = dot(p_s[h, rows, :width], v_s[:width, :], NN).astype(BF)

            @pl.when(h == 0)
            def _():
                part[rows, :] = o

            @pl.when(h > 0)
            def _():
                part[rows, :] = jnp.where(head_cols, o, part[rows, :])

    loop(0, GH, head)
    for k in range(1, 4):
        there = (z + k) % 4
        push(
            part.at[pl.ds(pl.multiple_of(there * TOK, TOK), TOK)], attn_all.at[z],
            send.at[11], recv.at[6], (there, x, y, c),
        )
    keep(part.at[pl.ds(pl.multiple_of(z * TOK, TOK), TOK)], attn_all.at[z], recv.at[6])
    keep(p_s, p_out, own.at[2])
    wait_bytes(d_rows.at[mine], recv.at[5])
    push(d_rows.at[mine], d_rows.at[mine], send.at[12], core_recv.at[4], sib)
    wait_bytes(attn_all, recv.at[6])
    wait_bytes(wa_all.at[:, :, :, 1 - c], core_recv.at[3])
    wait_bytes(d_rows.at[theirs], core_recv.at[4])
    wait_bytes(kv_s, own.at[1])
    wait_bytes(p_s, own.at[2])
    wait_bytes(wo, send.at[0])
    wait_bytes(tok_s.at[pl.ds(0, 3)], send.at[1])
    wait_bytes(xo, send.at[2])
    sent_to_chips(w_s, y, c, send.at[3])
    wait_bytes(wa_all.at[pl.ds(0, 3), x, y, c], send.at[4])
    wait_bytes(w_s.at[mine], send.at[5])
    wait_bytes(wa_all.at[:, pl.ds(0, 3), y, c], send.at[6])
    wait_bytes(kv_s.at[pl.ds(0, 1536)], send.at[7])
    wait_bytes(wa_all.at[:, :, pl.ds(0, 3), c], send.at[8])
    sent_to_chips(d_rows, y, c, send.at[9])
    wait_bytes(wa_all.at[:, :, :, c], send.at[10])
    wait_bytes(attn_all.at[pl.ds(0, 3)], send.at[11])
    wait_bytes(d_rows.at[mine], send.at[12])


def attn_forward(tab, tok, wmsg, wa, d_eo):
    probs = (GH, 512, 2048)
    vm = pltpu.VMEM
    return pl.pallas_call(
        attn_forward_kernel,
        out_shape=(
            jax.ShapeDtypeStruct((4, TOK, GW), BF),
            jax.ShapeDtypeStruct((512, GW), BF),
            jax.ShapeDtypeStruct(probs, BF),
            jax.ShapeDtypeStruct((2048, 2 * GW), BF),
            jax.ShapeDtypeStruct((4, 4, 4, 2, 8, D), BF),
            jax.ShapeDtypeStruct((1024, D), BF),
            jax.ShapeDtypeStruct((512, D), BF),
            jax.ShapeDtypeStruct((D, 3 * GW), BF),
            jax.ShapeDtypeStruct((512, GW), BF),
            jax.ShapeDtypeStruct((8, D), F32),
        ),
        in_specs=[SMEM, VMEM, VMEM, VMEM, VMEM],
        out_specs=(ANY, VMEM, ANY, ANY, ANY, ANY, VMEM, VMEM, VMEM, VMEM),
        scratch_shapes=[
            vm((4, 16, 3 * GW), BF), vm((4, 16, 3 * GW), BF), vm((1024, 3 * GW), BF),
            vm((4, TOK, D), BF), vm((D, 1024), BF), vm((32, 1024), BF),
            vm((TOK, 8), F32), vm((16, TOK), F32),
            vm((4, TOK, 2 * GW), BF), vm((2048, 2 * GW), BF), vm((2048, GW), BF),
            vm((GH, 512, GW), BF), vm((GH, 4, TOK, TOK), F32), vm(probs, F32), vm(probs, BF),
            vm((512, D), BF),
            DMA((13,)), DMA((7,)), DMA((4,)), DMA((5,)), DMA((3,)),
        ],
        compiler_params=pltpu.CompilerParams(
            collective_id=2, has_side_effects=True, vmem_limit_bytes=48 * 2**20
        ),
        name="attn_forward",
    )(tab, tok, wmsg, wa, d_eo)


def attn_backward_kernel(
    p, q, kv, home, picks, middle, gains, cotangent, w_proj, weight, normed, attn_part, tok,
    input_grad, qkv_out, att_out, small_out,
    p_s, v_s, do_s, dm, qm, dp_s, ds_s, near, messages, parts, branch_all, dq, tab,
    d_qkv, n_part, normed_in, att_f, q_blk, q_sib, q_tot, q_in, a_blk, a_sib, a_tot, a_in,
    s_own, s_sib, s_tot, s_in, qkv_sum, att_sum, s_sum, d_attn, branch, d_middle, send, recv, core_recv, own,
):
    z, x, y, c = place()
    sib = (z, x, y, 1 - c)
    p16 = x * 4 + y
    p32 = p16 * 2 + c
    me = z * 32 + p32
    source = me // 4

    def peer(i):
        return z, (x + i // 4) % 4, (y + i % 4) % 4, c

    keep(p, p_s, own.at[0])
    loop(1, 16, lambda i: signal(peer(i)))
    for k in range(1, 4):
        signal(((z + k) % 4, x, y, c))
    signal(sib)

    def greet(k):
        @pl.when(jnp.logical_not((k == z) & (source == p32)))
        def _():
            signal((k, source // 8, (source // 2) % 4, source % 2))

    loop(0, 4, greet)
    v_s[...] = kv[:, GW:]
    for h in range(GH):
        head_cols = lax.broadcasted_iota(jnp.int32, (1, GW), 1) // HD == h
        qm[h] = jnp.where(head_cols, q[...] * 0.125, 0.0).astype(BF)
    d_moe = dot(picks[:TOK, :], home[...], NN) + dot(picks[TOK:, :], home[...], NN)
    mid = middle[...]
    mid_r = lax.rsqrt(jnp.mean(mid * mid, axis=1, keepdims=True) + norm_eps)
    mid_unit = mid * mid_r
    s_own[...] = jnp.zeros_like(s_own)
    s_own[1:2, :] = jnp.sum(d_moe * mid_unit, axis=0, keepdims=True)
    d_mid_unit = d_moe * gains[1:2, :]
    d_mid = mid_r * (d_mid_unit - mid_unit * jnp.mean(d_mid_unit * mid_unit, axis=1, keepdims=True))
    d_mid = cotangent[...].astype(F32) + d_mid
    d_middle[...] = d_mid
    branch[...] = d_mid.astype(BF)
    for k in range(GROUPS):
        d_attn[k] = dot(branch[...], w_proj[GW * k : GW * (k + 1), :], NT).astype(BF)
    arrive(15 + 3 + 1 + 4 - jnp.where(source == p32, 1, 0))
    for k in range(1, 4):
        there = (z + k) % 4
        push(d_attn.at[there], do_s.at[z], send.at[0], recv.at[0], (there, x, y, c))
    keep(d_attn.at[z], do_s.at[z], recv.at[0])
    z_rows = pl.ds(pl.multiple_of(z * TOK, TOK), TOK)
    for k in range(1, 4):
        push(branch, branch_all.at[z_rows], send.at[1], recv.at[1], ((z + k) % 4, x, y, c))
    keep(branch, branch_all.at[z_rows], recv.at[1])
    wait_bytes(do_s, recv.at[0])
    for h in range(GH):
        head_cols = lax.broadcasted_iota(jnp.int32, (1, GW), 1) // HD == h
        for b in range(4):
            dm[h, b * TOK : (b + 1) * TOK, :] = jnp.where(head_cols, do_s[b], 0.0).astype(BF)
    wait_bytes(p_s, own.at[0])

    def key_sums(left, right, m, pair):
        for k in (1, 2, 3, 0):
            kx = (x + k) % 4
            for b in (2 * pair, 2 * pair + 1):
                cols = block_cols(b, kx)
                total = None
                for h in range(GH):
                    one = dot(left[h, b * TOK :, cols], right[h, b * TOK :, :], TN)
                    total = one if total is None else total + one
                side = GW * (b % 2)
                messages[k, m, :, side : side + GW] = total.astype(BF)
            if k:
                push(messages.at[k, m], parts.at[x, m], send.at[2], recv.at[2], (z, kx, y, c))
            else:
                keep(messages.at[k, m], parts.at[x, m], recv.at[2])

    key_sums(p_s, dm, 0, 0)
    key_sums(p_s, dm, 1, 1)
    near[...] = jnp.zeros_like(near)

    def score_grads(zq):
        rows = pl.ds(zq * TOK, TOK)
        width = (zq + 1) * 512

        def head(h):
            head_cols = lax.broadcasted_iota(jnp.int32, (1, GW), 1) // HD == h
            dp_s[:, :width] = dot(dm[h, rows, :], v_s[:width, :], NT)
            acc = jnp.zeros((TOK, TOK), F32)
            for kb in range(4 * (zq + 1)):
                cols = pl.ds(kb * TOK, TOK)
                acc = acc + p_s[h, rows, cols].astype(F32) * dp_s[:, cols]
            delta = jnp.sum(acc, axis=1, keepdims=True)
            far = jnp.zeros((TOK, TOK), F32)
            for zk in range(zq + 1):
                for kx in range(4):
                    cols = pl.ds((zk * 4 + kx) * TOK, TOK)
                    ds = (p_s[h, rows, cols].astype(F32) * (dp_s[:, cols] - delta)).astype(BF)
                    ds_s[h, rows, cols] = ds
                    if zk < zq - 1:
                        far = far + ds.astype(F32)
                    else:
                        near[h, table_kind(zq, zk, x, kx)] += ds.astype(F32)
            if zq > 1:
                near[h, 3] += far
            o = (dot(ds_s[h, rows, :width], kv[:width, :GW], NN) * 0.125).astype(BF)

            @pl.when(h == 0)
            def _():
                dq[rows, :] = o

            @pl.when(h > 0)
            def _():
                dq[rows, :] = jnp.where(head_cols, o, dq[rows, :])

        loop(0, GH, head)

    score_grads(3)
    score_grads(2)
    key_sums(ds_s, qm, 3, 1)
    score_grads(1)
    score_grads(0)
    key_sums(ds_s, qm, 2, 0)

    def bucket_sums(h):
        for dist in range(2):
            n = near_distance(dist)
            held = near[h, 1 + dist]
            bounds = [-(10**6)] + bucket_edges + [10**6]
            for b in range(BUCKETS):
                low, high = bounds[b], bounds[b + 1]
                if high <= dist * TOK - TOK + 1 or low > dist * TOK + TOK - 1:
                    if dist == 0:
                        tab[h, b : b + 1, :] = jnp.zeros((1, TOK), F32)
                    continue
                inside = jnp.sum(
                    jnp.where((n >= low) & (n < high), held, 0.0), axis=0, keepdims=True
                )
                if dist == 0:
                    tab[h, b : b + 1, :] = inside
                else:
                    tab[h, b : b + 1, :] += inside
        tab[h, BUCKETS - 1 :, :] += jnp.sum(near[h, 3], axis=0, keepdims=True)

    loop(0, GH, bucket_sums)

    wait_bytes(branch_all, recv.at[1])
    att_f[0:GW, :] = dot(attn_part[...], branch_all[...], TN)
    att_f[GW:, :] = jnp.zeros((8, D), F32)
    for j in range(32):
        a_blk[j // 2, j % 2] = att_f[6 * j : 6 * j + 8, :].astype(BF)
    push(a_blk.at[:, 1 - c], a_sib, send.at[4], core_recv.at[1], sib)
    for h in range(GH):
        s_own[2:3, BUCKETS * h : BUCKETS * (h + 1)] = jnp.sum(tab[h].T, axis=0, keepdims=True)

    wait_bytes(a_sib, core_recv.at[1])

    def att_blocks(i):
        there = peer(i)
        j = there[1] * 4 + there[2]
        a_tot[j] = (a_blk[j, c].astype(F32) + a_sib[j].astype(F32)).astype(BF)
        push(a_tot.at[j], a_in.at[p16], send.at[6], recv.at[4], there)

    loop(1, 16, att_blocks)
    a_tot[p16] = (a_blk[p16, c].astype(F32) + a_sib[p16].astype(F32)).astype(BF)
    keep(a_tot.at[p16], a_in.at[p16], recv.at[4])

    wait_bytes(parts, recv.at[2])
    d_qkv[:, :GW] = dq[...]
    for b in range(4):
        rows = slice(b * TOK, (b + 1) * TOK)
        side = GW * (b % 2)
        for m, at in ((2 + b // 2, GW), (b // 2, 2 * GW)):
            total = parts[0, m, :, side : side + GW].astype(F32)
            for k in range(1, 4):
                total = total + parts[k, m, :, side : side + GW].astype(F32)
            d_qkv[rows, at : at + GW] = total.astype(BF)
    d_normed = dot(d_qkv[...], weight[...], NT)
    n_part[...] = d_normed.astype(BF)
    for k in range(1, 4):
        there = (z + k) % 4
        push(
            n_part.at[pl.ds(pl.multiple_of(there * TOK, TOK), TOK)], normed_in.at[z],
            send.at[3], recv.at[3], (there, x, y, c),
        )
    keep(n_part.at[z_rows], normed_in.at[z], recv.at[3])
    along = jnp.sum(d_normed * normed[...].astype(F32), axis=0, keepdims=True)
    s_own[0:1, :] = along / gains[0:1, :]
    push(s_own, s_sib, send.at[8], core_recv.at[2], sib)
    total = dot(normed[...], d_qkv[...], TN)
    for j in range(32):
        q_blk[j // 2, j % 2] = total[24 * j : 24 * j + 24].astype(BF)
    push(q_blk.at[:, 1 - c], q_sib, send.at[5], core_recv.at[0], sib)
    wait_bytes(s_sib, core_recv.at[2])
    s_tot[...] = s_own[...] + s_sib[...]
    loop(1, 16, lambda i: push(s_tot, s_in.at[p16], send.at[9], recv.at[6], peer(i)))
    keep(s_tot, s_in.at[p16], recv.at[6])
    wait_bytes(q_sib, core_recv.at[0])

    def qkv_blocks(i):
        there = peer(i)
        j = there[1] * 4 + there[2]
        q_tot[j] = (q_blk[j, c].astype(F32) + q_sib[j].astype(F32)).astype(BF)
        push(q_tot.at[j], q_in.at[p16], send.at[7], recv.at[5], there)

    loop(1, 16, qkv_blocks)
    q_tot[p16] = (q_blk[p16, c].astype(F32) + q_sib[p16].astype(F32)).astype(BF)
    keep(q_tot.at[p16], q_in.at[p16], recv.at[5])

    wait_bytes(s_in, recv.at[6])
    s_total = s_in[0]
    for k in range(1, 16):
        s_total = s_total + s_in[k]
    s_sum[...] = s_total
    for k in range(1, 4):
        push(s_sum, small_out.at[z], send.at[11], recv.at[8], ((z + k) % 4, x, y, c))
    keep(s_sum, small_out.at[z], recv.at[8])
    wait_bytes(q_in, recv.at[5])
    q_total = q_in[0].astype(F32)
    for k in range(1, 16):
        q_total = q_total + q_in[k].astype(F32)
    for k in range(4):
        qkv_sum[k, 0:6, :] = q_total[6 * k : 6 * k + 6]
        qkv_sum[k, 6:8, :] = jnp.zeros((2, 3 * GW), F32)

    def final(k):
        d = 4 * p32 + k

        @pl.when(d != me)
        def _():
            push(qkv_sum.at[k], qkv_out.at[z], send.at[10], recv.at[7], device_of(d))

        @pl.when(d == me)
        def _():
            keep(qkv_sum.at[k], qkv_out.at[z], recv.at[7])

    loop(0, 4, final)
    wait_bytes(a_in, recv.at[4])
    a_total = a_in[0].astype(F32)
    for k in range(1, 16):
        a_total = a_total + a_in[k].astype(F32)
    att_sum[...] = a_total
    keep(att_sum, att_out, own.at[1])
    wait_bytes(normed_in, recv.at[3])
    d_normed = normed_in[0].astype(F32)
    for k in range(1, 4):
        d_normed = d_normed + normed_in[k].astype(F32)
    v = tok[...].astype(F32)
    r = lax.rsqrt(jnp.mean(v * v, axis=1, keepdims=True) + norm_eps)
    unit = v * r
    d_unit = d_normed * gains[0:1, :]
    d_in = r * (d_unit - unit * jnp.mean(d_unit * unit, axis=1, keepdims=True))
    input_grad[...] = (d_middle[...] + d_in).astype(BF)

    wait_bytes(att_sum, own.at[1])
    wait_bytes(qkv_out, recv.at[7])
    wait_bytes(small_out, recv.at[8])
    wait_bytes(do_s.at[pl.ds(0, 3)], send.at[0])
    wait_bytes(branch_all.at[pl.ds(0, 3 * TOK)], send.at[1])
    wait_bytes(parts.at[pl.ds(0, 3)], send.at[2])
    wait_bytes(normed_in.at[pl.ds(0, 3)], send.at[3])
    wait_bytes(a_sib, send.at[4])
    wait_bytes(q_sib, send.at[5])
    wait_bytes(a_in.at[pl.ds(0, 15)], send.at[6])
    wait_bytes(q_in.at[pl.ds(0, 15)], send.at[7])
    wait_bytes(s_own, send.at[8])
    wait_bytes(s_in.at[pl.ds(0, 15)], send.at[9])

    def sent(k):
        @pl.when(4 * p32 + k != me)
        def _():
            wait_bytes(qkv_sum.at[0], send.at[10])

    loop(0, 4, sent)
    wait_bytes(small_out.at[pl.ds(0, 3)], send.at[11])


def attn_backward(p, *rest):
    probs = (GH, 512, 2048)
    vm = pltpu.VMEM
    return pl.pallas_call(
        attn_backward_kernel,
        out_shape=(
            jax.ShapeDtypeStruct((TOK, D), BF),
            jax.ShapeDtypeStruct((4, 8, 3 * GW), F32),
            jax.ShapeDtypeStruct((8, D), F32),
            jax.ShapeDtypeStruct((4, 8, D), F32),
        ),
        in_specs=[ANY] + [VMEM] * len(rest),
        out_specs=(VMEM, ANY, ANY, ANY),
        scratch_shapes=[
            vm(probs, BF), vm((2048, GW), BF), vm((4, TOK, GW), BF), vm((GH, 512, GW), BF),
            vm((GH, 512, GW), BF), vm((TOK, 2048), F32), vm(probs, BF), vm((GH, 4, TOK, TOK), F32),
            vm((4, 4, TOK, 2 * GW), BF), vm((4, 4, TOK, 2 * GW), BF), vm((512, D), BF),
            vm((512, GW), BF), vm((GH, BUCKETS, TOK), F32),
            vm((512, 3 * GW), BF), vm((512, D), BF), vm((4, TOK, D), BF), vm((GW + 8, D), F32),
            vm((16, 2, 24, 3 * GW), BF), vm((16, 24, 3 * GW), BF),
            vm((16, 24, 3 * GW), BF), vm((16, 24, 3 * GW), BF),
            vm((16, 2, 8, D), BF), vm((16, 8, D), BF), vm((16, 8, D), BF), vm((16, 8, D), BF),
            vm((8, D), F32), vm((8, D), F32), vm((8, D), F32), vm((16, 8, D), F32),
            vm((4, 8, 3 * GW), F32), vm((8, D), F32), vm((8, D), F32),
            vm((4, TOK, GW), BF), vm((TOK, D), BF), vm((TOK, D), F32),
            DMA((12,)), DMA((9,)), DMA((3,)), DMA((2,)),
        ],
        compiler_params=pltpu.CompilerParams(
            collective_id=3, has_side_effects=True, vmem_limit_bytes=54 * 2**20
        ),
        name="attn_backward",
    )(p, *rest)


def per_device(
    tokens,
    gain_attn,
    w_qkv,
    w_attn_out,
    rel_table,
    gain_moe,
    w_in,
    w_out,
    expert_ids,
    gate_values,
    doc_ids,
    cotangent,
):
    z, x, y, c = place()
    experts = 64
    capacity = 8
    slots = 2 * experts * capacity
    own_tokens = tokens.reshape(TOK, D)
    grad_bf = cotangent.reshape(TOK, D)
    grad_out = grad_bf.astype(F32)

    routes = expert_ids.reshape(TOK, 2)
    gates = gate_values.reshape(TOK, 2)
    expert_list = jnp.arange(experts, dtype=jnp.int32)[None, :]
    marks = jnp.concatenate(
        [(routes[:, :1] == expert_list), (routes[:, 1:] == expert_list)], axis=1
    ).astype(BF)
    lower = jnp.tril(jnp.ones((TOK, TOK), BF), -1)
    earlier = dot(lower, marks, NN)
    marks = marks.astype(F32)
    firsts = jnp.sum(marks[:, :experts], axis=0, keepdims=True)
    rank_0 = jnp.sum(earlier[:, :experts] * marks[:, :experts], axis=1)
    rank_1 = jnp.sum((earlier[:, experts:] + firsts) * marks[:, experts:], axis=1)
    blocks = (routes % 2) * 32 + (routes // 4) * 2 + (routes % 4) // 2
    places = blocks * 16 + c * capacity + jnp.stack([rank_0, rank_1], axis=1).astype(jnp.int32)
    slot_ids = jnp.arange(slots, dtype=jnp.int32)[None, :]
    picks = jnp.concatenate(
        [(places[:, :1] == slot_ids), (places[:, 1:] == slot_ids)], axis=0
    ).astype(BF)
    gated = jnp.concatenate([gates[:, :1] * grad_out, gates[:, 1:] * grad_out], axis=0).astype(BF)
    d_eo = dot(picks, gated, TN).astype(BF)

    slab = w_qkv.reshape(6, 3, GROUPS, GW).transpose(2, 0, 1, 3).reshape(GROUPS, 6, 3 * GW)
    place_in = chip_of(z, x, y) * 2 + c
    among = (place_in % 64) * 6
    row_one = lax.dynamic_update_slice(jnp.zeros((3 * GW,), BF), gain_attn, (among,))
    row_one = lax.dynamic_update_slice(row_one, doc_ids.reshape(TOK).astype(BF), (384,))
    row_two = lax.dynamic_update_slice(jnp.zeros((3 * GW,), BF), gain_moe, (among,))
    note_one = jnp.broadcast_to(row_one, (GROUPS, 1, 3 * GW))
    note_two = jnp.broadcast_to(row_two, (GROUPS, 1, 3 * GW))
    nothing = jnp.zeros((GROUPS, 6, 3 * GW), BF)
    none = nothing[:, :1]
    message = jnp.where(
        c == 0,
        jnp.concatenate([slab, nothing, note_one, none, note_two, none], axis=1),
        jnp.concatenate([nothing, slab, none, note_one, none, note_two], axis=1),
    )
    out_slab = jnp.concatenate([w_attn_out, jnp.zeros((2, D), BF)], axis=0)
    table = lax.dynamic_slice(rel_table, (0, z * GH), (BUCKETS, GH)).astype(F32)
    (
        attn, attn_part, probs, kv_all, out_weights, d_eo_all, normed, weight, queries, gain_rows,
    ) = attn_forward(table, own_tokens, message, out_slab, d_eo)
    attention_weight = out_weights[:, :, :, :, :6, :].reshape(D, D)
    home, expert_out, expert_in_grad, expert_out_grad, middle = run_experts(
        attn, attention_weight, own_tokens, gain_rows, picks, d_eo_all, w_in[0], w_out[0]
    )
    input_grad, qkv_sum, att_sum, small_sum = attn_backward(
        probs, queries, kv_all, home, picks, middle, gain_rows, grad_bf, attention_weight, weight,
        normed, attn_part, own_tokens,
    )

    picked = dot(picks, expert_out, NN).reshape(2, TOK, D)
    block_out = middle + gates[:, :1] * picked[0] + gates[:, 1:] * picked[1]
    gate_grad = jnp.sum(picked * grad_out[None], axis=2).T

    qkv_grad = qkv_sum[:, :6, :].reshape(GROUPS, 6, 3, GW).transpose(1, 2, 0, 3).reshape(6, 3 * D)
    attn_out_grad = att_sum[:6]
    gains = lax.dynamic_slice(jnp.sum(small_sum[:, :2, :], axis=0), (0, place_in * 6), (2, 6))
    table_grad = small_sum[:, 2, : GH * BUCKETS].reshape(GROUPS * GH, BUCKETS).T
    return (
        block_out.reshape(1, TOK, D).astype(BF),
        input_grad.reshape(1, TOK, D),
        gate_grad.reshape(1, TOK, 2),
        gains[0],
        qkv_grad,
        attn_out_grad,
        table_grad,
        gains[1],
        expert_in_grad[None],
        expert_out_grad[None],
    )


def solution(mesh):
    torus = Mesh(mesh.devices.reshape(4, 4, 4, 2), AXES)
    in_specs = (
        P(EXP, CTX, None),
        P(AXES),
        P(AXES, None),
        P(AXES, None),
        P(),
        P(AXES),
        P(AXES, None, None),
        P(AXES, None, None),
        P(EXP, CTX, None),
        P(EXP, CTX, None),
        P(EXP, CTX),
        P(EXP, CTX, None),
    )
    out_specs = (
        P(EXP, CTX, None),
        P(EXP, CTX, None),
        P(EXP, CTX, None),
        P(AXES),
        P(AXES, None),
        P(AXES, None),
        P(),
        P(AXES),
        P(AXES, None, None),
        P(AXES, None, None),
    )
    return jax.shard_map(
        per_device, mesh=torus, in_specs=in_specs, out_specs=out_specs, check_vma=False
    )
```

```python
import functools

import jax
import jax.numpy as jnp
import numpy as np
from jax import lax
from jax.experimental import pallas as pl
from jax.experimental.pallas import tpu as pltpu
from jax.sharding import Mesh
from jax.sharding import PartitionSpec as P

D = 768
H = 12
HD = 64
BUCKETS = 32
GROUPS = 4
GH = H // GROUPS
GW = GH * HD
TOK = 128
CTX = ("ctx_0", "ctx_1")
EXP = ("exp_0", "exp_1")
AXES = ("ctx_0", "ctx_1", "exp_0", "exp_1")
MESH = pl.DeviceIdType.MESH
ANY = pl.BlockSpec(memory_space=pl.ANY)
BF = jnp.bfloat16
F32 = jnp.float32

norm_eps = 1e-06
bucket_edges = [int(e) for e in np.concatenate(
    [np.arange(1, 17), np.ceil(16.0 * 8.0 ** (np.arange(1, 16) / 16.0))]
).astype(np.int32)]
masked = -1e30


def scale_rows(values, gain):
    return values * lax.rsqrt(jnp.mean(values * values, axis=-1, keepdims=True) + norm_eps) * gain


def place():
    return tuple(lax.axis_index(a) for a in AXES)


def chip_of(z, x, y):
    return (z * 4 + x) * 4 + y


def chip_peer(i, z, x, y):
    return (z + i // 16) % 4, (x + (i // 4) % 4) % 4, (y + i % 4) % 4


def loop(first, last, body):
    lax.fori_loop(first, last, lambda i, carry: (body(i), carry)[1], 0)


def signal(device):
    pl.semaphore_signal(
        pltpu.get_barrier_semaphore(), inc=1, device_id=device, device_id_type=MESH
    )


def arrive(count):
    pl.semaphore_wait(pltpu.get_barrier_semaphore(), count)


def push(src, dst, send, recv, device):
    pltpu.make_async_remote_copy(
        src_ref=src, dst_ref=dst, send_sem=send, recv_sem=recv, device_id=device, device_id_type=MESH
    ).start()


def keep(src, dst, sem):
    pltpu.make_async_copy(src, dst, sem).start()


def wait_bytes(ref, sem):
    pltpu.make_async_copy(ref, ref, sem).wait()


def comm_call(kernel, outs, scratch, collective_id, name):
    return pl.pallas_call(
        kernel,
        out_shape=outs,
        in_specs=None,
        out_specs=jax.tree.map(lambda _: ANY, outs),
        scratch_shapes=scratch,
        compiler_params=pltpu.CompilerParams(
            collective_id=collective_id, has_side_effects=True, vmem_limit_bytes=32 * 2**20
        ),
        name=name,
    )


def run_comm(kernel, args, outs, scratch, collective_id, name):
    return pl.pallas_call(
        kernel,
        out_shape=outs,
        in_specs=[ANY] * len(args),
        out_specs=jax.tree.map(lambda _: ANY, outs),
        scratch_shapes=scratch,
        compiler_params=pltpu.CompilerParams(
            collective_id=collective_id, has_side_effects=True, vmem_limit_bytes=32 * 2**20
        ),
        name=name,
    )(*args)


DMA = pltpu.SemaphoreType.DMA


def half_peer(i, z, x, y, c):
    return (z + i // 8) % 4, (x + (i // 2) % 4) % 4, c + 2 * ((y // 2 + i % 2) % 2), y % 2


def block_of(z, x, y):
    return pl.multiple_of((y % 2) * 512 + ((z * 4 + x) * 2 + y // 2) * 16, 16)


def greet_chips(z, x, y, c):
    loop(1, 32, lambda i: signal(half_peer(i, z, x, y, c)))

    @pl.when(y % 2 != c)
    def _():
        signal(half_peer(0, z, x, y, c))

    signal((z, x, y, 1 - c))
    return 32 + jnp.where(y % 2 == c, 0, 1)


def to_chips(z, x, y, c, source, target, send, recv):
    def one(i):
        there = half_peer(i, z, x, y, c)
        push(source(there), target, send, recv, there)

    loop(1, 32, one)
    first = half_peer(0, z, x, y, c)

    @pl.when(y % 2 == c)
    def _():
        keep(source(first), target, recv)

    @pl.when(y % 2 != c)
    def _():
        push(source(first), target, send, recv, first)


def sent_to_chips(rows, y, c, send):
    wait_bytes(rows.at[pl.ds(0, 496)], send)

    @pl.when(y % 2 != c)
    def _():
        wait_bytes(rows.at[pl.ds(0, 16)], send)


FH = 1536
WIDE = 256


def experts_kernel(
    attn_at, w_proj_at, tok_at, gains_at, picks_at, d_rows, w_in, w_out,
    home_in, home_out, g_in, g_out, middle,
    attn, w_proj, tok, gains, picks, x16, xo, rows, dv, w1, w2, dh, hidden, dact, in_h, out_h, in_o, out_o, stage_out, stage_in,
    send, recv, core_recv, own, staged, fetched,
):
    z, x, y, c = place()
    sib = (z, x, y, 1 - c)
    at_mine = pl.multiple_of(c * 512, 512)
    at_theirs = pl.multiple_of((1 - c) * 512, 512)
    mine, theirs = pl.ds(at_mine, 512), pl.ds(at_theirs, 512)
    me = block_of(z, x, y)
    fetches = (
        (attn_at, attn), (w_proj_at, w_proj), (tok_at, tok), (gains_at, gains), (picks_at, picks)
    )
    for k, (source, target) in enumerate(fetches):
        keep(source, target, fetched.at[k])
    keep(d_rows, dv, own.at[1])
    keep(w_out, w2, own.at[2])
    keep(w_in, w1, own.at[3])
    expected = greet_chips(z, x, y, c)
    for k, (_, target) in enumerate(fetches):
        wait_bytes(target, fetched.at[k])
    total = tok[...].astype(F32)
    for k in range(GROUPS):
        total = total + dot(attn[k], w_proj[GW * k : GW * (k + 1), :], NN)
    middle[...] = total
    moe_in = scale_rows(total, gains[1:2, :]).astype(BF)
    for n in range(0, 1024, WIDE):
        x16[n : n + WIDE, :] = (
            dot(picks[:TOK, n : n + WIDE], moe_in, TN) + dot(picks[TOK:, n : n + WIDE], moe_in, TN)
        ).astype(BF)
    arrive(expected)
    push(x16.at[theirs], xo, send.at[0], core_recv.at[0], sib)
    wait_bytes(xo, core_recv.at[0])
    xo[...] = xo[...] + x16[mine, :]
    to_chips(
        z, x, y, c,
        lambda there: xo.at[pl.ds(pl.multiple_of(block_of(*there[:3]) - c * 512, 16), 16)],
        rows.at[pl.ds(me, 16)], send.at[1], recv.at[0],
    )
    wait_bytes(dv, own.at[1])
    wait_bytes(w2, own.at[2])

    def hidden_grads(n):
        cols = pl.ds(pl.multiple_of(n * WIDE, WIDE), WIDE)
        dh[:, cols] = dot(dv[...], w2[cols, :], NT)

    loop(0, FH // WIDE, hidden_grads)
    wait_bytes(w1, own.at[3])
    wait_bytes(rows.at[mine], recv.at[0])
    push(rows.at[mine], rows.at[mine], send.at[2], core_recv.at[1], sib)

    def activate(at):
        part = pl.ds(at, 512)

        def one(n):
            cols = pl.ds(pl.multiple_of(n * WIDE, WIDE), WIDE)
            a = dot(rows[part, :], w1[:, cols], NN)
            square = a * a
            t = jnp.tanh(0.7978845608028654 * (a + 0.044715 * (square * a)))
            cdf = 0.5 * (1.0 + t)
            hidden[part, cols] = (a * cdf).astype(BF)
            slope = cdf + 0.5 * a * (1.0 - t * t) * (
                0.7978845608028654 * (1.0 + 0.134145 * square)
            )
            dact[part, cols] = (slope * dh[part, cols]).astype(BF)

        loop(0, FH // WIDE, one)

    def in_half(at):
        part = pl.ds(at, 512)

        def one(n):
            cols = pl.ds(pl.multiple_of(n * WIDE, WIDE), WIDE)
            in_h[part, cols] = dot(dact[part, :], w1[cols, :], NT).astype(BF)

        loop(0, D // WIDE, one)

    def out_half(at):
        part = pl.ds(at, 512)

        def one(n):
            cols = pl.ds(pl.multiple_of(n * WIDE, WIDE), WIDE)
            out_h[part, cols] = dot(hidden[part, :], w2[:, cols], NN).astype(BF)

        loop(0, D // WIDE, one)

    activate(at_mine)
    wait_bytes(rows.at[theirs], core_recv.at[1])
    activate(at_theirs)
    in_half(at_theirs)
    push(in_h.at[theirs], in_o, send.at[3], core_recv.at[2], sib)
    in_half(at_mine)
    wait_bytes(in_o, core_recv.at[2])
    in_o[...] = (in_o[...].astype(F32) + in_h[mine, :].astype(F32)).astype(BF)
    to_chips(
        z, x, y, c,
        lambda there: in_o.at[pl.ds(pl.multiple_of(block_of(*there[:3]) - c * 512, 16), 16)],
        home_in.at[pl.ds(me, 16)], send.at[4], recv.at[1],
    )
    out_half(at_theirs)
    push(out_h.at[theirs], out_o, send.at[5], core_recv.at[3], sib)
    out_half(at_mine)
    wait_bytes(out_o, core_recv.at[3])
    out_o[...] = (out_o[...].astype(F32) + out_h[mine, :].astype(F32)).astype(BF)
    to_chips(
        z, x, y, c,
        lambda there: out_o.at[pl.ds(pl.multiple_of(block_of(*there[:3]) - c * 512, 16), 16)],
        home_out.at[pl.ds(me, 16)], send.at[6], recv.at[2],
    )

    def out_grads(n):
        cols = pl.ds(pl.multiple_of(n * WIDE, WIDE), WIDE)
        slot = n % 2

        @pl.when(n >= 2)
        def _():
            wait_bytes(stage_out.at[slot], staged.at[slot])

        stage_out[slot] = dot(hidden[:, cols], dv[...], TN)
        keep(stage_out.at[slot], g_out.at[cols], staged.at[slot])

    loop(0, FH // WIDE, out_grads)
    wait_bytes(home_in.at[mine], recv.at[1])
    push(home_in.at[mine], home_in.at[mine], send.at[7], core_recv.at[4], sib)

    def in_grads(n):
        cols = pl.ds(pl.multiple_of(n * WIDE, WIDE), WIDE)
        slot = n % 2

        @pl.when(n >= 2)
        def _():
            wait_bytes(stage_in.at[slot], staged.at[2 + slot])

        stage_in[slot] = dot(rows[:, cols], dact[...], TN)
        keep(stage_in.at[slot], g_in.at[cols], staged.at[2 + slot])

    loop(0, D // WIDE, in_grads)
    wait_bytes(home_out.at[mine], recv.at[2])
    push(home_out.at[mine], home_out.at[mine], send.at[8], core_recv.at[5], sib)
    for slot in range(2):
        wait_bytes(stage_out.at[slot], staged.at[slot])
        wait_bytes(stage_in.at[slot], staged.at[2 + slot])
    wait_bytes(xo, send.at[0])
    sent_to_chips(rows, y, c, send.at[1])
    wait_bytes(rows.at[mine], send.at[2])
    wait_bytes(in_o, send.at[3])
    sent_to_chips(home_in, y, c, send.at[4])
    wait_bytes(out_o, send.at[5])
    sent_to_chips(home_out, y, c, send.at[6])
    wait_bytes(home_in.at[theirs], core_recv.at[4])
    wait_bytes(home_out.at[theirs], core_recv.at[5])
    wait_bytes(home_in.at[mine], send.at[7])
    wait_bytes(home_out.at[mine], send.at[8])


def run_experts(*args):
    whole_rows = pltpu.VMEM((1024, D), BF)
    half_rows = pltpu.VMEM((512, D), BF)
    hid = pltpu.VMEM((1024, FH), BF)
    return pl.pallas_call(
        experts_kernel,
        out_shape=(
            jax.ShapeDtypeStruct((1024, D), BF),
            jax.ShapeDtypeStruct((1024, D), BF),
            jax.ShapeDtypeStruct((D, FH), F32),
            jax.ShapeDtypeStruct((FH, D), F32),
            jax.ShapeDtypeStruct((TOK, D), F32),
        ),
        in_specs=[ANY] * 8,
        out_specs=(ANY,) * 4 + (pl.BlockSpec(memory_space=pltpu.VMEM),),
        scratch_shapes=[
            pltpu.VMEM((4, TOK, GW), BF), pltpu.VMEM((D, D), BF), pltpu.VMEM((TOK, D), BF),
            pltpu.VMEM((8, D), F32), pltpu.VMEM((2 * TOK, 1024), BF),
            whole_rows, half_rows, whole_rows, whole_rows,
            pltpu.VMEM((D, FH), BF), pltpu.VMEM((FH, D), BF), pltpu.VMEM((1024, FH), F32),
            hid, hid, whole_rows, whole_rows, half_rows, half_rows,
            pltpu.VMEM((2, WIDE, D), F32), pltpu.VMEM((2, WIDE, FH), F32),
            DMA((9,)), DMA((3,)), DMA((6,)), DMA((4,)), DMA((4,)), DMA((5,)),
        ],
        compiler_params=pltpu.CompilerParams(
            collective_id=1, has_side_effects=True, vmem_limit_bytes=48 * 2**20
        ),
        name="experts",
    )(*args)


def device_of(d):
    return d // 32, (d // 8) % 4, (d // 2) % 4, d % 2


NT = (((1,), (1,)), ((), ()))
NN = (((1,), (0,)), ((), ()))
TN = (((0,), (0,)), ((), ()))


def dot(a, b, dims):
    return lax.dot_general(a, b, dims, preferred_element_type=F32)


def near_distance(dist):
    a = lax.broadcasted_iota(jnp.int32, (TOK, TOK), 0)
    b = lax.broadcasted_iota(jnp.int32, (TOK, TOK), 1)
    return dist * TOK + a - b


def table_kind(zq, zk, x, kx):
    return jnp.clip((zq - zk) * 4 + x - kx + 1, 0, 3)


def block_cols(zk, kx):
    return pl.ds(pl.multiple_of((zk * 4 + kx) * TOK, TOK), TOK)


VMEM = pl.BlockSpec(memory_space=pltpu.VMEM)
SMEM = pl.BlockSpec(memory_space=pltpu.SMEM)


def attn_forward_kernel(
    tab, tok, w_qkv, notes, wa, routes, gates, cotangent,
    attn_all, part, p_out, kv_out, wa_all, d_rows, normed, weight, q, gains, picks,
    d_eo, wmsg, wm, wo, w_s, tok_s, select, picker, qd, kd,
    kv, kv_s, v_s, qm, bias, s_s, p_s, xo,
    send, recv, kv_recv, core_recv, own,
):
    z, x, y, c = place()
    sib = (z, x, y, 1 - c)
    mine = pl.ds(pl.multiple_of(c * 512, 512), 512)
    theirs = pl.ds(pl.multiple_of((1 - c) * 512, 512), 512)
    me = block_of(z, x, y)
    keep(wa, wa_all.at[z, x, y, c], own.at[0])
    expected = greet_chips(z, x, y, c)
    for k in range(1, 4):
        signal(((z + k) % 4, x, y, c))
        signal((z, (x + k) % 4, y, c))
        signal((z, x, (y + k) % 4, c))
    lift = lax.broadcasted_iota(jnp.int32, (16, 8), 0)
    below = lax.broadcasted_iota(jnp.int32, (16, 8), 1)
    lift = jnp.where((lift == 6 * c + below) & (below < 6), 1.0, 0.0)
    lift = jnp.where(
        (below >= 6) & (lax.broadcasted_iota(jnp.int32, (16, 8), 0) == 12 + c + 2 * (below - 6)),
        1.0, lift,
    ).astype(BF)
    for g in range(GROUPS):
        for t in range(3):
            at = t * D + g * GW
            both = jnp.concatenate(
                [w_qkv[:, at : at + GW].astype(F32), notes[:, t * GW : (t + 1) * GW]], axis=0
            ).astype(BF)
            wmsg[g, :, t * GW : (t + 1) * GW] = dot(lift, both, NN).astype(BF)
    arrive(expected + 9)
    push(wmsg, wo, send.at[0], core_recv.at[0], sib)
    for k in range(1, 4):
        push(tok, tok_s.at[z], send.at[1], recv.at[0], ((z + k) % 4, x, y, c))
    keep(tok, tok_s.at[z], recv.at[0])
    wait_bytes(wo, core_recv.at[0])
    wm[...] = wmsg[...] + wo[...]
    to_chips(
        z, x, y, c, lambda there: wm.at[there[0]], w_s.at[pl.ds(me, 16)], send.at[3], recv.at[1]
    )
    for k in range(1, 4):
        push(wa, wa_all.at[z, x, y, c], send.at[4], recv.at[2], ((z + k) % 4, x, y, c))

    expert = lax.broadcasted_iota(jnp.int32, (1, 64), 1)
    first = jnp.where(routes[:, 0:1] == expert, 1.0, 0.0)
    second = jnp.where(routes[:, 1:2] == expert, 1.0, 0.0)
    lower = jnp.where(
        lax.broadcasted_iota(jnp.int32, (TOK, TOK), 0)
        > lax.broadcasted_iota(jnp.int32, (TOK, TOK), 1), 1.0, 0.0,
    ).astype(BF)
    before = jnp.sum(first, axis=0, keepdims=True)
    rank_1 = jnp.sum(dot(lower, first.astype(BF), NN) * first, axis=1, keepdims=True)
    rank_2 = jnp.sum(
        (dot(lower, second.astype(BF), NN) + before) * second, axis=1, keepdims=True
    )
    slot = lax.broadcasted_iota(jnp.int32, (TOK, 1024), 1)
    g_rows = cotangent[...].astype(F32)
    gated = []
    for side, rank in enumerate((rank_1, rank_2)):
        e = routes[:, side : side + 1]
        block = ((e & 1) * 32 + (e >> 2) * 2 + ((e >> 1) & 1)) * 16 + 8 * c
        here = slot - block == rank.astype(jnp.int32)
        picks[side * TOK : (side + 1) * TOK, :] = jnp.where(here, 1.0, 0.0).astype(BF)
        gated.append((gates[:, side : side + 1] * g_rows).astype(BF))
    for n in range(0, 1024, WIDE):
        d_eo[n : n + WIDE, :] = (
            dot(picks[:TOK, n : n + WIDE], gated[0], TN)
            + dot(picks[TOK:, n : n + WIDE], gated[1], TN)
        ).astype(BF)
    push(d_eo.at[theirs], xo, send.at[2], core_recv.at[1], sib)

    row = lax.broadcasted_iota(jnp.int32, (1, 1024), 1)
    r, half, at = row & 15, row >> 9, (row >> 4) & 31
    row_z, row_x, row_y = at >> 3, (at >> 1) & 3, (at & 1) * 2 + half
    feature = jnp.where(r < 12, (row_z * 16 + row_x * 4 + row_y) * 12 + r, -1)
    select[...] = jnp.where(
        lax.broadcasted_iota(jnp.int32, (D, 1024), 0) == feature, 1.0, 0.0
    ).astype(BF)
    j = lax.broadcasted_iota(jnp.int32, (32, 1024), 0)
    gain_rows = (j < 4) & (r >> 1 == 6 + (j >> 1)) & (row_z >> 1 == j & 1)
    notes = (r == 12 + c) & (row_y == y)
    key_rows = (j >= 8) & (row_z * 4 + row_x == j - 8)
    query_rows = (j >= 24) & (row_z == j - 24) & (row_x == x)
    picker[...] = jnp.where(gain_rows | (notes & (key_rows | query_rows)), 1.0, 0.0).astype(BF)

    def tables(h):
        for dist in range(2):
            n = near_distance(dist)
            acc = jnp.full((TOK, TOK), tab[0, h], F32)
            for k, edge in enumerate(bucket_edges):
                acc = jnp.where(n >= edge, tab[k + 1, h], acc)
            bias[h, 1 + dist] = jnp.where(n >= 0, acc, masked)
        bias[h, 0] = jnp.full((TOK, TOK), masked, F32)
        bias[h, 3] = jnp.full((TOK, TOK), tab[BUCKETS - 1, h], F32)

    loop(0, GH, tables)
    wait_bytes(xo, core_recv.at[1])
    xo[...] = xo[...] + d_eo[mine, :]
    wait_bytes(w_s.at[mine], recv.at[1])
    push(w_s.at[mine], w_s.at[mine], send.at[5], core_recv.at[2], sib)
    wait_bytes(wa_all.at[z, x, y, c], own.at[0])
    wait_bytes(wa_all.at[pl.ds(0, 3), x, y, c], recv.at[2])
    for k in range(1, 4):
        push(
            wa_all.at[:, x, y, c], wa_all.at[:, x, y, c], send.at[6], recv.at[3],
            (z, (x + k) % 4, y, c),
        )
    wait_bytes(w_s.at[theirs], core_recv.at[2])
    picked = dot(picker[...], w_s[...], NN)
    gain = jnp.concatenate([picked[0:1, :384], picked[1:2, :384]], axis=1)
    gains[0:1, :] = gain
    gains[1:2, :] = jnp.concatenate([picked[2:3, :384], picked[3:4, :384]], axis=1)
    gains[2:8, :] = jnp.zeros((6, D), F32)
    kd[...] = picked[8:24, 384:512]
    qd[...] = picked[24:32, 384:512].T
    weight[...] = dot(select[...], w_s[...], NN).astype(BF)
    wait_bytes(tok_s, recv.at[0])
    for b in range(4):
        v = tok_s[b].astype(F32)
        normed[b * TOK : (b + 1) * TOK, :] = scale_rows(v, gain).astype(BF)
    qkv = dot(normed[...], weight[...], NN).astype(BF)
    q[...] = qkv[:, :GW]
    for b in range(4):
        kv[b] = qkv[b * TOK : (b + 1) * TOK, GW:]
    for k in range(1, 4):
        for b in range(4):
            push(
                kv.at[b], kv_s.at[block_cols(b, x)], send.at[7], kv_recv.at[4 - k],
                (z, (x + k) % 4, y, c),
            )
    for b in range(4):
        keep(kv.at[b], kv_s.at[block_cols(b, x)], kv_recv.at[0])
    wait_bytes(wa_all.at[:, pl.ds(0, 3), y, c], recv.at[3])
    for k in range(1, 4):
        push(
            wa_all.at[:, :, y, c], wa_all.at[:, :, y, c], send.at[8], recv.at[4],
            (z, x, (y + k) % 4, c),
        )
    for h in range(GH):
        head_cols = lax.broadcasted_iota(jnp.int32, (1, GW), 1) // HD == h
        qm[h] = jnp.where(head_cols, q[...] * 0.125, 0.0).astype(BF)
    for k in range(4):
        kx = (x + k) % 4
        if k == 0:
            for b in range(4):
                wait_bytes(kv_s.at[block_cols(b, kx)], kv_recv.at[0])
        else:
            wait_bytes(kv_s.at[pl.ds(0, 512)], kv_recv.at[k])
        for b in range(4):
            cols = block_cols(b, kx)
            v_s[cols, :] = kv_s[cols, GW:]
            for h in range(GH):
                s_s[h, b * TOK :, cols] = dot(qm[h, b * TOK :, :], kv_s[cols, :GW], NT)
    keep(kv_s, kv_out, own.at[1])
    to_chips(
        z, x, y, c,
        lambda there: xo.at[pl.ds(pl.multiple_of(block_of(*there[:3]) - c * 512, 16), 16)],
        d_rows.at[pl.ds(me, 16)], send.at[9], recv.at[5],
    )
    wait_bytes(wa_all.at[:, :, pl.ds(0, 3), c], recv.at[4])
    push(wa_all.at[:, :, :, c], wa_all.at[:, :, :, c], send.at[10], core_recv.at[3], sib)

    def head(h):
        head_cols = lax.broadcasted_iota(jnp.int32, (1, GW), 1) // HD == h
        far = tab[BUCKETS - 1, h]
        for zq in range(4):
            rows = pl.ds(zq * TOK, TOK)
            docs = qd[:, zq : zq + 1]
            top = None
            for zk in range(zq + 1):
                for kx in range(4):
                    cols = pl.ds((zk * 4 + kx) * TOK, TOK)
                    s = s_s[h, rows, cols]
                    if zk < zq - 1:
                        s = s + far
                    else:
                        s = s + bias[h, table_kind(zq, zk, x, kx)]
                    kb = zk * 4 + kx
                    s = jnp.where(docs == kd[kb : kb + 1, :], s, masked)
                    s_s[h, rows, cols] = s
                    top = s if top is None else jnp.maximum(top, s)
            top = jnp.max(top, axis=1, keepdims=True)
            total = jnp.zeros((TOK, TOK), F32)
            for kb in range(4 * (zq + 1)):
                cols = pl.ds(kb * TOK, TOK)
                e = jnp.exp(s_s[h, rows, cols] - top)
                s_s[h, rows, cols] = e
                total = total + e
            inv = 1.0 / jnp.sum(total, axis=1, keepdims=True)
            for kb in range(4 * (zq + 1)):
                cols = pl.ds(kb * TOK, TOK)
                p_s[h, rows, cols] = (s_s[h, rows, cols] * inv).astype(BF)
            width = (zq + 1) * 512
            o = dot(p_s[h, rows, :width], v_s[:width, :], NN).astype(BF)

            @pl.when(h == 0)
            def _():
                part[rows, :] = o

            @pl.when(h > 0)
            def _():
                part[rows, :] = jnp.where(head_cols, o, part[rows, :])

    loop(0, GH, head)
    for k in range(1, 4):
        there = (z + k) % 4
        push(
            part.at[pl.ds(pl.multiple_of(there * TOK, TOK), TOK)], attn_all.at[z],
            send.at[11], recv.at[6], (there, x, y, c),
        )
    keep(part.at[pl.ds(pl.multiple_of(z * TOK, TOK), TOK)], attn_all.at[z], recv.at[6])
    keep(p_s, p_out, own.at[2])
    wait_bytes(d_rows.at[mine], recv.at[5])
    push(d_rows.at[mine], d_rows.at[mine], send.at[12], core_recv.at[4], sib)
    wait_bytes(attn_all, recv.at[6])
    wait_bytes(wa_all.at[:, :, :, 1 - c], core_recv.at[3])
    wait_bytes(d_rows.at[theirs], core_recv.at[4])
    wait_bytes(kv_s, own.at[1])
    wait_bytes(p_s, own.at[2])
    wait_bytes(wo, send.at[0])
    wait_bytes(tok_s.at[pl.ds(0, 3)], send.at[1])
    wait_bytes(xo, send.at[2])
    sent_to_chips(w_s, y, c, send.at[3])
    wait_bytes(wa_all.at[pl.ds(0, 3), x, y, c], send.at[4])
    wait_bytes(w_s.at[mine], send.at[5])
    wait_bytes(wa_all.at[:, pl.ds(0, 3), y, c], send.at[6])
    wait_bytes(kv_s.at[pl.ds(0, 1536)], send.at[7])
    wait_bytes(wa_all.at[:, :, pl.ds(0, 3), c], send.at[8])
    sent_to_chips(d_rows, y, c, send.at[9])
    wait_bytes(wa_all.at[:, :, :, c], send.at[10])
    wait_bytes(attn_all.at[pl.ds(0, 3)], send.at[11])
    wait_bytes(d_rows.at[mine], send.at[12])


def attn_forward(*args):
    probs = (GH, 512, 2048)
    vm = pltpu.VMEM
    return pl.pallas_call(
        attn_forward_kernel,
        out_shape=(
            jax.ShapeDtypeStruct((4, TOK, GW), BF),
            jax.ShapeDtypeStruct((512, GW), BF),
            jax.ShapeDtypeStruct(probs, BF),
            jax.ShapeDtypeStruct((2048, 2 * GW), BF),
            jax.ShapeDtypeStruct((4, 4, 4, 2, 8, D), BF),
            jax.ShapeDtypeStruct((1024, D), BF),
            jax.ShapeDtypeStruct((512, D), BF),
            jax.ShapeDtypeStruct((D, 3 * GW), BF),
            jax.ShapeDtypeStruct((512, GW), BF),
            jax.ShapeDtypeStruct((8, D), F32),
            jax.ShapeDtypeStruct((2 * TOK, 1024), BF),
        ),
        in_specs=[SMEM] + [VMEM] * 7,
        out_specs=(ANY, VMEM, ANY, ANY, ANY, ANY, VMEM, VMEM, VMEM, VMEM, VMEM),
        scratch_shapes=[
            vm((1024, D), BF), vm((4, 16, 3 * GW), BF),
            vm((4, 16, 3 * GW), BF), vm((4, 16, 3 * GW), BF), vm((1024, 3 * GW), BF),
            vm((4, TOK, D), BF), vm((D, 1024), BF), vm((32, 1024), BF),
            vm((TOK, 8), F32), vm((16, TOK), F32),
            vm((4, TOK, 2 * GW), BF), vm((2048, 2 * GW), BF), vm((2048, GW), BF),
            vm((GH, 512, GW), BF), vm((GH, 4, TOK, TOK), F32), vm(probs, F32), vm(probs, BF),
            vm((512, D), BF),
            DMA((13,)), DMA((7,)), DMA((4,)), DMA((5,)), DMA((3,)),
        ],
        compiler_params=pltpu.CompilerParams(
            collective_id=2, has_side_effects=True, vmem_limit_bytes=48 * 2**20
        ),
        name="attn_forward",
    )(*args)


def attn_backward_kernel(
    p, q_at, kv_at, home_at, picks_at, middle_at, gains_at, cotangent_at, w_proj_at, weight_at,
    normed_at, attn_part_at, tok_at,
    input_grad, qkv_out, att_out, small_out,
    p_s, v_s, do_s, dm, qm, dp_s, ds_s, near, messages, parts, branch_all, dq, tab,
    d_qkv, n_part, normed_in, att_f, q_blk, q_sib, q_tot, q_in, a_blk, a_sib, a_tot, a_in,
    s_own, s_sib, s_tot, s_in, qkv_sum, att_sum, s_sum, d_attn, branch, d_middle,
    q, kv, home, picks, middle, gains, cotangent, w_proj, weight, normed, attn_part, tok,
    send, recv, core_recv, own, fetched,
):
    z, x, y, c = place()
    sib = (z, x, y, 1 - c)
    p16 = x * 4 + y
    p32 = p16 * 2 + c
    me = z * 32 + p32
    source = me // 4

    def peer(i):
        return z, (x + i // 4) % 4, (y + i % 4) % 4, c

    fetches = (
        (home_at, home), (picks_at, picks), (middle_at, middle), (gains_at, gains),
        (cotangent_at, cotangent), (w_proj_at, w_proj), (kv_at, kv), (q_at, q),
        (weight_at, weight), (normed_at, normed), (attn_part_at, attn_part), (tok_at, tok),
    )
    for k, (source_ref, target) in enumerate(fetches):
        keep(source_ref, target, fetched.at[k])
    keep(p, p_s, own.at[0])
    loop(1, 16, lambda i: signal(peer(i)))
    for k in range(1, 4):
        signal(((z + k) % 4, x, y, c))
    signal(sib)

    def greet(k):
        @pl.when(jnp.logical_not((k == z) & (source == p32)))
        def _():
            signal((k, source // 8, (source // 2) % 4, source % 2))

    loop(0, 4, greet)
    for k in range(6):
        wait_bytes(fetches[k][1], fetched.at[k])
    d_moe = dot(picks[:TOK, :], home[...], NN) + dot(picks[TOK:, :], home[...], NN)
    mid = middle[...]
    mid_r = lax.rsqrt(jnp.mean(mid * mid, axis=1, keepdims=True) + norm_eps)
    mid_unit = mid * mid_r
    s_own[...] = jnp.zeros_like(s_own)
    s_own[1:2, :] = jnp.sum(d_moe * mid_unit, axis=0, keepdims=True)
    d_mid_unit = d_moe * gains[1:2, :]
    d_mid = mid_r * (d_mid_unit - mid_unit * jnp.mean(d_mid_unit * mid_unit, axis=1, keepdims=True))
    d_mid = cotangent[...].astype(F32) + d_mid
    d_middle[...] = d_mid
    branch[...] = d_mid.astype(BF)
    for k in range(GROUPS):
        d_attn[k] = dot(branch[...], w_proj[GW * k : GW * (k + 1), :], NT).astype(BF)
    for k in range(6, 12):
        wait_bytes(fetches[k][1], fetched.at[k])
    v_s[...] = kv[:, GW:]
    for h in range(GH):
        head_cols = lax.broadcasted_iota(jnp.int32, (1, GW), 1) // HD == h
        qm[h] = jnp.where(head_cols, q[...] * 0.125, 0.0).astype(BF)
    arrive(15 + 3 + 1 + 4 - jnp.where(source == p32, 1, 0))
    for k in range(1, 4):
        there = (z + k) % 4
        push(d_attn.at[there], do_s.at[z], send.at[0], recv.at[0], (there, x, y, c))
    keep(d_attn.at[z], do_s.at[z], recv.at[0])
    z_rows = pl.ds(pl.multiple_of(z * TOK, TOK), TOK)
    for k in range(1, 4):
        push(branch, branch_all.at[z_rows], send.at[1], recv.at[1], ((z + k) % 4, x, y, c))
    keep(branch, branch_all.at[z_rows], recv.at[1])
    wait_bytes(do_s, recv.at[0])
    for h in range(GH):
        head_cols = lax.broadcasted_iota(jnp.int32, (1, GW), 1) // HD == h
        for b in range(4):
            dm[h, b * TOK : (b + 1) * TOK, :] = jnp.where(head_cols, do_s[b], 0.0).astype(BF)
    wait_bytes(p_s, own.at[0])

    def key_sums(left, right, m, pair):
        for k in (1, 2, 3, 0):
            kx = (x + k) % 4
            for b in (2 * pair, 2 * pair + 1):
                cols = block_cols(b, kx)
                total = None
                for h in range(GH):
                    one = dot(left[h, b * TOK :, cols], right[h, b * TOK :, :], TN)
                    total = one if total is None else total + one
                side = GW * (b % 2)
                messages[k, m, :, side : side + GW] = total.astype(BF)
            if k:
                push(messages.at[k, m], parts.at[x, m], send.at[2], recv.at[2], (z, kx, y, c))
            else:
                keep(messages.at[k, m], parts.at[x, m], recv.at[2])

    key_sums(p_s, dm, 0, 0)
    key_sums(p_s, dm, 1, 1)
    near[...] = jnp.zeros_like(near)

    def score_grads(zq):
        rows = pl.ds(zq * TOK, TOK)
        width = (zq + 1) * 512

        def head(h):
            head_cols = lax.broadcasted_iota(jnp.int32, (1, GW), 1) // HD == h
            dp_s[:, :width] = dot(dm[h, rows, :], v_s[:width, :], NT)
            acc = jnp.zeros((TOK, TOK), F32)
            for kb in range(4 * (zq + 1)):
                cols = pl.ds(kb * TOK, TOK)
                acc = acc + p_s[h, rows, cols].astype(F32) * dp_s[:, cols]
            delta = jnp.sum(acc, axis=1, keepdims=True)
            far = jnp.zeros((TOK, TOK), F32)
            for zk in range(zq + 1):
                for kx in range(4):
                    cols = pl.ds((zk * 4 + kx) * TOK, TOK)
                    ds = (p_s[h, rows, cols].astype(F32) * (dp_s[:, cols] - delta)).astype(BF)
                    ds_s[h, rows, cols] = ds
                    if zk < zq - 1:
                        far = far + ds.astype(F32)
                    else:
                        near[h, table_kind(zq, zk, x, kx)] += ds.astype(F32)
            if zq > 1:
                near[h, 3] += far
            o = (dot(ds_s[h, rows, :width], kv[:width, :GW], NN) * 0.125).astype(BF)

            @pl.when(h == 0)
            def _():
                dq[rows, :] = o

            @pl.when(h > 0)
            def _():
                dq[rows, :] = jnp.where(head_cols, o, dq[rows, :])

        loop(0, GH, head)

    score_grads(3)
    score_grads(2)
    key_sums(ds_s, qm, 3, 1)
    score_grads(1)
    score_grads(0)
    key_sums(ds_s, qm, 2, 0)

    def bucket_sums(h):
        for dist in range(2):
            n = near_distance(dist)
            held = near[h, 1 + dist]
            bounds = [-(10**6)] + bucket_edges + [10**6]
            for b in range(BUCKETS):
                low, high = bounds[b], bounds[b + 1]
                if high <= dist * TOK - TOK + 1 or low > dist * TOK + TOK - 1:
                    if dist == 0:
                        tab[h, b : b + 1, :] = jnp.zeros((1, TOK), F32)
                    continue
                inside = jnp.sum(
                    jnp.where((n >= low) & (n < high), held, 0.0), axis=0, keepdims=True
                )
                if dist == 0:
                    tab[h, b : b + 1, :] = inside
                else:
                    tab[h, b : b + 1, :] += inside
        tab[h, BUCKETS - 1 :, :] += jnp.sum(near[h, 3], axis=0, keepdims=True)

    loop(0, GH, bucket_sums)

    wait_bytes(branch_all, recv.at[1])
    att_f[0:GW, :] = dot(attn_part[...], branch_all[...], TN)
    att_f[GW:, :] = jnp.zeros((8, D), F32)
    for j in range(32):
        a_blk[j // 2, j % 2] = att_f[6 * j : 6 * j + 8, :].astype(BF)
    push(a_blk.at[:, 1 - c], a_sib, send.at[4], core_recv.at[1], sib)
    for h in range(GH):
        s_own[2:3, BUCKETS * h : BUCKETS * (h + 1)] = jnp.sum(tab[h].T, axis=0, keepdims=True)

    wait_bytes(a_sib, core_recv.at[1])

    def att_blocks(i):
        there = peer(i)
        j = there[1] * 4 + there[2]
        a_tot[j] = (a_blk[j, c].astype(F32) + a_sib[j].astype(F32)).astype(BF)
        push(a_tot.at[j], a_in.at[p16], send.at[6], recv.at[4], there)

    loop(1, 16, att_blocks)
    a_tot[p16] = (a_blk[p16, c].astype(F32) + a_sib[p16].astype(F32)).astype(BF)
    keep(a_tot.at[p16], a_in.at[p16], recv.at[4])

    wait_bytes(parts, recv.at[2])
    d_qkv[:, :GW] = dq[...]
    for b in range(4):
        rows = slice(b * TOK, (b + 1) * TOK)
        side = GW * (b % 2)
        for m, at in ((2 + b // 2, GW), (b // 2, 2 * GW)):
            total = parts[0, m, :, side : side + GW].astype(F32)
            for k in range(1, 4):
                total = total + parts[k, m, :, side : side + GW].astype(F32)
            d_qkv[rows, at : at + GW] = total.astype(BF)
    d_normed = dot(d_qkv[...], weight[...], NT)
    n_part[...] = d_normed.astype(BF)
    for k in range(1, 4):
        there = (z + k) % 4
        push(
            n_part.at[pl.ds(pl.multiple_of(there * TOK, TOK), TOK)], normed_in.at[z],
            send.at[3], recv.at[3], (there, x, y, c),
        )
    keep(n_part.at[z_rows], normed_in.at[z], recv.at[3])
    along = jnp.sum(d_normed * normed[...].astype(F32), axis=0, keepdims=True)
    s_own[0:1, :] = along / gains[0:1, :]
    push(s_own, s_sib, send.at[8], core_recv.at[2], sib)
    total = dot(normed[...], d_qkv[...], TN)
    for j in range(32):
        q_blk[j // 2, j % 2] = total[24 * j : 24 * j + 24].astype(BF)
    push(q_blk.at[:, 1 - c], q_sib, send.at[5], core_recv.at[0], sib)
    wait_bytes(s_sib, core_recv.at[2])
    s_tot[...] = s_own[...] + s_sib[...]
    loop(1, 16, lambda i: push(s_tot, s_in.at[p16], send.at[9], recv.at[6], peer(i)))
    keep(s_tot, s_in.at[p16], recv.at[6])
    wait_bytes(q_sib, core_recv.at[0])

    def qkv_blocks(i):
        there = peer(i)
        j = there[1] * 4 + there[2]
        q_tot[j] = (q_blk[j, c].astype(F32) + q_sib[j].astype(F32)).astype(BF)
        push(q_tot.at[j], q_in.at[p16], send.at[7], recv.at[5], there)

    loop(1, 16, qkv_blocks)
    q_tot[p16] = (q_blk[p16, c].astype(F32) + q_sib[p16].astype(F32)).astype(BF)
    keep(q_tot.at[p16], q_in.at[p16], recv.at[5])

    wait_bytes(s_in, recv.at[6])
    s_total = s_in[0]
    for k in range(1, 16):
        s_total = s_total + s_in[k]
    s_sum[...] = s_total
    for k in range(1, 4):
        push(s_sum, small_out.at[z], send.at[11], recv.at[8], ((z + k) % 4, x, y, c))
    keep(s_sum, small_out.at[z], recv.at[8])
    wait_bytes(q_in, recv.at[5])
    q_total = q_in[0].astype(F32)
    for k in range(1, 16):
        q_total = q_total + q_in[k].astype(F32)
    for k in range(4):
        qkv_sum[k, 0:6, :] = q_total[6 * k : 6 * k + 6]
        qkv_sum[k, 6:8, :] = jnp.zeros((2, 3 * GW), F32)

    def final(k):
        d = 4 * p32 + k

        @pl.when(d != me)
        def _():
            push(qkv_sum.at[k], qkv_out.at[z], send.at[10], recv.at[7], device_of(d))

        @pl.when(d == me)
        def _():
            keep(qkv_sum.at[k], qkv_out.at[z], recv.at[7])

    loop(0, 4, final)
    wait_bytes(a_in, recv.at[4])
    a_total = a_in[0].astype(F32)
    for k in range(1, 16):
        a_total = a_total + a_in[k].astype(F32)
    att_sum[...] = a_total
    keep(att_sum, att_out, own.at[1])
    wait_bytes(normed_in, recv.at[3])
    d_normed = normed_in[0].astype(F32)
    for k in range(1, 4):
        d_normed = d_normed + normed_in[k].astype(F32)
    v = tok[...].astype(F32)
    r = lax.rsqrt(jnp.mean(v * v, axis=1, keepdims=True) + norm_eps)
    unit = v * r
    d_unit = d_normed * gains[0:1, :]
    d_in = r * (d_unit - unit * jnp.mean(d_unit * unit, axis=1, keepdims=True))
    input_grad[...] = (d_middle[...] + d_in).astype(BF)

    wait_bytes(att_sum, own.at[1])
    wait_bytes(qkv_out, recv.at[7])
    wait_bytes(small_out, recv.at[8])
    wait_bytes(do_s.at[pl.ds(0, 3)], send.at[0])
    wait_bytes(branch_all.at[pl.ds(0, 3 * TOK)], send.at[1])
    wait_bytes(parts.at[pl.ds(0, 3)], send.at[2])
    wait_bytes(normed_in.at[pl.ds(0, 3)], send.at[3])
    wait_bytes(a_sib, send.at[4])
    wait_bytes(q_sib, send.at[5])
    wait_bytes(a_in.at[pl.ds(0, 15)], send.at[6])
    wait_bytes(q_in.at[pl.ds(0, 15)], send.at[7])
    wait_bytes(s_own, send.at[8])
    wait_bytes(s_in.at[pl.ds(0, 15)], send.at[9])

    def sent(k):
        @pl.when(4 * p32 + k != me)
        def _():
            wait_bytes(qkv_sum.at[0], send.at[10])

    loop(0, 4, sent)
    wait_bytes(small_out.at[pl.ds(0, 3)], send.at[11])


def attn_backward(p, *rest):
    probs = (GH, 512, 2048)
    vm = pltpu.VMEM
    return pl.pallas_call(
        attn_backward_kernel,
        out_shape=(
            jax.ShapeDtypeStruct((TOK, D), BF),
            jax.ShapeDtypeStruct((4, 8, 3 * GW), F32),
            jax.ShapeDtypeStruct((8, D), F32),
            jax.ShapeDtypeStruct((4, 8, D), F32),
        ),
        in_specs=[ANY] * (1 + len(rest)),
        out_specs=(VMEM, ANY, ANY, ANY),
        scratch_shapes=[
            vm(probs, BF), vm((2048, GW), BF), vm((4, TOK, GW), BF), vm((GH, 512, GW), BF),
            vm((GH, 512, GW), BF), vm((TOK, 2048), F32), vm(probs, BF), vm((GH, 4, TOK, TOK), F32),
            vm((4, 4, TOK, 2 * GW), BF), vm((4, 4, TOK, 2 * GW), BF), vm((512, D), BF),
            vm((512, GW), BF), vm((GH, BUCKETS, TOK), F32),
            vm((512, 3 * GW), BF), vm((512, D), BF), vm((4, TOK, D), BF), vm((GW + 8, D), F32),
            vm((16, 2, 24, 3 * GW), BF), vm((16, 24, 3 * GW), BF),
            vm((16, 24, 3 * GW), BF), vm((16, 24, 3 * GW), BF),
            vm((16, 2, 8, D), BF), vm((16, 8, D), BF), vm((16, 8, D), BF), vm((16, 8, D), BF),
            vm((8, D), F32), vm((8, D), F32), vm((8, D), F32), vm((16, 8, D), F32),
            vm((4, 8, 3 * GW), F32), vm((8, D), F32), vm((8, D), F32),
            vm((4, TOK, GW), BF), vm((TOK, D), BF), vm((TOK, D), F32),
            vm((512, GW), BF), vm((2048, 2 * GW), BF), vm((1024, D), BF), vm((2 * TOK, 1024), BF),
            vm((TOK, D), F32), vm((8, D), F32), vm((TOK, D), BF), vm((D, D), BF),
            vm((D, 3 * GW), BF), vm((512, D), BF), vm((512, GW), BF), vm((TOK, D), BF),
            DMA((12,)), DMA((9,)), DMA((3,)), DMA((2,)), DMA((12,)),
        ],
        compiler_params=pltpu.CompilerParams(
            collective_id=3, has_side_effects=True, vmem_limit_bytes=54 * 2**20
        ),
        name="attn_backward",
    )(p, *rest)


def per_device(
    tokens,
    gain_attn,
    w_qkv,
    w_attn_out,
    rel_table,
    gain_moe,
    w_in,
    w_out,
    expert_ids,
    gate_values,
    doc_ids,
    cotangent,
):
    z, x, y, c = place()
    own_tokens = tokens.reshape(TOK, D)
    grad_bf = cotangent.reshape(TOK, D)
    grad_out = grad_bf.astype(F32)

    gates = gate_values.reshape(TOK, 2)

    place_in = chip_of(z, x, y) * 2 + c
    lane = jnp.arange(3 * GW, dtype=jnp.int32)[None, :]
    both_gains = jnp.stack([gain_attn, gain_moe]).astype(F32)
    notes = jnp.concatenate(
        [
            jnp.zeros((2, 384), F32),
            jnp.pad(doc_ids.reshape(1, TOK).astype(F32), ((0, 1), (0, 0))),
            jnp.zeros((2, 64), F32),
        ],
        axis=1,
    )
    for k in range(6):
        notes = jnp.where(lane == (place_in % 64) * 6 + k, both_gains[:, k : k + 1], notes)
    out_slab = jnp.concatenate([w_attn_out, jnp.zeros((2, D), BF)], axis=0)
    table = lax.dynamic_slice(rel_table, (0, z * GH), (BUCKETS, GH)).astype(F32)
    (
        attn, attn_part, probs, kv_all, out_weights, d_eo_all, normed, weight, queries, gain_rows,
        picks,
    ) = attn_forward(
        table, own_tokens, w_qkv, notes, out_slab, expert_ids.reshape(TOK, 2), gates, grad_bf
    )
    attention_weight = out_weights[:, :, :, :, :6, :].reshape(D, D)
    home, expert_out, expert_in_grad, expert_out_grad, middle = run_experts(
        attn, attention_weight, own_tokens, gain_rows, picks, d_eo_all, w_in[0], w_out[0]
    )
    input_grad, qkv_sum, att_sum, small_sum = attn_backward(
        probs, queries, kv_all, home, picks, middle, gain_rows, grad_bf, attention_weight, weight,
        normed, attn_part, own_tokens,
    )

    picked = dot(picks, expert_out, NN).reshape(2, TOK, D)
    block_out = middle + gates[:, :1] * picked[0] + gates[:, 1:] * picked[1]
    gate_grad = jnp.sum(picked * grad_out[None], axis=2).T

    qkv_grad = qkv_sum[:, :6, :].reshape(GROUPS, 6, 3, GW).transpose(1, 2, 0, 3).reshape(6, 3 * D)
    attn_out_grad = att_sum[:6]
    gains = lax.dynamic_slice(jnp.sum(small_sum[:, :2, :], axis=0), (0, place_in * 6), (2, 6))
    table_grad = small_sum[:, 2, : GH * BUCKETS].reshape(GROUPS * GH, BUCKETS).T
    return (
        block_out.reshape(1, TOK, D).astype(BF),
        input_grad.reshape(1, TOK, D),
        gate_grad.reshape(1, TOK, 2),
        gains[0],
        qkv_grad,
        attn_out_grad,
        table_grad,
        gains[1],
        expert_in_grad[None],
        expert_out_grad[None],
    )


def solution(mesh):
    torus = Mesh(mesh.devices.reshape(4, 4, 4, 2), AXES)
    in_specs = (
        P(EXP, CTX, None),
        P(AXES),
        P(AXES, None),
        P(AXES, None),
        P(),
        P(AXES),
        P(AXES, None, None),
        P(AXES, None, None),
        P(EXP, CTX, None),
        P(EXP, CTX, None),
        P(EXP, CTX),
        P(EXP, CTX, None),
    )
    out_specs = (
        P(EXP, CTX, None),
        P(EXP, CTX, None),
        P(EXP, CTX, None),
        P(AXES),
        P(AXES, None),
        P(AXES, None),
        P(),
        P(AXES),
        P(AXES, None, None),
        P(AXES, None, None),
    )
    return jax.shard_map(
        per_device, mesh=torus, in_specs=in_specs, out_specs=out_specs, check_vma=False
    )
```

```python
import functools

import jax
import jax.numpy as jnp
import numpy as np
from jax import lax
from jax.experimental import pallas as pl
from jax.experimental.pallas import tpu as pltpu
from jax.sharding import Mesh
from jax.sharding import PartitionSpec as P

D = 768
H = 12
HD = 64
BUCKETS = 32
GROUPS = 4
GH = H // GROUPS
GW = GH * HD
TOK = 128
CTX = ("ctx_0", "ctx_1")
EXP = ("exp_0", "exp_1")
AXES = ("ctx_0", "ctx_1", "exp_0", "exp_1")
MESH = pl.DeviceIdType.MESH
ANY = pl.BlockSpec(memory_space=pl.ANY)
HBM = pl.BlockSpec(memory_space=pltpu.HBM)
BF = jnp.bfloat16
F32 = jnp.float32

norm_eps = 1e-06
bucket_edges = [int(e) for e in np.concatenate(
    [np.arange(1, 17), np.ceil(16.0 * 8.0 ** (np.arange(1, 16) / 16.0))]
).astype(np.int32)]
masked = -1e30


def scale_rows(values, gain):
    return values * lax.rsqrt(jnp.mean(values * values, axis=-1, keepdims=True) + norm_eps) * gain


def place():
    return tuple(lax.axis_index(a) for a in AXES)


def chip_of(z, x, y):
    return (z * 4 + x) * 4 + y


def chip_peer(i, z, x, y):
    return (z + i // 16) % 4, (x + (i // 4) % 4) % 4, (y + i % 4) % 4


def loop(first, last, body):
    lax.fori_loop(first, last, lambda i, carry: (body(i), carry)[1], 0)


def signal(device):
    pl.semaphore_signal(
        pltpu.get_barrier_semaphore(), inc=1, device_id=device, device_id_type=MESH
    )


def arrive(count):
    pl.semaphore_wait(pltpu.get_barrier_semaphore(), count)


def push(src, dst, send, recv, device):
    pltpu.make_async_remote_copy(
        src_ref=src, dst_ref=dst, send_sem=send, recv_sem=recv, device_id=device, device_id_type=MESH
    ).start()


def keep(src, dst, sem):
    pltpu.make_async_copy(src, dst, sem).start()


def wait_bytes(ref, sem):
    pltpu.make_async_copy(ref, ref, sem).wait()


def comm_call(kernel, outs, scratch, collective_id, name):
    return pl.pallas_call(
        kernel,
        out_shape=outs,
        in_specs=None,
        out_specs=jax.tree.map(lambda _: ANY, outs),
        scratch_shapes=scratch,
        compiler_params=pltpu.CompilerParams(
            collective_id=collective_id, has_side_effects=True, vmem_limit_bytes=32 * 2**20
        ),
        name=name,
    )


def run_comm(kernel, args, outs, scratch, collective_id, name):
    return pl.pallas_call(
        kernel,
        out_shape=outs,
        in_specs=[ANY] * len(args),
        out_specs=jax.tree.map(lambda _: ANY, outs),
        scratch_shapes=scratch,
        compiler_params=pltpu.CompilerParams(
            collective_id=collective_id, has_side_effects=True, vmem_limit_bytes=32 * 2**20
        ),
        name=name,
    )(*args)


DMA = pltpu.SemaphoreType.DMA


def half_peer(i, z, x, y, c):
    return (z + i // 8) % 4, (x + (i // 2) % 4) % 4, c + 2 * ((y // 2 + i % 2) % 2), y % 2


def block_of(z, x, y):
    return pl.multiple_of((y % 2) * 512 + ((z * 4 + x) * 2 + y // 2) * 16, 16)


def greet_chips(z, x, y, c):
    loop(1, 32, lambda i: signal(half_peer(i, z, x, y, c)))

    @pl.when(y % 2 != c)
    def _():
        signal(half_peer(0, z, x, y, c))

    signal((z, x, y, 1 - c))
    return 32 + jnp.where(y % 2 == c, 0, 1)


def to_chips(z, x, y, c, source, target, send, recv):
    def one(i):
        there = half_peer(i, z, x, y, c)
        push(source(there), target, send, recv, there)

    loop(1, 32, one)
    first = half_peer(0, z, x, y, c)

    @pl.when(y % 2 == c)
    def _():
        keep(source(first), target, recv)

    @pl.when(y % 2 != c)
    def _():
        push(source(first), target, send, recv, first)


def sent_to_chips(rows, y, c, send):
    wait_bytes(rows.at[pl.ds(0, 496)], send)

    @pl.when(y % 2 != c)
    def _():
        wait_bytes(rows.at[pl.ds(0, 16)], send)


FH = 1536
WIDE = 256


def experts_kernel(
    attn_at, w_proj_at, tok_at, gains_at, picks_at, d_rows, w_in, w_out,
    home_in, home_out, g_in, g_out, middle_out,
    middle, attn, w_proj, tok, gains, picks, x16, xo, rows, dv, w1, w2, dh, hidden, dact, in_h, out_h, in_o, out_o, stage_out, stage_in,
    send, recv, core_recv, own, staged, fetched,
):
    z, x, y, c = place()
    sib = (z, x, y, 1 - c)
    at_mine = pl.multiple_of(c * 512, 512)
    at_theirs = pl.multiple_of((1 - c) * 512, 512)
    mine, theirs = pl.ds(at_mine, 512), pl.ds(at_theirs, 512)
    me = block_of(z, x, y)
    fetches = (
        (attn_at, attn), (w_proj_at, w_proj), (tok_at, tok), (gains_at, gains), (picks_at, picks)
    )
    for k, (source, target) in enumerate(fetches):
        keep(source, target, fetched.at[k])
    keep(d_rows, dv, own.at[1])
    keep(w_out, w2, own.at[2])
    keep(w_in, w1, own.at[3])
    expected = greet_chips(z, x, y, c)
    for k, (_, target) in enumerate(fetches):
        wait_bytes(target, fetched.at[k])
    total = tok[...].astype(F32)
    for k in range(GROUPS):
        total = total + dot(attn[k], w_proj[GW * k : GW * (k + 1), :], NN)
    middle[...] = total
    keep(middle, middle_out, own.at[0])
    moe_in = scale_rows(total, gains[1:2, :]).astype(BF)
    for n in range(0, 1024, WIDE):
        x16[n : n + WIDE, :] = (
            dot(picks[:TOK, n : n + WIDE], moe_in, TN) + dot(picks[TOK:, n : n + WIDE], moe_in, TN)
        ).astype(BF)
    arrive(expected)
    push(x16.at[theirs], xo, send.at[0], core_recv.at[0], sib)
    wait_bytes(xo, core_recv.at[0])
    xo[...] = xo[...] + x16[mine, :]
    to_chips(
        z, x, y, c,
        lambda there: xo.at[pl.ds(pl.multiple_of(block_of(*there[:3]) - c * 512, 16), 16)],
        rows.at[pl.ds(me, 16)], send.at[1], recv.at[0],
    )
    wait_bytes(dv, own.at[1])
    wait_bytes(w2, own.at[2])

    def hidden_grads(n):
        cols = pl.ds(pl.multiple_of(n * WIDE, WIDE), WIDE)
        dh[:, cols] = dot(dv[...], w2[cols, :], NT)

    loop(0, FH // WIDE, hidden_grads)
    wait_bytes(w1, own.at[3])
    wait_bytes(rows.at[mine], recv.at[0])
    push(rows.at[mine], rows.at[mine], send.at[2], core_recv.at[1], sib)

    def activate(at):
        part = pl.ds(at, 512)

        def one(n):
            cols = pl.ds(pl.multiple_of(n * WIDE, WIDE), WIDE)
            a = dot(rows[part, :], w1[:, cols], NN)
            square = a * a
            t = jnp.tanh(0.7978845608028654 * (a + 0.044715 * (square * a)))
            cdf = 0.5 * (1.0 + t)
            hidden[part, cols] = (a * cdf).astype(BF)
            slope = cdf + 0.5 * a * (1.0 - t * t) * (
                0.7978845608028654 * (1.0 + 0.134145 * square)
            )
            dact[part, cols] = (slope * dh[part, cols]).astype(BF)

        loop(0, FH // WIDE, one)

    def in_half(at):
        part = pl.ds(at, 512)

        def one(n):
            cols = pl.ds(pl.multiple_of(n * WIDE, WIDE), WIDE)
            in_h[part, cols] = dot(dact[part, :], w1[cols, :], NT).astype(BF)

        loop(0, D // WIDE, one)

    def out_half(at):
        part = pl.ds(at, 512)

        def one(n):
            cols = pl.ds(pl.multiple_of(n * WIDE, WIDE), WIDE)
            out_h[part, cols] = dot(hidden[part, :], w2[:, cols], NN).astype(BF)

        loop(0, D // WIDE, one)

    activate(at_mine)
    wait_bytes(rows.at[theirs], core_recv.at[1])
    activate(at_theirs)
    in_half(at_theirs)
    push(in_h.at[theirs], in_o, send.at[3], core_recv.at[2], sib)
    in_half(at_mine)
    wait_bytes(in_o, core_recv.at[2])
    in_o[...] = (in_o[...].astype(F32) + in_h[mine, :].astype(F32)).astype(BF)
    to_chips(
        z, x, y, c,
        lambda there: in_o.at[pl.ds(pl.multiple_of(block_of(*there[:3]) - c * 512, 16), 16)],
        home_in.at[pl.ds(me, 16)], send.at[4], recv.at[1],
    )
    out_half(at_theirs)
    push(out_h.at[theirs], out_o, send.at[5], core_recv.at[3], sib)
    out_half(at_mine)
    wait_bytes(out_o, core_recv.at[3])
    out_o[...] = (out_o[...].astype(F32) + out_h[mine, :].astype(F32)).astype(BF)
    to_chips(
        z, x, y, c,
        lambda there: out_o.at[pl.ds(pl.multiple_of(block_of(*there[:3]) - c * 512, 16), 16)],
        home_out.at[pl.ds(me, 16)], send.at[6], recv.at[2],
    )

    def out_grads(n):
        cols = pl.ds(pl.multiple_of(n * WIDE, WIDE), WIDE)
        slot = n % 2

        @pl.when(n >= 2)
        def _():
            wait_bytes(stage_out.at[slot], staged.at[slot])

        stage_out[slot] = dot(hidden[:, cols], dv[...], TN)
        keep(stage_out.at[slot], g_out.at[cols], staged.at[slot])

    loop(0, FH // WIDE, out_grads)
    wait_bytes(home_in.at[mine], recv.at[1])
    push(home_in.at[mine], home_in.at[mine], send.at[7], core_recv.at[4], sib)

    def in_grads(n):
        cols = pl.ds(pl.multiple_of(n * WIDE, WIDE), WIDE)
        slot = n % 2

        @pl.when(n >= 2)
        def _():
            wait_bytes(stage_in.at[slot], staged.at[2 + slot])

        stage_in[slot] = dot(rows[:, cols], dact[...], TN)
        keep(stage_in.at[slot], g_in.at[cols], staged.at[2 + slot])

    loop(0, D // WIDE, in_grads)
    wait_bytes(home_out.at[mine], recv.at[2])
    push(home_out.at[mine], home_out.at[mine], send.at[8], core_recv.at[5], sib)
    for slot in range(2):
        wait_bytes(stage_out.at[slot], staged.at[slot])
        wait_bytes(stage_in.at[slot], staged.at[2 + slot])
    wait_bytes(xo, send.at[0])
    sent_to_chips(rows, y, c, send.at[1])
    wait_bytes(rows.at[mine], send.at[2])
    wait_bytes(in_o, send.at[3])
    sent_to_chips(home_in, y, c, send.at[4])
    wait_bytes(out_o, send.at[5])
    sent_to_chips(home_out, y, c, send.at[6])
    wait_bytes(home_in.at[theirs], core_recv.at[4])
    wait_bytes(home_out.at[theirs], core_recv.at[5])
    wait_bytes(home_in.at[mine], send.at[7])
    wait_bytes(home_out.at[mine], send.at[8])
    wait_bytes(middle, own.at[0])


def run_experts(*args):
    whole_rows = pltpu.VMEM((1024, D), BF)
    half_rows = pltpu.VMEM((512, D), BF)
    hid = pltpu.VMEM((1024, FH), BF)
    return pl.pallas_call(
        experts_kernel,
        out_shape=(
            jax.ShapeDtypeStruct((1024, D), BF),
            jax.ShapeDtypeStruct((1024, D), BF),
            jax.ShapeDtypeStruct((D, FH), F32),
            jax.ShapeDtypeStruct((FH, D), F32),
            jax.ShapeDtypeStruct((TOK, D), F32),
        ),
        in_specs=[HBM, ANY] + [HBM] * 6,
        out_specs=(HBM,) * 5,
        scratch_shapes=[
            pltpu.VMEM((TOK, D), F32),
            pltpu.VMEM((4, TOK, GW), BF), pltpu.VMEM((D, D), BF), pltpu.VMEM((TOK, D), BF),
            pltpu.VMEM((8, D), F32), pltpu.VMEM((2 * TOK, 1024), BF),
            whole_rows, half_rows, whole_rows, whole_rows,
            pltpu.VMEM((D, FH), BF), pltpu.VMEM((FH, D), BF), pltpu.VMEM((1024, FH), F32),
            hid, hid, whole_rows, whole_rows, half_rows, half_rows,
            pltpu.VMEM((2, WIDE, D), F32), pltpu.VMEM((2, WIDE, FH), F32),
            DMA((9,)), DMA((3,)), DMA((6,)), DMA((4,)), DMA((4,)), DMA((5,)),
        ],
        compiler_params=pltpu.CompilerParams(
            collective_id=1, has_side_effects=True, vmem_limit_bytes=63 * 2**20
        ),
        name="experts",
    )(*args)


def device_of(d):
    return d // 32, (d // 8) % 4, (d // 2) % 4, d % 2


NT = (((1,), (1,)), ((), ()))
NN = (((1,), (0,)), ((), ()))
TN = (((0,), (0,)), ((), ()))


def dot(a, b, dims):
    return lax.dot_general(a, b, dims, preferred_element_type=F32)


def near_distance(dist):
    a = lax.broadcasted_iota(jnp.int32, (TOK, TOK), 0)
    b = lax.broadcasted_iota(jnp.int32, (TOK, TOK), 1)
    return dist * TOK + a - b


def table_kind(zq, zk, x, kx):
    return jnp.clip((zq - zk) * 4 + x - kx + 1, 0, 3)


def block_cols(zk, kx):
    return pl.ds(pl.multiple_of((zk * 4 + kx) * TOK, TOK), TOK)


VMEM = pl.BlockSpec(memory_space=pltpu.VMEM)
SMEM = pl.BlockSpec(memory_space=pltpu.SMEM)


def attn_forward_kernel(
    tab, tok, w_qkv, notes, wa, routes, gates, cotangent_at,
    attn_all, part_out, p_out, kv_out, wa_all, d_rows, normed_out, weight_out, q_out, gains_out,
    picks_out, part, normed, weight, q, gains, picks, cotangent, d_eo, wmsg, wm, wo, w_s, tok_s, select, picker, qd, kd,
    kv, kv_s, v_s, qm, bias, s_s, p_s, xo,
    send, recv, kv_recv, core_recv, own,
):
    z, x, y, c = place()
    sib = (z, x, y, 1 - c)
    mine = pl.ds(pl.multiple_of(c * 512, 512), 512)
    theirs = pl.ds(pl.multiple_of((1 - c) * 512, 512), 512)
    me = block_of(z, x, y)
    keep(wa, wa_all.at[z, x, y, c], own.at[0])
    keep(cotangent_at, cotangent, own.at[3])
    expected = greet_chips(z, x, y, c)
    for k in range(1, 4):
        signal(((z + k) % 4, x, y, c))
        signal((z, (x + k) % 4, y, c))
        signal((z, x, (y + k) % 4, c))
    lift = lax.broadcasted_iota(jnp.int32, (16, 8), 0)
    below = lax.broadcasted_iota(jnp.int32, (16, 8), 1)
    lift = jnp.where((lift == 6 * c + below) & (below < 6), 1.0, 0.0)
    lift = jnp.where(
        (below >= 6) & (lax.broadcasted_iota(jnp.int32, (16, 8), 0) == 12 + c + 2 * (below - 6)),
        1.0, lift,
    ).astype(BF)
    for g in range(GROUPS):
        for t in range(3):
            at = t * D + g * GW
            both = jnp.concatenate(
                [w_qkv[:, at : at + GW].astype(F32), notes[:, t * GW : (t + 1) * GW]], axis=0
            ).astype(BF)
            wmsg[g, :, t * GW : (t + 1) * GW] = dot(lift, both, NN).astype(BF)
    arrive(expected + 9)
    push(wmsg, wo, send.at[0], core_recv.at[0], sib)
    for k in range(1, 4):
        push(tok, tok_s.at[z], send.at[1], recv.at[0], ((z + k) % 4, x, y, c))
    keep(tok, tok_s.at[z], recv.at[0])
    wait_bytes(wo, core_recv.at[0])
    wm[...] = wmsg[...] + wo[...]
    to_chips(
        z, x, y, c, lambda there: wm.at[there[0]], w_s.at[pl.ds(me, 16)], send.at[3], recv.at[1]
    )
    for k in range(1, 4):
        push(wa, wa_all.at[z, x, y, c], send.at[4], recv.at[2], ((z + k) % 4, x, y, c))

    expert = lax.broadcasted_iota(jnp.int32, (1, 64), 1)
    first = jnp.where(routes[:, 0:1] == expert, 1.0, 0.0)
    second = jnp.where(routes[:, 1:2] == expert, 1.0, 0.0)
    lower = jnp.where(
        lax.broadcasted_iota(jnp.int32, (TOK, TOK), 0)
        > lax.broadcasted_iota(jnp.int32, (TOK, TOK), 1), 1.0, 0.0,
    ).astype(BF)
    before = jnp.sum(first, axis=0, keepdims=True)
    rank_1 = jnp.sum(dot(lower, first.astype(BF), NN) * first, axis=1, keepdims=True)
    rank_2 = jnp.sum(
        (dot(lower, second.astype(BF), NN) + before) * second, axis=1, keepdims=True
    )
    slot = lax.broadcasted_iota(jnp.int32, (TOK, 1024), 1)
    wait_bytes(cotangent, own.at[3])
    g_rows = cotangent[...].astype(F32)
    gated = []
    for side, rank in enumerate((rank_1, rank_2)):
        e = routes[:, side : side + 1]
        block = ((e & 1) * 32 + (e >> 2) * 2 + ((e >> 1) & 1)) * 16 + 8 * c
        here = slot - block == rank.astype(jnp.int32)
        picks[side * TOK : (side + 1) * TOK, :] = jnp.where(here, 1.0, 0.0).astype(BF)
        gated.append((gates[:, side : side + 1] * g_rows).astype(BF))
    for n in range(0, 1024, WIDE):
        d_eo[n : n + WIDE, :] = (
            dot(picks[:TOK, n : n + WIDE], gated[0], TN)
            + dot(picks[TOK:, n : n + WIDE], gated[1], TN)
        ).astype(BF)
    push(d_eo.at[theirs], xo, send.at[2], core_recv.at[1], sib)
    keep(picks, picks_out, own.at[4])

    row = lax.broadcasted_iota(jnp.int32, (1, 1024), 1)
    r, half, at = row & 15, row >> 9, (row >> 4) & 31
    row_z, row_x, row_y = at >> 3, (at >> 1) & 3, (at & 1) * 2 + half
    feature = jnp.where(r < 12, (row_z * 16 + row_x * 4 + row_y) * 12 + r, -1)
    select[...] = jnp.where(
        lax.broadcasted_iota(jnp.int32, (D, 1024), 0) == feature, 1.0, 0.0
    ).astype(BF)
    j = lax.broadcasted_iota(jnp.int32, (32, 1024), 0)
    gain_rows = (j < 4) & (r >> 1 == 6 + (j >> 1)) & (row_z >> 1 == j & 1)
    notes = (r == 12 + c) & (row_y == y)
    key_rows = (j >= 8) & (row_z * 4 + row_x == j - 8)
    query_rows = (j >= 24) & (row_z == j - 24) & (row_x == x)
    picker[...] = jnp.where(gain_rows | (notes & (key_rows | query_rows)), 1.0, 0.0).astype(BF)

    def tables(h):
        for dist in range(2):
            n = near_distance(dist)
            acc = jnp.full((TOK, TOK), tab[0, h], F32)
            for k, edge in enumerate(bucket_edges):
                acc = jnp.where(n >= edge, tab[k + 1, h], acc)
            bias[h, 1 + dist] = jnp.where(n >= 0, acc, masked)
        bias[h, 0] = jnp.full((TOK, TOK), masked, F32)
        bias[h, 3] = jnp.full((TOK, TOK), tab[BUCKETS - 1, h], F32)

    loop(0, GH, tables)
    wait_bytes(xo, core_recv.at[1])
    xo[...] = xo[...] + d_eo[mine, :]
    wait_bytes(w_s.at[mine], recv.at[1])
    push(w_s.at[mine], w_s.at[mine], send.at[5], core_recv.at[2], sib)
    wait_bytes(wa_all.at[z, x, y, c], own.at[0])
    wait_bytes(wa_all.at[pl.ds(0, 3), x, y, c], recv.at[2])
    for k in range(1, 4):
        push(
            wa_all.at[:, x, y, c], wa_all.at[:, x, y, c], send.at[6], recv.at[3],
            (z, (x + k) % 4, y, c),
        )
    wait_bytes(w_s.at[theirs], core_recv.at[2])
    picked = dot(picker[...], w_s[...], NN)
    gain = jnp.concatenate([picked[0:1, :384], picked[1:2, :384]], axis=1)
    gains[0:1, :] = gain
    gains[1:2, :] = jnp.concatenate([picked[2:3, :384], picked[3:4, :384]], axis=1)
    gains[2:8, :] = jnp.zeros((6, D), F32)
    kd[...] = picked[8:24, 384:512]
    qd[...] = picked[24:32, 384:512].T
    weight[...] = dot(select[...], w_s[...], NN).astype(BF)
    wait_bytes(tok_s, recv.at[0])
    for b in range(4):
        v = tok_s[b].astype(F32)
        normed[b * TOK : (b + 1) * TOK, :] = scale_rows(v, gain).astype(BF)
    qkv = dot(normed[...], weight[...], NN).astype(BF)
    q[...] = qkv[:, :GW]
    for b in range(4):
        kv[b] = qkv[b * TOK : (b + 1) * TOK, GW:]
    results = ((normed, normed_out), (weight, weight_out), (q, q_out), (gains, gains_out))
    for k in range(1, 4):
        for b in range(4):
            push(
                kv.at[b], kv_s.at[block_cols(b, x)], send.at[7], kv_recv.at[4 - k],
                (z, (x + k) % 4, y, c),
            )
    for b in range(4):
        keep(kv.at[b], kv_s.at[block_cols(b, x)], kv_recv.at[0])
    for k, (source, target) in enumerate(results):
        keep(source, target, own.at[5 + k])
    wait_bytes(wa_all.at[:, pl.ds(0, 3), y, c], recv.at[3])
    for k in range(1, 4):
        push(
            wa_all.at[:, :, y, c], wa_all.at[:, :, y, c], send.at[8], recv.at[4],
            (z, x, (y + k) % 4, c),
        )
    for h in range(GH):
        head_cols = lax.broadcasted_iota(jnp.int32, (1, GW), 1) // HD == h
        qm[h] = jnp.where(head_cols, q[...] * 0.125, 0.0).astype(BF)
    for k in range(4):
        kx = (x + k) % 4
        if k == 0:
            for b in range(4):
                wait_bytes(kv_s.at[block_cols(b, kx)], kv_recv.at[0])
        else:
            wait_bytes(kv_s.at[pl.ds(0, 512)], kv_recv.at[k])
        for b in range(4):
            cols = block_cols(b, kx)
            v_s[cols, :] = kv_s[cols, GW:]
            for h in range(GH):
                s_s[h, b * TOK :, cols] = dot(qm[h, b * TOK :, :], kv_s[cols, :GW], NT)
    keep(kv_s, kv_out, own.at[1])
    to_chips(
        z, x, y, c,
        lambda there: xo.at[pl.ds(pl.multiple_of(block_of(*there[:3]) - c * 512, 16), 16)],
        d_rows.at[pl.ds(me, 16)], send.at[9], recv.at[5],
    )
    wait_bytes(wa_all.at[:, :, pl.ds(0, 3), c], recv.at[4])
    push(wa_all.at[:, :, :, c], wa_all.at[:, :, :, c], send.at[10], core_recv.at[3], sib)

    def head(h):
        head_cols = lax.broadcasted_iota(jnp.int32, (1, GW), 1) // HD == h
        far = tab[BUCKETS - 1, h]
        for zq in range(4):
            rows = pl.ds(zq * TOK, TOK)
            docs = qd[:, zq : zq + 1]
            top = None
            for zk in range(zq + 1):
                for kx in range(4):
                    cols = pl.ds((zk * 4 + kx) * TOK, TOK)
                    s = s_s[h, rows, cols]
                    if zk < zq - 1:
                        s = s + far
                    else:
                        s = s + bias[h, table_kind(zq, zk, x, kx)]
                    kb = zk * 4 + kx
                    s = jnp.where(docs == kd[kb : kb + 1, :], s, masked)
                    s_s[h, rows, cols] = s
                    top = s if top is None else jnp.maximum(top, s)
            top = jnp.max(top, axis=1, keepdims=True)
            total = jnp.zeros((TOK, TOK), F32)
            for kb in range(4 * (zq + 1)):
                cols = pl.ds(kb * TOK, TOK)
                e = jnp.exp(s_s[h, rows, cols] - top)
                s_s[h, rows, cols] = e
                total = total + e
            inv = 1.0 / jnp.sum(total, axis=1, keepdims=True)
            for kb in range(4 * (zq + 1)):
                cols = pl.ds(kb * TOK, TOK)
                p_s[h, rows, cols] = (s_s[h, rows, cols] * inv).astype(BF)
            width = (zq + 1) * 512
            o = dot(p_s[h, rows, :width], v_s[:width, :], NN).astype(BF)

            @pl.when(h == 0)
            def _():
                part[rows, :] = o

            @pl.when(h > 0)
            def _():
                part[rows, :] = jnp.where(head_cols, o, part[rows, :])

    loop(0, GH, head)
    for k in range(1, 4):
        there = (z + k) % 4
        push(
            part.at[pl.ds(pl.multiple_of(there * TOK, TOK), TOK)], attn_all.at[z],
            send.at[11], recv.at[6], (there, x, y, c),
        )
    keep(part.at[pl.ds(pl.multiple_of(z * TOK, TOK), TOK)], attn_all.at[z], recv.at[6])
    keep(p_s, p_out, own.at[2])
    keep(part, part_out, own.at[9])
    wait_bytes(d_rows.at[mine], recv.at[5])
    push(d_rows.at[mine], d_rows.at[mine], send.at[12], core_recv.at[4], sib)
    wait_bytes(attn_all, recv.at[6])
    wait_bytes(wa_all.at[:, :, :, 1 - c], core_recv.at[3])
    wait_bytes(d_rows.at[theirs], core_recv.at[4])
    wait_bytes(kv_s, own.at[1])
    wait_bytes(p_s, own.at[2])
    wait_bytes(picks, own.at[4])
    for k, (source, _) in enumerate(results):
        wait_bytes(source, own.at[5 + k])
    wait_bytes(part, own.at[9])
    wait_bytes(wo, send.at[0])
    wait_bytes(tok_s.at[pl.ds(0, 3)], send.at[1])
    wait_bytes(xo, send.at[2])
    sent_to_chips(w_s, y, c, send.at[3])
    wait_bytes(wa_all.at[pl.ds(0, 3), x, y, c], send.at[4])
    wait_bytes(w_s.at[mine], send.at[5])
    wait_bytes(wa_all.at[:, pl.ds(0, 3), y, c], send.at[6])
    wait_bytes(kv_s.at[pl.ds(0, 1536)], send.at[7])
    wait_bytes(wa_all.at[:, :, pl.ds(0, 3), c], send.at[8])
    sent_to_chips(d_rows, y, c, send.at[9])
    wait_bytes(wa_all.at[:, :, :, c], send.at[10])
    wait_bytes(attn_all.at[pl.ds(0, 3)], send.at[11])
    wait_bytes(d_rows.at[mine], send.at[12])


def attn_forward(*args):
    probs = (GH, 512, 2048)
    vm = pltpu.VMEM
    return pl.pallas_call(
        attn_forward_kernel,
        out_shape=(
            jax.ShapeDtypeStruct((4, TOK, GW), BF),
            jax.ShapeDtypeStruct((512, GW), BF),
            jax.ShapeDtypeStruct(probs, BF),
            jax.ShapeDtypeStruct((2048, 2 * GW), BF),
            jax.ShapeDtypeStruct((4, 4, 4, 2, 8, D), BF),
            jax.ShapeDtypeStruct((1024, D), BF),
            jax.ShapeDtypeStruct((512, D), BF),
            jax.ShapeDtypeStruct((D, 3 * GW), BF),
            jax.ShapeDtypeStruct((512, GW), BF),
            jax.ShapeDtypeStruct((8, D), F32),
            jax.ShapeDtypeStruct((2 * TOK, 1024), BF),
        ),
        in_specs=[SMEM, HBM, VMEM, VMEM, HBM, VMEM, VMEM, HBM],
        out_specs=(HBM,) * 11,
        scratch_shapes=[
            vm((512, GW), BF), vm((512, D), BF), vm((D, 3 * GW), BF), vm((512, GW), BF),
            vm((8, D), F32), vm((2 * TOK, 1024), BF),
            vm((TOK, D), BF), vm((1024, D), BF), vm((4, 16, 3 * GW), BF),
            vm((4, 16, 3 * GW), BF), vm((4, 16, 3 * GW), BF), vm((1024, 3 * GW), BF),
            vm((4, TOK, D), BF), vm((D, 1024), BF), vm((32, 1024), BF),
            vm((TOK, 8), F32), vm((16, TOK), F32),
            vm((4, TOK, 2 * GW), BF), vm((2048, 2 * GW), BF), vm((2048, GW), BF),
            vm((GH, 512, GW), BF), vm((GH, 4, TOK, TOK), F32), vm(probs, F32), vm(probs, BF),
            vm((512, D), BF),
            DMA((13,)), DMA((7,)), DMA((4,)), DMA((5,)), DMA((10,)),
        ],
        compiler_params=pltpu.CompilerParams(
            collective_id=2, has_side_effects=True, vmem_limit_bytes=63 * 2**20
        ),
        name="attn_forward",
    )(*args)


def attn_backward_kernel(
    p, q_at, kv_at, home_at, picks_at, middle_at, gains_at, cotangent_at, w_proj_at, weight_at,
    normed_at, attn_part_at, tok_at,
    input_grad, qkv_out, att_out, small_out,
    p_s, v_s, do_s, dm, qm, dp_s, ds_s, near, messages, parts, branch_all, dq, tab,
    d_qkv, n_part, normed_in, att_f, q_blk, q_sib, q_tot, q_in, a_blk, a_sib, a_tot, a_in,
    s_own, s_sib, s_tot, s_in, qkv_sum, att_sum, s_sum, d_attn, branch, d_middle,
    q, kv, home, picks, middle, gains, cotangent, w_proj, weight, normed, attn_part, tok,
    send, recv, core_recv, own, fetched,
):
    z, x, y, c = place()
    sib = (z, x, y, 1 - c)
    p16 = x * 4 + y
    p32 = p16 * 2 + c
    me = z * 32 + p32
    source = me // 4

    def peer(i):
        return z, (x + i // 4) % 4, (y + i % 4) % 4, c

    fetches = (
        (home_at, home), (picks_at, picks), (middle_at, middle), (gains_at, gains),
        (cotangent_at, cotangent), (w_proj_at, w_proj), (kv_at, kv), (q_at, q),
        (weight_at, weight), (normed_at, normed), (attn_part_at, attn_part), (tok_at, tok),
    )
    for k, (source_ref, target) in enumerate(fetches):
        keep(source_ref, target, fetched.at[k])
    keep(p, p_s, own.at[0])
    loop(1, 16, lambda i: signal(peer(i)))
    for k in range(1, 4):
        signal(((z + k) % 4, x, y, c))
    signal(sib)

    def greet(k):
        @pl.when(jnp.logical_not((k == z) & (source == p32)))
        def _():
            signal((k, source // 8, (source // 2) % 4, source % 2))

    loop(0, 4, greet)
    for k in range(6):
        wait_bytes(fetches[k][1], fetched.at[k])
    d_moe = dot(picks[:TOK, :], home[...], NN) + dot(picks[TOK:, :], home[...], NN)
    mid = middle[...]
    mid_r = lax.rsqrt(jnp.mean(mid * mid, axis=1, keepdims=True) + norm_eps)
    mid_unit = mid * mid_r
    s_own[...] = jnp.zeros_like(s_own)
    s_own[1:2, :] = jnp.sum(d_moe * mid_unit, axis=0, keepdims=True)
    d_mid_unit = d_moe * gains[1:2, :]
    d_mid = mid_r * (d_mid_unit - mid_unit * jnp.mean(d_mid_unit * mid_unit, axis=1, keepdims=True))
    d_mid = cotangent[...].astype(F32) + d_mid
    d_middle[...] = d_mid
    branch[...] = d_mid.astype(BF)
    for k in range(GROUPS):
        d_attn[k] = dot(branch[...], w_proj[GW * k : GW * (k + 1), :], NT).astype(BF)
    for k in range(6, 12):
        wait_bytes(fetches[k][1], fetched.at[k])
    v_s[...] = kv[:, GW:]
    for h in range(GH):
        head_cols = lax.broadcasted_iota(jnp.int32, (1, GW), 1) // HD == h
        qm[h] = jnp.where(head_cols, q[...] * 0.125, 0.0).astype(BF)
    arrive(15 + 3 + 1 + 4 - jnp.where(source == p32, 1, 0))
    for k in range(1, 4):
        there = (z + k) % 4
        push(d_attn.at[there], do_s.at[z], send.at[0], recv.at[0], (there, x, y, c))
    keep(d_attn.at[z], do_s.at[z], recv.at[0])
    z_rows = pl.ds(pl.multiple_of(z * TOK, TOK), TOK)
    for k in range(1, 4):
        push(branch, branch_all.at[z_rows], send.at[1], recv.at[1], ((z + k) % 4, x, y, c))
    keep(branch, branch_all.at[z_rows], recv.at[1])
    wait_bytes(do_s, recv.at[0])
    for h in range(GH):
        head_cols = lax.broadcasted_iota(jnp.int32, (1, GW), 1) // HD == h
        for b in range(4):
            dm[h, b * TOK : (b + 1) * TOK, :] = jnp.where(head_cols, do_s[b], 0.0).astype(BF)
    wait_bytes(p_s, own.at[0])

    def key_sums(left, right, m, pair):
        for k in (1, 2, 3, 0):
            kx = (x + k) % 4
            for b in (2 * pair, 2 * pair + 1):
                cols = block_cols(b, kx)
                total = None
                for h in range(GH):
                    one = dot(left[h, b * TOK :, cols], right[h, b * TOK :, :], TN)
                    total = one if total is None else total + one
                side = GW * (b % 2)
                messages[k, m, :, side : side + GW] = total.astype(BF)
            if k:
                push(messages.at[k, m], parts.at[x, m], send.at[2], recv.at[2], (z, kx, y, c))
            else:
                keep(messages.at[k, m], parts.at[x, m], recv.at[2])

    key_sums(p_s, dm, 0, 0)
    key_sums(p_s, dm, 1, 1)
    near[...] = jnp.zeros_like(near)

    def score_grads(zq):
        rows = pl.ds(zq * TOK, TOK)
        width = (zq + 1) * 512

        def head(h):
            head_cols = lax.broadcasted_iota(jnp.int32, (1, GW), 1) // HD == h
            dp_s[:, :width] = dot(dm[h, rows, :], v_s[:width, :], NT)
            acc = jnp.zeros((TOK, TOK), F32)
            for kb in range(4 * (zq + 1)):
                cols = pl.ds(kb * TOK, TOK)
                acc = acc + p_s[h, rows, cols].astype(F32) * dp_s[:, cols]
            delta = jnp.sum(acc, axis=1, keepdims=True)
            far = jnp.zeros((TOK, TOK), F32)
            for zk in range(zq + 1):
                for kx in range(4):
                    cols = pl.ds((zk * 4 + kx) * TOK, TOK)
                    ds = (p_s[h, rows, cols].astype(F32) * (dp_s[:, cols] - delta)).astype(BF)
                    ds_s[h, rows, cols] = ds
                    if zk < zq - 1:
                        far = far + ds.astype(F32)
                    else:
                        near[h, table_kind(zq, zk, x, kx)] += ds.astype(F32)
            if zq > 1:
                near[h, 3] += far
            o = (dot(ds_s[h, rows, :width], kv[:width, :GW], NN) * 0.125).astype(BF)

            @pl.when(h == 0)
            def _():
                dq[rows, :] = o

            @pl.when(h > 0)
            def _():
                dq[rows, :] = jnp.where(head_cols, o, dq[rows, :])

        loop(0, GH, head)

    score_grads(3)
    score_grads(2)
    key_sums(ds_s, qm, 3, 1)
    score_grads(1)
    score_grads(0)
    key_sums(ds_s, qm, 2, 0)

    def bucket_sums(h):
        for dist in range(2):
            n = near_distance(dist)
            held = near[h, 1 + dist]
            bounds = [-(10**6)] + bucket_edges + [10**6]
            for b in range(BUCKETS):
                low, high = bounds[b], bounds[b + 1]
                if high <= dist * TOK - TOK + 1 or low > dist * TOK + TOK - 1:
                    if dist == 0:
                        tab[h, b : b + 1, :] = jnp.zeros((1, TOK), F32)
                    continue
                inside = jnp.sum(
                    jnp.where((n >= low) & (n < high), held, 0.0), axis=0, keepdims=True
                )
                if dist == 0:
                    tab[h, b : b + 1, :] = inside
                else:
                    tab[h, b : b + 1, :] += inside
        tab[h, BUCKETS - 1 :, :] += jnp.sum(near[h, 3], axis=0, keepdims=True)

    loop(0, GH, bucket_sums)

    wait_bytes(branch_all, recv.at[1])
    att_f[0:GW, :] = dot(attn_part[...], branch_all[...], TN)
    att_f[GW:, :] = jnp.zeros((8, D), F32)
    for j in range(32):
        a_blk[j // 2, j % 2] = att_f[6 * j : 6 * j + 8, :].astype(BF)
    push(a_blk.at[:, 1 - c], a_sib, send.at[4], core_recv.at[1], sib)
    for h in range(GH):
        s_own[2:3, BUCKETS * h : BUCKETS * (h + 1)] = jnp.sum(tab[h].T, axis=0, keepdims=True)

    wait_bytes(a_sib, core_recv.at[1])

    def att_blocks(i):
        there = peer(i)
        j = there[1] * 4 + there[2]
        a_tot[j] = (a_blk[j, c].astype(F32) + a_sib[j].astype(F32)).astype(BF)
        push(a_tot.at[j], a_in.at[p16], send.at[6], recv.at[4], there)

    loop(1, 16, att_blocks)
    a_tot[p16] = (a_blk[p16, c].astype(F32) + a_sib[p16].astype(F32)).astype(BF)
    keep(a_tot.at[p16], a_in.at[p16], recv.at[4])

    wait_bytes(parts, recv.at[2])
    d_qkv[:, :GW] = dq[...]
    for b in range(4):
        rows = slice(b * TOK, (b + 1) * TOK)
        side = GW * (b % 2)
        for m, at in ((2 + b // 2, GW), (b // 2, 2 * GW)):
            total = parts[0, m, :, side : side + GW].astype(F32)
            for k in range(1, 4):
                total = total + parts[k, m, :, side : side + GW].astype(F32)
            d_qkv[rows, at : at + GW] = total.astype(BF)
    d_normed = dot(d_qkv[...], weight[...], NT)
    n_part[...] = d_normed.astype(BF)
    for k in range(1, 4):
        there = (z + k) % 4
        push(
            n_part.at[pl.ds(pl.multiple_of(there * TOK, TOK), TOK)], normed_in.at[z],
            send.at[3], recv.at[3], (there, x, y, c),
        )
    keep(n_part.at[z_rows], normed_in.at[z], recv.at[3])
    along = jnp.sum(d_normed * normed[...].astype(F32), axis=0, keepdims=True)
    s_own[0:1, :] = along / gains[0:1, :]
    push(s_own, s_sib, send.at[8], core_recv.at[2], sib)
    total = dot(normed[...], d_qkv[...], TN)
    for j in range(32):
        q_blk[j // 2, j % 2] = total[24 * j : 24 * j + 24].astype(BF)
    push(q_blk.at[:, 1 - c], q_sib, send.at[5], core_recv.at[0], sib)
    wait_bytes(s_sib, core_recv.at[2])
    s_tot[...] = s_own[...] + s_sib[...]
    loop(1, 16, lambda i: push(s_tot, s_in.at[p16], send.at[9], recv.at[6], peer(i)))
    keep(s_tot, s_in.at[p16], recv.at[6])
    wait_bytes(q_sib, core_recv.at[0])

    def qkv_blocks(i):
        there = peer(i)
        j = there[1] * 4 + there[2]
        q_tot[j] = (q_blk[j, c].astype(F32) + q_sib[j].astype(F32)).astype(BF)
        push(q_tot.at[j], q_in.at[p16], send.at[7], recv.at[5], there)

    loop(1, 16, qkv_blocks)
    q_tot[p16] = (q_blk[p16, c].astype(F32) + q_sib[p16].astype(F32)).astype(BF)
    keep(q_tot.at[p16], q_in.at[p16], recv.at[5])

    wait_bytes(s_in, recv.at[6])
    s_total = s_in[0]
    for k in range(1, 16):
        s_total = s_total + s_in[k]
    s_sum[...] = s_total
    for k in range(1, 4):
        push(s_sum, small_out.at[z], send.at[11], recv.at[8], ((z + k) % 4, x, y, c))
    keep(s_sum, small_out.at[z], recv.at[8])
    wait_bytes(q_in, recv.at[5])
    q_total = q_in[0].astype(F32)
    for k in range(1, 16):
        q_total = q_total + q_in[k].astype(F32)
    for k in range(4):
        qkv_sum[k, 0:6, :] = q_total[6 * k : 6 * k + 6]
        qkv_sum[k, 6:8, :] = jnp.zeros((2, 3 * GW), F32)

    def final(k):
        d = 4 * p32 + k

        @pl.when(d != me)
        def _():
            push(qkv_sum.at[k], qkv_out.at[z], send.at[10], recv.at[7], device_of(d))

        @pl.when(d == me)
        def _():
            keep(qkv_sum.at[k], qkv_out.at[z], recv.at[7])

    loop(0, 4, final)
    wait_bytes(a_in, recv.at[4])
    a_total = a_in[0].astype(F32)
    for k in range(1, 16):
        a_total = a_total + a_in[k].astype(F32)
    att_sum[...] = a_total
    keep(att_sum, att_out, own.at[1])
    wait_bytes(normed_in, recv.at[3])
    d_normed = normed_in[0].astype(F32)
    for k in range(1, 4):
        d_normed = d_normed + normed_in[k].astype(F32)
    v = tok[...].astype(F32)
    r = lax.rsqrt(jnp.mean(v * v, axis=1, keepdims=True) + norm_eps)
    unit = v * r
    d_unit = d_normed * gains[0:1, :]
    d_in = r * (d_unit - unit * jnp.mean(d_unit * unit, axis=1, keepdims=True))
    input_grad[...] = (d_middle[...] + d_in).astype(BF)

    wait_bytes(att_sum, own.at[1])
    wait_bytes(qkv_out, recv.at[7])
    wait_bytes(small_out, recv.at[8])
    wait_bytes(do_s.at[pl.ds(0, 3)], send.at[0])
    wait_bytes(branch_all.at[pl.ds(0, 3 * TOK)], send.at[1])
    wait_bytes(parts.at[pl.ds(0, 3)], send.at[2])
    wait_bytes(normed_in.at[pl.ds(0, 3)], send.at[3])
    wait_bytes(a_sib, send.at[4])
    wait_bytes(q_sib, send.at[5])
    wait_bytes(a_in.at[pl.ds(0, 15)], send.at[6])
    wait_bytes(q_in.at[pl.ds(0, 15)], send.at[7])
    wait_bytes(s_own, send.at[8])
    wait_bytes(s_in.at[pl.ds(0, 15)], send.at[9])

    def sent(k):
        @pl.when(4 * p32 + k != me)
        def _():
            wait_bytes(qkv_sum.at[0], send.at[10])

    loop(0, 4, sent)
    wait_bytes(small_out.at[pl.ds(0, 3)], send.at[11])


def attn_backward(p, *rest):
    probs = (GH, 512, 2048)
    vm = pltpu.VMEM
    return pl.pallas_call(
        attn_backward_kernel,
        out_shape=(
            jax.ShapeDtypeStruct((TOK, D), BF),
            jax.ShapeDtypeStruct((4, 8, 3 * GW), F32),
            jax.ShapeDtypeStruct((8, D), F32),
            jax.ShapeDtypeStruct((4, 8, D), F32),
        ),
        in_specs=[HBM] * (1 + len(rest)),
        out_specs=(VMEM, ANY, ANY, ANY),
        scratch_shapes=[
            vm(probs, BF), vm((2048, GW), BF), vm((4, TOK, GW), BF), vm((GH, 512, GW), BF),
            vm((GH, 512, GW), BF), vm((TOK, 2048), F32), vm(probs, BF), vm((GH, 4, TOK, TOK), F32),
            vm((4, 4, TOK, 2 * GW), BF), vm((4, 4, TOK, 2 * GW), BF), vm((512, D), BF),
            vm((512, GW), BF), vm((GH, BUCKETS, TOK), F32),
            vm((512, 3 * GW), BF), vm((512, D), BF), vm((4, TOK, D), BF), vm((GW + 8, D), F32),
            vm((16, 2, 24, 3 * GW), BF), vm((16, 24, 3 * GW), BF),
            vm((16, 24, 3 * GW), BF), vm((16, 24, 3 * GW), BF),
            vm((16, 2, 8, D), BF), vm((16, 8, D), BF), vm((16, 8, D), BF), vm((16, 8, D), BF),
            vm((8, D), F32), vm((8, D), F32), vm((8, D), F32), vm((16, 8, D), F32),
            vm((4, 8, 3 * GW), F32), vm((8, D), F32), vm((8, D), F32),
            vm((4, TOK, GW), BF), vm((TOK, D), BF), vm((TOK, D), F32),
            vm((512, GW), BF), vm((2048, 2 * GW), BF), vm((1024, D), BF), vm((2 * TOK, 1024), BF),
            vm((TOK, D), F32), vm((8, D), F32), vm((TOK, D), BF), vm((D, D), BF),
            vm((D, 3 * GW), BF), vm((512, D), BF), vm((512, GW), BF), vm((TOK, D), BF),
            DMA((12,)), DMA((9,)), DMA((3,)), DMA((2,)), DMA((12,)),
        ],
        compiler_params=pltpu.CompilerParams(
            collective_id=3, has_side_effects=True, vmem_limit_bytes=63 * 2**20
        ),
        name="attn_backward",
    )(p, *rest)


def per_device(
    tokens,
    gain_attn,
    w_qkv,
    w_attn_out,
    rel_table,
    gain_moe,
    w_in,
    w_out,
    expert_ids,
    gate_values,
    doc_ids,
    cotangent,
):
    z, x, y, c = place()
    own_tokens = tokens.reshape(TOK, D)
    grad_bf = cotangent.reshape(TOK, D)
    grad_out = grad_bf.astype(F32)

    gates = gate_values.reshape(TOK, 2)

    place_in = chip_of(z, x, y) * 2 + c
    lane = jnp.arange(3 * GW, dtype=jnp.int32)[None, :]
    both_gains = jnp.stack([gain_attn, gain_moe]).astype(F32)
    notes = jnp.concatenate(
        [
            jnp.zeros((2, 384), F32),
            jnp.pad(doc_ids.reshape(1, TOK).astype(F32), ((0, 1), (0, 0))),
            jnp.zeros((2, 64), F32),
        ],
        axis=1,
    )
    for k in range(6):
        notes = jnp.where(lane == (place_in % 64) * 6 + k, both_gains[:, k : k + 1], notes)
    out_slab = jnp.concatenate([w_attn_out, jnp.zeros((2, D), BF)], axis=0)
    table = lax.dynamic_slice(rel_table, (0, z * GH), (BUCKETS, GH)).astype(F32)
    (
        attn, attn_part, probs, kv_all, out_weights, d_eo_all, normed, weight, queries, gain_rows,
        picks,
    ) = attn_forward(
        table, own_tokens, w_qkv, notes, out_slab, expert_ids.reshape(TOK, 2), gates, grad_bf
    )
    attention_weight = out_weights[:, :, :, :, :6, :].reshape(D, D)
    home, expert_out, expert_in_grad, expert_out_grad, middle = run_experts(
        attn, attention_weight, own_tokens, gain_rows, picks, d_eo_all, w_in[0], w_out[0]
    )
    input_grad, qkv_sum, att_sum, small_sum = attn_backward(
        probs, queries, kv_all, home, picks, middle, gain_rows, grad_bf, attention_weight, weight,
        normed, attn_part, own_tokens,
    )

    picked = dot(picks, expert_out, NN).reshape(2, TOK, D)
    block_out = middle + gates[:, :1] * picked[0] + gates[:, 1:] * picked[1]
    gate_grad = jnp.sum(picked * grad_out[None], axis=2).T

    qkv_grad = qkv_sum[:, :6, :].reshape(GROUPS, 6, 3, GW).transpose(1, 2, 0, 3).reshape(6, 3 * D)
    attn_out_grad = att_sum[:6]
    gains = lax.dynamic_slice(jnp.sum(small_sum[:, :2, :], axis=0), (0, place_in * 6), (2, 6))
    table_grad = small_sum[:, 2, : GH * BUCKETS].reshape(GROUPS * GH, BUCKETS).T
    return (
        block_out.reshape(1, TOK, D).astype(BF),
        input_grad.reshape(1, TOK, D),
        gate_grad.reshape(1, TOK, 2),
        gains[0],
        qkv_grad,
        attn_out_grad,
        table_grad,
        gains[1],
        expert_in_grad[None],
        expert_out_grad[None],
    )


def solution(mesh):
    torus = Mesh(mesh.devices.reshape(4, 4, 4, 2), AXES)
    in_specs = (
        P(EXP, CTX, None),
        P(AXES),
        P(AXES, None),
        P(AXES, None),
        P(),
        P(AXES),
        P(AXES, None, None),
        P(AXES, None, None),
        P(EXP, CTX, None),
        P(EXP, CTX, None),
        P(EXP, CTX),
        P(EXP, CTX, None),
    )
    out_specs = (
        P(EXP, CTX, None),
        P(EXP, CTX, None),
        P(EXP, CTX, None),
        P(AXES),
        P(AXES, None),
        P(AXES, None),
        P(),
        P(AXES),
        P(AXES, None, None),
        P(AXES, None, None),
    )
    return jax.shard_map(
        per_device, mesh=torus, in_specs=in_specs, out_specs=out_specs, check_vma=False
    )
```

```python
import functools

import jax
import jax.numpy as jnp
import numpy as np
from jax import lax
from jax.experimental import pallas as pl
from jax.experimental.pallas import tpu as pltpu
from jax.sharding import Mesh
from jax.sharding import PartitionSpec as P

D = 768
H = 12
HD = 64
BUCKETS = 32
GROUPS = 4
GH = H // GROUPS
GW = GH * HD
TOK = 128
CTX = ("ctx_0", "ctx_1")
EXP = ("exp_0", "exp_1")
AXES = ("ctx_0", "ctx_1", "exp_0", "exp_1")
MESH = pl.DeviceIdType.MESH
ANY = pl.BlockSpec(memory_space=pl.ANY)
HBM = pl.BlockSpec(memory_space=pltpu.HBM)
BF = jnp.bfloat16
F32 = jnp.float32

norm_eps = 1e-06
bucket_edges = [int(e) for e in np.concatenate(
    [np.arange(1, 17), np.ceil(16.0 * 8.0 ** (np.arange(1, 16) / 16.0))]
).astype(np.int32)]
masked = -1e30


def scale_rows(values, gain):
    return values * lax.rsqrt(jnp.mean(values * values, axis=-1, keepdims=True) + norm_eps) * gain


def place():
    return tuple(lax.axis_index(a) for a in AXES)


def chip_of(z, x, y):
    return (z * 4 + x) * 4 + y


def chip_peer(i, z, x, y):
    return (z + i // 16) % 4, (x + (i // 4) % 4) % 4, (y + i % 4) % 4


def loop(first, last, body):
    lax.fori_loop(first, last, lambda i, carry: (body(i), carry)[1], 0)


def signal(device):
    pl.semaphore_signal(
        pltpu.get_barrier_semaphore(), inc=1, device_id=device, device_id_type=MESH
    )


def arrive(count):
    pl.semaphore_wait(pltpu.get_barrier_semaphore(), count)


def push(src, dst, send, recv, device):
    pltpu.make_async_remote_copy(
        src_ref=src, dst_ref=dst, send_sem=send, recv_sem=recv, device_id=device, device_id_type=MESH
    ).start()


def keep(src, dst, sem):
    pltpu.make_async_copy(src, dst, sem).start()


def wait_bytes(ref, sem):
    pltpu.make_async_copy(ref, ref, sem).wait()


def comm_call(kernel, outs, scratch, collective_id, name):
    return pl.pallas_call(
        kernel,
        out_shape=outs,
        in_specs=None,
        out_specs=jax.tree.map(lambda _: ANY, outs),
        scratch_shapes=scratch,
        compiler_params=pltpu.CompilerParams(
            collective_id=collective_id, has_side_effects=True, vmem_limit_bytes=32 * 2**20
        ),
        name=name,
    )


def run_comm(kernel, args, outs, scratch, collective_id, name):
    return pl.pallas_call(
        kernel,
        out_shape=outs,
        in_specs=[ANY] * len(args),
        out_specs=jax.tree.map(lambda _: ANY, outs),
        scratch_shapes=scratch,
        compiler_params=pltpu.CompilerParams(
            collective_id=collective_id, has_side_effects=True, vmem_limit_bytes=32 * 2**20
        ),
        name=name,
    )(*args)


DMA = pltpu.SemaphoreType.DMA


def half_peer(i, z, x, y, c):
    return (z + i // 8) % 4, (x + (i // 2) % 4) % 4, c + 2 * ((y // 2 + i % 2) % 2), y % 2


def block_of(z, x, y):
    return pl.multiple_of((y % 2) * 512 + ((z * 4 + x) * 2 + y // 2) * 16, 16)


def greet_chips(z, x, y, c):
    loop(1, 32, lambda i: signal(half_peer(i, z, x, y, c)))

    @pl.when(y % 2 != c)
    def _():
        signal(half_peer(0, z, x, y, c))

    signal((z, x, y, 1 - c))
    return 32 + jnp.where(y % 2 == c, 0, 1)


def to_chips(z, x, y, c, source, target, send, recv):
    def one(i):
        there = half_peer(i, z, x, y, c)
        push(source(there), target, send, recv, there)

    loop(1, 32, one)
    first = half_peer(0, z, x, y, c)

    @pl.when(y % 2 == c)
    def _():
        keep(source(first), target, recv)

    @pl.when(y % 2 != c)
    def _():
        push(source(first), target, send, recv, first)


def sent_to_chips(rows, y, c, send):
    wait_bytes(rows.at[pl.ds(0, 496)], send)

    @pl.when(y % 2 != c)
    def _():
        wait_bytes(rows.at[pl.ds(0, 16)], send)


FH = 1536
WIDE = 256


def experts_kernel(
    attn_at, w_proj_at, tok_at, gains_at, picks_at, d_rows, w_in, w_out,
    home_in, home_out, g_in, g_out, middle_out,
    middle, attn, w_proj, tok, gains, picks, x16, xo, rows, dv, w1, w2, dh, hidden, dact, in_h, out_h, in_o, out_o, stage_out, stage_in,
    send, recv, core_recv, own, staged, fetched,
):
    z, x, y, c = place()
    sib = (z, x, y, 1 - c)
    at_mine = pl.multiple_of(c * 512, 512)
    at_theirs = pl.multiple_of((1 - c) * 512, 512)
    mine, theirs = pl.ds(at_mine, 512), pl.ds(at_theirs, 512)
    me = block_of(z, x, y)
    fetches = (
        (attn_at, attn), (w_proj_at, w_proj), (tok_at, tok), (gains_at, gains), (picks_at, picks)
    )
    for k, (source, target) in enumerate(fetches):
        keep(source, target, fetched.at[k])
    keep(d_rows, dv, own.at[1])
    keep(w_out, w2, own.at[2])
    keep(w_in, w1, own.at[3])
    expected = greet_chips(z, x, y, c)
    for k, (_, target) in enumerate(fetches):
        wait_bytes(target, fetched.at[k])
    total = tok[...].astype(F32)
    for k in range(GROUPS):
        total = total + dot(attn[k], w_proj[GW * k : GW * (k + 1), :], NN)
    middle[...] = total
    keep(middle, middle_out, own.at[0])
    moe_in = scale_rows(total, gains[1:2, :]).astype(BF)
    for n in range(0, 1024, WIDE):
        x16[n : n + WIDE, :] = (
            dot(picks[:TOK, n : n + WIDE], moe_in, TN) + dot(picks[TOK:, n : n + WIDE], moe_in, TN)
        ).astype(BF)
    arrive(expected)
    push(x16.at[theirs], xo, send.at[0], core_recv.at[0], sib)
    wait_bytes(xo, core_recv.at[0])
    xo[...] = xo[...] + x16[mine, :]
    to_chips(
        z, x, y, c,
        lambda there: xo.at[pl.ds(pl.multiple_of(block_of(*there[:3]) - c * 512, 16), 16)],
        rows.at[pl.ds(me, 16)], send.at[1], recv.at[0],
    )
    wait_bytes(dv, own.at[1])
    wait_bytes(w2, own.at[2])

    def hidden_grads(n):
        cols = pl.ds(pl.multiple_of(n * WIDE, WIDE), WIDE)
        dh[:, cols] = dot(dv[...], w2[cols, :], NT)

    loop(0, FH // WIDE, hidden_grads)
    wait_bytes(w1, own.at[3])
    wait_bytes(rows.at[mine], recv.at[0])
    push(rows.at[mine], rows.at[mine], send.at[2], core_recv.at[1], sib)

    def activate(at):
        part = pl.ds(at, 512)

        def one(n):
            cols = pl.ds(pl.multiple_of(n * WIDE, WIDE), WIDE)
            a = dot(rows[part, :], w1[:, cols], NN)
            square = a * a
            t = jnp.tanh(0.7978845608028654 * (a + 0.044715 * (square * a)))
            cdf = 0.5 * (1.0 + t)
            hidden[part, cols] = (a * cdf).astype(BF)
            slope = cdf + 0.5 * a * (1.0 - t * t) * (
                0.7978845608028654 * (1.0 + 0.134145 * square)
            )
            dact[part, cols] = (slope * dh[part, cols]).astype(BF)

        loop(0, FH // WIDE, one)

    def in_half(at):
        part = pl.ds(at, 512)

        def one(n):
            cols = pl.ds(pl.multiple_of(n * WIDE, WIDE), WIDE)
            in_h[part, cols] = dot(dact[part, :], w1[cols, :], NT).astype(BF)

        loop(0, D // WIDE, one)

    def out_half(at):
        part = pl.ds(at, 512)

        def one(n):
            cols = pl.ds(pl.multiple_of(n * WIDE, WIDE), WIDE)
            out_h[part, cols] = dot(hidden[part, :], w2[:, cols], NN).astype(BF)

        loop(0, D // WIDE, one)

    activate(at_mine)
    wait_bytes(rows.at[theirs], core_recv.at[1])
    activate(at_theirs)
    in_half(at_theirs)
    push(in_h.at[theirs], in_o, send.at[3], core_recv.at[2], sib)
    in_half(at_mine)
    wait_bytes(in_o, core_recv.at[2])
    in_o[...] = (in_o[...].astype(F32) + in_h[mine, :].astype(F32)).astype(BF)
    to_chips(
        z, x, y, c,
        lambda there: in_o.at[pl.ds(pl.multiple_of(block_of(*there[:3]) - c * 512, 16), 16)],
        home_in.at[pl.ds(me, 16)], send.at[4], recv.at[1],
    )
    out_half(at_theirs)
    push(out_h.at[theirs], out_o, send.at[5], core_recv.at[3], sib)
    out_half(at_mine)
    wait_bytes(out_o, core_recv.at[3])
    out_o[...] = (out_o[...].astype(F32) + out_h[mine, :].astype(F32)).astype(BF)
    to_chips(
        z, x, y, c,
        lambda there: out_o.at[pl.ds(pl.multiple_of(block_of(*there[:3]) - c * 512, 16), 16)],
        home_out.at[pl.ds(me, 16)], send.at[6], recv.at[2],
    )

    def out_grads(n):
        cols = pl.ds(pl.multiple_of(n * WIDE, WIDE), WIDE)
        slot = n % 2

        @pl.when(n >= 2)
        def _():
            wait_bytes(stage_out.at[slot], staged.at[slot])

        stage_out[slot] = dot(hidden[:, cols], dv[...], TN)
        keep(stage_out.at[slot], g_out.at[cols], staged.at[slot])

    loop(0, FH // WIDE, out_grads)
    wait_bytes(home_in.at[mine], recv.at[1])
    push(home_in.at[mine], home_in.at[mine], send.at[7], core_recv.at[4], sib)

    def in_grads(n):
        cols = pl.ds(pl.multiple_of(n * WIDE, WIDE), WIDE)
        slot = n % 2

        @pl.when(n >= 2)
        def _():
            wait_bytes(stage_in.at[slot], staged.at[2 + slot])

        stage_in[slot] = dot(rows[:, cols], dact[...], TN)
        keep(stage_in.at[slot], g_in.at[cols], staged.at[2 + slot])

    loop(0, D // WIDE, in_grads)
    wait_bytes(home_out.at[mine], recv.at[2])
    push(home_out.at[mine], home_out.at[mine], send.at[8], core_recv.at[5], sib)
    for slot in range(2):
        wait_bytes(stage_out.at[slot], staged.at[slot])
        wait_bytes(stage_in.at[slot], staged.at[2 + slot])
    wait_bytes(xo, send.at[0])
    sent_to_chips(rows, y, c, send.at[1])
    wait_bytes(rows.at[mine], send.at[2])
    wait_bytes(in_o, send.at[3])
    sent_to_chips(home_in, y, c, send.at[4])
    wait_bytes(out_o, send.at[5])
    sent_to_chips(home_out, y, c, send.at[6])
    wait_bytes(home_in.at[theirs], core_recv.at[4])
    wait_bytes(home_out.at[theirs], core_recv.at[5])
    wait_bytes(home_in.at[mine], send.at[7])
    wait_bytes(home_out.at[mine], send.at[8])
    wait_bytes(middle, own.at[0])


def run_experts(*args):
    whole_rows = pltpu.VMEM((1024, D), BF)
    half_rows = pltpu.VMEM((512, D), BF)
    hid = pltpu.VMEM((1024, FH), BF)
    return pl.pallas_call(
        experts_kernel,
        out_shape=(
            jax.ShapeDtypeStruct((1024, D), BF),
            jax.ShapeDtypeStruct((1024, D), BF),
            jax.ShapeDtypeStruct((D, FH), F32),
            jax.ShapeDtypeStruct((FH, D), F32),
            jax.ShapeDtypeStruct((TOK, D), F32),
        ),
        in_specs=[HBM, ANY] + [HBM] * 6,
        out_specs=(HBM,) * 5,
        scratch_shapes=[
            pltpu.VMEM((TOK, D), F32),
            pltpu.VMEM((4, TOK, GW), BF), pltpu.VMEM((D, D), BF), pltpu.VMEM((TOK, D), BF),
            pltpu.VMEM((8, D), F32), pltpu.VMEM((2 * TOK, 1024), BF),
            whole_rows, half_rows, whole_rows, whole_rows,
            pltpu.VMEM((D, FH), BF), pltpu.VMEM((FH, D), BF), pltpu.VMEM((1024, FH), F32),
            hid, hid, whole_rows, whole_rows, half_rows, half_rows,
            pltpu.VMEM((2, WIDE, D), F32), pltpu.VMEM((2, WIDE, FH), F32),
            DMA((9,)), DMA((3,)), DMA((6,)), DMA((4,)), DMA((4,)), DMA((5,)),
        ],
        compiler_params=pltpu.CompilerParams(
            collective_id=1, has_side_effects=True, vmem_limit_bytes=63 * 2**20
        ),
        name="experts",
    )(*args)


def device_of(d):
    return d // 32, (d // 8) % 4, (d // 2) % 4, d % 2


NT = (((1,), (1,)), ((), ()))
NN = (((1,), (0,)), ((), ()))
TN = (((0,), (0,)), ((), ()))


def dot(a, b, dims):
    return lax.dot_general(a, b, dims, preferred_element_type=F32)


def near_distance(dist):
    a = lax.broadcasted_iota(jnp.int32, (TOK, TOK), 0)
    b = lax.broadcasted_iota(jnp.int32, (TOK, TOK), 1)
    return dist * TOK + a - b


def table_kind(zq, zk, x, kx):
    return jnp.clip((zq - zk) * 4 + x - kx + 1, 0, 3)


def block_cols(zk, kx):
    return pl.ds(pl.multiple_of((zk * 4 + kx) * TOK, TOK), TOK)


VMEM = pl.BlockSpec(memory_space=pltpu.VMEM)
SMEM = pl.BlockSpec(memory_space=pltpu.SMEM)


def attn_forward_kernel(
    tab, tok, w_qkv, notes, wa, routes, gates, cotangent_at,
    attn_all, part_out, p_out, kv_out, wa_all, d_rows, normed_out, weight_out, q_out, gains_out,
    picks_out, part, normed, weight, q, gains, picks, cotangent, d_eo, wmsg, wm, wo, w_s, tok_s, select, picker, qd, kd,
    kv, kv_s, v_s, qm, bias, s_s, p_s, xo,
    send, recv, kv_recv, core_recv, own,
):
    z, x, y, c = place()
    sib = (z, x, y, 1 - c)
    mine = pl.ds(pl.multiple_of(c * 512, 512), 512)
    theirs = pl.ds(pl.multiple_of((1 - c) * 512, 512), 512)
    me = block_of(z, x, y)
    keep(wa, wa_all.at[z, x, y, c], own.at[0])
    keep(cotangent_at, cotangent, own.at[3])
    expected = greet_chips(z, x, y, c)
    for k in range(1, 4):
        signal(((z + k) % 4, x, y, c))
        signal((z, (x + k) % 4, y, c))
        signal((z, x, (y + k) % 4, c))
    lift = lax.broadcasted_iota(jnp.int32, (16, 8), 0)
    below = lax.broadcasted_iota(jnp.int32, (16, 8), 1)
    lift = jnp.where((lift == 6 * c + below) & (below < 6), 1.0, 0.0)
    lift = jnp.where(
        (below >= 6) & (lax.broadcasted_iota(jnp.int32, (16, 8), 0) == 12 + c + 2 * (below - 6)),
        1.0, lift,
    ).astype(BF)
    for g in range(GROUPS):
        for t in range(3):
            at = t * D + g * GW
            both = jnp.concatenate(
                [w_qkv[:, at : at + GW].astype(F32), notes[:, t * GW : (t + 1) * GW]], axis=0
            ).astype(BF)
            wmsg[g, :, t * GW : (t + 1) * GW] = dot(lift, both, NN).astype(BF)
    arrive(expected + 9)
    push(wmsg, wo, send.at[0], core_recv.at[0], sib)
    wait_bytes(wo, core_recv.at[0])
    wm[...] = wmsg[...] + wo[...]
    to_chips(
        z, x, y, c, lambda there: wm.at[there[0]], w_s.at[pl.ds(me, 16)], send.at[3], recv.at[1]
    )
    for k in range(1, 4):
        push(tok, tok_s.at[z], send.at[1], recv.at[0], ((z + k) % 4, x, y, c))
    keep(tok, tok_s.at[z], recv.at[0])
    for k in range(1, 4):
        push(wa, wa_all.at[z, x, y, c], send.at[4], recv.at[2], ((z + k) % 4, x, y, c))

    expert = lax.broadcasted_iota(jnp.int32, (1, 64), 1)
    first = jnp.where(routes[:, 0:1] == expert, 1.0, 0.0)
    second = jnp.where(routes[:, 1:2] == expert, 1.0, 0.0)
    lower = jnp.where(
        lax.broadcasted_iota(jnp.int32, (TOK, TOK), 0)
        > lax.broadcasted_iota(jnp.int32, (TOK, TOK), 1), 1.0, 0.0,
    ).astype(BF)
    before = jnp.sum(first, axis=0, keepdims=True)
    rank_1 = jnp.sum(dot(lower, first.astype(BF), NN) * first, axis=1, keepdims=True)
    rank_2 = jnp.sum(
        (dot(lower, second.astype(BF), NN) + before) * second, axis=1, keepdims=True
    )
    slot = lax.broadcasted_iota(jnp.int32, (TOK, 1024), 1)
    wait_bytes(cotangent, own.at[3])
    g_rows = cotangent[...].astype(F32)
    gated = []
    for side, rank in enumerate((rank_1, rank_2)):
        e = routes[:, side : side + 1]
        block = ((e & 1) * 32 + (e >> 2) * 2 + ((e >> 1) & 1)) * 16 + 8 * c
        here = slot - block == rank.astype(jnp.int32)
        picks[side * TOK : (side + 1) * TOK, :] = jnp.where(here, 1.0, 0.0).astype(BF)
        gated.append((gates[:, side : side + 1] * g_rows).astype(BF))
    for n in range(0, 1024, WIDE):
        d_eo[n : n + WIDE, :] = (
            dot(picks[:TOK, n : n + WIDE], gated[0], TN)
            + dot(picks[TOK:, n : n + WIDE], gated[1], TN)
        ).astype(BF)
    push(d_eo.at[theirs], xo, send.at[2], core_recv.at[1], sib)
    keep(picks, picks_out, own.at[4])

    row = lax.broadcasted_iota(jnp.int32, (1, 1024), 1)
    r, half, at = row & 15, row >> 9, (row >> 4) & 31
    row_z, row_x, row_y = at >> 3, (at >> 1) & 3, (at & 1) * 2 + half
    feature = jnp.where(r < 12, (row_z * 16 + row_x * 4 + row_y) * 12 + r, -1)
    select[...] = jnp.where(
        lax.broadcasted_iota(jnp.int32, (D, 1024), 0) == feature, 1.0, 0.0
    ).astype(BF)
    j = lax.broadcasted_iota(jnp.int32, (32, 1024), 0)
    gain_rows = (j < 4) & (r >> 1 == 6 + (j >> 1)) & (row_z >> 1 == j & 1)
    notes = (r == 12 + c) & (row_y == y)
    key_rows = (j >= 8) & (row_z * 4 + row_x == j - 8)
    query_rows = (j >= 24) & (row_z == j - 24) & (row_x == x)
    picker[...] = jnp.where(gain_rows | (notes & (key_rows | query_rows)), 1.0, 0.0).astype(BF)

    def tables(h):
        for dist in range(2):
            n = near_distance(dist)
            acc = jnp.full((TOK, TOK), tab[0, h], F32)
            for k, edge in enumerate(bucket_edges):
                acc = jnp.where(n >= edge, tab[k + 1, h], acc)
            bias[h, 1 + dist] = jnp.where(n >= 0, acc, masked)
        bias[h, 0] = jnp.full((TOK, TOK), masked, F32)
        bias[h, 3] = jnp.full((TOK, TOK), tab[BUCKETS - 1, h], F32)

    loop(0, GH, tables)
    wait_bytes(xo, core_recv.at[1])
    xo[...] = xo[...] + d_eo[mine, :]
    wait_bytes(w_s.at[mine], recv.at[1])
    push(w_s.at[mine], w_s.at[mine], send.at[5], core_recv.at[2], sib)
    wait_bytes(wa_all.at[z, x, y, c], own.at[0])
    wait_bytes(wa_all.at[pl.ds(0, 3), x, y, c], recv.at[2])
    for k in range(1, 4):
        push(
            wa_all.at[:, x, y, c], wa_all.at[:, x, y, c], send.at[6], recv.at[3],
            (z, (x + k) % 4, y, c),
        )
    wait_bytes(w_s.at[theirs], core_recv.at[2])
    picked = dot(picker[...], w_s[...], NN)
    gain = jnp.concatenate([picked[0:1, :384], picked[1:2, :384]], axis=1)
    gains[0:1, :] = gain
    gains[1:2, :] = jnp.concatenate([picked[2:3, :384], picked[3:4, :384]], axis=1)
    gains[2:8, :] = jnp.zeros((6, D), F32)
    kd[...] = picked[8:24, 384:512]
    qd[...] = picked[24:32, 384:512].T
    weight[...] = dot(select[...], w_s[...], NN).astype(BF)
    wait_bytes(tok_s, recv.at[0])
    for b in range(4):
        v = tok_s[b].astype(F32)
        normed[b * TOK : (b + 1) * TOK, :] = scale_rows(v, gain).astype(BF)
    qkv = dot(normed[...], weight[...], NN).astype(BF)
    q[...] = qkv[:, :GW]
    for b in range(4):
        kv[b] = qkv[b * TOK : (b + 1) * TOK, GW:]
    results = ((normed, normed_out), (weight, weight_out), (q, q_out), (gains, gains_out))
    for k in range(1, 4):
        for b in range(4):
            push(
                kv.at[b], kv_s.at[block_cols(b, x)], send.at[7], kv_recv.at[4 - k],
                (z, (x + k) % 4, y, c),
            )
    for b in range(4):
        keep(kv.at[b], kv_s.at[block_cols(b, x)], kv_recv.at[0])
    for k, (source, target) in enumerate(results):
        keep(source, target, own.at[5 + k])
    wait_bytes(wa_all.at[:, pl.ds(0, 3), y, c], recv.at[3])
    for k in range(1, 4):
        push(
            wa_all.at[:, :, y, c], wa_all.at[:, :, y, c], send.at[8], recv.at[4],
            (z, x, (y + k) % 4, c),
        )
    for h in range(GH):
        head_cols = lax.broadcasted_iota(jnp.int32, (1, GW), 1) // HD == h
        qm[h] = jnp.where(head_cols, q[...] * 0.125, 0.0).astype(BF)
    for k in range(4):
        kx = (x + k) % 4
        if k == 0:
            for b in range(4):
                wait_bytes(kv_s.at[block_cols(b, kx)], kv_recv.at[0])
        else:
            wait_bytes(kv_s.at[pl.ds(0, 512)], kv_recv.at[k])
        for b in range(4):
            cols = block_cols(b, kx)
            v_s[cols, :] = kv_s[cols, GW:]
            for h in range(GH):
                s_s[h, b * TOK :, cols] = dot(qm[h, b * TOK :, :], kv_s[cols, :GW], NT)
    keep(kv_s, kv_out, own.at[1])
    to_chips(
        z, x, y, c,
        lambda there: xo.at[pl.ds(pl.multiple_of(block_of(*there[:3]) - c * 512, 16), 16)],
        d_rows.at[pl.ds(me, 16)], send.at[9], recv.at[5],
    )
    wait_bytes(wa_all.at[:, :, pl.ds(0, 3), c], recv.at[4])
    push(wa_all.at[:, :, :, c], wa_all.at[:, :, :, c], send.at[10], core_recv.at[3], sib)

    def head(h):
        head_cols = lax.broadcasted_iota(jnp.int32, (1, GW), 1) // HD == h
        far = tab[BUCKETS - 1, h]
        for zq in range(4):
            rows = pl.ds(zq * TOK, TOK)
            docs = qd[:, zq : zq + 1]
            top = None
            for zk in range(zq + 1):
                for kx in range(4):
                    cols = pl.ds((zk * 4 + kx) * TOK, TOK)
                    s = s_s[h, rows, cols]
                    if zk < zq - 1:
                        s = s + far
                    else:
                        s = s + bias[h, table_kind(zq, zk, x, kx)]
                    kb = zk * 4 + kx
                    s = jnp.where(docs == kd[kb : kb + 1, :], s, masked)
                    s_s[h, rows, cols] = s
                    top = s if top is None else jnp.maximum(top, s)
            top = jnp.max(top, axis=1, keepdims=True)
            total = jnp.zeros((TOK, TOK), F32)
            for kb in range(4 * (zq + 1)):
                cols = pl.ds(kb * TOK, TOK)
                e = jnp.exp(s_s[h, rows, cols] - top)
                s_s[h, rows, cols] = e
                total = total + e
            inv = 1.0 / jnp.sum(total, axis=1, keepdims=True)
            for kb in range(4 * (zq + 1)):
                cols = pl.ds(kb * TOK, TOK)
                p_s[h, rows, cols] = (s_s[h, rows, cols] * inv).astype(BF)
            width = (zq + 1) * 512
            o = dot(p_s[h, rows, :width], v_s[:width, :], NN).astype(BF)

            @pl.when(h == 0)
            def _():
                part[rows, :] = o

            @pl.when(h > 0)
            def _():
                part[rows, :] = jnp.where(head_cols, o, part[rows, :])

    loop(0, GH, head)
    for k in range(1, 4):
        there = (z + k) % 4
        push(
            part.at[pl.ds(pl.multiple_of(there * TOK, TOK), TOK)], attn_all.at[z],
            send.at[11], recv.at[6], (there, x, y, c),
        )
    keep(part.at[pl.ds(pl.multiple_of(z * TOK, TOK), TOK)], attn_all.at[z], recv.at[6])
    keep(p_s, p_out, own.at[2])
    keep(part, part_out, own.at[9])
    wait_bytes(d_rows.at[mine], recv.at[5])
    push(d_rows.at[mine], d_rows.at[mine], send.at[12], core_recv.at[4], sib)
    wait_bytes(attn_all, recv.at[6])
    wait_bytes(wa_all.at[:, :, :, 1 - c], core_recv.at[3])
    wait_bytes(d_rows.at[theirs], core_recv.at[4])
    wait_bytes(kv_s, own.at[1])
    wait_bytes(p_s, own.at[2])
    wait_bytes(picks, own.at[4])
    for k, (source, _) in enumerate(results):
        wait_bytes(source, own.at[5 + k])
    wait_bytes(part, own.at[9])
    wait_bytes(wo, send.at[0])
    wait_bytes(tok_s.at[pl.ds(0, 3)], send.at[1])
    wait_bytes(xo, send.at[2])
    sent_to_chips(w_s, y, c, send.at[3])
    wait_bytes(wa_all.at[pl.ds(0, 3), x, y, c], send.at[4])
    wait_bytes(w_s.at[mine], send.at[5])
    wait_bytes(wa_all.at[:, pl.ds(0, 3), y, c], send.at[6])
    wait_bytes(kv_s.at[pl.ds(0, 1536)], send.at[7])
    wait_bytes(wa_all.at[:, :, pl.ds(0, 3), c], send.at[8])
    sent_to_chips(d_rows, y, c, send.at[9])
    wait_bytes(wa_all.at[:, :, :, c], send.at[10])
    wait_bytes(attn_all.at[pl.ds(0, 3)], send.at[11])
    wait_bytes(d_rows.at[mine], send.at[12])


def attn_forward(*args):
    probs = (GH, 512, 2048)
    vm = pltpu.VMEM
    return pl.pallas_call(
        attn_forward_kernel,
        out_shape=(
            jax.ShapeDtypeStruct((4, TOK, GW), BF),
            jax.ShapeDtypeStruct((512, GW), BF),
            jax.ShapeDtypeStruct(probs, BF),
            jax.ShapeDtypeStruct((2048, 2 * GW), BF),
            jax.ShapeDtypeStruct((4, 4, 4, 2, 8, D), BF),
            jax.ShapeDtypeStruct((1024, D), BF),
            jax.ShapeDtypeStruct((512, D), BF),
            jax.ShapeDtypeStruct((D, 3 * GW), BF),
            jax.ShapeDtypeStruct((512, GW), BF),
            jax.ShapeDtypeStruct((8, D), F32),
            jax.ShapeDtypeStruct((2 * TOK, 1024), BF),
        ),
        in_specs=[SMEM, HBM, VMEM, VMEM, HBM, VMEM, VMEM, HBM],
        out_specs=(HBM,) * 11,
        scratch_shapes=[
            vm((512, GW), BF), vm((512, D), BF), vm((D, 3 * GW), BF), vm((512, GW), BF),
            vm((8, D), F32), vm((2 * TOK, 1024), BF),
            vm((TOK, D), BF), vm((1024, D), BF), vm((4, 16, 3 * GW), BF),
            vm((4, 16, 3 * GW), BF), vm((4, 16, 3 * GW), BF), vm((1024, 3 * GW), BF),
            vm((4, TOK, D), BF), vm((D, 1024), BF), vm((32, 1024), BF),
            vm((TOK, 8), F32), vm((16, TOK), F32),
            vm((4, TOK, 2 * GW), BF), vm((2048, 2 * GW), BF), vm((2048, GW), BF),
            vm((GH, 512, GW), BF), vm((GH, 4, TOK, TOK), F32), vm(probs, F32), vm(probs, BF),
            vm((512, D), BF),
            DMA((13,)), DMA((7,)), DMA((4,)), DMA((5,)), DMA((10,)),
        ],
        compiler_params=pltpu.CompilerParams(
            collective_id=2, has_side_effects=True, vmem_limit_bytes=63 * 2**20
        ),
        name="attn_forward",
    )(*args)


def attn_backward_kernel(
    p, q_at, kv_at, home_at, picks_at, middle_at, gains_at, cotangent_at, w_proj_at, weight_at,
    normed_at, attn_part_at, tok_at,
    input_grad, qkv_out, att_out, small_out,
    p_s, v_s, do_s, dm, qm, dp_s, ds_s, near, messages, parts, branch_all, dq, tab,
    d_qkv, n_part, normed_in, att_f, q_blk, q_sib, q_tot, q_in, a_blk, a_sib, a_tot, a_in,
    s_own, s_sib, s_tot, s_in, qkv_sum, att_sum, s_sum, d_attn, branch, d_middle,
    q, kv, home, picks, middle, gains, cotangent, w_proj, weight, normed, attn_part, tok,
    send, recv, core_recv, own, fetched,
):
    z, x, y, c = place()
    sib = (z, x, y, 1 - c)
    p16 = x * 4 + y
    p32 = p16 * 2 + c
    me = z * 32 + p32
    source = me // 4

    def peer(i):
        return z, (x + i // 4) % 4, (y + i % 4) % 4, c

    fetches = (
        (home_at, home), (picks_at, picks), (middle_at, middle), (gains_at, gains),
        (cotangent_at, cotangent), (w_proj_at, w_proj), (kv_at, kv), (q_at, q),
        (weight_at, weight), (normed_at, normed), (attn_part_at, attn_part), (tok_at, tok),
    )
    for k, (source_ref, target) in enumerate(fetches):
        keep(source_ref, target, fetched.at[k])
    keep(p, p_s, own.at[0])
    loop(1, 16, lambda i: signal(peer(i)))
    for k in range(1, 4):
        signal(((z + k) % 4, x, y, c))
    signal(sib)

    def greet(k):
        @pl.when(jnp.logical_not((k == z) & (source == p32)))
        def _():
            signal((k, source // 8, (source // 2) % 4, source % 2))

    loop(0, 4, greet)
    for k in range(6):
        wait_bytes(fetches[k][1], fetched.at[k])
    d_moe = dot(picks[:TOK, :], home[...], NN) + dot(picks[TOK:, :], home[...], NN)
    mid = middle[...]
    mid_r = lax.rsqrt(jnp.mean(mid * mid, axis=1, keepdims=True) + norm_eps)
    mid_unit = mid * mid_r
    s_own[...] = jnp.zeros_like(s_own)
    s_own[1:2, :] = jnp.sum(d_moe * mid_unit, axis=0, keepdims=True)
    d_mid_unit = d_moe * gains[1:2, :]
    d_mid = mid_r * (d_mid_unit - mid_unit * jnp.mean(d_mid_unit * mid_unit, axis=1, keepdims=True))
    d_mid = cotangent[...].astype(F32) + d_mid
    d_middle[...] = d_mid
    branch[...] = d_mid.astype(BF)
    for k in range(GROUPS):
        d_attn[k] = dot(branch[...], w_proj[GW * k : GW * (k + 1), :], NT).astype(BF)
    for k in range(6, 12):
        wait_bytes(fetches[k][1], fetched.at[k])
    v_s[...] = kv[:, GW:]
    for h in range(GH):
        head_cols = lax.broadcasted_iota(jnp.int32, (1, GW), 1) // HD == h
        qm[h] = jnp.where(head_cols, q[...] * 0.125, 0.0).astype(BF)
    arrive(15 + 3 + 1 + 4 - jnp.where(source == p32, 1, 0))
    for k in range(1, 4):
        there = (z + k) % 4
        push(d_attn.at[there], do_s.at[z], send.at[0], recv.at[0], (there, x, y, c))
    keep(d_attn.at[z], do_s.at[z], recv.at[0])
    z_rows = pl.ds(pl.multiple_of(z * TOK, TOK), TOK)
    for k in range(1, 4):
        push(branch, branch_all.at[z_rows], send.at[1], recv.at[1], ((z + k) % 4, x, y, c))
    keep(branch, branch_all.at[z_rows], recv.at[1])
    wait_bytes(do_s, recv.at[0])
    for h in range(GH):
        head_cols = lax.broadcasted_iota(jnp.int32, (1, GW), 1) // HD == h
        for b in range(4):
            dm[h, b * TOK : (b + 1) * TOK, :] = jnp.where(head_cols, do_s[b], 0.0).astype(BF)
    wait_bytes(p_s, own.at[0])

    def key_sums(left, right, m, pair):
        for k in (1, 2, 3, 0):
            kx = (x + k) % 4
            for b in (2 * pair, 2 * pair + 1):
                cols = block_cols(b, kx)
                total = None
                for h in range(GH):
                    one = dot(left[h, b * TOK :, cols], right[h, b * TOK :, :], TN)
                    total = one if total is None else total + one
                side = GW * (b % 2)
                messages[k, m, :, side : side + GW] = total.astype(BF)
            if k:
                push(messages.at[k, m], parts.at[x, m], send.at[2], recv.at[2], (z, kx, y, c))
            else:
                keep(messages.at[k, m], parts.at[x, m], recv.at[2])

    key_sums(p_s, dm, 0, 0)
    key_sums(p_s, dm, 1, 1)
    near[...] = jnp.zeros_like(near)

    def score_grads(zq):
        rows = pl.ds(zq * TOK, TOK)
        width = (zq + 1) * 512

        def head(h):
            head_cols = lax.broadcasted_iota(jnp.int32, (1, GW), 1) // HD == h
            dp_s[:, :width] = dot(dm[h, rows, :], v_s[:width, :], NT)
            acc = jnp.zeros((TOK, TOK), F32)
            for kb in range(4 * (zq + 1)):
                cols = pl.ds(kb * TOK, TOK)
                acc = acc + p_s[h, rows, cols].astype(F32) * dp_s[:, cols]
            delta = jnp.sum(acc, axis=1, keepdims=True)
            far = jnp.zeros((TOK, TOK), F32)
            for zk in range(zq + 1):
                for kx in range(4):
                    cols = pl.ds((zk * 4 + kx) * TOK, TOK)
                    ds = (p_s[h, rows, cols].astype(F32) * (dp_s[:, cols] - delta)).astype(BF)
                    ds_s[h, rows, cols] = ds
                    if zk < zq - 1:
                        far = far + ds.astype(F32)
                    else:
                        near[h, table_kind(zq, zk, x, kx)] += ds.astype(F32)
            if zq > 1:
                near[h, 3] += far
            o = (dot(ds_s[h, rows, :width], kv[:width, :GW], NN) * 0.125).astype(BF)

            @pl.when(h == 0)
            def _():
                dq[rows, :] = o

            @pl.when(h > 0)
            def _():
                dq[rows, :] = jnp.where(head_cols, o, dq[rows, :])

        loop(0, GH, head)

    score_grads(3)
    score_grads(2)
    key_sums(ds_s, qm, 3, 1)
    score_grads(1)
    score_grads(0)
    key_sums(ds_s, qm, 2, 0)

    def bucket_sums(h):
        for dist in range(2):
            n = near_distance(dist)
            held = near[h, 1 + dist]
            bounds = [-(10**6)] + bucket_edges + [10**6]
            for b in range(BUCKETS):
                low, high = bounds[b], bounds[b + 1]
                if high <= dist * TOK - TOK + 1 or low > dist * TOK + TOK - 1:
                    if dist == 0:
                        tab[h, b : b + 1, :] = jnp.zeros((1, TOK), F32)
                    continue
                inside = jnp.sum(
                    jnp.where((n >= low) & (n < high), held, 0.0), axis=0, keepdims=True
                )
                if dist == 0:
                    tab[h, b : b + 1, :] = inside
                else:
                    tab[h, b : b + 1, :] += inside
        tab[h, BUCKETS - 1 :, :] += jnp.sum(near[h, 3], axis=0, keepdims=True)

    loop(0, GH, bucket_sums)

    wait_bytes(branch_all, recv.at[1])
    att_f[0:GW, :] = dot(attn_part[...], branch_all[...], TN)
    att_f[GW:, :] = jnp.zeros((8, D), F32)
    for j in range(32):
        a_blk[j // 2, j % 2] = att_f[6 * j : 6 * j + 8, :].astype(BF)
    push(a_blk.at[:, 1 - c], a_sib, send.at[4], core_recv.at[1], sib)
    for h in range(GH):
        s_own[2:3, BUCKETS * h : BUCKETS * (h + 1)] = jnp.sum(tab[h].T, axis=0, keepdims=True)

    wait_bytes(a_sib, core_recv.at[1])

    def att_blocks(i):
        there = peer(i)
        j = there[1] * 4 + there[2]
        a_tot[j] = (a_blk[j, c].astype(F32) + a_sib[j].astype(F32)).astype(BF)
        push(a_tot.at[j], a_in.at[p16], send.at[6], recv.at[4], there)

    loop(1, 16, att_blocks)
    a_tot[p16] = (a_blk[p16, c].astype(F32) + a_sib[p16].astype(F32)).astype(BF)
    keep(a_tot.at[p16], a_in.at[p16], recv.at[4])

    wait_bytes(parts, recv.at[2])
    d_qkv[:, :GW] = dq[...]
    for b in range(4):
        rows = slice(b * TOK, (b + 1) * TOK)
        side = GW * (b % 2)
        for m, at in ((2 + b // 2, GW), (b // 2, 2 * GW)):
            total = parts[0, m, :, side : side + GW].astype(F32)
            for k in range(1, 4):
                total = total + parts[k, m, :, side : side + GW].astype(F32)
            d_qkv[rows, at : at + GW] = total.astype(BF)
    d_normed = dot(d_qkv[...], weight[...], NT)
    n_part[...] = d_normed.astype(BF)
    for k in range(1, 4):
        there = (z + k) % 4
        push(
            n_part.at[pl.ds(pl.multiple_of(there * TOK, TOK), TOK)], normed_in.at[z],
            send.at[3], recv.at[3], (there, x, y, c),
        )
    keep(n_part.at[z_rows], normed_in.at[z], recv.at[3])
    along = jnp.sum(d_normed * normed[...].astype(F32), axis=0, keepdims=True)
    s_own[0:1, :] = along / gains[0:1, :]
    push(s_own, s_sib, send.at[8], core_recv.at[2], sib)
    total = dot(normed[...], d_qkv[...], TN)
    for j in range(32):
        q_blk[j // 2, j % 2] = total[24 * j : 24 * j + 24].astype(BF)
    push(q_blk.at[:, 1 - c], q_sib, send.at[5], core_recv.at[0], sib)
    wait_bytes(s_sib, core_recv.at[2])
    s_tot[...] = s_own[...] + s_sib[...]
    loop(1, 16, lambda i: push(s_tot, s_in.at[p16], send.at[9], recv.at[6], peer(i)))
    keep(s_tot, s_in.at[p16], recv.at[6])
    wait_bytes(q_sib, core_recv.at[0])

    def qkv_blocks(i):
        there = peer(i)
        j = there[1] * 4 + there[2]
        q_tot[j] = (q_blk[j, c].astype(F32) + q_sib[j].astype(F32)).astype(BF)
        push(q_tot.at[j], q_in.at[p16], send.at[7], recv.at[5], there)

    loop(1, 16, qkv_blocks)
    q_tot[p16] = (q_blk[p16, c].astype(F32) + q_sib[p16].astype(F32)).astype(BF)
    keep(q_tot.at[p16], q_in.at[p16], recv.at[5])

    wait_bytes(s_in, recv.at[6])
    s_total = s_in[0]
    for k in range(1, 16):
        s_total = s_total + s_in[k]
    s_sum[...] = s_total
    for k in range(1, 4):
        push(s_sum, small_out.at[z], send.at[11], recv.at[8], ((z + k) % 4, x, y, c))
    keep(s_sum, small_out.at[z], recv.at[8])
    wait_bytes(q_in, recv.at[5])
    q_total = q_in[0].astype(F32)
    for k in range(1, 16):
        q_total = q_total + q_in[k].astype(F32)
    for k in range(4):
        qkv_sum[k, 0:6, :] = q_total[6 * k : 6 * k + 6]
        qkv_sum[k, 6:8, :] = jnp.zeros((2, 3 * GW), F32)

    def final(k):
        d = 4 * p32 + k

        @pl.when(d != me)
        def _():
            push(qkv_sum.at[k], qkv_out.at[z], send.at[10], recv.at[7], device_of(d))

        @pl.when(d == me)
        def _():
            keep(qkv_sum.at[k], qkv_out.at[z], recv.at[7])

    loop(0, 4, final)
    wait_bytes(a_in, recv.at[4])
    a_total = a_in[0].astype(F32)
    for k in range(1, 16):
        a_total = a_total + a_in[k].astype(F32)
    att_sum[...] = a_total
    keep(att_sum, att_out, own.at[1])
    wait_bytes(normed_in, recv.at[3])
    d_normed = normed_in[0].astype(F32)
    for k in range(1, 4):
        d_normed = d_normed + normed_in[k].astype(F32)
    v = tok[...].astype(F32)
    r = lax.rsqrt(jnp.mean(v * v, axis=1, keepdims=True) + norm_eps)
    unit = v * r
    d_unit = d_normed * gains[0:1, :]
    d_in = r * (d_unit - unit * jnp.mean(d_unit * unit, axis=1, keepdims=True))
    input_grad[...] = (d_middle[...] + d_in).astype(BF)

    wait_bytes(att_sum, own.at[1])
    wait_bytes(qkv_out, recv.at[7])
    wait_bytes(small_out, recv.at[8])
    wait_bytes(do_s.at[pl.ds(0, 3)], send.at[0])
    wait_bytes(branch_all.at[pl.ds(0, 3 * TOK)], send.at[1])
    wait_bytes(parts.at[pl.ds(0, 3)], send.at[2])
    wait_bytes(normed_in.at[pl.ds(0, 3)], send.at[3])
    wait_bytes(a_sib, send.at[4])
    wait_bytes(q_sib, send.at[5])
    wait_bytes(a_in.at[pl.ds(0, 15)], send.at[6])
    wait_bytes(q_in.at[pl.ds(0, 15)], send.at[7])
    wait_bytes(s_own, send.at[8])
    wait_bytes(s_in.at[pl.ds(0, 15)], send.at[9])

    def sent(k):
        @pl.when(4 * p32 + k != me)
        def _():
            wait_bytes(qkv_sum.at[0], send.at[10])

    loop(0, 4, sent)
    wait_bytes(small_out.at[pl.ds(0, 3)], send.at[11])


def attn_backward(p, *rest):
    probs = (GH, 512, 2048)
    vm = pltpu.VMEM
    return pl.pallas_call(
        attn_backward_kernel,
        out_shape=(
            jax.ShapeDtypeStruct((TOK, D), BF),
            jax.ShapeDtypeStruct((4, 8, 3 * GW), F32),
            jax.ShapeDtypeStruct((8, D), F32),
            jax.ShapeDtypeStruct((4, 8, D), F32),
        ),
        in_specs=[HBM] * (1 + len(rest)),
        out_specs=(VMEM, ANY, ANY, ANY),
        scratch_shapes=[
            vm(probs, BF), vm((2048, GW), BF), vm((4, TOK, GW), BF), vm((GH, 512, GW), BF),
            vm((GH, 512, GW), BF), vm((TOK, 2048), F32), vm(probs, BF), vm((GH, 4, TOK, TOK), F32),
            vm((4, 4, TOK, 2 * GW), BF), vm((4, 4, TOK, 2 * GW), BF), vm((512, D), BF),
            vm((512, GW), BF), vm((GH, BUCKETS, TOK), F32),
            vm((512, 3 * GW), BF), vm((512, D), BF), vm((4, TOK, D), BF), vm((GW + 8, D), F32),
            vm((16, 2, 24, 3 * GW), BF), vm((16, 24, 3 * GW), BF),
            vm((16, 24, 3 * GW), BF), vm((16, 24, 3 * GW), BF),
            vm((16, 2, 8, D), BF), vm((16, 8, D), BF), vm((16, 8, D), BF), vm((16, 8, D), BF),
            vm((8, D), F32), vm((8, D), F32), vm((8, D), F32), vm((16, 8, D), F32),
            vm((4, 8, 3 * GW), F32), vm((8, D), F32), vm((8, D), F32),
            vm((4, TOK, GW), BF), vm((TOK, D), BF), vm((TOK, D), F32),
            vm((512, GW), BF), vm((2048, 2 * GW), BF), vm((1024, D), BF), vm((2 * TOK, 1024), BF),
            vm((TOK, D), F32), vm((8, D), F32), vm((TOK, D), BF), vm((D, D), BF),
            vm((D, 3 * GW), BF), vm((512, D), BF), vm((512, GW), BF), vm((TOK, D), BF),
            DMA((12,)), DMA((9,)), DMA((3,)), DMA((2,)), DMA((12,)),
        ],
        compiler_params=pltpu.CompilerParams(
            collective_id=3, has_side_effects=True, vmem_limit_bytes=63 * 2**20
        ),
        name="attn_backward",
    )(p, *rest)


def per_device(
    tokens,
    gain_attn,
    w_qkv,
    w_attn_out,
    rel_table,
    gain_moe,
    w_in,
    w_out,
    expert_ids,
    gate_values,
    doc_ids,
    cotangent,
):
    z, x, y, c = place()
    own_tokens = tokens.reshape(TOK, D)
    grad_bf = cotangent.reshape(TOK, D)
    grad_out = grad_bf.astype(F32)

    gates = gate_values.reshape(TOK, 2)

    place_in = chip_of(z, x, y) * 2 + c
    lane = jnp.arange(3 * GW, dtype=jnp.int32)[None, :]
    both_gains = jnp.stack([gain_attn, gain_moe]).astype(F32)
    notes = jnp.concatenate(
        [
            jnp.zeros((2, 384), F32),
            jnp.pad(doc_ids.reshape(1, TOK).astype(F32), ((0, 1), (0, 0))),
            jnp.zeros((2, 64), F32),
        ],
        axis=1,
    )
    for k in range(6):
        notes = jnp.where(lane == (place_in % 64) * 6 + k, both_gains[:, k : k + 1], notes)
    out_slab = jnp.concatenate([w_attn_out, jnp.zeros((2, D), BF)], axis=0)
    table = lax.dynamic_slice(rel_table, (0, z * GH), (BUCKETS, GH)).astype(F32)
    (
        attn, attn_part, probs, kv_all, out_weights, d_eo_all, normed, weight, queries, gain_rows,
        picks,
    ) = attn_forward(
        table, own_tokens, w_qkv, notes, out_slab, expert_ids.reshape(TOK, 2), gates, grad_bf
    )
    attention_weight = out_weights[:, :, :, :, :6, :].reshape(D, D)
    home, expert_out, expert_in_grad, expert_out_grad, middle = run_experts(
        attn, attention_weight, own_tokens, gain_rows, picks, d_eo_all, w_in[0], w_out[0]
    )
    input_grad, qkv_sum, att_sum, small_sum = attn_backward(
        probs, queries, kv_all, home, picks, middle, gain_rows, grad_bf, attention_weight, weight,
        normed, attn_part, own_tokens,
    )

    picked = dot(picks, expert_out, NN).reshape(2, TOK, D)
    block_out = middle + gates[:, :1] * picked[0] + gates[:, 1:] * picked[1]
    gate_grad = jnp.sum(picked * grad_out[None], axis=2).T

    qkv_grad = qkv_sum[:, :6, :].reshape(GROUPS, 6, 3, GW).transpose(1, 2, 0, 3).reshape(6, 3 * D)
    attn_out_grad = att_sum[:6]
    gains = lax.dynamic_slice(jnp.sum(small_sum[:, :2, :], axis=0), (0, place_in * 6), (2, 6))
    table_grad = small_sum[:, 2, : GH * BUCKETS].reshape(GROUPS * GH, BUCKETS).T
    return (
        block_out.reshape(1, TOK, D).astype(BF),
        input_grad.reshape(1, TOK, D),
        gate_grad.reshape(1, TOK, 2),
        gains[0],
        qkv_grad,
        attn_out_grad,
        table_grad,
        gains[1],
        expert_in_grad[None],
        expert_out_grad[None],
    )


def solution(mesh):
    torus = Mesh(mesh.devices.reshape(4, 4, 4, 2), AXES)
    in_specs = (
        P(EXP, CTX, None),
        P(AXES),
        P(AXES, None),
        P(AXES, None),
        P(),
        P(AXES),
        P(AXES, None, None),
        P(AXES, None, None),
        P(EXP, CTX, None),
        P(EXP, CTX, None),
        P(EXP, CTX),
        P(EXP, CTX, None),
    )
    out_specs = (
        P(EXP, CTX, None),
        P(EXP, CTX, None),
        P(EXP, CTX, None),
        P(AXES),
        P(AXES, None),
        P(AXES, None),
        P(),
        P(AXES),
        P(AXES, None, None),
        P(AXES, None, None),
    )
    return jax.shard_map(
        per_device, mesh=torus, in_specs=in_specs, out_specs=out_specs, check_vma=False
    )
```
